32 devices in a mesh: dp: 8 (over z, x), tensor: 4 (over y, core).
Axes of the slice: x: 2, y: 2, z: 4, core: 2. Of those that a mesh axis runs over, the one named last changes fastest.
Arguments:
- block_input: bfloat16 [6304, 768], P(('dp', 'tensor')), may hold values from -6 to 6
- first_norm: bfloat16 [768], P('dp'), may hold values from 0.5 to 1.5
- first_qkv: bfloat16 [768, 3, 768], P('dp', None, 'tensor')
- first_out: bfloat16 [768, 768], P('tensor', 'dp'), may hold values from -0.875 to 0.875
- second_norm: bfloat16 [768], P('dp'), may hold values from 0.5 to 1.5
- dense_up: bfloat16 [768, 3072], P('dp', 'tensor'), may hold values from -0.21875 to 0.21875
- dense_down: bfloat16 [3072, 768], P('tensor', 'dp'), may hold values from -0.15625 to 0.15625
- third_norm: bfloat16 [768], P('dp'), may hold values from 0.5 to 1.5
- second_qkv: bfloat16 [768, 3, 768], P('dp', None, 'tensor')
- second_out: bfloat16 [768, 768], P('tensor', 'dp'), may hold values from -0.875 to 0.875
- fourth_norm: bfloat16 [768], P('dp'), may hold values from 0.5 to 1.5
- router_weight: bfloat16 [768, 8], P('dp'), may hold values from -0.4375 to 0.4375
- expert_up: bfloat16 [8, 768, 3072], P(None, 'dp', 'tensor'), may hold values from -0.21875 to 0.21875
- expert_down: bfloat16 [8, 3072, 768], P(None, 'tensor', 'dp'), may hold values from -0.4375 to 0.4375
- expert_ids: int32 [6304, 2], P('dp'), may hold values from 0 to 7, as said below
- expert_slots: int32 [6304, 2], P('dp'), may hold values from 0 to 197, as said below
- image_counts: int32 [8], P('dp'), may hold values from 3 to 4, as said below
- cotangent: bfloat16 [6304, 768], P(('dp', 'tensor')), may hold values from -6 to 6
Outputs:
- block_output: float32 [6304, 768], P(('dp', 'tensor'))
- input_grad: float32 [6304, 768], P(('dp', 'tensor'))
- grad_first_norm: float32 [768], P('dp')
- grad_first_qkv: float32 [768, 3, 768], P('dp', None, 'tensor')
- grad_first_out: float32 [768, 768], P('tensor', 'dp')
- grad_second_norm: float32 [768], P('dp')
- grad_dense_up: float32 [768, 3072], P('dp', 'tensor')
- grad_dense_down: float32 [3072, 768], P('tensor', 'dp')
- grad_third_norm: float32 [768], P('dp')
- grad_second_qkv: float32 [768, 3, 768], P('dp', None, 'tensor')
- grad_second_out: float32 [768, 768], P('tensor', 'dp')
- grad_fourth_norm: float32 [768], P('dp')
- grad_router: float32 [768, 8], P('dp')
- grad_expert_up: float32 [8, 768, 3072], P(None, 'dp', 'tensor')
- grad_expert_down: float32 [8, 3072, 768], P(None, 'tensor', 'dp')
- clipped_first_qkv: float32 [768, 3, 768], P('dp', None, 'tensor')
- clipped_second_qkv: float32 [768, 3, 768], P('dp', None, 'tensor')
- clip_scales: float32 [2, 12], P(None, 'tensor')
The draws below stay inside these ranges and needn't reach their ends.
Inputs may be any that keep to these rules, and one draw needn't show every extreme that they name: `expert_ids`: each token names two different experts. `expert_slots`: the rank of a token's choice among the choices of its expert within its group of 788 tokens, counted in token order and then choice order; ranks of 197 or more are given as 197 and mark dropped choices. `image_counts`: the live images of a group are its first image slots.
All inputs are finite; a program needn't handle non-finite values.
Results may differ from the reference program's by a relative error of at most 0.04.
Values may be sent and summed in bfloat16 or wider, within the bound.
No kernel may reach another device: no remote copies, remote signals or barrier semaphores. Data moves between devices by JAX's collectives and lax.ppermute only.
A program may use at most 256 MiB of HBM per device.

```python
import jax
import jax.numpy as jnp
from jax import lax

D = 768
HEADS = 12
HD = 64
FF = 3072
EXPERTS = 8
L = 197
IMG_DEV = 4
GROUPS = 8
TG = 788
TOKENS = 6304
CAP = 197


def shared_signs(key):
    sign_key = jax.random.fold_in(key, 13)
    return (2 * jax.random.randint(sign_key, (D,), 0, 2) - 1).astype(jnp.float32)


def qkv_weights(key, salt):
    own_key = jax.random.fold_in(key, salt)
    normal_key, scale_key, plant_key = jax.random.split(own_key, 3)
    base_draw = jax.random.normal(normal_key, (D, 3, HEADS * HD), jnp.float32) * D ** (-0.5)
    head_scale = jnp.exp(jax.random.uniform(scale_key, (2, HEADS), jnp.float32, jnp.log(0.6), jnp.log(1.6)))
    column = jnp.repeat(head_scale, HD, axis=1)
    scales = jnp.concatenate([column, jnp.ones((1, HEADS * HD), jnp.float32)], axis=0)
    beta = (30.0 / (D * HD ** 0.5)) ** 0.5
    direction = jax.random.normal(plant_key, (HEADS * HD,), jnp.float32)
    signs = shared_signs(key) * D ** (-0.5)
    planted = beta * signs[:, None] * direction[None, :]
    extra = jnp.stack([planted, planted, jnp.zeros_like(planted)], axis=1)
    return base_draw * scales[None] + extra


def draw_first_qkv(key, part):
    return qkv_weights(key, 3).astype(jnp.bfloat16)


def draw_second_qkv(key, part):
    return qkv_weights(key, 7).astype(jnp.bfloat16)


def draw_block_input(key, part):
    own_key = jax.random.fold_in(key, 17)
    noise_key, order_key = jax.random.split(own_key)
    noise = jnp.clip(jax.random.normal(noise_key, (TOKENS, D), jnp.float32), -5.0, 5.0)
    order = jax.random.permutation(order_key, GROUPS)
    share = 0.6 * (order.astype(jnp.float32) + 1.0) / GROUPS
    group_sign = (1 - 2 * (order % 2)).astype(jnp.float32)
    row_share = jnp.repeat(share, TG)
    row_sign = jnp.repeat(group_sign, TG)
    signs = shared_signs(key)
    return (jnp.sqrt(1.0 - row_share)[:, None] * noise + (jnp.sqrt(row_share) * row_sign)[:, None] * signs[None, :]).astype(jnp.bfloat16)


def routing(key):
    route_key = jax.random.fold_in(key, 11)
    first_key, second_key, shift_key = jax.random.split(route_key, 3)
    base_ids = jax.random.randint(first_key, (GROUPS, TG), 0, EXPERTS + 2)
    shift_ids = jax.random.randint(shift_key, (GROUPS, 1), 0, EXPERTS)
    first_ids = (base_ids % EXPERTS + shift_ids) % EXPERTS
    second_ids = (first_ids + 1 + jax.random.randint(second_key, (GROUPS, TG), 0, EXPERTS - 1)) % EXPERTS
    both_ids = jnp.stack([first_ids, second_ids], axis=-1).reshape(GROUPS, 2 * TG)
    onehot = (both_ids[:, :, None] == jnp.arange(EXPERTS)[None, None, :]).astype(jnp.int32)
    ranks = jnp.sum((jnp.cumsum(onehot, axis=1) - 1) * onehot, axis=-1)
    slot_ranks = jnp.minimum(ranks, CAP)
    return (both_ids.reshape(TOKENS, 2).astype(jnp.int32), slot_ranks.reshape(TOKENS, 2).astype(jnp.int32))


def draw_expert_ids(key, part):
    return routing(key)[0]


def draw_expert_slots(key, part):
    return routing(key)[1]


def draw_image_counts(key, part):
    count_key = jax.random.fold_in(key, 5)
    first_key, second_key, third_key = jax.random.split(count_key, 3)
    counts = IMG_DEV - jax.random.randint(first_key, (GROUPS,), 0, 2)
    full_group = jax.random.randint(second_key, (), 0, GROUPS)
    short_group = (full_group + 1 + jax.random.randint(third_key, (), 0, GROUPS - 1)) % GROUPS
    counts = counts.at[full_group].set(IMG_DEV).at[short_group].set(IMG_DEV - 1)
    return counts.astype(jnp.int32)


def level_of(rng, dims, shards, least, high):
    loudness = 1.0
    for dim, blocks in shards:
        draws = jax.random.uniform(jax.random.fold_in(jax.random.fold_in(rng, 6), dim), (blocks,), jnp.float32, least / len(shards), high / len(shards))
        loudness = loudness * jnp.repeat(jnp.exp(draws), dims[dim] // blocks).reshape((-1,) + (1,) * (len(dims) - 1 - dim))
    return loudness


def bell_draw(key, extent, width, most, cuts=(), kind=jnp.bfloat16):
    values = width * jax.random.normal(key, extent, jnp.float32)
    if cuts:
        values = values * level_of(key, extent, cuts, -0.22, 0.18)
    return jnp.clip(values, -most, most).astype(kind)


def setup_inputs(seed: int = 0) -> dict:
    key_of = jax.random.split(jax.random.key(seed), 19)
    block_input = draw_block_input(jax.random.fold_in(key_of[18], 71), 0)
    first_norm = jnp.clip(1.0 + 0.1 * jax.random.normal(key_of[1], (D,), jnp.float32), 0.5, 1.5).astype(jnp.bfloat16)
    first_qkv = draw_first_qkv(jax.random.fold_in(key_of[18], 71), 0)
    first_out = bell_draw(key_of[3], (D, D), (D // 16) ** -0.5, 0.875, ((0, 4), (1, 8)))
    second_norm = jnp.clip(1.0 + 0.1 * jax.random.normal(key_of[4], (D,), jnp.float32), 0.5, 1.5).astype(jnp.bfloat16)
    dense_up = bell_draw(key_of[5], (D, FF), D ** -0.5, 0.21875, ((0, 8), (1, 4)))
    dense_down = bell_draw(key_of[6], (FF, D), (FF // 2) ** -0.5, 0.15625, ((0, 4), (1, 8)))
    third_norm = jnp.clip(1.0 + 0.1 * jax.random.normal(key_of[7], (D,), jnp.float32), 0.5, 1.5).astype(jnp.bfloat16)
    second_qkv = draw_second_qkv(jax.random.fold_in(key_of[18], 71), 0)
    second_out = bell_draw(key_of[9], (D, D), (D // 16) ** -0.5, 0.875, ((0, 4), (1, 8)))
    fourth_norm = jnp.clip(1.0 + 0.1 * jax.random.normal(key_of[10], (D,), jnp.float32), 0.5, 1.5).astype(jnp.bfloat16)
    router_weight = bell_draw(key_of[11], (D, EXPERTS), (D // 4) ** -0.5, 0.4375, ((0, 8),))
    expert_up = bell_draw(key_of[12], (EXPERTS, D, FF), D ** -0.5, 0.21875, ((1, 8), (2, 4)))
    expert_down = bell_draw(key_of[13], (EXPERTS, FF, D), (FF // 16) ** -0.5, 0.4375, ((1, 4), (2, 8)))
    expert_ids = draw_expert_ids(jax.random.fold_in(key_of[18], 71), 0)
    expert_slots = draw_expert_slots(jax.random.fold_in(key_of[18], 71), 0)
    image_counts = draw_image_counts(jax.random.fold_in(key_of[18], 71), 0)
    cotangent = bell_draw(key_of[17], (TOKENS, D), 1.0, 6.0, ((0, 32),))
    return {"block_input": block_input, "first_norm": first_norm, "first_qkv": first_qkv, "first_out": first_out, "second_norm": second_norm, "dense_up": dense_up, "dense_down": dense_down, "third_norm": third_norm, "second_qkv": second_qkv, "second_out": second_out, "fourth_norm": fourth_norm, "router_weight": router_weight, "expert_up": expert_up, "expert_down": expert_down, "expert_ids": expert_ids, "expert_slots": expert_slots, "image_counts": image_counts, "cotangent": cotangent}


epsilon = 1e-06
clip_tau = 2.5
highest = lax.Precision.HIGHEST

@jax.custom_vjp
def low(v):
    return lax.optimization_barrier(v.astype(jnp.bfloat16)).astype(jnp.float32)

@jax.custom_vjp
def low_back(v):
    return v

def low_keep(v):
    return (low(v), None)

def low_pass(kept, grad):
    return (grad,)

def back_keep(v):
    return (v, None)

def back_low(kept, grad):
    return (low(grad),)
low.defvjp(low_keep, low_pass)
low_back.defvjp(back_keep, back_low)

def layer_norm(values, norm_gain):
    center = values - lax.optimization_barrier(jnp.mean(values, axis=-1, keepdims=True))
    spread = lax.optimization_barrier(jnp.mean(center * center, axis=-1, keepdims=True))
    return center * lax.rsqrt(spread + epsilon) * norm_gain

def exact_gelu(values):
    return jax.nn.gelu(values, approximate=False)

def attention(normed, weight_qkv, weight_out, live_images):
    projected = low_back(low(jnp.einsum('rd,dcf->rcf', normed, weight_qkv, precision=highest)))
    pieces = projected.reshape(IMG_DEV, L, 3, HEADS, HD)

    def one_image(operands):
        queries, keyset, values = operands
        scores = low_back(jnp.einsum('qhd,khd->hqk', queries, keyset, precision=highest) * HD ** (-0.5))
        attn_probs = jax.nn.softmax(scores, axis=-1)
        mixed_out = jnp.einsum('hqk,khd->qhd', low(attn_probs), values, precision=highest)
        return (mixed_out, lax.optimization_barrier(jnp.max(scores, axis=(1, 2))))
    outputs, peaks = lax.map(jax.checkpoint(one_image), (pieces[:, :, 0], pieces[:, :, 1], pieces[:, :, 2]))
    head_peak = lax.optimization_barrier(jnp.max(jnp.where(live_images[:, None], peaks, -1e+30), axis=0))
    attended = low_back(low(outputs.reshape(IMG_DEV * L, HEADS * HD)))
    return (low_back(jnp.dot(attended, weight_out, precision=highest)), head_peak)

def dense_mlp(normed, weight_up, weight_down):
    hidden = low_back(jnp.dot(normed, weight_up, precision=highest))
    active = low(exact_gelu(hidden))
    return low_back(jnp.dot(active, weight_down, precision=highest))

def experts_mlp(normed, weight_route, weight_up, weight_down, group_ids, group_slots, live_rows):
    logits = low_back(jnp.dot(normed, weight_route, precision=highest))
    route = jax.nn.softmax(logits, axis=-1)
    kept_mask = group_slots < CAP
    pair_number = jnp.arange(2 * TG, dtype=jnp.int32)
    slot_index = (group_ids * CAP + group_slots).reshape(-1).astype(jnp.int32)
    kept_flat = kept_mask.reshape(-1)
    write_target = jnp.where(kept_flat, slot_index, EXPERTS * CAP + pair_number).astype(jnp.int32)
    read_target = jnp.where(kept_flat, slot_index, EXPERTS * CAP).astype(jnp.int32)
    pair_of_slot = jnp.zeros((EXPERTS * CAP + 2 * TG,), jnp.int32).at[write_target].set(pair_number)[:EXPERTS * CAP]
    slot_filled = jnp.zeros((EXPERTS * CAP + 2 * TG,), jnp.float32).at[write_target].set(1.0)[:EXPERTS * CAP]
    chosen = (group_ids[:, :, None] == jnp.arange(EXPERTS, dtype=jnp.int32)[None, None, :]).astype(jnp.float32)
    gates = lax.optimization_barrier(jnp.sum(chosen * route[:, None, :], axis=-1)) * kept_mask.astype(jnp.float32) * live_rows[:, None]
    dispatched = (normed[pair_of_slot // 2] * slot_filled[:, None]).reshape(EXPERTS, CAP, D)
    hidden = low_back(jnp.einsum('ecd,edf->ecf', dispatched, weight_up, precision=highest))
    active = low(exact_gelu(hidden))
    expert_result = low_back(jnp.einsum('ecf,efd->ecd', active, weight_down, precision=highest))
    padded = jnp.concatenate([expert_result.reshape(EXPERTS * CAP, D), jnp.zeros((1, D), jnp.float32)], axis=0)
    combined = lax.optimization_barrier(jnp.sum(gates[:, :, None] * padded[read_target].reshape(TG, 2, D), axis=1))
    return low_back(combined)

def group_forward(weights, residual, group_ids, group_slots, live_count):
    norm_one, qkv_one, out_one, norm_two, up_dense, down_dense, norm_three, qkv_two, out_two, norm_four, route_weight, up_expert, down_expert = weights
    live_images = jnp.arange(IMG_DEV, dtype=jnp.int32) < live_count
    live_rows = (jnp.arange(TG, dtype=jnp.int32) // L < live_count).astype(jnp.float32)
    branch, peak_one = attention(low(layer_norm(residual, norm_one)), qkv_one, out_one, live_images)
    residual = residual + branch
    residual = residual + dense_mlp(low(layer_norm(residual, norm_two)), up_dense, down_dense)
    branch, peak_two = attention(low(layer_norm(residual, norm_three)), qkv_two, out_two, live_images)
    residual = residual + branch
    residual = residual + experts_mlp(low(layer_norm(residual, norm_four)), route_weight, up_expert, down_expert, group_ids, group_slots, live_rows)
    return (residual * live_rows[:, None], (peak_one, peak_two))

def clip_root(head_peak):
    return jnp.sqrt(clip_tau / jnp.maximum(head_peak, clip_tau))

def clip_columns(weight_qkv, head_peak):
    column = jnp.repeat(clip_root(head_peak), HD)
    scales = jnp.stack([column, column, jnp.ones_like(column)])
    return weight_qkv.astype(jnp.float32) * scales[None]

def reference(block_input, first_norm, first_qkv, first_out, second_norm, dense_up, dense_down, third_norm, second_qkv, second_out, fourth_norm, router_weight, expert_up, expert_down, expert_ids, expert_slots, image_counts, cotangent):
    weights = tuple((w.astype(jnp.float32) for w in (first_norm, first_qkv, first_out, second_norm, dense_up, dense_down, third_norm, second_qkv, second_out, fourth_norm, router_weight, expert_up, expert_down)))
    inputs = block_input.astype(jnp.float32).reshape(GROUPS, TG, D)
    group_ids = expert_ids.reshape(GROUPS, TG, 2)
    group_slots = expert_slots.reshape(GROUPS, TG, 2)

    def forward(weight_set, start):

        def one_group(operands):
            residual, ids_here, slots_here, count_here = operands
            return group_forward(weight_set, residual, ids_here, slots_here, count_here)
        outputs, (peak_one, peak_two) = lax.map(jax.checkpoint(one_group), (start, group_ids, group_slots, image_counts))
        return (outputs, (lax.optimization_barrier(jnp.max(peak_one, axis=0)), lax.optimization_barrier(jnp.max(peak_two, axis=0))))
    outputs, pullback, peaks = jax.vjp(forward, weights, inputs, has_aux=True)
    grad_weights, grad_input = pullback(cotangent.astype(jnp.float32).reshape(GROUPS, TG, D))
    scales_out = jnp.stack([clip_root(peaks[0]), clip_root(peaks[1])])
    return (outputs.reshape(TOKENS, D), grad_input.reshape(TOKENS, D), grad_weights[0], grad_weights[1], grad_weights[2], grad_weights[3], grad_weights[4], grad_weights[5], grad_weights[6], grad_weights[7], grad_weights[8], grad_weights[9], grad_weights[10], grad_weights[11], grad_weights[12], clip_columns(first_qkv, peaks[0]), clip_columns(second_qkv, peaks[1]), scales_out)
```

```python
import jax
import jax.numpy as jnp
from jax import lax
from jax.sharding import PartitionSpec as P

HD = 64
L = 197
CAP = 197


epsilon = 1e-06
clip_tau = 2.5


def layer_norm(values, norm_gain):
    center = values - jnp.mean(values, axis=-1, keepdims=True)
    spread = jnp.mean(center * center, axis=-1, keepdims=True)
    return center * lax.rsqrt(spread + epsilon) * norm_gain


def exact_gelu(values):
    return jax.nn.gelu(values, approximate=False)


def gelu_back(values, upstream):
    return jax.vjp(exact_gelu, values)[1](upstream)[0]


def norm_back(residual, norm_gain, upstream):
    pullback = jax.vjp(layer_norm, residual, norm_gain.astype(jnp.float32))[1]
    return pullback(upstream)


def gather_rows(values):
    return lax.all_gather(values, "tensor", axis=0, tiled=True)


def scatter_rows(values):
    return lax.psum_scatter(
        values.astype(jnp.bfloat16), "tensor", scatter_dimension=0, tiled=True
    ).astype(jnp.float32)


def sum_gains(first_gain, second_gain):
    return lax.psum((first_gain, second_gain), "tensor")


def split_heads(projected, images, head_size):
    row_count, triple, columns = projected.shape
    pieces = projected.reshape(images, row_count // images, triple, columns // head_size, head_size)
    return (pieces[:, :, 0], pieces[:, :, 1], pieces[:, :, 2])


def attend_scores(queries, keyset, head_size):
    scores = jnp.einsum("iqhd,ikhd->ihqk", queries, keyset, preferred_element_type=jnp.float32)
    return scores * head_size ** (-0.5)


def attend_forward(normed_full, weight_qkv, images, head_size, live_images):
    projected = jnp.einsum(
        "rd,dcf->rcf", normed_full, weight_qkv, preferred_element_type=jnp.float32
    ).astype(jnp.bfloat16)
    queries, keyset, values = split_heads(projected, images, head_size)
    scores = attend_scores(queries, keyset, head_size)
    head_peak = jnp.max(jnp.where(live_images[:, None, None, None], scores, -1e30), axis=(0, 2, 3))
    attn_probs = jax.nn.softmax(scores, axis=-1).astype(jnp.bfloat16)
    attended = jnp.einsum("ihqk,ikhd->iqhd", attn_probs, values, preferred_element_type=jnp.float32)
    return (projected, attended.astype(jnp.bfloat16).reshape(normed_full.shape[0], -1), head_peak)


def attend_backward(projected, grad_attended, images, head_size):
    queries, keyset, values = split_heads(projected, images, head_size)
    scores = attend_scores(queries, keyset, head_size)
    attn_probs = jax.nn.softmax(scores, axis=-1)
    grad_heads = grad_attended.reshape(queries.shape)
    grad_values = jnp.einsum(
        "ihqk,iqhd->ikhd",
        attn_probs.astype(jnp.bfloat16),
        grad_heads,
        preferred_element_type=jnp.float32,
    )
    grad_probs = jnp.einsum(
        "iqhd,ikhd->ihqk", grad_heads, values, preferred_element_type=jnp.float32
    )
    grad_scores = attn_probs * (
        grad_probs - jnp.sum(grad_probs * attn_probs, axis=-1, keepdims=True)
    )
    grad_scores = grad_scores.astype(jnp.bfloat16)
    factor = head_size ** (-0.5)
    grad_queries = (
        jnp.einsum("ihqk,ikhd->iqhd", grad_scores, keyset, preferred_element_type=jnp.float32)
        * factor
    )
    grad_keyset = (
        jnp.einsum("ihqk,iqhd->ikhd", grad_scores, queries, preferred_element_type=jnp.float32)
        * factor
    )
    stacked = jnp.stack([grad_queries, grad_keyset, grad_values], axis=2).astype(jnp.bfloat16)
    return stacked.reshape(projected.shape)


def block_attention(residual, norm_gain, weight_qkv, weight_out, images, head_size, live_images):
    normed = layer_norm(residual, norm_gain.astype(jnp.float32)).astype(jnp.bfloat16)
    normed_full = gather_rows(normed)
    projected, attended, head_peak = attend_forward(
        normed_full, weight_qkv, images, head_size, live_images
    )
    branch = scatter_rows(jnp.dot(attended, weight_out, preferred_element_type=jnp.float32))
    return (residual + branch, (normed_full, projected, attended), head_peak)


def block_attention_back(
    residual, upstream, norm_gain, weight_qkv, weight_out, stored, images, head_size
):
    normed_full, projected, attended = stored
    grad_full = gather_rows(upstream.astype(jnp.bfloat16))
    grad_out = jnp.einsum("rf,rd->fd", attended, grad_full, preferred_element_type=jnp.float32)
    grad_attended = jnp.einsum(
        "rd,fd->rf", grad_full, weight_out, preferred_element_type=jnp.float32
    ).astype(jnp.bfloat16)
    grad_projected = attend_backward(projected, grad_attended, images, head_size)
    grad_qkv = jnp.einsum(
        "rd,rcf->dcf", normed_full, grad_projected, preferred_element_type=jnp.float32
    )
    grad_normed = scatter_rows(
        jnp.einsum("rcf,dcf->rd", grad_projected, weight_qkv, preferred_element_type=jnp.float32)
    )
    grad_residual, grad_gain = norm_back(residual, norm_gain, grad_normed)
    return (upstream + grad_residual, grad_gain, grad_qkv, grad_out)


def block_mlp(residual, norm_gain, weight_up, weight_down):
    normed = layer_norm(residual, norm_gain.astype(jnp.float32)).astype(jnp.bfloat16)
    normed_full = gather_rows(normed)
    hidden = jnp.dot(normed_full, weight_up, preferred_element_type=jnp.float32)
    active = exact_gelu(hidden).astype(jnp.bfloat16)
    branch = scatter_rows(jnp.dot(active, weight_down, preferred_element_type=jnp.float32))
    return (residual + branch, (normed_full, hidden, active))


def block_mlp_back(residual, upstream, norm_gain, weight_up, weight_down, stored):
    normed_full, hidden, active = stored
    grad_full = gather_rows(upstream.astype(jnp.bfloat16))
    grad_down = jnp.einsum("rf,rd->fd", active, grad_full, preferred_element_type=jnp.float32)
    grad_active = jnp.einsum(
        "rd,fd->rf", grad_full, weight_down, preferred_element_type=jnp.float32
    )
    grad_hidden = gelu_back(hidden, grad_active).astype(jnp.bfloat16)
    grad_up = jnp.einsum("rd,rf->df", normed_full, grad_hidden, preferred_element_type=jnp.float32)
    grad_normed = scatter_rows(
        jnp.einsum("rf,df->rd", grad_hidden, weight_up, preferred_element_type=jnp.float32)
    )
    grad_residual, grad_gain = norm_back(residual, norm_gain, grad_normed)
    return (upstream + grad_residual, grad_gain, grad_up, grad_down)


def clip_root(head_peak):
    return jnp.sqrt(clip_tau / jnp.maximum(head_peak, clip_tau))


def clip_columns(weight_local, head_root, head_size):
    column = jnp.repeat(head_root, head_size)
    scales = jnp.stack([column, column, jnp.ones_like(column)])
    return weight_local.astype(jnp.float32) * scales[None]


def local(
    block_input,
    first_norm,
    first_qkv,
    first_out,
    second_norm,
    dense_up,
    dense_down,
    third_norm,
    second_qkv,
    second_out,
    fourth_norm,
    router_weight,
    expert_up,
    expert_down,
    expert_ids,
    expert_slots,
    image_counts,
    cotangent,
):
    rows_local = block_input.shape[0]
    rows_full = rows_local * lax.axis_size("tensor")
    images = rows_full // L
    head_size = HD
    experts = expert_up.shape[0]
    capacity = CAP
    first_row = lax.axis_index("tensor") * rows_local
    live_count = image_counts[0]
    local_live = ((first_row + jnp.arange(rows_local)) // L < live_count).astype(jnp.float32)
    full_live = (jnp.arange(rows_full) // L < live_count).astype(jnp.float32)
    live_images = jnp.arange(images) < live_count

    def dense_fetch():
        return (
            lax.all_gather(first_norm, "dp", axis=0, tiled=True),
            lax.all_gather(first_qkv, "dp", axis=0, tiled=True),
            lax.all_gather(first_out, "dp", axis=1, tiled=True),
            lax.all_gather(second_norm, "dp", axis=0, tiled=True),
            lax.all_gather(dense_up, "dp", axis=0, tiled=True),
            lax.all_gather(dense_down, "dp", axis=1, tiled=True),
        )

    def moe_fetch():
        return (
            lax.all_gather(third_norm, "dp", axis=0, tiled=True),
            lax.all_gather(second_qkv, "dp", axis=0, tiled=True),
            lax.all_gather(second_out, "dp", axis=1, tiled=True),
            lax.all_gather(fourth_norm, "dp", axis=0, tiled=True),
            lax.all_gather(router_weight, "dp", axis=0, tiled=True),
            lax.all_gather(expert_up, "dp", axis=1, tiled=True),
            lax.all_gather(expert_down, "dp", axis=2, tiled=True),
        )

    dense_full = dense_fetch()
    residual_zero = block_input.astype(jnp.float32)
    residual_one, attn_first, peak_first = block_attention(
        residual_zero, dense_full[0], dense_full[1], dense_full[2], images, head_size, live_images
    )
    residual_two, mlp_stored = block_mlp(residual_one, dense_full[3], dense_full[4], dense_full[5])
    moe_full = moe_fetch()
    residual_three, attn_second, peak_second = block_attention(
        residual_two, moe_full[0], moe_full[1], moe_full[2], images, head_size, live_images
    )
    moe_normed = layer_norm(residual_three, moe_full[3].astype(jnp.float32)).astype(jnp.bfloat16)
    moe_input = gather_rows(moe_normed)
    logits = jnp.dot(moe_input, moe_full[4], preferred_element_type=jnp.float32)
    route_probs = jax.nn.softmax(logits, axis=-1)
    kept_mask = expert_slots < capacity
    pair_number = jnp.arange(2 * rows_full, dtype=jnp.int32)
    slot_index = (expert_ids * capacity + expert_slots).reshape(-1)
    kept_flat = kept_mask.reshape(-1)
    write_target = jnp.where(kept_flat, slot_index, experts * capacity + pair_number)
    target = jnp.where(kept_flat, slot_index, experts * capacity)
    pair_of_slot = (
        jnp.zeros((experts * capacity + 2 * rows_full,), jnp.int32)
        .at[write_target]
        .set(pair_number)[: experts * capacity]
    )
    slot_filled = (
        jnp.zeros((experts * capacity + 2 * rows_full,), jnp.float32)
        .at[write_target]
        .set(1.0)[: experts * capacity]
    )
    chosen = (expert_ids[:, :, None] == jnp.arange(experts)[None, None, :]).astype(jnp.float32)
    keep_live = kept_mask.astype(jnp.float32) * full_live[:, None]
    gates = jnp.sum(chosen * route_probs[:, None, :], axis=-1) * keep_live
    slot_token = pair_of_slot // 2
    slot_gate = gates.reshape(-1)[pair_of_slot] * slot_filled
    dispatched = (moe_input[slot_token] * slot_filled[:, None].astype(jnp.bfloat16)).reshape(
        experts, capacity, -1
    )
    expert_hidden = jnp.einsum(
        "ecd,edf->ecf", dispatched, moe_full[5], preferred_element_type=jnp.float32
    )
    expert_act = exact_gelu(expert_hidden).astype(jnp.bfloat16)
    expert_result = jnp.einsum(
        "ecf,efd->ecd", expert_act, moe_full[6], preferred_element_type=jnp.float32
    )
    feature_count = expert_result.shape[2]
    padded_result = jnp.concatenate(
        [
            expert_result.reshape(experts * capacity, feature_count),
            jnp.zeros((1, feature_count), jnp.float32),
        ],
        axis=0,
    )
    pair_result = padded_result[target].reshape(rows_full, 2, feature_count)
    combined = jnp.sum(gates[:, :, None] * pair_result, axis=1)
    residual_four = residual_three + scatter_rows(combined)
    block_output = residual_four * local_live[:, None]
    peak_first_all, peak_second_all = lax.pmax((peak_first, peak_second), "dp")
    root_first = clip_root(peak_first_all)
    root_second = clip_root(peak_second_all)
    clipped_first = clip_columns(first_qkv, root_first, head_size)
    clipped_second = clip_columns(second_qkv, root_second, head_size)
    clip_scales = jnp.stack([root_first, root_second])
    moe_back = moe_fetch()
    grad_four = cotangent.astype(jnp.float32) * local_live[:, None]
    moe_grad_full = gather_rows(grad_four.astype(jnp.bfloat16))
    partial_gates = jnp.sum(moe_grad_full.astype(jnp.float32)[:, None, :] * pair_result, axis=-1)
    grad_gates = lax.psum(partial_gates, "tensor")
    grad_result = (slot_gate[:, None] * moe_grad_full[slot_token].astype(jnp.float32)).astype(
        jnp.bfloat16
    )
    grad_result = grad_result.reshape(experts, capacity, feature_count)
    grad_expert_down = jnp.einsum(
        "ecf,ecd->efd", expert_act, grad_result, preferred_element_type=jnp.float32
    )
    grad_act = jnp.einsum(
        "ecd,efd->ecf", grad_result, moe_back[6], preferred_element_type=jnp.float32
    )
    grad_hidden = gelu_back(expert_hidden, grad_act).astype(jnp.bfloat16)
    grad_expert_up = jnp.einsum(
        "ecd,ecf->edf", dispatched, grad_hidden, preferred_element_type=jnp.float32
    )
    grad_dispatch = jnp.einsum(
        "ecf,edf->ecd", grad_hidden, moe_back[5], preferred_element_type=jnp.float32
    )
    grad_dispatch = jnp.concatenate(
        [
            grad_dispatch.reshape(experts * capacity, feature_count),
            jnp.zeros((1, feature_count), jnp.float32),
        ],
        axis=0,
    )
    grad_from_experts = jnp.sum(grad_dispatch[target].reshape(rows_full, 2, feature_count), axis=1)
    grad_picked = grad_gates * keep_live
    grad_probs = jnp.sum(chosen * grad_picked[:, :, None], axis=1)
    grad_logits = route_probs * (
        grad_probs - jnp.sum(grad_probs * route_probs, axis=-1, keepdims=True)
    )
    grad_logits = grad_logits.astype(jnp.bfloat16)
    grad_router = jnp.einsum(
        "rd,re->de", moe_input, grad_logits, preferred_element_type=jnp.float32
    )
    local_logits = lax.dynamic_slice_in_dim(grad_logits, first_row, rows_local, 0)
    grad_moe_normed = scatter_rows(grad_from_experts) + jnp.einsum(
        "re,de->rd", local_logits, moe_back[4], preferred_element_type=jnp.float32
    )
    grad_rows_four, grad_fourth_norm = norm_back(residual_three, moe_back[3], grad_moe_normed)
    grad_three = grad_four + grad_rows_four
    grad_two, grad_third_norm, grad_second_qkv, grad_second_out = block_attention_back(
        residual_two,
        grad_three,
        moe_back[0],
        moe_back[1],
        moe_back[2],
        attn_second,
        images,
        head_size,
    )
    third_sum, fourth_sum = sum_gains(grad_third_norm, grad_fourth_norm)
    moe_owned = (
        lax.psum_scatter(third_sum, "dp", scatter_dimension=0, tiled=True),
        lax.psum_scatter(grad_second_qkv, "dp", scatter_dimension=0, tiled=True),
        lax.psum_scatter(grad_second_out, "dp", scatter_dimension=1, tiled=True),
        lax.psum_scatter(fourth_sum, "dp", scatter_dimension=0, tiled=True),
        lax.psum_scatter(grad_router, "dp", scatter_dimension=0, tiled=True),
        lax.psum_scatter(grad_expert_up, "dp", scatter_dimension=1, tiled=True),
        lax.psum_scatter(grad_expert_down, "dp", scatter_dimension=2, tiled=True),
    )
    dense_back = dense_fetch()
    grad_one, grad_second_norm, grad_dense_up, grad_dense_down = block_mlp_back(
        residual_one, grad_two, dense_back[3], dense_back[4], dense_back[5], mlp_stored
    )
    input_grad, grad_first_norm, grad_first_qkv, grad_first_out = block_attention_back(
        residual_zero,
        grad_one,
        dense_back[0],
        dense_back[1],
        dense_back[2],
        attn_first,
        images,
        head_size,
    )
    first_sum, second_sum = sum_gains(grad_first_norm, grad_second_norm)
    dense_owned = (
        lax.psum_scatter(first_sum, "dp", scatter_dimension=0, tiled=True),
        lax.psum_scatter(grad_first_qkv, "dp", scatter_dimension=0, tiled=True),
        lax.psum_scatter(grad_first_out, "dp", scatter_dimension=1, tiled=True),
        lax.psum_scatter(second_sum, "dp", scatter_dimension=0, tiled=True),
        lax.psum_scatter(grad_dense_up, "dp", scatter_dimension=0, tiled=True),
        lax.psum_scatter(grad_dense_down, "dp", scatter_dimension=1, tiled=True),
    )
    owned = tuple(dense_owned) + tuple(moe_owned)
    return (
        block_output,
        input_grad,
        owned[0],
        owned[1],
        owned[2],
        owned[3],
        owned[4],
        owned[5],
        owned[6],
        owned[7],
        owned[8],
        owned[9],
        owned[10],
        owned[11],
        owned[12],
        clipped_first,
        clipped_second,
        clip_scales,
    )


ROWS = 208
AXES = ("dp", "tensor")
BF = jnp.bfloat16
F32 = jnp.float32


def swap(values, z=0, x=0, y=0, core=0):
    shift_d, shift_t = 2 * z + x, 2 * y + core
    pairs = [(d * 4 + t, (d ^ shift_d) * 4 + (t ^ shift_t)) for d in range(8) for t in range(4)]
    return lax.ppermute(values, AXES, pairs)


def place_of(position):
    return 2 * (position & 3) + (position >> 2)


def gather_z(shard):
    return jnp.concatenate([shard] + [swap(shard, z=k) for k in (1, 2, 3)], axis=0)


def gather_weight(shard, x_first):
    quarter = gather_z(shard)
    if x_first:
        other = swap(quarter, x=1)
        own = (quarter, other)
        far = (swap(quarter, y=1), swap(other, y=1))
    else:
        far_quarter = swap(quarter, y=1)
        own = (quarter, swap(quarter, x=1))
        far = (far_quarter, swap(far_quarter, x=1))
    return jnp.concatenate(own, axis=0), jnp.concatenate(far, axis=0)


def add_pair(mine, arrived):
    return mine.astype(F32) + arrived.astype(F32)


def scatter_weight(own, far, y_first):
    half = own.shape[0] // 2
    width = half // 4
    if y_first:
        whole = add_pair(own, swap(far.astype(BF), y=1)).astype(BF)
        part = add_pair(whole[:half], swap(whole[half:], x=1)).astype(BF)
    else:
        own_half = add_pair(own[:half], swap(own[half:].astype(BF), x=1)).astype(BF)
        far_half = add_pair(far[:half], swap(far[half:].astype(BF), x=1)).astype(BF)
        part = add_pair(own_half, swap(far_half, y=1)).astype(BF)
    total = part[:width].astype(F32)
    for k in (1, 2, 3):
        total = total + swap(part[k * width : (k + 1) * width], z=k).astype(F32)
    return total


def exchange_rows(pieces):
    return [pieces[0]] + [
        swap(pieces[p], z=p & 3, x=p >> 2) for p in range(1, 8)
    ]


def pair_gather(values):
    return jnp.concatenate([values, swap(values, core=1)], axis=0)


def pair_scatter(partial):
    half = partial.shape[0] // 2
    return partial[:half] + swap(partial[half:].astype(BF), core=1).astype(F32)


def dot(a, b, ca, cb):
    return lax.dot_general(a, b, (((ca,), (cb,)), ((), ())), preferred_element_type=F32)


def norm_stats(values):
    center = values - jnp.mean(values, axis=-1, keepdims=True)
    scale = lax.rsqrt(jnp.mean(center * center, axis=-1, keepdims=True) + epsilon)
    return center * scale, scale


def norm_rows(values, gain):
    return (norm_stats(values)[0] * gain).astype(BF)


def norm_rows_back(values, gain, upstream):
    normed, scale = norm_stats(values)
    scaled = upstream * gain
    grad = scale * (
        scaled
        - jnp.mean(scaled, axis=-1, keepdims=True)
        - normed * jnp.mean(scaled * normed, axis=-1, keepdims=True)
    )
    return grad, jnp.sum(upstream * normed, axis=0)


def heads_of(parts):
    cut = [m.reshape(2, ROWS, 3, -1, HD) for m in parts]
    joined = jnp.concatenate(cut, axis=3)
    return joined[:, :, 0], joined[:, :, 1], joined[:, :, 2]


def softmax_scores(queries, keyset):
    scores = jnp.einsum("iqhd,ikhd->ihqk", queries, keyset, preferred_element_type=F32)
    scores = scores * HD ** (-0.5)
    key_ok = (jnp.arange(ROWS) < L)[None, None, None, :]
    masked = jnp.where(key_ok, scores, -1e30)
    return masked, jax.nn.softmax(masked, axis=-1)


def fast_attention(residual, gain, qkv, out, live_pair):
    normed = pair_gather(norm_rows(residual, gain))
    mixed = [dot(normed, w, 1, 0).astype(BF) for w in qkv]
    queries, keyset, values = heads_of(mixed)
    masked, probs = softmax_scores(queries, keyset)
    query_ok = (jnp.arange(ROWS) < L)[None, None, :, None] & live_pair[:, None, None, None]
    peak = jnp.max(jnp.where(query_ok, masked, -1e30), axis=(0, 2, 3))
    attended = jnp.einsum("ihqk,ikhd->iqhd", probs.astype(BF), values, preferred_element_type=F32)
    attended = attended.astype(BF).reshape(2 * ROWS, -1)
    half = attended.shape[1] // 2
    partial = dot(attended[:, :half], out[0], 1, 1) + dot(attended[:, half:], out[1], 1, 1)
    return residual + pair_scatter(partial), (normed, mixed, attended), peak


def fast_attention_back(residual, upstream, gain, qkv, out, stored):
    normed, mixed, attended = stored
    grad_full = pair_gather(upstream.astype(BF))
    half = attended.shape[1] // 2
    grad_out = [
        dot(grad_full, attended[:, :half], 0, 0).astype(BF),
        dot(grad_full, attended[:, half:], 0, 0).astype(BF),
    ]
    grad_att = jnp.concatenate([dot(grad_full, w, 1, 0).astype(BF) for w in out], axis=1)
    queries, keyset, values = heads_of(mixed)
    _, probs = softmax_scores(queries, keyset)
    grad_heads = grad_att.reshape(queries.shape)
    grad_values = jnp.einsum(
        "ihqk,iqhd->ikhd", probs.astype(BF), grad_heads, preferred_element_type=F32
    )
    grad_probs = jnp.einsum("iqhd,ikhd->ihqk", grad_heads, values, preferred_element_type=F32)
    grad_scores = probs * (grad_probs - jnp.sum(grad_probs * probs, axis=-1, keepdims=True))
    grad_scores = grad_scores.astype(BF)
    factor = HD ** (-0.5)
    grad_queries = factor * jnp.einsum(
        "ihqk,ikhd->iqhd", grad_scores, keyset, preferred_element_type=F32
    )
    grad_keyset = factor * jnp.einsum(
        "ihqk,iqhd->ikhd", grad_scores, queries, preferred_element_type=F32
    )
    stacked = jnp.stack([grad_queries, grad_keyset, grad_values], axis=2).astype(BF)
    heads = stacked.shape[3] // 2
    grad_mixed = [
        stacked[:, :, :, :heads].reshape(2 * ROWS, -1),
        stacked[:, :, :, heads:].reshape(2 * ROWS, -1),
    ]
    grad_qkv = [dot(normed, g, 0, 0).astype(BF) for g in grad_mixed]
    partial = dot(grad_mixed[0], qkv[0], 1, 1) + dot(grad_mixed[1], qkv[1], 1, 1)
    grad_rows, grad_gain = norm_rows_back(residual, gain, pair_scatter(partial))
    return upstream + grad_rows, grad_gain, grad_qkv, grad_out


def gelu_pair(hidden):
    cdf = 0.5 * (1.0 + lax.erf(hidden * 0.7071067811865476))
    slope = cdf + hidden * jnp.exp(-0.5 * hidden * hidden) * 0.3989422804014327
    return (hidden * cdf).astype(BF), slope


def reduce_peak(peaks):
    half = peaks.shape[1] // 2
    best = jnp.maximum(peaks[:, :half], swap(peaks[:, half:], y=1))
    best = jnp.maximum(best, swap(best, core=0, x=1))
    far = [swap(best, z=k) for k in (1, 2, 3)]
    for f in far:
        best = jnp.maximum(best, f)
    return best


def fast_local(
    block_input,
    first_norm,
    first_qkv,
    first_out,
    second_norm,
    dense_up,
    dense_down,
    third_norm,
    second_qkv,
    second_out,
    fourth_norm,
    router_weight,
    expert_up,
    expert_down,
    expert_ids,
    expert_slots,
    image_counts,
    cotangent,
):
    d = lax.axis_index("dp")
    t = lax.axis_index("tensor")
    z_index, x_index = d // 2, d % 2
    width = first_norm.shape[0]
    features = width * 8
    experts = expert_up.shape[0]
    live_count = image_counts[0]
    heads_cols = first_out.shape[0]
    ff_cols = dense_up.shape[1]

    small = jnp.concatenate(
        [
            jnp.stack([first_norm, second_norm, third_norm, fourth_norm], axis=1),
            router_weight,
            jnp.zeros((width, 128 - 4 - experts), BF),
        ],
        axis=1,
    )
    pack_one = jnp.concatenate([first_qkv.reshape(width, -1), small], axis=1)
    pack_two = jnp.concatenate([first_out.T, dense_up], axis=1)
    pack_three = jnp.concatenate([dense_down.T, second_out.T], axis=1)
    pack_four = second_qkv.reshape(width, -1)
    full_one = gather_weight(pack_one, True)
    full_two = gather_weight(pack_two, False)
    full_three = gather_weight(pack_three, True)
    full_four = gather_weight(pack_four, False)
    qkv_cols = 3 * heads_cols
    qkv_one = [w[:, :qkv_cols] for w in full_one]
    small_full = full_one[0][:, qkv_cols:]
    small_rows = small_full[:, : 4 + experts].astype(F32).T
    gains = [small_rows[i][None] for i in range(4)]
    router_rows = small_rows[4:].astype(BF)
    out_one = [w[:, :heads_cols] for w in full_two]
    up_full = [w[:, heads_cols:] for w in full_two]
    down_full = [w[:, :ff_cols] for w in full_three]
    out_two = [w[:, ff_cols:] for w in full_three]
    qkv_two = list(full_four)

    rel = jnp.arange(features)
    rel_place = jnp.bitwise_xor(d, 2 * ((rel // width) % 4) + (rel // width) // 4) * width + rel % width
    to_whole = (rel_place[:, None] == rel[None, :]).astype(BF)

    pad = ((0, ROWS - L), (0, 0))
    start = dot(jnp.pad(block_input, pad), to_whole, 1, 1)
    live_here = t < live_count
    live_scale = jnp.where(live_here, 1.0, 0.0).astype(F32)
    grad_four = dot(jnp.pad(cotangent, pad), to_whole, 1, 1) * live_scale
    live_pair = jnp.stack([t, t ^ 1]) < live_count

    expert_pack = jnp.concatenate([expert_up, jnp.swapaxes(expert_down, 1, 2)], axis=2)
    expert_grid = expert_pack.reshape(4, 2, width, -1)
    mine_x = lax.dynamic_index_in_dim(expert_grid, x_index, 1, keepdims=False)
    send_x = lax.dynamic_index_in_dim(expert_grid, x_index ^ 1, 1, keepdims=False)
    both_x = jnp.stack([mine_x, swap(send_x, x=1)])
    cut = [lax.dynamic_index_in_dim(both_x, z_index ^ k, 1, keepdims=False) for k in range(4)]
    cut = [cut[0]] + [swap(cut[k], z=k) for k in (1, 2, 3)]
    expert_own = jnp.stack(cut, axis=1).reshape(features, -1)
    expert_far = swap(expert_own, y=1)
    e_up = [expert_own[:, :ff_cols], expert_far[:, :ff_cols]]
    e_down = [expert_own[:, ff_cols:], expert_far[:, ff_cols:]]

    slots_block = -(-CAP // (4 * 8)) * 8
    order = jnp.stack([t, t ^ 2, t ^ 1, t ^ 3])
    ids = jnp.pad(expert_ids.reshape(4, L, 2), ((0, 0), (0, ROWS - L), (0, 0)), constant_values=-1)
    slots = jnp.pad(expert_slots.reshape(4, L, 2), ((0, 0), (0, ROWS - L), (0, 0)), constant_values=CAP)
    flat = jnp.where((slots < CAP) & (slots // slots_block == t), ids * slots_block + slots % slots_block, -1)
    flat = jnp.concatenate(
        [lax.dynamic_index_in_dim(flat, order[i], 0, keepdims=False) for i in range(4)], axis=0
    )
    position = jnp.arange(experts)
    expert_at = jnp.bitwise_xor(d, 2 * (position % 4) + position // 4)
    row_code = (expert_at[:, None] * slots_block + jnp.arange(slots_block)[None, :]).reshape(-1)
    pick = (
        (row_code[:, None] == flat[None, :, 0]) | (row_code[:, None] == flat[None, :, 1])
    ).astype(BF)

    def group_rows(rows):
        pair = jnp.concatenate([rows, swap(rows, y=1)], axis=0)
        return jnp.concatenate([pair, swap(pair, core=1)], axis=0)

    def to_experts(rows):
        whole = dot(dot(pick, group_rows(rows), 1, 0).astype(BF), to_whole, 1, 0).astype(BF)
        pieces = exchange_rows(
            [whole[p * slots_block : (p + 1) * slots_block] for p in range(experts)]
        )
        return dot(jnp.concatenate(pieces, axis=0), to_whole, 1, 1).astype(BF)

    def from_experts(rows):
        whole = dot(rows, to_whole, 1, 0).astype(BF)
        pieces = exchange_rows(
            [whole[p * slots_block : (p + 1) * slots_block] for p in range(experts)]
        )
        back = dot(jnp.concatenate(pieces, axis=0), to_whole, 1, 1).astype(BF)
        partial = dot(pick, back, 0, 0)
        half = pair_scatter(partial)
        return half[:ROWS] + swap(half[ROWS:].astype(BF), y=1).astype(F32)

    grad_slots = pair_gather(to_experts(grad_four.astype(BF)))

    one, stored_one, peak_one = fast_attention(start, gains[0], qkv_one, out_one, live_pair)
    normed_mlp = pair_gather(norm_rows(one, gains[1]))
    hidden = [dot(normed_mlp, w, 1, 0) for w in up_full]
    pairs = [gelu_pair(h) for h in hidden]
    partial = dot(pairs[0][0], down_full[0], 1, 1) + dot(pairs[1][0], down_full[1], 1, 1)
    two = one + pair_scatter(partial)
    three, stored_two, peak_two = fast_attention(two, gains[2], qkv_two, out_two, live_pair)

    tokens = pair_gather(to_experts(norm_rows(three, gains[3])))
    count = tokens.shape[0] // 2
    logits = dot(tokens, router_rows, 1, 1)
    route = jax.nn.softmax(logits, axis=-1)
    mine = (jnp.arange(experts) == d).astype(F32)[None]
    gate = jnp.sum(route * mine, axis=-1, keepdims=True)
    grad_result = (gate * grad_slots.astype(F32)).astype(BF)
    e_pairs = [gelu_pair(dot(tokens, w, 1, 0)) for w in e_up]
    result = pair_scatter(dot(e_pairs[0][0], e_down[0], 1, 1) + dot(e_pairs[1][0], e_down[1], 1, 1))
    e_hidden = [(dot(grad_result, w, 1, 0) * p[1]).astype(BF) for w, p in zip(e_down, e_pairs)]
    grad_tokens = pair_scatter(dot(e_hidden[0], e_up[0], 1, 1) + dot(e_hidden[1], e_up[1], 1, 1))
    grad_gate = jnp.sum(result * grad_slots[:count].astype(F32), axis=-1, keepdims=True)
    grad_logit = (grad_gate * route[:count] * (mine - gate[:count])).astype(BF)
    grad_tokens = grad_tokens + dot(grad_logit, router_rows, 1, 0)
    grad_router = dot(grad_logit, tokens[:count], 0, 0)
    grad_normed = from_experts(grad_tokens.astype(BF))
    mixed_in = from_experts((gate[:count] * result).astype(BF))
    four = three + mixed_in
    block_output = jnp.dot(four, to_whole.astype(F32), precision=lax.Precision.HIGHEST)[:L] * live_scale

    e_grads = [
        jnp.concatenate(
            [dot(tokens, h, 0, 0).astype(BF), dot(grad_result, p[0], 0, 0).astype(BF)], axis=1
        )
        for h, p in zip(e_hidden, e_pairs)
    ]
    e_sum = add_pair(e_grads[0], swap(e_grads[1], y=1)).astype(BF).reshape(2, 4, width, -1)
    e_cut = [e_sum[:, 0]] + [swap(e_sum[:, k], z=k) for k in (1, 2, 3)]
    e_near = jnp.stack([c[0] for c in e_cut])
    e_side = swap(jnp.stack([c[1] for c in e_cut]), x=1)
    e_all = jnp.concatenate([e_near, e_side], axis=0)
    where_x = [(x_index ^ (e % 2)) * 4 + (z_index ^ (e // 2)) for e in range(experts)]
    e_back = jnp.stack([lax.dynamic_index_in_dim(e_all, w, 0, keepdims=False) for w in where_x])
    grad_expert_up = e_back[:, :, :ff_cols].astype(F32)
    grad_expert_down = jnp.swapaxes(e_back[:, :, ff_cols:], 1, 2).astype(F32)

    grad_rows, gain_four = norm_rows_back(three, gains[3], grad_normed)
    grad_three = grad_four + grad_rows
    grad_two, gain_three, g_qkv_two, g_out_two = fast_attention_back(
        two, grad_three, gains[2], qkv_two, out_two, stored_two
    )
    sum_second = scatter_weight(
        jnp.concatenate([g_qkv_two[0], g_out_two[0]], axis=1),
        jnp.concatenate([g_qkv_two[1], g_out_two[1]], axis=1),
        True,
    )

    grad_full = pair_gather(grad_two.astype(BF))
    g_hidden = [(dot(grad_full, w, 1, 0) * p[1]).astype(BF) for w, p in zip(down_full, pairs)]
    g_mlp = [
        jnp.concatenate(
            [dot(normed_mlp, h, 0, 0).astype(BF), dot(grad_full, p[0], 0, 0).astype(BF)], axis=1
        )
        for h, p in zip(g_hidden, pairs)
    ]
    sum_mlp = scatter_weight(g_mlp[0], g_mlp[1], False)
    partial = dot(g_hidden[0], up_full[0], 1, 1) + dot(g_hidden[1], up_full[1], 1, 1)
    grad_rows, gain_two = norm_rows_back(one, gains[1], pair_scatter(partial))
    grad_one = grad_two + grad_rows

    grad_zero, gain_one, g_qkv_one, g_out_one = fast_attention_back(
        start, grad_one, gains[0], qkv_one, out_one, stored_one
    )
    sum_first = scatter_weight(
        jnp.concatenate([g_qkv_one[0], g_out_one[0]], axis=1),
        jnp.concatenate([g_qkv_one[1], g_out_one[1]], axis=1),
        True,
    )
    input_grad = jnp.dot(grad_zero, to_whole.astype(F32), precision=lax.Precision.HIGHEST)[:L]

    tail = jnp.concatenate([jnp.stack([gain_one, gain_two, gain_three, gain_four]), grad_router])
    tail = jnp.swapaxes(tail.reshape(4 + experts, 8, width), 0, 1)
    tail = tail + swap(tail, core=1)
    tail = tail + swap(tail, y=1)
    tail = tail[:4] + swap(tail[4:], x=1)
    tail = tail[0] + swap(tail[1], z=1) + swap(tail[2], z=2) + swap(tail[3], z=3)

    roots = clip_root(reduce_peak(jnp.stack([peak_one, peak_two])))
    return (
        block_output,
        input_grad,
        tail[0],
        sum_first[:, :qkv_cols].reshape(first_qkv.shape),
        sum_first[:, qkv_cols:].T,
        tail[1],
        sum_mlp[:, :ff_cols],
        sum_mlp[:, ff_cols:].T,
        tail[2],
        sum_second[:, :qkv_cols].reshape(second_qkv.shape),
        sum_second[:, qkv_cols:].T,
        tail[3],
        tail[4:].T,
        grad_expert_up,
        grad_expert_down,
        clip_columns(first_qkv, roots[0], HD),
        clip_columns(second_qkv, roots[1], HD),
        roots,
    )


def solution(mesh):
    placed = (
        P(("dp", "tensor"), None),
        P("dp"),
        P("dp", None, "tensor"),
        P("tensor", "dp"),
        P("dp"),
        P("dp", "tensor"),
        P("tensor", "dp"),
        P("dp"),
        P("dp", None, "tensor"),
        P("tensor", "dp"),
        P("dp"),
        P("dp", None),
        P(None, "dp", "tensor"),
        P(None, "tensor", "dp"),
        P("dp", None),
        P("dp", None),
        P("dp"),
        P(("dp", "tensor"), None),
    )
    quick = mesh.shape["dp"] == 8 and mesh.shape["tensor"] == 4
    return jax.shard_map(
        fast_local if quick else local,
        mesh=mesh,
        in_specs=placed,
        out_specs=(
            P(("dp", "tensor"), None),
            P(("dp", "tensor"), None),
            P("dp"),
            P("dp", None, "tensor"),
            P("tensor", "dp"),
            P("dp"),
            P("dp", "tensor"),
            P("tensor", "dp"),
            P("dp"),
            P("dp", None, "tensor"),
            P("tensor", "dp"),
            P("dp"),
            P("dp", None),
            P(None, "dp", "tensor"),
            P(None, "tensor", "dp"),
            P("dp", None, "tensor"),
            P("dp", None, "tensor"),
            P(None, "tensor"),
        ),
        check_vma=False,
    )
```

```python
import jax
import jax.numpy as jnp
from jax import lax
from jax.experimental import pallas as pl
from jax.experimental.pallas import tpu as pltpu
from jax.sharding import PartitionSpec as P

HD = 64
L = 197
CAP = 197


epsilon = 1e-06
clip_tau = 2.5


def layer_norm(values, norm_gain):
    center = values - jnp.mean(values, axis=-1, keepdims=True)
    spread = jnp.mean(center * center, axis=-1, keepdims=True)
    return center * lax.rsqrt(spread + epsilon) * norm_gain


def exact_gelu(values):
    return jax.nn.gelu(values, approximate=False)


def gelu_back(values, upstream):
    return jax.vjp(exact_gelu, values)[1](upstream)[0]


def norm_back(residual, norm_gain, upstream):
    pullback = jax.vjp(layer_norm, residual, norm_gain.astype(jnp.float32))[1]
    return pullback(upstream)


def gather_rows(values):
    return lax.all_gather(values, "tensor", axis=0, tiled=True)


def scatter_rows(values):
    return lax.psum_scatter(
        values.astype(jnp.bfloat16), "tensor", scatter_dimension=0, tiled=True
    ).astype(jnp.float32)


def sum_gains(first_gain, second_gain):
    return lax.psum((first_gain, second_gain), "tensor")


def split_heads(projected, images, head_size):
    row_count, triple, columns = projected.shape
    pieces = projected.reshape(images, row_count // images, triple, columns // head_size, head_size)
    return (pieces[:, :, 0], pieces[:, :, 1], pieces[:, :, 2])


def attend_scores(queries, keyset, head_size):
    scores = jnp.einsum("iqhd,ikhd->ihqk", queries, keyset, preferred_element_type=jnp.float32)
    return scores * head_size ** (-0.5)


def attend_forward(normed_full, weight_qkv, images, head_size, live_images):
    projected = jnp.einsum(
        "rd,dcf->rcf", normed_full, weight_qkv, preferred_element_type=jnp.float32
    ).astype(jnp.bfloat16)
    queries, keyset, values = split_heads(projected, images, head_size)
    scores = attend_scores(queries, keyset, head_size)
    head_peak = jnp.max(jnp.where(live_images[:, None, None, None], scores, -1e30), axis=(0, 2, 3))
    attn_probs = jax.nn.softmax(scores, axis=-1).astype(jnp.bfloat16)
    attended = jnp.einsum("ihqk,ikhd->iqhd", attn_probs, values, preferred_element_type=jnp.float32)
    return (projected, attended.astype(jnp.bfloat16).reshape(normed_full.shape[0], -1), head_peak)


def attend_backward(projected, grad_attended, images, head_size):
    queries, keyset, values = split_heads(projected, images, head_size)
    scores = attend_scores(queries, keyset, head_size)
    attn_probs = jax.nn.softmax(scores, axis=-1)
    grad_heads = grad_attended.reshape(queries.shape)
    grad_values = jnp.einsum(
        "ihqk,iqhd->ikhd",
        attn_probs.astype(jnp.bfloat16),
        grad_heads,
        preferred_element_type=jnp.float32,
    )
    grad_probs = jnp.einsum(
        "iqhd,ikhd->ihqk", grad_heads, values, preferred_element_type=jnp.float32
    )
    grad_scores = attn_probs * (
        grad_probs - jnp.sum(grad_probs * attn_probs, axis=-1, keepdims=True)
    )
    grad_scores = grad_scores.astype(jnp.bfloat16)
    factor = head_size ** (-0.5)
    grad_queries = (
        jnp.einsum("ihqk,ikhd->iqhd", grad_scores, keyset, preferred_element_type=jnp.float32)
        * factor
    )
    grad_keyset = (
        jnp.einsum("ihqk,iqhd->ikhd", grad_scores, queries, preferred_element_type=jnp.float32)
        * factor
    )
    stacked = jnp.stack([grad_queries, grad_keyset, grad_values], axis=2).astype(jnp.bfloat16)
    return stacked.reshape(projected.shape)


def block_attention(residual, norm_gain, weight_qkv, weight_out, images, head_size, live_images):
    normed = layer_norm(residual, norm_gain.astype(jnp.float32)).astype(jnp.bfloat16)
    normed_full = gather_rows(normed)
    projected, attended, head_peak = attend_forward(
        normed_full, weight_qkv, images, head_size, live_images
    )
    branch = scatter_rows(jnp.dot(attended, weight_out, preferred_element_type=jnp.float32))
    return (residual + branch, (normed_full, projected, attended), head_peak)


def block_attention_back(
    residual, upstream, norm_gain, weight_qkv, weight_out, stored, images, head_size
):
    normed_full, projected, attended = stored
    grad_full = gather_rows(upstream.astype(jnp.bfloat16))
    grad_out = jnp.einsum("rf,rd->fd", attended, grad_full, preferred_element_type=jnp.float32)
    grad_attended = jnp.einsum(
        "rd,fd->rf", grad_full, weight_out, preferred_element_type=jnp.float32
    ).astype(jnp.bfloat16)
    grad_projected = attend_backward(projected, grad_attended, images, head_size)
    grad_qkv = jnp.einsum(
        "rd,rcf->dcf", normed_full, grad_projected, preferred_element_type=jnp.float32
    )
    grad_normed = scatter_rows(
        jnp.einsum("rcf,dcf->rd", grad_projected, weight_qkv, preferred_element_type=jnp.float32)
    )
    grad_residual, grad_gain = norm_back(residual, norm_gain, grad_normed)
    return (upstream + grad_residual, grad_gain, grad_qkv, grad_out)


def block_mlp(residual, norm_gain, weight_up, weight_down):
    normed = layer_norm(residual, norm_gain.astype(jnp.float32)).astype(jnp.bfloat16)
    normed_full = gather_rows(normed)
    hidden = jnp.dot(normed_full, weight_up, preferred_element_type=jnp.float32)
    active = exact_gelu(hidden).astype(jnp.bfloat16)
    branch = scatter_rows(jnp.dot(active, weight_down, preferred_element_type=jnp.float32))
    return (residual + branch, (normed_full, hidden, active))


def block_mlp_back(residual, upstream, norm_gain, weight_up, weight_down, stored):
    normed_full, hidden, active = stored
    grad_full = gather_rows(upstream.astype(jnp.bfloat16))
    grad_down = jnp.einsum("rf,rd->fd", active, grad_full, preferred_element_type=jnp.float32)
    grad_active = jnp.einsum(
        "rd,fd->rf", grad_full, weight_down, preferred_element_type=jnp.float32
    )
    grad_hidden = gelu_back(hidden, grad_active).astype(jnp.bfloat16)
    grad_up = jnp.einsum("rd,rf->df", normed_full, grad_hidden, preferred_element_type=jnp.float32)
    grad_normed = scatter_rows(
        jnp.einsum("rf,df->rd", grad_hidden, weight_up, preferred_element_type=jnp.float32)
    )
    grad_residual, grad_gain = norm_back(residual, norm_gain, grad_normed)
    return (upstream + grad_residual, grad_gain, grad_up, grad_down)


def clip_root(head_peak):
    return jnp.sqrt(clip_tau / jnp.maximum(head_peak, clip_tau))


def clip_columns(weight_local, head_root, head_size):
    column = jnp.repeat(head_root, head_size)
    scales = jnp.stack([column, column, jnp.ones_like(column)])
    return weight_local.astype(jnp.float32) * scales[None]


def local(
    block_input,
    first_norm,
    first_qkv,
    first_out,
    second_norm,
    dense_up,
    dense_down,
    third_norm,
    second_qkv,
    second_out,
    fourth_norm,
    router_weight,
    expert_up,
    expert_down,
    expert_ids,
    expert_slots,
    image_counts,
    cotangent,
):
    rows_local = block_input.shape[0]
    rows_full = rows_local * lax.axis_size("tensor")
    images = rows_full // L
    head_size = HD
    experts = expert_up.shape[0]
    capacity = CAP
    first_row = lax.axis_index("tensor") * rows_local
    live_count = image_counts[0]
    local_live = ((first_row + jnp.arange(rows_local)) // L < live_count).astype(jnp.float32)
    full_live = (jnp.arange(rows_full) // L < live_count).astype(jnp.float32)
    live_images = jnp.arange(images) < live_count

    def dense_fetch():
        return (
            lax.all_gather(first_norm, "dp", axis=0, tiled=True),
            lax.all_gather(first_qkv, "dp", axis=0, tiled=True),
            lax.all_gather(first_out, "dp", axis=1, tiled=True),
            lax.all_gather(second_norm, "dp", axis=0, tiled=True),
            lax.all_gather(dense_up, "dp", axis=0, tiled=True),
            lax.all_gather(dense_down, "dp", axis=1, tiled=True),
        )

    def moe_fetch():
        return (
            lax.all_gather(third_norm, "dp", axis=0, tiled=True),
            lax.all_gather(second_qkv, "dp", axis=0, tiled=True),
            lax.all_gather(second_out, "dp", axis=1, tiled=True),
            lax.all_gather(fourth_norm, "dp", axis=0, tiled=True),
            lax.all_gather(router_weight, "dp", axis=0, tiled=True),
            lax.all_gather(expert_up, "dp", axis=1, tiled=True),
            lax.all_gather(expert_down, "dp", axis=2, tiled=True),
        )

    dense_full = dense_fetch()
    residual_zero = block_input.astype(jnp.float32)
    residual_one, attn_first, peak_first = block_attention(
        residual_zero, dense_full[0], dense_full[1], dense_full[2], images, head_size, live_images
    )
    residual_two, mlp_stored = block_mlp(residual_one, dense_full[3], dense_full[4], dense_full[5])
    moe_full = moe_fetch()
    residual_three, attn_second, peak_second = block_attention(
        residual_two, moe_full[0], moe_full[1], moe_full[2], images, head_size, live_images
    )
    moe_normed = layer_norm(residual_three, moe_full[3].astype(jnp.float32)).astype(jnp.bfloat16)
    moe_input = gather_rows(moe_normed)
    logits = jnp.dot(moe_input, moe_full[4], preferred_element_type=jnp.float32)
    route_probs = jax.nn.softmax(logits, axis=-1)
    kept_mask = expert_slots < capacity
    pair_number = jnp.arange(2 * rows_full, dtype=jnp.int32)
    slot_index = (expert_ids * capacity + expert_slots).reshape(-1)
    kept_flat = kept_mask.reshape(-1)
    write_target = jnp.where(kept_flat, slot_index, experts * capacity + pair_number)
    target = jnp.where(kept_flat, slot_index, experts * capacity)
    pair_of_slot = (
        jnp.zeros((experts * capacity + 2 * rows_full,), jnp.int32)
        .at[write_target]
        .set(pair_number)[: experts * capacity]
    )
    slot_filled = (
        jnp.zeros((experts * capacity + 2 * rows_full,), jnp.float32)
        .at[write_target]
        .set(1.0)[: experts * capacity]
    )
    chosen = (expert_ids[:, :, None] == jnp.arange(experts)[None, None, :]).astype(jnp.float32)
    keep_live = kept_mask.astype(jnp.float32) * full_live[:, None]
    gates = jnp.sum(chosen * route_probs[:, None, :], axis=-1) * keep_live
    slot_token = pair_of_slot // 2
    slot_gate = gates.reshape(-1)[pair_of_slot] * slot_filled
    dispatched = (moe_input[slot_token] * slot_filled[:, None].astype(jnp.bfloat16)).reshape(
        experts, capacity, -1
    )
    expert_hidden = jnp.einsum(
        "ecd,edf->ecf", dispatched, moe_full[5], preferred_element_type=jnp.float32
    )
    expert_act = exact_gelu(expert_hidden).astype(jnp.bfloat16)
    expert_result = jnp.einsum(
        "ecf,efd->ecd", expert_act, moe_full[6], preferred_element_type=jnp.float32
    )
    feature_count = expert_result.shape[2]
    padded_result = jnp.concatenate(
        [
            expert_result.reshape(experts * capacity, feature_count),
            jnp.zeros((1, feature_count), jnp.float32),
        ],
        axis=0,
    )
    pair_result = padded_result[target].reshape(rows_full, 2, feature_count)
    combined = jnp.sum(gates[:, :, None] * pair_result, axis=1)
    residual_four = residual_three + scatter_rows(combined)
    block_output = residual_four * local_live[:, None]
    peak_first_all, peak_second_all = lax.pmax((peak_first, peak_second), "dp")
    root_first = clip_root(peak_first_all)
    root_second = clip_root(peak_second_all)
    clipped_first = clip_columns(first_qkv, root_first, head_size)
    clipped_second = clip_columns(second_qkv, root_second, head_size)
    clip_scales = jnp.stack([root_first, root_second])
    moe_back = moe_fetch()
    grad_four = cotangent.astype(jnp.float32) * local_live[:, None]
    moe_grad_full = gather_rows(grad_four.astype(jnp.bfloat16))
    partial_gates = jnp.sum(moe_grad_full.astype(jnp.float32)[:, None, :] * pair_result, axis=-1)
    grad_gates = lax.psum(partial_gates, "tensor")
    grad_result = (slot_gate[:, None] * moe_grad_full[slot_token].astype(jnp.float32)).astype(
        jnp.bfloat16
    )
    grad_result = grad_result.reshape(experts, capacity, feature_count)
    grad_expert_down = jnp.einsum(
        "ecf,ecd->efd", expert_act, grad_result, preferred_element_type=jnp.float32
    )
    grad_act = jnp.einsum(
        "ecd,efd->ecf", grad_result, moe_back[6], preferred_element_type=jnp.float32
    )
    grad_hidden = gelu_back(expert_hidden, grad_act).astype(jnp.bfloat16)
    grad_expert_up = jnp.einsum(
        "ecd,ecf->edf", dispatched, grad_hidden, preferred_element_type=jnp.float32
    )
    grad_dispatch = jnp.einsum(
        "ecf,edf->ecd", grad_hidden, moe_back[5], preferred_element_type=jnp.float32
    )
    grad_dispatch = jnp.concatenate(
        [
            grad_dispatch.reshape(experts * capacity, feature_count),
            jnp.zeros((1, feature_count), jnp.float32),
        ],
        axis=0,
    )
    grad_from_experts = jnp.sum(grad_dispatch[target].reshape(rows_full, 2, feature_count), axis=1)
    grad_picked = grad_gates * keep_live
    grad_probs = jnp.sum(chosen * grad_picked[:, :, None], axis=1)
    grad_logits = route_probs * (
        grad_probs - jnp.sum(grad_probs * route_probs, axis=-1, keepdims=True)
    )
    grad_logits = grad_logits.astype(jnp.bfloat16)
    grad_router = jnp.einsum(
        "rd,re->de", moe_input, grad_logits, preferred_element_type=jnp.float32
    )
    local_logits = lax.dynamic_slice_in_dim(grad_logits, first_row, rows_local, 0)
    grad_moe_normed = scatter_rows(grad_from_experts) + jnp.einsum(
        "re,de->rd", local_logits, moe_back[4], preferred_element_type=jnp.float32
    )
    grad_rows_four, grad_fourth_norm = norm_back(residual_three, moe_back[3], grad_moe_normed)
    grad_three = grad_four + grad_rows_four
    grad_two, grad_third_norm, grad_second_qkv, grad_second_out = block_attention_back(
        residual_two,
        grad_three,
        moe_back[0],
        moe_back[1],
        moe_back[2],
        attn_second,
        images,
        head_size,
    )
    third_sum, fourth_sum = sum_gains(grad_third_norm, grad_fourth_norm)
    moe_owned = (
        lax.psum_scatter(third_sum, "dp", scatter_dimension=0, tiled=True),
        lax.psum_scatter(grad_second_qkv, "dp", scatter_dimension=0, tiled=True),
        lax.psum_scatter(grad_second_out, "dp", scatter_dimension=1, tiled=True),
        lax.psum_scatter(fourth_sum, "dp", scatter_dimension=0, tiled=True),
        lax.psum_scatter(grad_router, "dp", scatter_dimension=0, tiled=True),
        lax.psum_scatter(grad_expert_up, "dp", scatter_dimension=1, tiled=True),
        lax.psum_scatter(grad_expert_down, "dp", scatter_dimension=2, tiled=True),
    )
    dense_back = dense_fetch()
    grad_one, grad_second_norm, grad_dense_up, grad_dense_down = block_mlp_back(
        residual_one, grad_two, dense_back[3], dense_back[4], dense_back[5], mlp_stored
    )
    input_grad, grad_first_norm, grad_first_qkv, grad_first_out = block_attention_back(
        residual_zero,
        grad_one,
        dense_back[0],
        dense_back[1],
        dense_back[2],
        attn_first,
        images,
        head_size,
    )
    first_sum, second_sum = sum_gains(grad_first_norm, grad_second_norm)
    dense_owned = (
        lax.psum_scatter(first_sum, "dp", scatter_dimension=0, tiled=True),
        lax.psum_scatter(grad_first_qkv, "dp", scatter_dimension=0, tiled=True),
        lax.psum_scatter(grad_first_out, "dp", scatter_dimension=1, tiled=True),
        lax.psum_scatter(second_sum, "dp", scatter_dimension=0, tiled=True),
        lax.psum_scatter(grad_dense_up, "dp", scatter_dimension=0, tiled=True),
        lax.psum_scatter(grad_dense_down, "dp", scatter_dimension=1, tiled=True),
    )
    owned = tuple(dense_owned) + tuple(moe_owned)
    return (
        block_output,
        input_grad,
        owned[0],
        owned[1],
        owned[2],
        owned[3],
        owned[4],
        owned[5],
        owned[6],
        owned[7],
        owned[8],
        owned[9],
        owned[10],
        owned[11],
        owned[12],
        clipped_first,
        clipped_second,
        clip_scales,
    )


ROWS = 208
AXES = ("dp", "tensor")
BF = jnp.bfloat16
F32 = jnp.float32
VM = pl.BlockSpec(memory_space=pltpu.VMEM)
SM = pl.BlockSpec(memory_space=pltpu.SMEM)


def swap(values, z=0, x=0, y=0, core=0):
    shift_d, shift_t = 2 * z + x, 2 * y + core
    pairs = [(d * 4 + t, (d ^ shift_d) * 4 + (t ^ shift_t)) for d in range(8) for t in range(4)]
    return lax.ppermute(values, AXES, pairs)


def hold(values, *tokens):
    return lax.optimization_barrier((values,) + tokens)[0]


def run(kernel, outs, args, flops, scratch=(), scalars=0, mib=32):
    shapes = [jax.ShapeDtypeStruct(s, dt) for s, dt in outs]
    moved = sum(a.size * a.dtype.itemsize for a in args)
    moved += sum(s.size * s.dtype.itemsize for s in shapes)
    return pl.pallas_call(
        kernel,
        out_shape=shapes,
        in_specs=[SM] * scalars + [VM] * (len(args) - scalars),
        out_specs=[VM] * len(shapes),
        scratch_shapes=list(scratch),
        compiler_params=pltpu.CompilerParams(vmem_limit_bytes=mib * 2**20),
        cost_estimate=pl.CostEstimate(flops=int(flops), bytes_accessed=int(moved), transcendentals=0),
    )(*args)


def dot(a, b, ca, cb):
    return lax.dot_general(a, b, (((ca,), (cb,)), ((), ())), preferred_element_type=F32)


def norm_stats(values):
    center = values - jnp.mean(values, axis=-1, keepdims=True)
    scale = lax.rsqrt(jnp.mean(center * center, axis=-1, keepdims=True) + epsilon)
    return center * scale, scale


def enter_kernel(live, x_ref, c_ref, perm_ref, start_ref, grad_ref, low_ref):
    rows = x_ref.shape[0]
    scale = live[0].astype(F32)
    extra = jnp.zeros((ROWS - rows, x_ref.shape[1]), F32)
    start_ref[:rows] = dot(x_ref[...], perm_ref[...], 1, 1)
    start_ref[rows:] = extra
    grad = dot(c_ref[...], perm_ref[...], 1, 1) * scale
    grad_ref[:rows] = grad
    grad_ref[rows:] = extra
    low_ref[:rows] = grad.astype(BF)
    low_ref[rows:] = extra.astype(BF)


def norm_kernel(x_ref, gain_ref, out_ref):
    out_ref[...] = (norm_stats(x_ref[...])[0] * gain_ref[...]).astype(BF)


def join_norm_kernel(x_ref, own_ref, far_ref, gain_ref, sum_ref, out_ref):
    total = x_ref[...] + (own_ref[...] + far_ref[...].astype(F32))
    sum_ref[...] = total
    out_ref[...] = (norm_stats(total)[0] * gain_ref[...]).astype(BF)


def norm_back_kernel(x_ref, up_ref, own_ref, far_ref, gain_ref, grad_ref, low_ref, gain_out):
    upstream = own_ref[...] + far_ref[...].astype(F32)
    normed, scale = norm_stats(x_ref[...])
    scaled = upstream * gain_ref[...]
    grad = up_ref[...] + scale * (
        scaled
        - jnp.mean(scaled, axis=-1, keepdims=True)
        - normed * jnp.mean(scaled * normed, axis=-1, keepdims=True)
    )
    grad_ref[...] = grad
    low_ref[...] = grad.astype(BF)
    gain_out[...] = jnp.sum(upstream * normed, axis=0, keepdims=True)


def fill_pair(pair, first_ref, second_ref):
    rows = first_ref.shape[0]
    pair[:rows] = first_ref[...]
    pair[rows:] = second_ref[...]


def score_block(queries, keyset):
    scores = dot(queries, keyset, 1, 1) * HD ** (-0.5)
    column = lax.broadcasted_iota(jnp.int32, scores.shape, 1)
    scores = jnp.where(column < L, scores, -1e30)
    top = jnp.max(scores, axis=-1, keepdims=True)
    weight = jnp.exp(scores - top)
    return weight * (1.0 / jnp.sum(weight, axis=-1, keepdims=True)), top


def attend_kernel(
    live, a0, a1, w0, w1, o0, o1, mix_ref, att_ref, own_ref, sib_ref, peak_ref, pair
):
    fill_pair(pair, a0, a1)
    part = o0.shape[1]
    heads = part // HD
    for y, w in enumerate((w0, w1)):
        mix_ref[y] = dot(pair[...], w[...], 1, 0).astype(BF)
    row_ok = lax.broadcasted_iota(jnp.int32, (ROWS, 1), 0) < L
    for y in range(2):
        for h in range(heads):
            peaks = []
            for i in range(2):
                rows = slice(i * ROWS, (i + 1) * ROWS)
                cut = [
                    mix_ref[y, rows, c * part + h * HD : c * part + (h + 1) * HD] for c in range(3)
                ]
                probs, top = score_block(cut[0], cut[1])
                place = y * part + h * HD
                att_ref[rows, place : place + HD] = dot(probs.astype(BF), cut[2], 1, 0).astype(BF)
                best = jnp.max(jnp.where(row_ok, top, -1e30), axis=0, keepdims=True)
                peaks.append(jnp.where(live[i] > 0, best, -1e30))
            number = y * heads + h
            peak_ref[number : number + 1, :] = jnp.broadcast_to(
                jnp.maximum(peaks[0], peaks[1]), (1, peak_ref.shape[1])
            )
    partial = dot(att_ref[:, :part], o0[...], 1, 1) + dot(att_ref[:, part:], o1[...], 1, 1)
    own_ref[...] = partial[:ROWS]
    sib_ref[...] = partial[ROWS:].astype(BF)


def attend_back_kernel(
    g0, g1, a0, a1, mix_ref, att_ref, w0, w1, o0, o1,
    pack_own, pack_far, own_ref, sib_ref, pair, grad_att, grad_mix,
):
    part = o0.shape[1]
    heads = part // HD
    fill_pair(pair, g0, g1)
    for y, (o, pack) in enumerate(((o0, pack_own), (o1, pack_far))):
        grad_att[:, y * part : (y + 1) * part] = dot(pair[...], o[...], 1, 0).astype(BF)
        pack[:, 3 * part :] = dot(pair[...], att_ref[:, y * part : (y + 1) * part], 0, 0).astype(BF)
    factor = HD ** (-0.5)
    for y in range(2):
        for h in range(heads):
            for i in range(2):
                rows = slice(i * ROWS, (i + 1) * ROWS)
                spans = [slice(c * part + h * HD, c * part + (h + 1) * HD) for c in range(3)]
                queries, keyset, values = (mix_ref[y, rows, s] for s in spans)
                place = y * part + h * HD
                grad = grad_att[rows, place : place + HD]
                probs, _ = score_block(queries, keyset)
                grad_mix[y, rows, spans[2]] = dot(probs.astype(BF), grad, 0, 0).astype(BF)
                grad_probs = dot(grad, values, 1, 1)
                slope = probs * (
                    grad_probs - jnp.sum(grad_probs * probs, axis=-1, keepdims=True)
                )
                slope = slope.astype(BF)
                grad_mix[y, rows, spans[0]] = (factor * dot(slope, keyset, 1, 0)).astype(BF)
                grad_mix[y, rows, spans[1]] = (factor * dot(slope, queries, 0, 0)).astype(BF)
    fill_pair(pair, a0, a1)
    pack_own[:, : 3 * part] = dot(pair[...], grad_mix[0], 0, 0).astype(BF)
    pack_far[:, : 3 * part] = dot(pair[...], grad_mix[1], 0, 0).astype(BF)
    partial = dot(grad_mix[0], w0[...], 1, 1) + dot(grad_mix[1], w1[...], 1, 1)
    own_ref[...] = partial[:ROWS]
    sib_ref[...] = partial[ROWS:].astype(BF)


def gelu_pair(hidden):
    cdf = 0.5 * (1.0 + lax.erf(hidden * 0.7071067811865476))
    slope = cdf + hidden * jnp.exp(-0.5 * hidden * hidden) * 0.3989422804014327
    return (hidden * cdf).astype(BF), slope.astype(BF)


def mlp_kernel(b0, b1, u0, u1, d0, d1, act_ref, slope_ref, own_ref, sib_ref, pair):
    fill_pair(pair, b0, b1)
    for y, u in enumerate((u0, u1)):
        for c in range(0, u.shape[1], 256):
            span = slice(c, c + 256)
            act, slope = gelu_pair(dot(pair[...], u[:, span], 1, 0))
            act_ref[y, :, span] = act
            slope_ref[y, :, span] = slope
    partial = dot(act_ref[0], d0[...], 1, 1) + dot(act_ref[1], d1[...], 1, 1)
    own_ref[...] = partial[:ROWS]
    sib_ref[...] = partial[ROWS:].astype(BF)


def mlp_back_kernel(
    g0, g1, b0, b1, act_ref, slope_ref, u0, u1, d0, d1,
    pack_own, pack_far, own_ref, sib_ref, pair, grad_hidden,
):
    fill_pair(pair, g0, g1)
    wide = u0.shape[1]
    for y, (d, pack) in enumerate(((d0, pack_own), (d1, pack_far))):
        grad_hidden[y] = (dot(pair[...], d[...], 1, 0) * slope_ref[y].astype(F32)).astype(BF)
        pack[:, wide:] = dot(pair[...], act_ref[y], 0, 0).astype(BF)
    partial = dot(grad_hidden[0], u0[...], 1, 1) + dot(grad_hidden[1], u1[...], 1, 1)
    own_ref[...] = partial[:ROWS]
    sib_ref[...] = partial[ROWS:].astype(BF)
    fill_pair(pair, b0, b1)
    pack_own[:, :wide] = dot(pair[...], grad_hidden[0], 0, 0).astype(BF)
    pack_far[:, :wide] = dot(pair[...], grad_hidden[1], 0, 0).astype(BF)


def picked(row_code, codes):
    hit = (row_code[...] == codes[0:1, :]) | (row_code[...] == codes[1:2, :])
    return jnp.where(hit, 1.0, 0.0).astype(BF)


def dispatch_kernel(row_code, codes, p0, p1, perm_ref, *rest):
    outs, rows = rest[:8], rest[8]
    fill_pair(rows, p0, p1)
    picks = dot(picked(row_code, codes), rows[...], 1, 0).astype(BF)
    whole = dot(picks, perm_ref[...], 1, 0).astype(BF)
    size = outs[0].shape[0]
    for p, out in enumerate(outs):
        out[...] = whole[p * size : (p + 1) * size]


def collect_kernel(perm_ref, *rest):
    pieces, out, rows = rest[:8], rest[8], rest[9]
    size = pieces[0].shape[0]
    for p, piece in enumerate(pieces):
        rows[p * size : (p + 1) * size] = piece[...]
    out[...] = dot(rows[...], perm_ref[...], 1, 1).astype(BF)


def combine_kernel(row_code, codes, perm_ref, *rest):
    pieces, own_ref, sib_ref, rows = rest[:8], rest[8], rest[9], rest[10]
    size = pieces[0].shape[0]
    for p, piece in enumerate(pieces):
        rows[p * size : (p + 1) * size] = piece[...]
    back = dot(rows[...], perm_ref[...], 1, 1).astype(BF)
    partial = dot(picked(row_code, codes), back, 0, 0)
    half = partial.shape[0] // 2
    own_ref[...] = partial[:half]
    sib_ref[...] = partial[half:].astype(BF)


def pair_add_kernel(own_ref, far_ref, near_ref, send_ref):
    total = own_ref[...] + far_ref[...].astype(F32)
    near_ref[...] = total[:ROWS]
    send_ref[...] = total[ROWS:].astype(BF)


def route_of(tokens, router, number):
    logits = dot(tokens, router, 1, 1)
    column = lax.broadcasted_iota(jnp.int32, logits.shape, 1)
    logits = jnp.where(column < 8, logits, -1e30)
    weight = jnp.exp(logits - jnp.max(logits, axis=-1, keepdims=True))
    route = weight / jnp.sum(weight, axis=-1, keepdims=True)
    mine = jnp.where(column == number, 1.0, 0.0)
    return route, mine, jnp.sum(route * mine, axis=-1, keepdims=True)


def expert_kernel(
    number, t0, t1, g0, g1, router, u0, u1, d0, d1,
    act_ref, hid_ref, gout_ref, res_own, res_sib, grad_own, grad_sib, slope,
):
    size = t0.shape[0]
    for i, (t, g, res, grad) in enumerate(
        ((t1, g1, res_sib, grad_sib), (t0, g0, res_own, grad_own))
    ):
        rows = slice((1 - i) * size, (2 - i) * size)
        gate = route_of(t[...], router[...], number[0])[2]
        gout = (gate * g[...].astype(F32)).astype(BF)
        gout_ref[rows] = gout
        for y, (u, d) in enumerate(((u0, d0), (u1, d1))):
            for c in range(0, u.shape[1], 256):
                span = slice(c, c + 256)
                act, lean = gelu_pair(dot(t[...], u[:, span], 1, 0))
                act_ref[y, rows, span] = act
                hid_ref[y, rows, span] = (dot(gout, d[:, span], 1, 0) * lean.astype(F32)).astype(BF)
        res[...] = (
            dot(act_ref[0, rows], d0[...], 1, 1) + dot(act_ref[1, rows], d1[...], 1, 1)
        ).astype(res.dtype)
        grad[...] = (
            dot(hid_ref[0, rows], u0[...], 1, 1) + dot(hid_ref[1, rows], u1[...], 1, 1)
        ).astype(grad.dtype)


def expert_grad_kernel(t0, t1, act_ref, hid_ref, gout_ref, pack_own, pack_far, pair):
    fill_pair(pair, t0, t1)
    wide = act_ref.shape[2]
    for y, pack in enumerate((pack_own, pack_far)):
        pack[:, :wide] = dot(pair[...], hid_ref[y], 0, 0).astype(BF)
        pack[:, wide:] = dot(gout_ref[...], act_ref[y], 0, 0).astype(BF)


def answer_kernel(
    number, t_ref, g_ref, router, res_own, res_far, grad_own, grad_far, perm_ref, *rest
):
    grads, results, router_out = rest[:8], rest[8:16], rest[16]
    route, mine, gate = route_of(t_ref[...], router[...], number[0])
    result = res_own[...] + res_far[...].astype(F32)
    grad_gate = jnp.sum(result * g_ref[...].astype(F32), axis=-1, keepdims=True)
    grad_logit = (grad_gate * route * (mine - gate)).astype(BF)
    router_out[...] = dot(grad_logit, t_ref[...], 0, 0)
    grad = grad_own[...] + grad_far[...].astype(F32) + dot(grad_logit, router[...], 1, 0)
    size = grads[0].shape[0]
    whole = dot(grad.astype(BF), perm_ref[...], 1, 0).astype(BF)
    for p, out in enumerate(grads):
        out[...] = whole[p * size : (p + 1) * size]
    whole = dot((gate * result).astype(BF), perm_ref[...], 1, 0).astype(BF)
    for p, out in enumerate(results):
        out[...] = whole[p * size : (p + 1) * size]


def reorder(values, perm):
    high = values.astype(BF)
    rest = values - high.astype(F32)
    middle = rest.astype(BF)
    low = (rest - middle.astype(F32)).astype(BF)
    return dot(high, perm, 1, 0) + (dot(middle, perm, 1, 0) + dot(low, perm, 1, 0))


def leave_kernel(x_ref, perm_ref, out_ref):
    out_ref[...] = reorder(x_ref[...], perm_ref[...])[: out_ref.shape[0]]


def finish_kernel(live, x_ref, own_ref, far_ref, perm_ref, out_ref):
    total = x_ref[...] + (own_ref[...] + far_ref[...].astype(F32))
    total = reorder(total, perm_ref[...]) * live[0].astype(F32)
    out_ref[...] = total[: out_ref.shape[0]]


def choose_kernel(places, up_ref, down_ref, *outs):
    wide = up_ref.shape[2]
    rows = up_ref.shape[1]
    for k, out in enumerate(outs):
        for x in range(2):
            place = places[2 * k + x]
            out[x * rows : (x + 1) * rows, :wide] = up_ref[place]
            out[x * rows : (x + 1) * rows, wide:] = down_ref[place]


def split_kernel(q0, q1, q2, q3, near, send):
    rows = q0.shape[0] // 2
    for k, q in enumerate((q0, q1, q2, q3)):
        near[k * rows : (k + 1) * rows] = q[:rows]
        send[k * rows : (k + 1) * rows] = q[rows:]


def regroup_kernel(near, side, *outs):
    rows = outs[0].shape[0] // 2
    for k, out in enumerate(outs):
        out[:rows] = near[k * rows : (k + 1) * rows]
        out[rows:] = side[k * rows : (k + 1) * rows]


def add_split_kernel(own_ref, far_ref, near, send):
    half = near.shape[0]
    total = own_ref[...].astype(F32) + far_ref[...].astype(F32)
    near[...] = total[:half].astype(BF)
    send[...] = total[half:].astype(BF)


def place_kernel(places, q0, q1, q2, q3, up_out, down_out):
    wide = up_out.shape[2]
    rows = up_out.shape[1]
    for k, q in enumerate((q0, q1, q2, q3)):
        for x in range(2):
            place = places[2 * k + x]
            block = q[x * rows : (x + 1) * rows].astype(F32)
            up_out[place] = block[:, :wide]
            down_out[place] = block[:, wide:]


def assemble_kernel(left_own, left_far, right_both, right_side, own_ref, far_ref):
    left = left_own.shape[1]
    right = right_both.shape[1] // 2
    half = right_both.shape[0]
    own_ref[:, :left] = left_own[...]
    far_ref[:, :left] = left_far[...]
    own_ref[:half, left:] = right_both[:, :right]
    own_ref[half:, left:] = right_side[:, :right]
    far_ref[:half, left:] = right_both[:, right:]
    far_ref[half:, left:] = right_side[:, right:]


def gather_z(shard):
    return jnp.concatenate([shard] + [swap(shard, z=k) for k in (1, 2, 3)], axis=0)


def gather_first(quarter):
    half = quarter.shape[1] // 256 * 128
    left, right = quarter[:, :half], quarter[:, half:]
    left_own = jnp.concatenate([left, swap(left, x=1)], axis=0)
    return left_own, jnp.concatenate([right, swap(right, y=1)], axis=1)


def gather_second(parts):
    left_own, right_both = parts
    rows = left_own.shape[0]
    width = left_own.shape[1] + right_both.shape[1] // 2
    left_far = swap(left_own, y=1)
    right_side = swap(right_both, x=1)
    return run(
        assemble_kernel,
        [((rows, width), BF)] * 2,
        (left_own, left_far, right_both, right_side),
        rows * width,
    )


def cut_pack(own_ref, far_ref, left_own, left_far, right_near, right_send):
    left = left_own.shape[1]
    right = right_near.shape[1] // 2
    half = right_near.shape[0]
    left_own[...] = own_ref[:, :left]
    left_far[...] = far_ref[:, :left]
    right_near[:, :right] = own_ref[:half, left:]
    right_near[:, right:] = far_ref[:half, left:]
    right_send[:, :right] = own_ref[half:, left:]
    right_send[:, right:] = far_ref[half:, left:]


def sum_one(left_own, left_got, right_near, right_got, left_keep, left_send, right_keep, right_send):
    half, right = right_keep.shape
    total = left_own[...].astype(F32) + left_got[...].astype(F32)
    left_keep[...] = total[:half].astype(BF)
    left_send[...] = total[half:].astype(BF)
    total = right_near[...].astype(F32) + right_got[...].astype(F32)
    right_keep[...] = total[:, :right].astype(BF)
    right_send[...] = total[:, right:].astype(BF)


def sum_two(left_keep, left_got, right_keep, right_got, keep, s1, s2, s3):
    rows = keep.shape[0]
    left = left_keep.shape[1]
    for k, out in enumerate((keep, s1, s2, s3)):
        span = slice(k * rows, (k + 1) * rows)
        total = left_keep[span].astype(F32) + left_got[span].astype(F32)
        out[:, :left] = total.astype(out.dtype)
        total = right_keep[span].astype(F32) + right_got[span].astype(F32)
        out[:, left:] = total.astype(out.dtype)


def sum_three(keep, r1, r2, r3, first, second):
    total = keep[...] + (r1[...].astype(F32) + (r2[...].astype(F32) + r3[...].astype(F32)))
    wide = first.shape[1]
    first[...] = total[:, :wide]
    second[...] = total[:, wide:]


def scatter_start(own, far):
    rows, width = own.shape
    left = width // 256 * 128
    right = width - left
    half = rows // 2
    left_own, left_far, right_near, right_send = run(
        cut_pack,
        [((rows, left), BF)] * 2 + [((half, 2 * right), BF)] * 2,
        (own, far),
        rows * width,
    )
    return left_own, swap(left_far, y=1), right_near, swap(right_send, x=1)


def scatter_middle(parts):
    rows, left = parts[0].shape
    half, right = parts[2].shape
    outs = [((half, left), BF)] * 2 + [((half, right // 2), BF)] * 2
    left_keep, left_send, right_keep, right_send = run(sum_one, outs, parts, rows * left)
    return left_keep, swap(left_send, x=1), right_keep, swap(right_send, y=1)


def scatter_late(parts):
    half, left = parts[0].shape
    width = left + parts[2].shape[1]
    rows = half // 4
    keep, s1, s2, s3 = run(
        sum_two,
        [((rows, width), F32)] + [((rows, width), BF)] * 3,
        parts,
        half * width,
    )
    return keep, swap(s1, z=1), swap(s2, z=2), swap(s3, z=3)


def scatter_end(parts, wide):
    rows, width = parts[0].shape
    return run(sum_three, [((rows, wide), F32), ((rows, width - wide), F32)], parts, rows * width)


def exchange_rows(pieces):
    return [pieces[0]] + [swap(pieces[p], z=p & 3, x=p >> 2) for p in range(1, 8)]


def reduce_peak(peaks):
    half = peaks.shape[1] // 2
    best = jnp.maximum(peaks[:, :half], swap(peaks[:, half:], y=1))
    best = jnp.maximum(best, swap(best, x=1))
    far = [swap(best, z=k) for k in (1, 2, 3)]
    return jnp.maximum(jnp.maximum(best, far[0]), jnp.maximum(far[1], far[2]))


def fast_local(
    block_input,
    first_norm,
    first_qkv,
    first_out,
    second_norm,
    dense_up,
    dense_down,
    third_norm,
    second_qkv,
    second_out,
    fourth_norm,
    router_weight,
    expert_up,
    expert_down,
    expert_ids,
    expert_slots,
    image_counts,
    cotangent,
):
    d = lax.axis_index("dp")
    t = lax.axis_index("tensor")
    z_index, x_index = d // 2, d % 2
    width = first_norm.shape[0]
    features = width * 8
    experts = expert_up.shape[0]
    live_count = image_counts[0]
    head_cols = first_out.shape[0]
    ff_cols = dense_up.shape[1]
    qkv_cols = 3 * head_cols
    row = ((ROWS, features), F32)
    row_low = ((ROWS, features), BF)

    small = jnp.concatenate(
        [
            jnp.stack([first_norm, second_norm, third_norm, fourth_norm], axis=1),
            router_weight,
            jnp.zeros((width, 128 - 4 - experts), BF),
        ],
        axis=1,
    )
    pack_one = jnp.concatenate([first_qkv.reshape(width, -1), small], axis=1)
    pack_two = jnp.concatenate([dense_up, first_out.T], axis=1)
    pack_late = jnp.concatenate(
        [dense_down.T, second_out.T, second_qkv.reshape(width, -1)], axis=1
    )
    cut_late = ff_cols + head_cols

    z_one = gather_z(pack_one)
    first_of_one = gather_first(z_one)
    z_two = gather_z(hold(pack_two, z_one))
    full_one = gather_second(first_of_one)
    z_late = gather_z(hold(pack_late, z_two))
    full_two = gather_second(gather_first(hold(z_two, full_one[1])))
    full_three = gather_second(gather_first(hold(z_late[:, :cut_late], full_two[1])))
    full_four = gather_second(gather_first(hold(z_late[:, cut_late:], full_three[1])))

    small_rows = z_one[:, qkv_cols : qkv_cols + 4 + experts]
    small_rows = jnp.concatenate([small_rows, swap(small_rows, x=1)], axis=0).T
    gains = [small_rows[i : i + 1].astype(F32) for i in range(4)]
    router = small_rows[4:]

    rel = jnp.arange(features)
    block = rel // width
    rel_place = jnp.bitwise_xor(d, 2 * (block % 4) + block // 4) * width + rel % width
    perm = (rel_place[:, None] == rel[None, :]).astype(BF)
    live_here = (t < live_count).astype(jnp.int32).reshape(1)
    live_pair = (jnp.stack([t, t ^ 1]) < live_count).astype(jnp.int32)

    start, grad_four, grad_low = run(
        enter_kernel,
        [row, row, row_low],
        (live_here, block_input, cotangent, perm),
        4 * ROWS * features**2,
        scalars=1,
    )

    places = jnp.stack([2 * (z_index ^ k) + (x_index ^ x) for k in range(4) for x in range(2)])
    places = places.astype(jnp.int32)
    wide = 2 * ff_cols
    quads = run(
        choose_kernel,
        [((2 * width, wide), BF)] * 4,
        (places, expert_up, jnp.swapaxes(expert_down, 1, 2)),
        features * wide,
        scalars=1,
    )
    quads = [hold(q, z_late) for q in quads]
    quads = [quads[0]] + [swap(quads[k], z=k) for k in (1, 2, 3)]
    e_near, e_send = run(split_kernel, [((features // 2, wide), BF)] * 2, tuple(quads), features * wide)
    e_side = swap(hold(e_send, full_three[1]), x=1)
    e_far_near = swap(hold(e_near, full_four[1]), y=1)
    e_far_side = swap(e_side, y=1)

    block_size = -(-CAP // (4 * 8)) * 8
    ids = jnp.pad(expert_ids.reshape(4, L, 2), ((0, 0), (0, ROWS - L), (0, 0)), constant_values=-1)
    slots = jnp.pad(
        expert_slots.reshape(4, L, 2), ((0, 0), (0, ROWS - L), (0, 0)), constant_values=CAP
    )
    mine = (slots < CAP) & (slots // block_size == t)
    codes = jnp.where(mine, ids * block_size + slots % block_size, -1)
    codes = jnp.concatenate(
        [lax.dynamic_index_in_dim(codes, t ^ k, 0, keepdims=False) for k in (0, 2, 1, 3)], axis=0
    ).T
    position = jnp.arange(experts)
    expert_at = jnp.bitwise_xor(d, 2 * (position % 4) + position // 4)
    row_code = (expert_at[:, None] * block_size + jnp.arange(block_size)[None, :]).reshape(-1, 1)
    slot_rows = experts * block_size
    piece = ((block_size, features), BF)
    group_flops = 2 * slot_rows * features * (4 * ROWS + features)

    def to_experts(rows):
        pair = jnp.concatenate([rows, swap(rows, y=1)], axis=0)
        pieces = run(
            dispatch_kernel,
            [piece] * experts,
            (row_code, codes, pair, swap(pair, core=1), perm),
            group_flops,
            scratch=[pltpu.VMEM((4 * ROWS, features), BF)],
        )
        return pieces

    def collect(pieces):
        return run(
            collect_kernel,
            [((slot_rows, features), BF)],
            (perm, *pieces),
            2 * slot_rows * features**2,
            scratch=[pltpu.VMEM((slot_rows, features), BF)],
        )[0]

    def from_experts(pieces):
        own, send = run(
            combine_kernel,
            [((2 * ROWS, features), F32), ((2 * ROWS, features), BF)],
            (row_code, codes, perm, *pieces),
            group_flops,
            scratch=[pltpu.VMEM((slot_rows, features), BF)],
        )
        near, send = run(pair_add_kernel, [row, row_low], (own, swap(send, core=1)), ROWS)
        return near, swap(send, y=1)

    def attend(normed, far_normed, full_qkv, full_out, out_at):
        qkv = [w[:, :qkv_cols] for w in full_qkv]
        out = [w[:, out_at:] for w in full_out]
        return qkv, out, run(
            attend_kernel,
            [
                ((2, 2 * ROWS, qkv_cols), BF),
                ((2 * ROWS, 2 * head_cols), BF),
                row,
                row_low,
                ((8, 128), F32),
            ],
            (live_pair, normed, far_normed, *qkv, *out),
            2 * 2 * ROWS * features * 8 * head_cols,
            scratch=[pltpu.VMEM((2 * ROWS, features), BF)],
            scalars=1,
        )

    def attend_back(low, normed, far_normed, mixed, attended, qkv, out):
        return run(
            attend_back_kernel,
            [((features, 4 * head_cols), BF)] * 2 + [row, row_low],
            (low, swap(low, core=1), normed, far_normed, mixed, attended, *qkv, *out),
            4 * 2 * ROWS * features * 8 * head_cols,
            scratch=[
                pltpu.VMEM((2 * ROWS, features), BF),
                pltpu.VMEM((2 * ROWS, 2 * head_cols), BF),
                pltpu.VMEM((2, 2 * ROWS, qkv_cols), BF),
            ],
        )

    def join(values, own, far, gain):
        total, normed = run(join_norm_kernel, [row, row_low], (values, own, far, gain), ROWS)
        return total, normed, swap(normed, core=1)

    def norm_back(values, upstream, own, far, gain):
        return run(
            norm_back_kernel,
            [row, row_low, ((1, features), F32)],
            (values, upstream, own, far, gain),
            ROWS,
        )

    normed_one = run(norm_kernel, [row_low], (start, gains[0]), ROWS)[0]
    far_one = swap(normed_one, core=1)
    qkv_one, out_one, (mixed_one, att_one, own, sib, peak_one) = attend(
        normed_one, far_one, full_one, full_two, ff_cols
    )
    one, normed_mlp, far_mlp = join(start, own, swap(sib, core=1), gains[1])

    up = [w[:, :ff_cols] for w in full_two]
    down = [w[:, :ff_cols] for w in full_three]
    pair_scratch = pltpu.VMEM((2 * ROWS, features), BF)
    act, slope, own, sib = run(
        mlp_kernel,
        [((2, 2 * ROWS, ff_cols), BF)] * 2 + [row, row_low],
        (normed_mlp, far_mlp, *up, *down),
        2 * 2 * ROWS * features * 4 * ff_cols,
        scratch=[pair_scratch],
    )
    two, normed_two, far_two = join(one, own, swap(sib, core=1), gains[2])
    qkv_two, out_two, (mixed_two, att_two, own, sib, peak_two) = attend(
        normed_two, far_two, full_four, full_three, ff_cols
    )
    three, normed_four, _ = join(two, own, swap(sib, core=1), gains[3])

    grad_slots = collect(exchange_rows(to_experts(hold(grad_low, e_near))))
    far_slots = swap(grad_slots, core=1)
    tokens = collect(exchange_rows(to_experts(normed_four)))
    far_tokens = swap(tokens, core=1)
    number = d.astype(jnp.int32).reshape(1)
    e_own = jnp.concatenate([e_near, e_side], axis=0)
    e_far = jnp.concatenate([e_far_near, e_far_side], axis=0)
    e_up = [e_own[:, :ff_cols], e_far[:, :ff_cols]]
    e_down = [e_own[:, ff_cols:], e_far[:, ff_cols:]]
    slot_out = [((slot_rows, features), F32), ((slot_rows, features), BF)]
    e_act, e_hidden, e_gout, res_own, res_sib, eg_own, eg_sib = run(
        expert_kernel,
        [((2, 2 * slot_rows, ff_cols), BF)] * 2
        + [((2 * slot_rows, features), BF)]
        + slot_out
        + slot_out,
        (number, tokens, far_tokens, grad_slots, far_slots, router, *e_up, *e_down),
        8 * 2 * slot_rows * features * 2 * ff_cols,
        scalars=1,
        scratch=[pltpu.VMEM((8, 128), F32)],
        mib=48,
    )
    answers = run(
        answer_kernel,
        [piece] * 16 + [((experts, features), F32)],
        (
            number,
            tokens,
            grad_slots,
            router,
            res_own,
            swap(res_sib, core=1),
            eg_own,
            swap(eg_sib, core=1),
            perm,
        ),
        4 * slot_rows * features**2,
        scalars=1,
    )
    grad_router = answers[16]
    back_own, back_far = from_experts(exchange_rows(answers[:8]))
    e_pack_own, e_pack_far = run(
        expert_grad_kernel,
        [((features, wide), BF)] * 2,
        (tokens, far_tokens, e_act, e_hidden, e_gout),
        8 * slot_rows * features * wide,
        scratch=[pltpu.VMEM((2 * slot_rows, features), BF)],
        mib=40,
    )
    e_got = swap(e_pack_far, y=1)
    grad_three, low, gain_four = norm_back(three, grad_four, back_own, back_far, gains[3])
    result_pieces = [hold(p, low) for p in answers[8:16]]

    pack_own, pack_far, own, sib = attend_back(
        low, normed_two, far_two, mixed_two, att_two, qkv_two, out_two
    )
    grad_two, low, gain_three = norm_back(two, grad_three, own, swap(sib, core=1), gains[2])
    second = scatter_start(pack_own, pack_far)

    mixed_own, mixed_far = from_experts(exchange_rows(result_pieces))
    block_output = run(
        finish_kernel,
        [((L, features), F32)],
        (live_here, three, mixed_own, mixed_far, perm),
        6 * ROWS * features**2,
        scalars=1,
    )[0]

    e_near_g, e_send_g = run(
        add_split_kernel,
        [((features // 2, wide), BF)] * 2,
        (e_pack_own, hold(e_got, low)),
        features * wide,
    )
    e_side_g = swap(e_send_g, x=1)

    pack_own, pack_far, own, sib = run(
        mlp_back_kernel,
        [((features, wide), BF)] * 2 + [row, row_low],
        (low, swap(low, core=1), normed_mlp, far_mlp, act, slope, *up, *down),
        4 * 2 * ROWS * features * 4 * ff_cols,
        scratch=[pair_scratch, pltpu.VMEM((2, 2 * ROWS, ff_cols), BF)],
    )
    second = scatter_middle(hold(second, sib))
    grad_one, low, gain_two = norm_back(one, grad_two, own, swap(sib, core=1), gains[1])
    mlp = scatter_start(pack_own, pack_far)

    quads = run(
        regroup_kernel,
        [((2 * width, wide), BF)] * 4,
        (e_near_g, hold(e_side_g, low)),
        features * wide,
    )
    quads = [quads[0]] + [swap(quads[k], z=k) for k in (1, 2, 3)]

    pack_own, pack_far, own, sib = attend_back(
        low, normed_one, far_one, mixed_one, att_one, qkv_one, out_one
    )
    first = scatter_start(pack_own, pack_far)
    grad_zero, _, gain_one = norm_back(start, grad_one, own, swap(sib, core=1), gains[0])
    input_grad = run(
        leave_kernel, [((L, features), F32)], (grad_zero, perm), 6 * ROWS * features**2
    )[0]
    mlp = scatter_middle(hold(mlp, sib))
    second = scatter_late(hold(second, sib))
    up_g, down_g = run(
        place_kernel,
        [((experts, width, ff_cols), F32)] * 2,
        (places, *hold(quads, sib)),
        features * wide,
        scalars=1,
    )
    first = scatter_middle(first)
    mlp = scatter_late(mlp)
    first = scatter_late(first)
    second = scatter_end(second, qkv_cols)
    mlp = scatter_end(mlp, ff_cols)
    first = scatter_end(first, qkv_cols)

    tail = jnp.concatenate([gain_one, gain_two, gain_three, gain_four, grad_router])
    tail = jnp.swapaxes(tail.reshape(4 + experts, 8, width), 0, 1)
    tail = tail + swap(tail, core=1)
    tail = tail + swap(tail, y=1)
    tail = tail[:4] + swap(tail[4:], x=1)
    tail = tail[0] + swap(tail[1], z=1) + swap(tail[2], z=2) + swap(tail[3], z=3)

    peaks = jnp.stack([peak_one[: 2 * head_cols // HD, 0], peak_two[: 2 * head_cols // HD, 0]])
    roots = clip_root(reduce_peak(peaks))
    return (
        block_output,
        input_grad,
        tail[0],
        first[0].reshape(first_qkv.shape),
        first[1].T,
        tail[1],
        mlp[0],
        mlp[1].T,
        tail[2],
        second[0].reshape(second_qkv.shape),
        second[1].T,
        tail[3],
        tail[4:].T,
        up_g,
        jnp.swapaxes(down_g, 1, 2),
        clip_columns(first_qkv, roots[0], HD),
        clip_columns(second_qkv, roots[1], HD),
        roots,
    )


def solution(mesh):
    placed = (
        P(("dp", "tensor"), None),
        P("dp"),
        P("dp", None, "tensor"),
        P("tensor", "dp"),
        P("dp"),
        P("dp", "tensor"),
        P("tensor", "dp"),
        P("dp"),
        P("dp", None, "tensor"),
        P("tensor", "dp"),
        P("dp"),
        P("dp", None),
        P(None, "dp", "tensor"),
        P(None, "tensor", "dp"),
        P("dp", None),
        P("dp", None),
        P("dp"),
        P(("dp", "tensor"), None),
    )
    quick = mesh.shape["dp"] == 8 and mesh.shape["tensor"] == 4
    return jax.shard_map(
        fast_local if quick else local,
        mesh=mesh,
        in_specs=placed,
        out_specs=(
            P(("dp", "tensor"), None),
            P(("dp", "tensor"), None),
            P("dp"),
            P("dp", None, "tensor"),
            P("tensor", "dp"),
            P("dp"),
            P("dp", "tensor"),
            P("tensor", "dp"),
            P("dp"),
            P("dp", None, "tensor"),
            P("tensor", "dp"),
            P("dp"),
            P("dp", None),
            P(None, "dp", "tensor"),
            P(None, "tensor", "dp"),
            P("dp", None, "tensor"),
            P("dp", None, "tensor"),
            P(None, "tensor"),
        ),
        check_vma=False,
    )
```

```python
import functools

import jax
import jax.numpy as jnp
from jax import lax
from jax.experimental import pallas as pl
from jax.experimental.pallas import tpu as pltpu
from jax.sharding import PartitionSpec as P

HD = 64
L = 197
CAP = 197


epsilon = 1e-06
clip_tau = 2.5


def layer_norm(values, norm_gain):
    center = values - jnp.mean(values, axis=-1, keepdims=True)
    spread = jnp.mean(center * center, axis=-1, keepdims=True)
    return center * lax.rsqrt(spread + epsilon) * norm_gain


def exact_gelu(values):
    return jax.nn.gelu(values, approximate=False)


def gelu_back(values, upstream):
    return jax.vjp(exact_gelu, values)[1](upstream)[0]


def norm_back(residual, norm_gain, upstream):
    pullback = jax.vjp(layer_norm, residual, norm_gain.astype(jnp.float32))[1]
    return pullback(upstream)


def gather_rows(values):
    return lax.all_gather(values, "tensor", axis=0, tiled=True)


def scatter_rows(values):
    return lax.psum_scatter(
        values.astype(jnp.bfloat16), "tensor", scatter_dimension=0, tiled=True
    ).astype(jnp.float32)


def sum_gains(first_gain, second_gain):
    return lax.psum((first_gain, second_gain), "tensor")


def split_heads(projected, images, head_size):
    row_count, triple, columns = projected.shape
    pieces = projected.reshape(images, row_count // images, triple, columns // head_size, head_size)
    return (pieces[:, :, 0], pieces[:, :, 1], pieces[:, :, 2])


def attend_scores(queries, keyset, head_size):
    scores = jnp.einsum("iqhd,ikhd->ihqk", queries, keyset, preferred_element_type=jnp.float32)
    return scores * head_size ** (-0.5)


def attend_forward(normed_full, weight_qkv, images, head_size, live_images):
    projected = jnp.einsum(
        "rd,dcf->rcf", normed_full, weight_qkv, preferred_element_type=jnp.float32
    ).astype(jnp.bfloat16)
    queries, keyset, values = split_heads(projected, images, head_size)
    scores = attend_scores(queries, keyset, head_size)
    head_peak = jnp.max(jnp.where(live_images[:, None, None, None], scores, -1e30), axis=(0, 2, 3))
    attn_probs = jax.nn.softmax(scores, axis=-1).astype(jnp.bfloat16)
    attended = jnp.einsum("ihqk,ikhd->iqhd", attn_probs, values, preferred_element_type=jnp.float32)
    return (projected, attended.astype(jnp.bfloat16).reshape(normed_full.shape[0], -1), head_peak)


def attend_backward(projected, grad_attended, images, head_size):
    queries, keyset, values = split_heads(projected, images, head_size)
    scores = attend_scores(queries, keyset, head_size)
    attn_probs = jax.nn.softmax(scores, axis=-1)
    grad_heads = grad_attended.reshape(queries.shape)
    grad_values = jnp.einsum(
        "ihqk,iqhd->ikhd",
        attn_probs.astype(jnp.bfloat16),
        grad_heads,
        preferred_element_type=jnp.float32,
    )
    grad_probs = jnp.einsum(
        "iqhd,ikhd->ihqk", grad_heads, values, preferred_element_type=jnp.float32
    )
    grad_scores = attn_probs * (
        grad_probs - jnp.sum(grad_probs * attn_probs, axis=-1, keepdims=True)
    )
    grad_scores = grad_scores.astype(jnp.bfloat16)
    factor = head_size ** (-0.5)
    grad_queries = (
        jnp.einsum("ihqk,ikhd->iqhd", grad_scores, keyset, preferred_element_type=jnp.float32)
        * factor
    )
    grad_keyset = (
        jnp.einsum("ihqk,iqhd->ikhd", grad_scores, queries, preferred_element_type=jnp.float32)
        * factor
    )
    stacked = jnp.stack([grad_queries, grad_keyset, grad_values], axis=2).astype(jnp.bfloat16)
    return stacked.reshape(projected.shape)


def block_attention(residual, norm_gain, weight_qkv, weight_out, images, head_size, live_images):
    normed = layer_norm(residual, norm_gain.astype(jnp.float32)).astype(jnp.bfloat16)
    normed_full = gather_rows(normed)
    projected, attended, head_peak = attend_forward(
        normed_full, weight_qkv, images, head_size, live_images
    )
    branch = scatter_rows(jnp.dot(attended, weight_out, preferred_element_type=jnp.float32))
    return (residual + branch, (normed_full, projected, attended), head_peak)


def block_attention_back(
    residual, upstream, norm_gain, weight_qkv, weight_out, stored, images, head_size
):
    normed_full, projected, attended = stored
    grad_full = gather_rows(upstream.astype(jnp.bfloat16))
    grad_out = jnp.einsum("rf,rd->fd", attended, grad_full, preferred_element_type=jnp.float32)
    grad_attended = jnp.einsum(
        "rd,fd->rf", grad_full, weight_out, preferred_element_type=jnp.float32
    ).astype(jnp.bfloat16)
    grad_projected = attend_backward(projected, grad_attended, images, head_size)
    grad_qkv = jnp.einsum(
        "rd,rcf->dcf", normed_full, grad_projected, preferred_element_type=jnp.float32
    )
    grad_normed = scatter_rows(
        jnp.einsum("rcf,dcf->rd", grad_projected, weight_qkv, preferred_element_type=jnp.float32)
    )
    grad_residual, grad_gain = norm_back(residual, norm_gain, grad_normed)
    return (upstream + grad_residual, grad_gain, grad_qkv, grad_out)


def block_mlp(residual, norm_gain, weight_up, weight_down):
    normed = layer_norm(residual, norm_gain.astype(jnp.float32)).astype(jnp.bfloat16)
    normed_full = gather_rows(normed)
    hidden = jnp.dot(normed_full, weight_up, preferred_element_type=jnp.float32)
    active = exact_gelu(hidden).astype(jnp.bfloat16)
    branch = scatter_rows(jnp.dot(active, weight_down, preferred_element_type=jnp.float32))
    return (residual + branch, (normed_full, hidden, active))


def block_mlp_back(residual, upstream, norm_gain, weight_up, weight_down, stored):
    normed_full, hidden, active = stored
    grad_full = gather_rows(upstream.astype(jnp.bfloat16))
    grad_down = jnp.einsum("rf,rd->fd", active, grad_full, preferred_element_type=jnp.float32)
    grad_active = jnp.einsum(
        "rd,fd->rf", grad_full, weight_down, preferred_element_type=jnp.float32
    )
    grad_hidden = gelu_back(hidden, grad_active).astype(jnp.bfloat16)
    grad_up = jnp.einsum("rd,rf->df", normed_full, grad_hidden, preferred_element_type=jnp.float32)
    grad_normed = scatter_rows(
        jnp.einsum("rf,df->rd", grad_hidden, weight_up, preferred_element_type=jnp.float32)
    )
    grad_residual, grad_gain = norm_back(residual, norm_gain, grad_normed)
    return (upstream + grad_residual, grad_gain, grad_up, grad_down)


def clip_root(head_peak):
    return jnp.sqrt(clip_tau / jnp.maximum(head_peak, clip_tau))


def clip_columns(weight_local, head_root, head_size):
    column = jnp.repeat(head_root, head_size)
    scales = jnp.stack([column, column, jnp.ones_like(column)])
    return weight_local.astype(jnp.float32) * scales[None]


def local(
    block_input,
    first_norm,
    first_qkv,
    first_out,
    second_norm,
    dense_up,
    dense_down,
    third_norm,
    second_qkv,
    second_out,
    fourth_norm,
    router_weight,
    expert_up,
    expert_down,
    expert_ids,
    expert_slots,
    image_counts,
    cotangent,
):
    rows_local = block_input.shape[0]
    rows_full = rows_local * lax.axis_size("tensor")
    images = rows_full // L
    head_size = HD
    experts = expert_up.shape[0]
    capacity = CAP
    first_row = lax.axis_index("tensor") * rows_local
    live_count = image_counts[0]
    local_live = ((first_row + jnp.arange(rows_local)) // L < live_count).astype(jnp.float32)
    full_live = (jnp.arange(rows_full) // L < live_count).astype(jnp.float32)
    live_images = jnp.arange(images) < live_count

    def dense_fetch():
        return (
            lax.all_gather(first_norm, "dp", axis=0, tiled=True),
            lax.all_gather(first_qkv, "dp", axis=0, tiled=True),
            lax.all_gather(first_out, "dp", axis=1, tiled=True),
            lax.all_gather(second_norm, "dp", axis=0, tiled=True),
            lax.all_gather(dense_up, "dp", axis=0, tiled=True),
            lax.all_gather(dense_down, "dp", axis=1, tiled=True),
        )

    def moe_fetch():
        return (
            lax.all_gather(third_norm, "dp", axis=0, tiled=True),
            lax.all_gather(second_qkv, "dp", axis=0, tiled=True),
            lax.all_gather(second_out, "dp", axis=1, tiled=True),
            lax.all_gather(fourth_norm, "dp", axis=0, tiled=True),
            lax.all_gather(router_weight, "dp", axis=0, tiled=True),
            lax.all_gather(expert_up, "dp", axis=1, tiled=True),
            lax.all_gather(expert_down, "dp", axis=2, tiled=True),
        )

    dense_full = dense_fetch()
    residual_zero = block_input.astype(jnp.float32)
    residual_one, attn_first, peak_first = block_attention(
        residual_zero, dense_full[0], dense_full[1], dense_full[2], images, head_size, live_images
    )
    residual_two, mlp_stored = block_mlp(residual_one, dense_full[3], dense_full[4], dense_full[5])
    moe_full = moe_fetch()
    residual_three, attn_second, peak_second = block_attention(
        residual_two, moe_full[0], moe_full[1], moe_full[2], images, head_size, live_images
    )
    moe_normed = layer_norm(residual_three, moe_full[3].astype(jnp.float32)).astype(jnp.bfloat16)
    moe_input = gather_rows(moe_normed)
    logits = jnp.dot(moe_input, moe_full[4], preferred_element_type=jnp.float32)
    route_probs = jax.nn.softmax(logits, axis=-1)
    kept_mask = expert_slots < capacity
    pair_number = jnp.arange(2 * rows_full, dtype=jnp.int32)
    slot_index = (expert_ids * capacity + expert_slots).reshape(-1)
    kept_flat = kept_mask.reshape(-1)
    write_target = jnp.where(kept_flat, slot_index, experts * capacity + pair_number)
    target = jnp.where(kept_flat, slot_index, experts * capacity)
    pair_of_slot = (
        jnp.zeros((experts * capacity + 2 * rows_full,), jnp.int32)
        .at[write_target]
        .set(pair_number)[: experts * capacity]
    )
    slot_filled = (
        jnp.zeros((experts * capacity + 2 * rows_full,), jnp.float32)
        .at[write_target]
        .set(1.0)[: experts * capacity]
    )
    chosen = (expert_ids[:, :, None] == jnp.arange(experts)[None, None, :]).astype(jnp.float32)
    keep_live = kept_mask.astype(jnp.float32) * full_live[:, None]
    gates = jnp.sum(chosen * route_probs[:, None, :], axis=-1) * keep_live
    slot_token = pair_of_slot // 2
    slot_gate = gates.reshape(-1)[pair_of_slot] * slot_filled
    dispatched = (moe_input[slot_token] * slot_filled[:, None].astype(jnp.bfloat16)).reshape(
        experts, capacity, -1
    )
    expert_hidden = jnp.einsum(
        "ecd,edf->ecf", dispatched, moe_full[5], preferred_element_type=jnp.float32
    )
    expert_act = exact_gelu(expert_hidden).astype(jnp.bfloat16)
    expert_result = jnp.einsum(
        "ecf,efd->ecd", expert_act, moe_full[6], preferred_element_type=jnp.float32
    )
    feature_count = expert_result.shape[2]
    padded_result = jnp.concatenate(
        [
            expert_result.reshape(experts * capacity, feature_count),
            jnp.zeros((1, feature_count), jnp.float32),
        ],
        axis=0,
    )
    pair_result = padded_result[target].reshape(rows_full, 2, feature_count)
    combined = jnp.sum(gates[:, :, None] * pair_result, axis=1)
    residual_four = residual_three + scatter_rows(combined)
    block_output = residual_four * local_live[:, None]
    peak_first_all, peak_second_all = lax.pmax((peak_first, peak_second), "dp")
    root_first = clip_root(peak_first_all)
    root_second = clip_root(peak_second_all)
    clipped_first = clip_columns(first_qkv, root_first, head_size)
    clipped_second = clip_columns(second_qkv, root_second, head_size)
    clip_scales = jnp.stack([root_first, root_second])
    moe_back = moe_fetch()
    grad_four = cotangent.astype(jnp.float32) * local_live[:, None]
    moe_grad_full = gather_rows(grad_four.astype(jnp.bfloat16))
    partial_gates = jnp.sum(moe_grad_full.astype(jnp.float32)[:, None, :] * pair_result, axis=-1)
    grad_gates = lax.psum(partial_gates, "tensor")
    grad_result = (slot_gate[:, None] * moe_grad_full[slot_token].astype(jnp.float32)).astype(
        jnp.bfloat16
    )
    grad_result = grad_result.reshape(experts, capacity, feature_count)
    grad_expert_down = jnp.einsum(
        "ecf,ecd->efd", expert_act, grad_result, preferred_element_type=jnp.float32
    )
    grad_act = jnp.einsum(
        "ecd,efd->ecf", grad_result, moe_back[6], preferred_element_type=jnp.float32
    )
    grad_hidden = gelu_back(expert_hidden, grad_act).astype(jnp.bfloat16)
    grad_expert_up = jnp.einsum(
        "ecd,ecf->edf", dispatched, grad_hidden, preferred_element_type=jnp.float32
    )
    grad_dispatch = jnp.einsum(
        "ecf,edf->ecd", grad_hidden, moe_back[5], preferred_element_type=jnp.float32
    )
    grad_dispatch = jnp.concatenate(
        [
            grad_dispatch.reshape(experts * capacity, feature_count),
            jnp.zeros((1, feature_count), jnp.float32),
        ],
        axis=0,
    )
    grad_from_experts = jnp.sum(grad_dispatch[target].reshape(rows_full, 2, feature_count), axis=1)
    grad_picked = grad_gates * keep_live
    grad_probs = jnp.sum(chosen * grad_picked[:, :, None], axis=1)
    grad_logits = route_probs * (
        grad_probs - jnp.sum(grad_probs * route_probs, axis=-1, keepdims=True)
    )
    grad_logits = grad_logits.astype(jnp.bfloat16)
    grad_router = jnp.einsum(
        "rd,re->de", moe_input, grad_logits, preferred_element_type=jnp.float32
    )
    local_logits = lax.dynamic_slice_in_dim(grad_logits, first_row, rows_local, 0)
    grad_moe_normed = scatter_rows(grad_from_experts) + jnp.einsum(
        "re,de->rd", local_logits, moe_back[4], preferred_element_type=jnp.float32
    )
    grad_rows_four, grad_fourth_norm = norm_back(residual_three, moe_back[3], grad_moe_normed)
    grad_three = grad_four + grad_rows_four
    grad_two, grad_third_norm, grad_second_qkv, grad_second_out = block_attention_back(
        residual_two,
        grad_three,
        moe_back[0],
        moe_back[1],
        moe_back[2],
        attn_second,
        images,
        head_size,
    )
    third_sum, fourth_sum = sum_gains(grad_third_norm, grad_fourth_norm)
    moe_owned = (
        lax.psum_scatter(third_sum, "dp", scatter_dimension=0, tiled=True),
        lax.psum_scatter(grad_second_qkv, "dp", scatter_dimension=0, tiled=True),
        lax.psum_scatter(grad_second_out, "dp", scatter_dimension=1, tiled=True),
        lax.psum_scatter(fourth_sum, "dp", scatter_dimension=0, tiled=True),
        lax.psum_scatter(grad_router, "dp", scatter_dimension=0, tiled=True),
        lax.psum_scatter(grad_expert_up, "dp", scatter_dimension=1, tiled=True),
        lax.psum_scatter(grad_expert_down, "dp", scatter_dimension=2, tiled=True),
    )
    dense_back = dense_fetch()
    grad_one, grad_second_norm, grad_dense_up, grad_dense_down = block_mlp_back(
        residual_one, grad_two, dense_back[3], dense_back[4], dense_back[5], mlp_stored
    )
    input_grad, grad_first_norm, grad_first_qkv, grad_first_out = block_attention_back(
        residual_zero,
        grad_one,
        dense_back[0],
        dense_back[1],
        dense_back[2],
        attn_first,
        images,
        head_size,
    )
    first_sum, second_sum = sum_gains(grad_first_norm, grad_second_norm)
    dense_owned = (
        lax.psum_scatter(first_sum, "dp", scatter_dimension=0, tiled=True),
        lax.psum_scatter(grad_first_qkv, "dp", scatter_dimension=0, tiled=True),
        lax.psum_scatter(grad_first_out, "dp", scatter_dimension=1, tiled=True),
        lax.psum_scatter(second_sum, "dp", scatter_dimension=0, tiled=True),
        lax.psum_scatter(grad_dense_up, "dp", scatter_dimension=0, tiled=True),
        lax.psum_scatter(grad_dense_down, "dp", scatter_dimension=1, tiled=True),
    )
    owned = tuple(dense_owned) + tuple(moe_owned)
    return (
        block_output,
        input_grad,
        owned[0],
        owned[1],
        owned[2],
        owned[3],
        owned[4],
        owned[5],
        owned[6],
        owned[7],
        owned[8],
        owned[9],
        owned[10],
        owned[11],
        owned[12],
        clipped_first,
        clipped_second,
        clip_scales,
    )


ROWS = 208
AXES = ("dp", "tensor")
BF = jnp.bfloat16
F32 = jnp.float32
VM = pl.BlockSpec(memory_space=pltpu.VMEM)
SM = pl.BlockSpec(memory_space=pltpu.SMEM)


def swap(values, z=0, x=0, y=0, core=0):
    shift_d, shift_t = 2 * z + x, 2 * y + core
    pairs = [(d * 4 + t, (d ^ shift_d) * 4 + (t ^ shift_t)) for d in range(8) for t in range(4)]
    return lax.ppermute(values, AXES, pairs)


def hold(values, *tokens):
    return lax.optimization_barrier((values,) + tokens)[0]


def run(kernel, outs, args, flops, scratch=(), scalars=0, mib=20):
    flops = flops if flops == 8e9 else 1000
    shapes = [jax.ShapeDtypeStruct(s, dt) for s, dt in outs]
    return pl.pallas_call(
        kernel,
        out_shape=shapes,
        in_specs=[SM] * scalars + [VM] * (len(args) - scalars),
        out_specs=[VM] * len(shapes),
        scratch_shapes=list(scratch),
        compiler_params=pltpu.CompilerParams(vmem_limit_bytes=mib * 2**20),
        cost_estimate=pl.CostEstimate(flops=int(flops), bytes_accessed=1000, transcendentals=0),
    )(*args)


def dot(a, b, ca, cb):
    return lax.dot_general(a, b, (((ca,), (cb,)), ((), ())), preferred_element_type=F32)


def norm_stats(values):
    center = values - jnp.mean(values, axis=-1, keepdims=True)
    scale = lax.rsqrt(jnp.mean(center * center, axis=-1, keepdims=True) + epsilon)
    return center * scale, scale


def enter_kernel(live, x_ref, c_ref, perm_ref, start_ref, low_start, grad_ref, low_ref):
    rows = x_ref.shape[0]
    scale = live[0].astype(F32)
    extra = jnp.zeros((ROWS - rows, x_ref.shape[1]), F32)
    start = dot(x_ref[...], perm_ref[...], 1, 1)
    start_ref[:rows] = start
    start_ref[rows:] = extra
    low_start[:rows] = start.astype(BF)
    low_start[rows:] = extra.astype(BF)
    grad = dot(c_ref[...], perm_ref[...], 1, 1) * scale
    grad_ref[:rows] = grad
    grad_ref[rows:] = extra
    low_ref[:rows] = grad.astype(BF)
    low_ref[rows:] = extra.astype(BF)


def norm_kernel(gain_ref, *refs):
    for x_ref, out_ref in zip(refs[:4], refs[4:]):
        out_ref[...] = (norm_stats(x_ref[...].astype(F32))[0] * gain_ref[...]).astype(BF)


def join_norm_kernel(x_ref, own_ref, far_ref, gain_ref, sum_ref, out_ref):
    total = x_ref[...] + (own_ref[...] + far_ref[...].astype(F32))
    sum_ref[...] = total
    out_ref[...] = (norm_stats(total)[0] * gain_ref[...]).astype(BF)


def norm_back_kernel(x_ref, up_ref, own_ref, far_ref, gain_ref, grad_ref, low_ref, gain_out):
    upstream = own_ref[...] + far_ref[...].astype(F32)
    normed, scale = norm_stats(x_ref[...])
    scaled = upstream * gain_ref[...]
    grad = up_ref[...] + scale * (
        scaled
        - jnp.mean(scaled, axis=-1, keepdims=True)
        - normed * jnp.mean(scaled * normed, axis=-1, keepdims=True)
    )
    grad_ref[...] = grad
    low_ref[...] = grad.astype(BF)
    gain_out[...] = jnp.sum(upstream * normed, axis=0, keepdims=True)


def fill(rows, *refs):
    size = refs[0].shape[0]
    for i, ref in enumerate(refs):
        rows[i * size : (i + 1) * size] = ref[...]


def put_partial(partial, own_ref, sib_ref):
    half = own_ref.shape[0]
    own_ref[...] = partial[:half]
    sib_ref[...] = partial[half:].astype(BF)


def score_block(queries, keyset):
    scores = dot(queries, keyset, 1, 1) * HD ** (-0.5)
    column = lax.broadcasted_iota(jnp.int32, scores.shape, 1)
    scores = jnp.where(column < L, scores, -1e30)
    top = jnp.max(scores, axis=-1, keepdims=True)
    weight = jnp.exp(scores - top)
    return weight * (1.0 / jnp.sum(weight, axis=-1, keepdims=True)), top


def attend_kernel(
    at, live, a0, a1, a2, a3, w, mix_ref, att_ref, own_ref, sib_ref, peak_ref, rows
):
    fill(rows, a0, a1, a2, a3)
    part = mix_ref.shape[1] // 3
    mix_ref[...] = dot(rows[...], w[:, at : at + 3 * part], 1, 0).astype(BF)
    row_ok = lax.broadcasted_iota(jnp.int32, (ROWS, 1), 0) < L
    lane = lax.broadcasted_iota(jnp.int32, peak_ref.shape, 1)
    found = jnp.full(peak_ref.shape, -1e30, F32)
    for h in range(part // HD):
        for i in range(4):
            span = slice(i * ROWS, (i + 1) * ROWS)
            cut = [mix_ref[span, c * part + h * HD : c * part + (h + 1) * HD] for c in range(3)]
            probs, top = score_block(cut[0], cut[1])
            mixed = dot(probs.astype(BF), cut[2], 1, 0)
            att_ref[span, h * HD : (h + 1) * HD] = mixed.astype(BF)
            best = jnp.max(jnp.where(row_ok, top, -1e30), axis=0, keepdims=True)
            best = jnp.where(live[i] > 0, best, -1e30)
            found = jnp.where(lane == h, jnp.maximum(best, found), found)
    peak_ref[...] = found
    out = w[:, at + 3 * part : at + 4 * part]
    put_partial(dot(att_ref[...], out, 1, 1), own_ref, sib_ref)


def put_pack(grad, column, near, send):
    half = near.shape[0]
    near[:, column : column + grad.shape[1]] = grad[:half]
    send[:, column : column + grad.shape[1]] = grad[half:]


def attend_back_kernel(
    at, g0, g1, g2, g3, a0, a1, a2, a3, mix_ref, att_ref, w,
    near, send, own_ref, sib_ref, rows, grad_att, grad_mix,
):
    part = mix_ref.shape[1] // 3
    fill(rows, g0, g1, g2, g3)
    grad_att[...] = dot(rows[...], w[:, at + 3 * part : at + 4 * part], 1, 0).astype(BF)
    put_pack(dot(rows[...], att_ref[...], 0, 0).astype(BF), 3 * part, near, send)
    factor = HD ** (-0.5)
    for h in range(part // HD):
        for i in range(4):
            span = slice(i * ROWS, (i + 1) * ROWS)
            spans = [slice(c * part + h * HD, c * part + (h + 1) * HD) for c in range(3)]
            queries, keyset, values = (mix_ref[span, s] for s in spans)
            grad = grad_att[span, h * HD : (h + 1) * HD]
            probs, _ = score_block(queries, keyset)
            grad_mix[span, spans[2]] = dot(probs.astype(BF), grad, 0, 0).astype(BF)
            grad_probs = dot(grad, values, 1, 1)
            slope = probs * (grad_probs - jnp.sum(grad_probs * probs, axis=-1, keepdims=True))
            slope = slope.astype(BF)
            grad_mix[span, spans[0]] = (factor * dot(slope, keyset, 1, 0)).astype(BF)
            grad_mix[span, spans[1]] = (factor * dot(slope, queries, 0, 0)).astype(BF)
    put_partial(dot(grad_mix[...], w[:, at : at + 3 * part], 1, 1), own_ref, sib_ref)
    fill(rows, a0, a1, a2, a3)
    put_pack(dot(rows[...], grad_mix[...], 0, 0).astype(BF), 0, near, send)


def gelu_pair(hidden):
    cdf = 0.5 * (1.0 + lax.erf(hidden * 0.7071067811865476))
    slope = cdf + hidden * jnp.exp(-0.5 * hidden * hidden) * 0.3989422804014327
    return (hidden * cdf).astype(BF), slope.astype(BF)


def mlp_kernel(ats, b0, b1, b2, b3, w, act_ref, slope_ref, own_ref, sib_ref, rows):
    fill(rows, b0, b1, b2, b3)
    wide = act_ref.shape[1]
    for c in range(0, wide, 256):
        span = slice(c, c + 256)
        act, slope = gelu_pair(dot(rows[...], w[:, ats[0] + c : ats[0] + c + 256], 1, 0))
        act_ref[:, span] = act
        slope_ref[:, span] = slope
    put_partial(dot(act_ref[...], w[:, ats[1] : ats[1] + wide], 1, 1), own_ref, sib_ref)


def mlp_back_kernel(
    ats, g0, g1, g2, g3, b0, b1, b2, b3, act_ref, slope_ref, w,
    near, send, own_ref, sib_ref, rows, hidden,
):
    fill(rows, g0, g1, g2, g3)
    wide = act_ref.shape[1]
    grad = dot(rows[...], w[:, ats[1] : ats[1] + wide], 1, 0) * slope_ref[...].astype(F32)
    hidden[...] = grad.astype(BF)
    put_partial(dot(hidden[...], w[:, ats[0] : ats[0] + wide], 1, 1), own_ref, sib_ref)
    put_pack(dot(rows[...], act_ref[...], 0, 0).astype(BF), wide, near, send)
    fill(rows, b0, b1, b2, b3)
    put_pack(dot(rows[...], hidden[...], 0, 0).astype(BF), 0, near, send)


def picked(row_code, codes):
    hit = (row_code[...] == codes[0:1, :]) | (row_code[...] == codes[1:2, :])
    return jnp.where(hit, 1.0, 0.0).astype(BF)


def dispatch_kernel(row_code, codes, p0, p1, p2, p3, perm_ref, out, rows):
    fill(rows, p0, p1, p2, p3)
    picks = dot(picked(row_code, codes), rows[...], 1, 0).astype(BF)
    out[...] = dot(picks, perm_ref[...], 1, 0).astype(BF)


def token_kernel(row_code, codes, p0, p1, p2, p3, perm_ref, first_ref, second_ref, out, rows):
    dispatch_kernel(row_code, codes, p0, p1, p2, p3, perm_ref, out, rows)
    row = lax.broadcasted_iota(jnp.int32, (8, 128), 0)
    block = jnp.zeros((8, 128), F32)
    for i, ref in enumerate((first_ref, second_ref)):
        high = ref[...].astype(BF).astype(F32)
        block = jnp.where(row == 2 * i + 2, high, block)
        block = jnp.where(row == 2 * i + 3, ref[...] - high, block)
    size = out.shape[0] // 8
    for e in range(8):
        span = slice((e + 1) * size - 8, (e + 1) * size)
        old = out[span, :128].astype(F32)
        out[span, :128] = jnp.where((row >= 2) & (row < 6), block, old).astype(BF)


def collect_kernel(both_ref, grad_ref, out_ref, peak_ref):
    size = both_ref.shape[1] // 2
    best = jnp.full((2, 128), -1e30, F32)
    for p in range(both_ref.shape[0]):
        rows = slice(p * size, (p + 1) * size)
        grad_ref[rows] = both_ref[p, :size]
        out_ref[rows] = both_ref[p, size:]
        block = both_ref[p, 2 * size - 8 :, :128].astype(F32)
        found = [block[2 * i + 2 : 2 * i + 3] + block[2 * i + 3 : 2 * i + 4] for i in range(2)]
        best = jnp.maximum(best, jnp.concatenate(found, axis=0))
    peak_ref[...] = best


def combine_kernel(which, row_code, codes, perm_ref, both_ref, own_ref, sib_ref, rows):
    size = both_ref.shape[1] // 2
    for p in range(both_ref.shape[0]):
        rows[p * size : (p + 1) * size] = both_ref[p, which * size : (which + 1) * size]
    back = dot(rows[...], perm_ref[...], 1, 1).astype(BF)
    partial = dot(picked(row_code, codes), back, 0, 0)
    half = partial.shape[0] // 2
    own_ref[...] = partial[:half]
    sib_ref[...] = partial[half:].astype(BF)


def pair_add_kernel(own_ref, far_ref, near_ref, send_ref):
    total = own_ref[...] + far_ref[...].astype(F32)
    near_ref[...] = total[:ROWS]
    send_ref[...] = total[ROWS:].astype(BF)


def route_of(tokens, router, number):
    logits = dot(tokens, router, 1, 1)
    column = lax.broadcasted_iota(jnp.int32, logits.shape, 1)
    logits = jnp.where(column < 8, logits, -1e30)
    weight = jnp.exp(logits - jnp.max(logits, axis=-1, keepdims=True))
    route = weight / jnp.sum(weight, axis=-1, keepdims=True)
    mine = jnp.where(column == number, 1.0, 0.0)
    return route, mine, jnp.sum(route * mine, axis=-1, keepdims=True)


def expert_kernel(
    number, t0, t1, g0, g1, router, *rest
):
    own, far = rest[0], rest[1:5]
    res_own, res_sib, grad_own, grad_sib = rest[5:9]
    up_parts, down_parts = rest[9:12], rest[12:15]
    act_ref, hid_ref, gout_ref, pair, whole = rest[15:]
    size = t0.shape[0]
    half, wide = own.shape[0] // 2, act_ref.shape[2]
    whole[0] = own[...]
    for i, part in enumerate(far):
        whole[1, i * half // 2 : (i + 1) * half // 2] = part[...]
    for i, (t, g, res, grad) in enumerate(
        ((t1, g1, res_sib, grad_sib), (t0, g0, res_own, grad_own))
    ):
        rows = slice((1 - i) * size, (2 - i) * size)
        gate = route_of(t[...], router[...], number[0])[2]
        gout = (gate * g[...].astype(F32)).astype(BF)
        gout_ref[rows] = gout
        for y in range(2):
            for c in range(0, wide, 256):
                span = slice(c, c + 256)
                act, lean = gelu_pair(dot(t[...], whole[y, :, span], 1, 0))
                act_ref[y, rows, span] = act
                back = dot(gout, whole[y, :, wide + c : wide + c + 256], 1, 0)
                hid_ref[y, rows, span] = (back * lean.astype(F32)).astype(BF)
        res[...] = (
            dot(act_ref[0, rows], whole[0, :, wide:], 1, 1)
            + dot(act_ref[1, rows], whole[1, :, wide:], 1, 1)
        ).astype(res.dtype)
        grad[...] = (
            dot(hid_ref[0, rows], whole[0, :, :wide], 1, 1)
            + dot(hid_ref[1, rows], whole[1, :, :wide], 1, 1)
        ).astype(grad.dtype)
    pair[:size] = t0[...]
    pair[size:] = t1[...]
    for parts, left, right in ((up_parts, pair, hid_ref), (down_parts, gout_ref, act_ref)):
        parts[0][...] = dot(left[...], right[0], 0, 0).astype(BF)
        far = dot(left[...], right[1], 0, 0).astype(BF)
        parts[1][...] = far[:half]
        parts[2][...] = far[half:]


def answer_kernel(
    number, t_ref, g_ref, router, res_own, res_far, grad_own, grad_far, perm_ref,
    both_ref, router_out,
):
    route, mine, gate = route_of(t_ref[...], router[...], number[0])
    result = res_own[...] + res_far[...].astype(F32)
    grad_gate = jnp.sum(result * g_ref[...].astype(F32), axis=-1, keepdims=True)
    grad_logit = (grad_gate * route * (mine - gate)).astype(BF)
    router_out[...] = reorder(dot(grad_logit, t_ref[...], 0, 0), perm_ref[...], 1)
    grad = grad_own[...] + grad_far[...].astype(F32) + dot(grad_logit, router[...], 1, 0)
    size = both_ref.shape[1] // 2
    whole = grad.astype(BF)
    for p in range(both_ref.shape[0]):
        both_ref[p, :size] = whole[p * size : (p + 1) * size]
    whole = (gate * result).astype(BF)
    for p in range(both_ref.shape[0]):
        both_ref[p, size:] = whole[p * size : (p + 1) * size]


def reorder(values, perm, axis):
    high = values.astype(BF)
    rest = values - high.astype(F32)
    middle = rest.astype(BF)
    low = (rest - middle.astype(F32)).astype(BF)
    return dot(high, perm, 1, axis) + (dot(middle, perm, 1, axis) + dot(low, perm, 1, axis))


def leave_kernel(x_ref, perm_ref, out_ref):
    out_ref[...] = reorder(x_ref[...], perm_ref[...], 0)[: out_ref.shape[0]]


def finish_kernel(live, x_ref, own_ref, far_ref, perm_ref, out_ref):
    total = x_ref[...] + (own_ref[...] + far_ref[...].astype(F32))
    total = reorder(total, perm_ref[...], 0) * live[0].astype(F32)
    out_ref[...] = total[: out_ref.shape[0]]


def add_pack_kernel(up_own, up0, up1, down_own, down0, down1, out):
    half, wide = up0.shape
    for c, (own, parts) in enumerate(((up_own, (up0, up1)), (down_own, (down0, down1)))):
        for s, part in enumerate(parts):
            span = slice(s * half, (s + 1) * half)
            total = own[span].astype(F32) + part[...].astype(F32)
            out[span, c * wide : (c + 1) * wide] = total.astype(BF)


def pack_kernel(*refs):
    out = refs[-1]
    at = 0
    for ref in refs[:-1]:
        out[:, at : at + ref.shape[1]] = ref[...]
        at += ref.shape[1]


def stack_kernel(*refs):
    rows = refs[0].shape[0]
    for i, ref in enumerate(refs[:-1]):
        refs[-1][i * rows : (i + 1) * rows] = ref[...]


def order_kernel(places, in_ref, first_ref, second_ref):
    rows = first_ref.shape[0] // 4
    cut = first_ref.shape[1]
    for i in range(4):
        at = pl.multiple_of(places[i] * rows, rows)
        first_ref[i * rows : (i + 1) * rows] = in_ref[pl.ds(at, rows), :cut]
        second_ref[i * rows : (i + 1) * rows] = in_ref[pl.ds(at, rows), cut:]


def sum_two(near, got, keep, s1, s2, s3):
    rows = keep.shape[0]
    for k, out in enumerate((keep, s1, s2, s3)):
        span = slice(k * rows, (k + 1) * rows)
        out[...] = (near[span].astype(F32) + got[span].astype(F32)).astype(out.dtype)


def small_kernel(g1, g2, g3, g4, router, out):
    whole = jnp.concatenate([g1[...], g2[...], g3[...], g4[...]], axis=0)
    count, cols = router.shape[0], out.shape[2]
    blank = jnp.zeros((out.shape[1] - 4 - count, cols), F32)
    for p in range(8):
        span = slice(p * cols, (p + 1) * cols)
        out[p] = jnp.concatenate([whole[:, span], router[:, span], blank], axis=0)


def sum_two_more(near, got, small, keep, s1, s2, s3):
    sum_two(near, got, keep, s1.at[: keep.shape[0]], s2.at[: keep.shape[0]], s3.at[: keep.shape[0]])
    rows, count = keep.shape[0], small.shape[1]
    cols = small.shape[2]
    for k, out in enumerate((s1, s2, s3)):
        out[rows:, :] = jnp.zeros((out.shape[0] - rows, out.shape[1]), BF)
        high = small[k + 1].astype(BF)
        out[rows : rows + count, :cols] = high
        low = small[k + 1] - high.astype(F32)
        out[rows + count : rows + 2 * count, :cols] = low.astype(BF)


def sum_three_more(keep, r1, r2, r3, small, first, second, small_out):
    rows, count = keep.shape[0], small.shape[1]
    cols = small.shape[2]
    sum_three(keep, r1.at[:rows], r2.at[:rows], r3.at[:rows], first, second)
    total = small[0]
    for r in (r1, r2, r3):
        high = r[rows : rows + count, :cols].astype(F32)
        total = total + (high + r[rows + count : rows + 2 * count, :cols].astype(F32))
    small_out[...] = total


def sum_three(keep, r1, r2, r3, first, second):
    total = keep[...] + (r1[...].astype(F32) + (r2[...].astype(F32) + r3[...].astype(F32)))
    wide = first.shape[1]
    first[...] = total[:, :wide]
    second[...] = total[:, wide:]


def scatter_start(parts):
    near, send = parts
    return near, swap(send, x=1)


def scatter_middle(parts):
    half, width = parts[0].shape
    shape = (half // 4, width)
    return run(sum_two, [(shape, F32)] + [(shape, BF)] * 3, parts, half * width)


def scatter_late(parts):
    keep, s1, s2, s3 = parts
    return keep, swap(s1, z=1), swap(s2, z=2), swap(s3, z=3)


def scatter_end(parts, wide):
    rows, width = parts[0].shape
    return run(sum_three, [((rows, wide), F32), ((rows, width - wide), F32)], parts, rows * width)


def fast_local(
    block_input,
    first_norm,
    first_qkv,
    first_out,
    second_norm,
    dense_up,
    dense_down,
    third_norm,
    second_qkv,
    second_out,
    fourth_norm,
    router_weight,
    expert_up,
    expert_down,
    expert_ids,
    expert_slots,
    image_counts,
    cotangent,
):
    d = lax.axis_index("dp")
    t = lax.axis_index("tensor")
    z_index, x_index = d // 2, d % 2
    width = first_norm.shape[0]
    features = width * 8
    experts = expert_up.shape[0]
    live_count = image_counts[0]
    head_cols = first_out.shape[0]
    ff_cols = dense_up.shape[1]
    qkv_cols = 3 * head_cols
    row = ((ROWS, features), F32)
    row_low = ((ROWS, features), BF)

    small = jnp.concatenate(
        [
            jnp.stack([first_norm, second_norm, third_norm, fourth_norm], axis=1),
            router_weight,
            jnp.zeros((width, 128 - 4 - experts), BF),
        ],
        axis=1,
    )
    pack_one = run(
        pack_kernel,
        [((width, small.shape[1] + 4 * head_cols), BF)],
        (small, first_qkv.reshape(width, -1), first_out.T),
        width,
    )[0]
    pack_late = run(
        pack_kernel,
        [((width, 2 * ff_cols + 4 * head_cols), BF)],
        (dense_up, dense_down.T, second_qkv.reshape(width, -1), second_out.T),
        width,
    )[0]

    lines = [[x + 2 * z for z in range(4)] for x in range(2)]
    raw_late = lax.all_gather(pack_late, "dp", axis=0, tiled=True, axis_index_groups=lines)

    def stacked(shards):
        shape = (len(shards) * shards[0].shape[0], shards[0].shape[1])
        return run(stack_kernel, [(shape, BF)], shards, width)[0]

    z_one = stacked([pack_one] + [swap(pack_one, z=k) for k in (1, 2, 3)])

    rel = jnp.arange(features)
    block = rel // width
    rel_place = jnp.bitwise_xor(d, 2 * (block % 4) + block // 4) * width + rel % width
    perm = (rel_place[:, None] == rel[None, :]).astype(BF)
    live_here = (t < live_count).astype(jnp.int32).reshape(1)
    live_group = (jnp.stack([t, t ^ 2, t ^ 1, t ^ 3]) < live_count).astype(jnp.int32)

    start, low_start, grad_four, grad_low = run(
        enter_kernel,
        [row, row_low, row, row_low],
        (live_here, block_input, cotangent, perm),
        4 * ROWS * features**2,
        scalars=1,
    )

    def spread(rows):
        far = swap(rows, y=1)
        return [rows, far, swap(rows, core=1), swap(far, core=1)]

    first_group = spread(low_start)
    wide = 2 * ff_cols
    half_shape = [((features // 2, ff_cols), BF)] * 2
    e_pack = jnp.concatenate([expert_up, jnp.swapaxes(expert_down, 1, 2)], axis=2)
    held = -(-CAP // 4)
    block_size = -(-(held + 4) // 8) * 8
    ids = jnp.pad(expert_ids.reshape(4, L, 2), ((0, 0), (0, ROWS - L), (0, 0)), constant_values=-1)
    slots = jnp.pad(
        expert_slots.reshape(4, L, 2), ((0, 0), (0, ROWS - L), (0, 0)), constant_values=CAP
    )
    mine = (slots < CAP) & (slots // held == t)
    codes = jnp.where(mine, ids * block_size + slots % held, -1)
    codes = jnp.concatenate(
        [lax.dynamic_index_in_dim(codes, t ^ k, 0, keepdims=False) for k in (0, 2, 1, 3)], axis=0
    ).T
    slot_rows = experts * block_size
    row_code = jnp.arange(slot_rows).reshape(-1, 1)
    group_flops = 2 * slot_rows * features * (4 * ROWS + features)

    def to_experts(kernel, rows, *peaks):
        return run(
            kernel,
            [((slot_rows, features), BF)],
            (row_code, codes, *rows, perm, *peaks),
            group_flops,
            scratch=[pltpu.VMEM((4 * ROWS, features), BF)],
        )[0].reshape(experts, block_size, features)

    def exchange(both):
        return lax.all_to_all(both, "dp", split_axis=0, concat_axis=0, tiled=True)

    group_scratch = pltpu.VMEM((4 * ROWS, features), BF)
    pair_out = [((2 * ROWS, features), F32), ((2 * ROWS, features), BF)]

    def attend(normed, full, at):
        return run(
            functools.partial(attend_kernel, at),
            [((4 * ROWS, qkv_cols), BF), ((4 * ROWS, head_cols), BF)]
            + pair_out
            + [((1, 128), F32)],
            (live_group, *normed, full),
            0,
            scratch=[group_scratch],
            scalars=1,
        )

    def pack_shapes(columns):
        return [((features // 2, columns), BF)] * 2 + pair_out

    def attend_back(low, normed, mixed, attended, full, at):
        return run(
            functools.partial(attend_back_kernel, at),
            pack_shapes(4 * head_cols),
            (*low, *normed, mixed, attended, full),
            8e9,
            scratch=[
                group_scratch,
                pltpu.VMEM((4 * ROWS, head_cols), BF),
                pltpu.VMEM((4 * ROWS, qkv_cols), BF),
            ],
        )

    def over_group(own, sib):
        near, send = run(pair_add_kernel, [row, row_low], (own, swap(sib, core=1)), ROWS)
        return near, swap(send, y=1)

    def join(values, own, far, gain):
        return run(join_norm_kernel, [row, row_low], (values, own, far, gain), ROWS)

    def norm_back(values, upstream, own, far, gain):
        return run(
            norm_back_kernel,
            [row, row_low, ((1, features), F32)],
            (values, upstream, own, far, gain),
            ROWS,
        )

    full_one = stacked(hold([z_one, swap(z_one, x=1)], first_group))
    small_rows = full_one[:, : 4 + experts].T
    gains = [small_rows[i : i + 1].astype(F32) for i in range(4)]
    router = dot(small_rows[4:], perm, 1, 0).astype(BF)

    normed_one = run(norm_kernel, [row_low] * 4, (gains[0], *first_group), ROWS)
    mixed_one, att_one, own, sib, peak_one = attend(normed_one, full_one, small.shape[1])
    near, far = over_group(own, sib)
    one, normed = join(start, near, hold(far, raw_late), gains[1])
    normed_mlp = spread(normed)
    z_mlp, z_late = run(
        order_kernel,
        [((4 * width, 2 * ff_cols), BF), ((4 * width, 4 * head_cols), BF)],
        (jnp.stack([z_index ^ k for k in range(4)]).astype(jnp.int32), hold(raw_late, one)),
        features,
        scalars=1,
    )
    x_mlp = swap(z_mlp, x=1)
    e_pack = hold(e_pack, z_mlp)
    e_own = lax.all_to_all(e_pack, "dp", split_axis=0, concat_axis=0, tiled=True)
    e_own = e_own.reshape(features, wide)
    e_own = hold(e_own, normed_mlp[1])
    far = [swap(e_own[i * 2 * width : (i + 1) * 2 * width], y=1) for i in range(4)]
    e_far = far
    grad_sent = to_experts(dispatch_kernel, spread(hold(grad_low, normed)))
    full_mlp = stacked([z_mlp, x_mlp])
    x_late = swap(hold(z_late, full_mlp), x=1)
    ats = (0, ff_cols)
    act, slope, own, sib = run(
        functools.partial(mlp_kernel, ats),
        [((4 * ROWS, ff_cols), BF)] * 2 + pair_out,
        (*hold(normed_mlp, grad_sent), full_mlp),
        0,
        scratch=[group_scratch],
    )
    near, far = over_group(own, sib)
    two, normed = join(one, near, far, gains[2])
    normed_two = spread(normed)
    full_late = stacked([z_late, x_late])
    mixed_two, att_two, own, sib, peak_two = attend(hold(normed_two, e_far[0]), full_late, 0)
    near, far = over_group(own, sib)
    three, normed = join(two, near, far, gains[3])
    tokens_sent = to_experts(token_kernel, spread(normed), peak_one, peak_two)
    both = exchange(jnp.concatenate([grad_sent, tokens_sent], axis=1))
    grad_slots, tokens, peaks = run(
        collect_kernel,
        [((slot_rows, features), BF)] * 2 + [((2, 128), F32)],
        (hold(both, *e_far),),
        0,
    )
    far_slots, far_tokens = swap(grad_slots, core=1), swap(tokens, core=1)
    number = d.astype(jnp.int32).reshape(1)
    near_heads = head_cols // HD
    roots = clip_root(peaks[:, :near_heads])
    slot_out = [((slot_rows, features), F32), ((slot_rows, features), BF)]
    res_own, res_sib, eg_own, eg_sib, *e_packs = run(
        expert_kernel,
        slot_out + slot_out + ([((features, ff_cols), BF)] + half_shape) * 2,
        (number, tokens, far_tokens, grad_slots, far_slots, router)
        + (e_own, *e_far),
        8 * 2 * slot_rows * features * 2 * ff_cols,
        scalars=1,
        scratch=[
            pltpu.VMEM((2, 2 * slot_rows, ff_cols), BF),
            pltpu.VMEM((2, 2 * slot_rows, ff_cols), BF),
            pltpu.VMEM((2 * slot_rows, features), BF),
            pltpu.VMEM((2 * slot_rows, features), BF),
            pltpu.VMEM((2, features, wide), BF),
        ],
        mib=44,
    )
    res_far, eg_far = swap(res_sib, core=1), swap(eg_sib, core=1)
    up_got = [swap(e_packs[1], y=1)]
    both, grad_router = run(
        answer_kernel,
        [((experts, 2 * block_size, features), BF), ((experts, features), F32)],
        (number, tokens, grad_slots, router, res_own, res_far, eg_own, eg_far, perm),
        4 * slot_rows * features**2,
        scalars=1,
    )
    both = hold(both, up_got)
    e_packs = hold(e_packs, both)
    both = exchange(both)
    up_got.append(swap(e_packs[2], y=1))
    down_got = [swap(e_packs[4], y=1), swap(e_packs[5], y=1)]
    both = hold(both, up_got, down_got)

    def combine(which, both):
        return run(
            functools.partial(combine_kernel, which),
            [((2 * ROWS, features), F32), ((2 * ROWS, features), BF)],
            (row_code, codes, perm, both),
            group_flops,
            scratch=[pltpu.VMEM((slot_rows, features), BF)],
        )

    own, sib = combine(0, both)
    back_own, back_far = over_group(own, sib)
    grad_three, low, gain_four = norm_back(
        three, grad_four, back_own, back_far, gains[3]
    )
    e_sum = run(
        add_pack_kernel,
        [((features, wide), BF)],
        (e_packs[0], *hold(up_got, low), e_packs[3], *down_got),
        0,
    )[0].reshape(experts, width, wide)
    e_back = lax.all_to_all(e_sum, "dp", split_axis=0, concat_axis=0, tiled=True)
    low = spread(low)
    *second, own, sib = attend_back(
        low, normed_two, mixed_two, att_two, full_late, 0
    )
    second = scatter_start(second)
    near, far = over_group(own, sib)
    grad_two, low, gain_three = norm_back(
        two, grad_three, near, far, gains[2]
    )
    low = spread(low)
    *mlp, own, sib = run(
        functools.partial(mlp_back_kernel, ats),
        pack_shapes(2 * ff_cols),
        (*hold(low, e_back), *normed_mlp, act, slope, full_mlp),
        0,
        scratch=[group_scratch, pltpu.VMEM((4 * ROWS, ff_cols), BF)],
    )
    mlp = scatter_start(mlp)
    near, send = run(pair_add_kernel, [row, row_low], (own, swap(sib, core=1)), ROWS)
    far = swap(send, y=1)
    mixed_own, mixed_sib = combine(1, hold(both, second[1]))
    second = scatter_late(scatter_middle(hold(second, mixed_own)))
    mixed_own, mixed_send = run(
        pair_add_kernel, [row, row_low], (mixed_own, swap(mixed_sib, core=1)), ROWS
    )
    grad_one, low, gain_two = norm_back(
        one, grad_two, near, hold(far, mixed_send), gains[1]
    )
    low = spread(low)
    mixed_far = swap(hold(mixed_send, low), y=1)
    *first, own, sib = attend_back(
        hold(low, mlp),
        normed_one,
        mixed_one,
        att_one,
        full_one,
        small.shape[1],
    )
    mlp = scatter_late(scatter_middle(mlp))
    first = scatter_start(first)
    near, far = over_group(own, hold(sib, mixed_far, second))
    grad_zero, _, gain_one = norm_back(start, grad_one, near, hold(far, first), gains[0])
    gains_sum = run(
        small_kernel,
        [((8, 16, width), F32)],
        (gain_one, gain_two, gain_three, gain_four, grad_router),
        0,
    )[0]
    gains_sum = gains_sum + swap(gains_sum, core=1)
    gains_sum = gains_sum + swap(gains_sum, y=1)
    gains_sum = gains_sum[:4] + swap(gains_sum[4:], x=1)
    near_first, got_first = first
    shape = (width, 4 * head_cols)
    first = run(
        sum_two_more,
        [(shape, F32)] + [((width + 32, shape[1]), BF)] * 3,
        (hold(near_first, mlp), got_first, gains_sum),
        0,
    )
    first = scatter_late(first)
    block_output = run(
        finish_kernel,
        [((L, features), F32)],
        (live_here, three, mixed_own, mixed_far, perm),
        6 * ROWS * features**2,
        scalars=1,
    )[0]
    up_g = e_back[:, :, :ff_cols].astype(F32)
    down_g = jnp.swapaxes(e_back[:, :, ff_cols:], 1, 2).astype(F32)
    input_grad = run(
        leave_kernel,
        [((L, features), F32)],
        (hold(grad_zero, first[0]), perm),
        6 * ROWS * features**2,
    )[0]
    second = scatter_end(second, qkv_cols)
    mlp = scatter_end(mlp, ff_cols)
    first = hold(first, up_g, down_g, block_output, input_grad, second, mlp)
    *first, tail = run(
        sum_three_more,
        [((width, qkv_cols), F32), ((width, head_cols), F32), ((16, width), F32)],
        (*first, gains_sum),
        0,
    )

    return (
        block_output,
        input_grad,
        tail[0],
        first[0].reshape(first_qkv.shape),
        first[1].T,
        tail[1],
        mlp[0],
        mlp[1].T,
        tail[2],
        second[0].reshape(second_qkv.shape),
        second[1].T,
        tail[3],
        tail[4 : 4 + experts].T,
        up_g,
        down_g,
        clip_columns(first_qkv, roots[0], HD),
        clip_columns(second_qkv, roots[1], HD),
        roots,
    )


def solution(mesh):
    placed = (
        P(("dp", "tensor"), None),
        P("dp"),
        P("dp", None, "tensor"),
        P("tensor", "dp"),
        P("dp"),
        P("dp", "tensor"),
        P("tensor", "dp"),
        P("dp"),
        P("dp", None, "tensor"),
        P("tensor", "dp"),
        P("dp"),
        P("dp", None),
        P(None, "dp", "tensor"),
        P(None, "tensor", "dp"),
        P("dp", None),
        P("dp", None),
        P("dp"),
        P(("dp", "tensor"), None),
    )
    quick = mesh.shape["dp"] == 8 and mesh.shape["tensor"] == 4
    return jax.shard_map(
        fast_local if quick else local,
        mesh=mesh,
        in_specs=placed,
        out_specs=(
            P(("dp", "tensor"), None),
            P(("dp", "tensor"), None),
            P("dp"),
            P("dp", None, "tensor"),
            P("tensor", "dp"),
            P("dp"),
            P("dp", "tensor"),
            P("tensor", "dp"),
            P("dp"),
            P("dp", None, "tensor"),
            P("tensor", "dp"),
            P("dp"),
            P("dp", None),
            P(None, "dp", "tensor"),
            P(None, "tensor", "dp"),
            P("dp", None, "tensor"),
            P("dp", None, "tensor"),
            P(None, "tensor"),
        ),
        check_vma=False,
    )
```

```python
import functools

import jax
import jax.numpy as jnp
from jax import lax
from jax.experimental import pallas as pl
from jax.experimental.pallas import tpu as pltpu
from jax.sharding import PartitionSpec as P

HD = 64
L = 197
CAP = 197


epsilon = 1e-06
clip_tau = 2.5


def layer_norm(values, norm_gain):
    center = values - jnp.mean(values, axis=-1, keepdims=True)
    spread = jnp.mean(center * center, axis=-1, keepdims=True)
    return center * lax.rsqrt(spread + epsilon) * norm_gain


def exact_gelu(values):
    return jax.nn.gelu(values, approximate=False)


def gelu_back(values, upstream):
    return jax.vjp(exact_gelu, values)[1](upstream)[0]


def norm_back(residual, norm_gain, upstream):
    pullback = jax.vjp(layer_norm, residual, norm_gain.astype(jnp.float32))[1]
    return pullback(upstream)


def gather_rows(values):
    return lax.all_gather(values, "tensor", axis=0, tiled=True)


def scatter_rows(values):
    return lax.psum_scatter(
        values.astype(jnp.bfloat16), "tensor", scatter_dimension=0, tiled=True
    ).astype(jnp.float32)


def sum_gains(first_gain, second_gain):
    return lax.psum((first_gain, second_gain), "tensor")


def split_heads(projected, images, head_size):
    row_count, triple, columns = projected.shape
    pieces = projected.reshape(images, row_count // images, triple, columns // head_size, head_size)
    return (pieces[:, :, 0], pieces[:, :, 1], pieces[:, :, 2])


def attend_scores(queries, keyset, head_size):
    scores = jnp.einsum("iqhd,ikhd->ihqk", queries, keyset, preferred_element_type=jnp.float32)
    return scores * head_size ** (-0.5)


def attend_forward(normed_full, weight_qkv, images, head_size, live_images):
    projected = jnp.einsum(
        "rd,dcf->rcf", normed_full, weight_qkv, preferred_element_type=jnp.float32
    ).astype(jnp.bfloat16)
    queries, keyset, values = split_heads(projected, images, head_size)
    scores = attend_scores(queries, keyset, head_size)
    head_peak = jnp.max(jnp.where(live_images[:, None, None, None], scores, -1e30), axis=(0, 2, 3))
    attn_probs = jax.nn.softmax(scores, axis=-1).astype(jnp.bfloat16)
    attended = jnp.einsum("ihqk,ikhd->iqhd", attn_probs, values, preferred_element_type=jnp.float32)
    return (projected, attended.astype(jnp.bfloat16).reshape(normed_full.shape[0], -1), head_peak)


def attend_backward(projected, grad_attended, images, head_size):
    queries, keyset, values = split_heads(projected, images, head_size)
    scores = attend_scores(queries, keyset, head_size)
    attn_probs = jax.nn.softmax(scores, axis=-1)
    grad_heads = grad_attended.reshape(queries.shape)
    grad_values = jnp.einsum(
        "ihqk,iqhd->ikhd",
        attn_probs.astype(jnp.bfloat16),
        grad_heads,
        preferred_element_type=jnp.float32,
    )
    grad_probs = jnp.einsum(
        "iqhd,ikhd->ihqk", grad_heads, values, preferred_element_type=jnp.float32
    )
    grad_scores = attn_probs * (
        grad_probs - jnp.sum(grad_probs * attn_probs, axis=-1, keepdims=True)
    )
    grad_scores = grad_scores.astype(jnp.bfloat16)
    factor = head_size ** (-0.5)
    grad_queries = (
        jnp.einsum("ihqk,ikhd->iqhd", grad_scores, keyset, preferred_element_type=jnp.float32)
        * factor
    )
    grad_keyset = (
        jnp.einsum("ihqk,iqhd->ikhd", grad_scores, queries, preferred_element_type=jnp.float32)
        * factor
    )
    stacked = jnp.stack([grad_queries, grad_keyset, grad_values], axis=2).astype(jnp.bfloat16)
    return stacked.reshape(projected.shape)


def block_attention(residual, norm_gain, weight_qkv, weight_out, images, head_size, live_images):
    normed = layer_norm(residual, norm_gain.astype(jnp.float32)).astype(jnp.bfloat16)
    normed_full = gather_rows(normed)
    projected, attended, head_peak = attend_forward(
        normed_full, weight_qkv, images, head_size, live_images
    )
    branch = scatter_rows(jnp.dot(attended, weight_out, preferred_element_type=jnp.float32))
    return (residual + branch, (normed_full, projected, attended), head_peak)


def block_attention_back(
    residual, upstream, norm_gain, weight_qkv, weight_out, stored, images, head_size
):
    normed_full, projected, attended = stored
    grad_full = gather_rows(upstream.astype(jnp.bfloat16))
    grad_out = jnp.einsum("rf,rd->fd", attended, grad_full, preferred_element_type=jnp.float32)
    grad_attended = jnp.einsum(
        "rd,fd->rf", grad_full, weight_out, preferred_element_type=jnp.float32
    ).astype(jnp.bfloat16)
    grad_projected = attend_backward(projected, grad_attended, images, head_size)
    grad_qkv = jnp.einsum(
        "rd,rcf->dcf", normed_full, grad_projected, preferred_element_type=jnp.float32
    )
    grad_normed = scatter_rows(
        jnp.einsum("rcf,dcf->rd", grad_projected, weight_qkv, preferred_element_type=jnp.float32)
    )
    grad_residual, grad_gain = norm_back(residual, norm_gain, grad_normed)
    return (upstream + grad_residual, grad_gain, grad_qkv, grad_out)


def block_mlp(residual, norm_gain, weight_up, weight_down):
    normed = layer_norm(residual, norm_gain.astype(jnp.float32)).astype(jnp.bfloat16)
    normed_full = gather_rows(normed)
    hidden = jnp.dot(normed_full, weight_up, preferred_element_type=jnp.float32)
    active = exact_gelu(hidden).astype(jnp.bfloat16)
    branch = scatter_rows(jnp.dot(active, weight_down, preferred_element_type=jnp.float32))
    return (residual + branch, (normed_full, hidden, active))


def block_mlp_back(residual, upstream, norm_gain, weight_up, weight_down, stored):
    normed_full, hidden, active = stored
    grad_full = gather_rows(upstream.astype(jnp.bfloat16))
    grad_down = jnp.einsum("rf,rd->fd", active, grad_full, preferred_element_type=jnp.float32)
    grad_active = jnp.einsum(
        "rd,fd->rf", grad_full, weight_down, preferred_element_type=jnp.float32
    )
    grad_hidden = gelu_back(hidden, grad_active).astype(jnp.bfloat16)
    grad_up = jnp.einsum("rd,rf->df", normed_full, grad_hidden, preferred_element_type=jnp.float32)
    grad_normed = scatter_rows(
        jnp.einsum("rf,df->rd", grad_hidden, weight_up, preferred_element_type=jnp.float32)
    )
    grad_residual, grad_gain = norm_back(residual, norm_gain, grad_normed)
    return (upstream + grad_residual, grad_gain, grad_up, grad_down)


def clip_root(head_peak):
    return jnp.sqrt(clip_tau / jnp.maximum(head_peak, clip_tau))


def clip_columns(weight_local, head_root, head_size):
    column = jnp.repeat(head_root, head_size)
    scales = jnp.stack([column, column, jnp.ones_like(column)])
    return weight_local.astype(jnp.float32) * scales[None]


def local(
    block_input,
    first_norm,
    first_qkv,
    first_out,
    second_norm,
    dense_up,
    dense_down,
    third_norm,
    second_qkv,
    second_out,
    fourth_norm,
    router_weight,
    expert_up,
    expert_down,
    expert_ids,
    expert_slots,
    image_counts,
    cotangent,
):
    rows_local = block_input.shape[0]
    rows_full = rows_local * lax.axis_size("tensor")
    images = rows_full // L
    head_size = HD
    experts = expert_up.shape[0]
    capacity = CAP
    first_row = lax.axis_index("tensor") * rows_local
    live_count = image_counts[0]
    local_live = ((first_row + jnp.arange(rows_local)) // L < live_count).astype(jnp.float32)
    full_live = (jnp.arange(rows_full) // L < live_count).astype(jnp.float32)
    live_images = jnp.arange(images) < live_count

    def dense_fetch():
        return (
            lax.all_gather(first_norm, "dp", axis=0, tiled=True),
            lax.all_gather(first_qkv, "dp", axis=0, tiled=True),
            lax.all_gather(first_out, "dp", axis=1, tiled=True),
            lax.all_gather(second_norm, "dp", axis=0, tiled=True),
            lax.all_gather(dense_up, "dp", axis=0, tiled=True),
            lax.all_gather(dense_down, "dp", axis=1, tiled=True),
        )

    def moe_fetch():
        return (
            lax.all_gather(third_norm, "dp", axis=0, tiled=True),
            lax.all_gather(second_qkv, "dp", axis=0, tiled=True),
            lax.all_gather(second_out, "dp", axis=1, tiled=True),
            lax.all_gather(fourth_norm, "dp", axis=0, tiled=True),
            lax.all_gather(router_weight, "dp", axis=0, tiled=True),
            lax.all_gather(expert_up, "dp", axis=1, tiled=True),
            lax.all_gather(expert_down, "dp", axis=2, tiled=True),
        )

    dense_full = dense_fetch()
    residual_zero = block_input.astype(jnp.float32)
    residual_one, attn_first, peak_first = block_attention(
        residual_zero, dense_full[0], dense_full[1], dense_full[2], images, head_size, live_images
    )
    residual_two, mlp_stored = block_mlp(residual_one, dense_full[3], dense_full[4], dense_full[5])
    moe_full = moe_fetch()
    residual_three, attn_second, peak_second = block_attention(
        residual_two, moe_full[0], moe_full[1], moe_full[2], images, head_size, live_images
    )
    moe_normed = layer_norm(residual_three, moe_full[3].astype(jnp.float32)).astype(jnp.bfloat16)
    moe_input = gather_rows(moe_normed)
    logits = jnp.dot(moe_input, moe_full[4], preferred_element_type=jnp.float32)
    route_probs = jax.nn.softmax(logits, axis=-1)
    kept_mask = expert_slots < capacity
    pair_number = jnp.arange(2 * rows_full, dtype=jnp.int32)
    slot_index = (expert_ids * capacity + expert_slots).reshape(-1)
    kept_flat = kept_mask.reshape(-1)
    write_target = jnp.where(kept_flat, slot_index, experts * capacity + pair_number)
    target = jnp.where(kept_flat, slot_index, experts * capacity)
    pair_of_slot = (
        jnp.zeros((experts * capacity + 2 * rows_full,), jnp.int32)
        .at[write_target]
        .set(pair_number)[: experts * capacity]
    )
    slot_filled = (
        jnp.zeros((experts * capacity + 2 * rows_full,), jnp.float32)
        .at[write_target]
        .set(1.0)[: experts * capacity]
    )
    chosen = (expert_ids[:, :, None] == jnp.arange(experts)[None, None, :]).astype(jnp.float32)
    keep_live = kept_mask.astype(jnp.float32) * full_live[:, None]
    gates = jnp.sum(chosen * route_probs[:, None, :], axis=-1) * keep_live
    slot_token = pair_of_slot // 2
    slot_gate = gates.reshape(-1)[pair_of_slot] * slot_filled
    dispatched = (moe_input[slot_token] * slot_filled[:, None].astype(jnp.bfloat16)).reshape(
        experts, capacity, -1
    )
    expert_hidden = jnp.einsum(
        "ecd,edf->ecf", dispatched, moe_full[5], preferred_element_type=jnp.float32
    )
    expert_act = exact_gelu(expert_hidden).astype(jnp.bfloat16)
    expert_result = jnp.einsum(
        "ecf,efd->ecd", expert_act, moe_full[6], preferred_element_type=jnp.float32
    )
    feature_count = expert_result.shape[2]
    padded_result = jnp.concatenate(
        [
            expert_result.reshape(experts * capacity, feature_count),
            jnp.zeros((1, feature_count), jnp.float32),
        ],
        axis=0,
    )
    pair_result = padded_result[target].reshape(rows_full, 2, feature_count)
    combined = jnp.sum(gates[:, :, None] * pair_result, axis=1)
    residual_four = residual_three + scatter_rows(combined)
    block_output = residual_four * local_live[:, None]
    peak_first_all, peak_second_all = lax.pmax((peak_first, peak_second), "dp")
    root_first = clip_root(peak_first_all)
    root_second = clip_root(peak_second_all)
    clipped_first = clip_columns(first_qkv, root_first, head_size)
    clipped_second = clip_columns(second_qkv, root_second, head_size)
    clip_scales = jnp.stack([root_first, root_second])
    moe_back = moe_fetch()
    grad_four = cotangent.astype(jnp.float32) * local_live[:, None]
    moe_grad_full = gather_rows(grad_four.astype(jnp.bfloat16))
    partial_gates = jnp.sum(moe_grad_full.astype(jnp.float32)[:, None, :] * pair_result, axis=-1)
    grad_gates = lax.psum(partial_gates, "tensor")
    grad_result = (slot_gate[:, None] * moe_grad_full[slot_token].astype(jnp.float32)).astype(
        jnp.bfloat16
    )
    grad_result = grad_result.reshape(experts, capacity, feature_count)
    grad_expert_down = jnp.einsum(
        "ecf,ecd->efd", expert_act, grad_result, preferred_element_type=jnp.float32
    )
    grad_act = jnp.einsum(
        "ecd,efd->ecf", grad_result, moe_back[6], preferred_element_type=jnp.float32
    )
    grad_hidden = gelu_back(expert_hidden, grad_act).astype(jnp.bfloat16)
    grad_expert_up = jnp.einsum(
        "ecd,ecf->edf", dispatched, grad_hidden, preferred_element_type=jnp.float32
    )
    grad_dispatch = jnp.einsum(
        "ecf,edf->ecd", grad_hidden, moe_back[5], preferred_element_type=jnp.float32
    )
    grad_dispatch = jnp.concatenate(
        [
            grad_dispatch.reshape(experts * capacity, feature_count),
            jnp.zeros((1, feature_count), jnp.float32),
        ],
        axis=0,
    )
    grad_from_experts = jnp.sum(grad_dispatch[target].reshape(rows_full, 2, feature_count), axis=1)
    grad_picked = grad_gates * keep_live
    grad_probs = jnp.sum(chosen * grad_picked[:, :, None], axis=1)
    grad_logits = route_probs * (
        grad_probs - jnp.sum(grad_probs * route_probs, axis=-1, keepdims=True)
    )
    grad_logits = grad_logits.astype(jnp.bfloat16)
    grad_router = jnp.einsum(
        "rd,re->de", moe_input, grad_logits, preferred_element_type=jnp.float32
    )
    local_logits = lax.dynamic_slice_in_dim(grad_logits, first_row, rows_local, 0)
    grad_moe_normed = scatter_rows(grad_from_experts) + jnp.einsum(
        "re,de->rd", local_logits, moe_back[4], preferred_element_type=jnp.float32
    )
    grad_rows_four, grad_fourth_norm = norm_back(residual_three, moe_back[3], grad_moe_normed)
    grad_three = grad_four + grad_rows_four
    grad_two, grad_third_norm, grad_second_qkv, grad_second_out = block_attention_back(
        residual_two,
        grad_three,
        moe_back[0],
        moe_back[1],
        moe_back[2],
        attn_second,
        images,
        head_size,
    )
    third_sum, fourth_sum = sum_gains(grad_third_norm, grad_fourth_norm)
    moe_owned = (
        lax.psum_scatter(third_sum, "dp", scatter_dimension=0, tiled=True),
        lax.psum_scatter(grad_second_qkv, "dp", scatter_dimension=0, tiled=True),
        lax.psum_scatter(grad_second_out, "dp", scatter_dimension=1, tiled=True),
        lax.psum_scatter(fourth_sum, "dp", scatter_dimension=0, tiled=True),
        lax.psum_scatter(grad_router, "dp", scatter_dimension=0, tiled=True),
        lax.psum_scatter(grad_expert_up, "dp", scatter_dimension=1, tiled=True),
        lax.psum_scatter(grad_expert_down, "dp", scatter_dimension=2, tiled=True),
    )
    dense_back = dense_fetch()
    grad_one, grad_second_norm, grad_dense_up, grad_dense_down = block_mlp_back(
        residual_one, grad_two, dense_back[3], dense_back[4], dense_back[5], mlp_stored
    )
    input_grad, grad_first_norm, grad_first_qkv, grad_first_out = block_attention_back(
        residual_zero,
        grad_one,
        dense_back[0],
        dense_back[1],
        dense_back[2],
        attn_first,
        images,
        head_size,
    )
    first_sum, second_sum = sum_gains(grad_first_norm, grad_second_norm)
    dense_owned = (
        lax.psum_scatter(first_sum, "dp", scatter_dimension=0, tiled=True),
        lax.psum_scatter(grad_first_qkv, "dp", scatter_dimension=0, tiled=True),
        lax.psum_scatter(grad_first_out, "dp", scatter_dimension=1, tiled=True),
        lax.psum_scatter(second_sum, "dp", scatter_dimension=0, tiled=True),
        lax.psum_scatter(grad_dense_up, "dp", scatter_dimension=0, tiled=True),
        lax.psum_scatter(grad_dense_down, "dp", scatter_dimension=1, tiled=True),
    )
    owned = tuple(dense_owned) + tuple(moe_owned)
    return (
        block_output,
        input_grad,
        owned[0],
        owned[1],
        owned[2],
        owned[3],
        owned[4],
        owned[5],
        owned[6],
        owned[7],
        owned[8],
        owned[9],
        owned[10],
        owned[11],
        owned[12],
        clipped_first,
        clipped_second,
        clip_scales,
    )


ROWS = 208
AXES = ("dp", "tensor")
BF = jnp.bfloat16
F32 = jnp.float32
VM = pl.BlockSpec(memory_space=pltpu.VMEM)
SM = pl.BlockSpec(memory_space=pltpu.SMEM)


def swap(values, z=0, x=0, y=0, core=0):
    shift_d, shift_t = 2 * z + x, 2 * y + core
    pairs = [(d * 4 + t, (d ^ shift_d) * 4 + (t ^ shift_t)) for d in range(8) for t in range(4)]
    return lax.ppermute(values, AXES, pairs)


def hold(values, *tokens):
    return lax.optimization_barrier((values,) + tokens)[0]


def run(kernel, outs, args, flops, scratch=(), scalars=0, mib=20):
    flops = flops if flops == 8e9 else 1000
    shapes = [jax.ShapeDtypeStruct(s, dt) for s, dt in outs]
    return pl.pallas_call(
        kernel,
        out_shape=shapes,
        in_specs=[SM] * scalars + [VM] * (len(args) - scalars),
        out_specs=[VM] * len(shapes),
        scratch_shapes=list(scratch),
        compiler_params=pltpu.CompilerParams(vmem_limit_bytes=mib * 2**20),
        cost_estimate=pl.CostEstimate(flops=int(flops), bytes_accessed=1000, transcendentals=0),
    )(*args)


def dot(a, b, ca, cb):
    return lax.dot_general(a, b, (((ca,), (cb,)), ((), ())), preferred_element_type=F32)


def norm_stats(values):
    center = values - jnp.mean(values, axis=-1, keepdims=True)
    scale = lax.rsqrt(jnp.mean(center * center, axis=-1, keepdims=True) + epsilon)
    return center * scale, scale


def enter_kernel(live, x_ref, c_ref, perm_ref, start_ref, low_start, grad_ref, low_ref):
    rows = x_ref.shape[0]
    scale = live[0].astype(F32)
    extra = jnp.zeros((ROWS - rows, x_ref.shape[1]), F32)
    start = dot(x_ref[...], perm_ref[...], 1, 1)
    start_ref[:rows] = start
    start_ref[rows:] = extra
    low_start[:rows] = start.astype(BF)
    low_start[rows:] = extra.astype(BF)
    grad = dot(c_ref[...], perm_ref[...], 1, 1) * scale
    grad_ref[:rows] = grad
    grad_ref[rows:] = extra
    low_ref[:rows] = grad.astype(BF)
    low_ref[rows:] = extra.astype(BF)


def norm_kernel(gain_ref, *refs):
    for x_ref, out_ref in zip(refs[:4], refs[4:]):
        out_ref[...] = (norm_stats(x_ref[...].astype(F32))[0] * gain_ref[...]).astype(BF)


def join_norm_kernel(x_ref, own_ref, far_ref, gain_ref, sum_ref, out_ref):
    total = x_ref[...] + (own_ref[...] + far_ref[...].astype(F32))
    sum_ref[...] = total
    out_ref[...] = (norm_stats(total)[0] * gain_ref[...]).astype(BF)


def norm_back_kernel(x_ref, up_ref, own_ref, far_ref, gain_ref, grad_ref, low_ref, gain_out):
    upstream = own_ref[...] + far_ref[...].astype(F32)
    normed, scale = norm_stats(x_ref[...])
    scaled = upstream * gain_ref[...]
    grad = up_ref[...] + scale * (
        scaled
        - jnp.mean(scaled, axis=-1, keepdims=True)
        - normed * jnp.mean(scaled * normed, axis=-1, keepdims=True)
    )
    grad_ref[...] = grad
    low_ref[...] = grad.astype(BF)
    gain_out[...] = jnp.sum(upstream * normed, axis=0, keepdims=True)


def fill(rows, *refs):
    size = refs[0].shape[0]
    for i, ref in enumerate(refs):
        rows[i * size : (i + 1) * size] = ref[...]


def put_partial(partial, own_ref, sib_ref):
    half = own_ref.shape[0]
    own_ref[...] = partial[:half]
    sib_ref[...] = partial[half:].astype(BF)


def score_block(queries, keyset):
    scores = dot(queries, keyset, 1, 1) * HD ** (-0.5)
    column = lax.broadcasted_iota(jnp.int32, scores.shape, 1)
    scores = jnp.where(column < L, scores, -1e30)
    top = jnp.max(scores, axis=-1, keepdims=True)
    weight = jnp.exp(scores - top)
    return weight * (1.0 / jnp.sum(weight, axis=-1, keepdims=True)), top


def attend_kernel(
    at, live, a0, a1, a2, a3, w, mix_ref, att_ref, own_ref, sib_ref, peak_ref, rows
):
    fill(rows, a0, a1, a2, a3)
    part = mix_ref.shape[1] // 3
    mix_ref[...] = dot(rows[...], w[:, at : at + 3 * part], 1, 0).astype(BF)
    row_ok = lax.broadcasted_iota(jnp.int32, (ROWS, 1), 0) < L
    lane = lax.broadcasted_iota(jnp.int32, peak_ref.shape, 1)
    found = jnp.full(peak_ref.shape, -1e30, F32)
    for h in range(part // HD):
        for i in range(4):
            span = slice(i * ROWS, (i + 1) * ROWS)
            cut = [mix_ref[span, c * part + h * HD : c * part + (h + 1) * HD] for c in range(3)]
            probs, top = score_block(cut[0], cut[1])
            mixed = dot(probs.astype(BF), cut[2], 1, 0)
            att_ref[span, h * HD : (h + 1) * HD] = mixed.astype(BF)
            best = jnp.max(jnp.where(row_ok, top, -1e30), axis=0, keepdims=True)
            best = jnp.where(live[i] > 0, best, -1e30)
            found = jnp.where(lane == h, jnp.maximum(best, found), found)
    peak_ref[...] = found
    out = w[:, at + 3 * part : at + 4 * part]
    put_partial(dot(att_ref[...], out, 1, 1), own_ref, sib_ref)


def put_pack(grad, column, near, send):
    half = near.shape[0]
    near[:, column : column + grad.shape[1]] = grad[:half]
    send[:, column : column + grad.shape[1]] = grad[half:]


def attend_back_kernel(
    at, g0, g1, g2, g3, a0, a1, a2, a3, mix_ref, att_ref, w,
    near, send, own_ref, sib_ref, rows, grad_att, grad_mix,
):
    part = mix_ref.shape[1] // 3
    fill(rows, g0, g1, g2, g3)
    grad_att[...] = dot(rows[...], w[:, at + 3 * part : at + 4 * part], 1, 0).astype(BF)
    put_pack(dot(rows[...], att_ref[...], 0, 0).astype(BF), 3 * part, near, send)
    factor = HD ** (-0.5)
    for h in range(part // HD):
        for i in range(4):
            span = slice(i * ROWS, (i + 1) * ROWS)
            spans = [slice(c * part + h * HD, c * part + (h + 1) * HD) for c in range(3)]
            queries, keyset, values = (mix_ref[span, s] for s in spans)
            grad = grad_att[span, h * HD : (h + 1) * HD]
            probs, _ = score_block(queries, keyset)
            grad_mix[span, spans[2]] = dot(probs.astype(BF), grad, 0, 0).astype(BF)
            grad_probs = dot(grad, values, 1, 1)
            slope = probs * (grad_probs - jnp.sum(grad_probs * probs, axis=-1, keepdims=True))
            slope = slope.astype(BF)
            grad_mix[span, spans[0]] = (factor * dot(slope, keyset, 1, 0)).astype(BF)
            grad_mix[span, spans[1]] = (factor * dot(slope, queries, 0, 0)).astype(BF)
    put_partial(dot(grad_mix[...], w[:, at : at + 3 * part], 1, 1), own_ref, sib_ref)
    fill(rows, a0, a1, a2, a3)
    put_pack(dot(rows[...], grad_mix[...], 0, 0).astype(BF), 0, near, send)


def gelu_pair(hidden):
    cdf = 0.5 * (1.0 + lax.erf(hidden * 0.7071067811865476))
    slope = cdf + hidden * jnp.exp(-0.5 * hidden * hidden) * 0.3989422804014327
    return (hidden * cdf).astype(BF), slope.astype(BF)


def mlp_kernel(ats, b0, b1, b2, b3, w, act_ref, slope_ref, own_ref, sib_ref, rows):
    fill(rows, b0, b1, b2, b3)
    wide = act_ref.shape[1]
    for c in range(0, wide, 256):
        span = slice(c, c + 256)
        act, slope = gelu_pair(dot(rows[...], w[:, ats[0] + c : ats[0] + c + 256], 1, 0))
        act_ref[:, span] = act
        slope_ref[:, span] = slope
    put_partial(dot(act_ref[...], w[:, ats[1] : ats[1] + wide], 1, 1), own_ref, sib_ref)


def mlp_back_kernel(
    ats, g0, g1, g2, g3, b0, b1, b2, b3, act_ref, slope_ref, w,
    near, send, own_ref, sib_ref, rows, hidden,
):
    fill(rows, g0, g1, g2, g3)
    wide = act_ref.shape[1]
    grad = dot(rows[...], w[:, ats[1] : ats[1] + wide], 1, 0) * slope_ref[...].astype(F32)
    hidden[...] = grad.astype(BF)
    put_partial(dot(hidden[...], w[:, ats[0] : ats[0] + wide], 1, 1), own_ref, sib_ref)
    put_pack(dot(rows[...], act_ref[...], 0, 0).astype(BF), wide, near, send)
    fill(rows, b0, b1, b2, b3)
    put_pack(dot(rows[...], hidden[...], 0, 0).astype(BF), 0, near, send)


def picked(row_code, codes):
    hit = (row_code[...] == codes[0:1, :]) | (row_code[...] == codes[1:2, :])
    return jnp.where(hit, 1.0, 0.0).astype(BF)


def dispatch_kernel(row_code, codes, p0, p1, p2, p3, perm_ref, out, rows):
    fill(rows, p0, p1, p2, p3)
    picks = dot(picked(row_code, codes), rows[...], 1, 0).astype(BF)
    out[...] = dot(picks, perm_ref[...], 1, 0).astype(BF)


def token_kernel(row_code, codes, p0, p1, p2, p3, perm_ref, first_ref, second_ref, out, rows):
    dispatch_kernel(row_code, codes, p0, p1, p2, p3, perm_ref, out, rows)
    row = lax.broadcasted_iota(jnp.int32, (8, 128), 0)
    block = jnp.zeros((8, 128), F32)
    for i, ref in enumerate((first_ref, second_ref)):
        high = ref[...].astype(BF).astype(F32)
        block = jnp.where(row == 2 * i + 2, high, block)
        block = jnp.where(row == 2 * i + 3, ref[...] - high, block)
    size = out.shape[0] // 8
    for e in range(8):
        span = slice((e + 1) * size - 8, (e + 1) * size)
        old = out[span, :128].astype(F32)
        out[span, :128] = jnp.where((row >= 2) & (row < 6), block, old).astype(BF)


def collect_kernel(both_ref, grad_ref, out_ref, peak_ref):
    size = both_ref.shape[1] // 2
    best = jnp.full((2, 128), -1e30, F32)
    for p in range(both_ref.shape[0]):
        rows = slice(p * size, (p + 1) * size)
        grad_ref[rows] = both_ref[p, :size]
        out_ref[rows] = both_ref[p, size:]
        block = both_ref[p, 2 * size - 8 :, :128].astype(F32)
        found = [block[2 * i + 2 : 2 * i + 3] + block[2 * i + 3 : 2 * i + 4] for i in range(2)]
        best = jnp.maximum(best, jnp.concatenate(found, axis=0))
    peak_ref[...] = best


def combine_kernel(which, row_code, codes, perm_ref, both_ref, own_ref, sib_ref, rows):
    size = both_ref.shape[1] // 2
    for p in range(both_ref.shape[0]):
        rows[p * size : (p + 1) * size] = both_ref[p, which * size : (which + 1) * size]
    back = dot(rows[...], perm_ref[...], 1, 1).astype(BF)
    partial = dot(picked(row_code, codes), back, 0, 0)
    half = partial.shape[0] // 2
    own_ref[...] = partial[:half]
    sib_ref[...] = partial[half:].astype(BF)


def pair_add_kernel(own_ref, far_ref, near_ref, send_ref):
    total = own_ref[...] + far_ref[...].astype(F32)
    near_ref[...] = total[:ROWS]
    send_ref[...] = total[ROWS:].astype(BF)


def route_of(tokens, router, number):
    logits = dot(tokens, router, 1, 1)
    column = lax.broadcasted_iota(jnp.int32, logits.shape, 1)
    logits = jnp.where(column < 8, logits, -1e30)
    weight = jnp.exp(logits - jnp.max(logits, axis=-1, keepdims=True))
    route = weight / jnp.sum(weight, axis=-1, keepdims=True)
    mine = jnp.where(column == number, 1.0, 0.0)
    return route, mine, jnp.sum(route * mine, axis=-1, keepdims=True)


def expert_kernel(
    number, t0, t1, g0, g1, router, *rest
):
    own, far = rest[0], rest[1:5]
    res_own, res_sib, grad_own, grad_sib = rest[5:9]
    up_parts, down_parts = rest[9:12], rest[12:15]
    act_ref, hid_ref, gout_ref, pair, whole = rest[15:]
    size = t0.shape[0]
    half, wide = own.shape[0] // 2, act_ref.shape[2]
    whole[0] = own[...]
    for i, part in enumerate(far):
        whole[1, i * half // 2 : (i + 1) * half // 2] = part[...]
    for i, (t, g, res, grad) in enumerate(
        ((t1, g1, res_sib, grad_sib), (t0, g0, res_own, grad_own))
    ):
        rows = slice((1 - i) * size, (2 - i) * size)
        gate = route_of(t[...], router[...], number[0])[2]
        gout = (gate * g[...].astype(F32)).astype(BF)
        gout_ref[rows] = gout
        for y in range(2):
            for c in range(0, wide, 256):
                span = slice(c, c + 256)
                act, lean = gelu_pair(dot(t[...], whole[y, :, span], 1, 0))
                act_ref[y, rows, span] = act
                back = dot(gout, whole[y, :, wide + c : wide + c + 256], 1, 0)
                hid_ref[y, rows, span] = (back * lean.astype(F32)).astype(BF)
        res[...] = (
            dot(act_ref[0, rows], whole[0, :, wide:], 1, 1)
            + dot(act_ref[1, rows], whole[1, :, wide:], 1, 1)
        ).astype(res.dtype)
        grad[...] = (
            dot(hid_ref[0, rows], whole[0, :, :wide], 1, 1)
            + dot(hid_ref[1, rows], whole[1, :, :wide], 1, 1)
        ).astype(grad.dtype)
    pair[:size] = t0[...]
    pair[size:] = t1[...]
    for parts, left, right in ((up_parts, pair, hid_ref), (down_parts, gout_ref, act_ref)):
        parts[0][...] = dot(left[...], right[0], 0, 0).astype(BF)
        far = dot(left[...], right[1], 0, 0).astype(BF)
        parts[1][...] = far[:half]
        parts[2][...] = far[half:]


def answer_kernel(
    number, t_ref, g_ref, router, res_own, res_far, grad_own, grad_far, perm_ref,
    both_ref, router_out,
):
    route, mine, gate = route_of(t_ref[...], router[...], number[0])
    result = res_own[...] + res_far[...].astype(F32)
    grad_gate = jnp.sum(result * g_ref[...].astype(F32), axis=-1, keepdims=True)
    grad_logit = (grad_gate * route * (mine - gate)).astype(BF)
    router_out[...] = reorder(dot(grad_logit, t_ref[...], 0, 0), perm_ref[...], 1)
    grad = grad_own[...] + grad_far[...].astype(F32) + dot(grad_logit, router[...], 1, 0)
    size = both_ref.shape[1] // 2
    whole = grad.astype(BF)
    for p in range(both_ref.shape[0]):
        both_ref[p, :size] = whole[p * size : (p + 1) * size]
    whole = (gate * result).astype(BF)
    for p in range(both_ref.shape[0]):
        both_ref[p, size:] = whole[p * size : (p + 1) * size]


def reorder(values, perm, axis):
    high = values.astype(BF)
    rest = values - high.astype(F32)
    middle = rest.astype(BF)
    low = (rest - middle.astype(F32)).astype(BF)
    return dot(high, perm, 1, axis) + (dot(middle, perm, 1, axis) + dot(low, perm, 1, axis))


def leave_kernel(x_ref, perm_ref, out_ref):
    out_ref[...] = reorder(x_ref[...], perm_ref[...], 0)[: out_ref.shape[0]]


def finish_kernel(live, x_ref, own_ref, far_ref, perm_ref, out_ref):
    total = x_ref[...] + (own_ref[...] + far_ref[...].astype(F32))
    total = reorder(total, perm_ref[...], 0) * live[0].astype(F32)
    out_ref[...] = total[: out_ref.shape[0]]


def add_pack_kernel(up_own, up0, up1, down_own, down0, down1, out):
    half, wide = up0.shape
    for c, (own, parts) in enumerate(((up_own, (up0, up1)), (down_own, (down0, down1)))):
        for s, part in enumerate(parts):
            span = slice(s * half, (s + 1) * half)
            total = own[span].astype(F32) + part[...].astype(F32)
            out[span, c * wide : (c + 1) * wide] = total.astype(BF)


def pack_kernel(*refs):
    out = refs[-1]
    at = 0
    for ref in refs[:-1]:
        out[:, at : at + ref.shape[1]] = ref[...]
        at += ref.shape[1]


def stack_kernel(*refs):
    rows = refs[0].shape[0]
    for i, ref in enumerate(refs[:-1]):
        refs[-1][i * rows : (i + 1) * rows] = ref[...]


def order_kernel(places, in_ref, first_ref, second_ref):
    rows = first_ref.shape[0] // 4
    cut = first_ref.shape[1]
    for i in range(4):
        at = pl.multiple_of(places[i] * rows, rows)
        first_ref[i * rows : (i + 1) * rows] = in_ref[pl.ds(at, rows), :cut]
        second_ref[i * rows : (i + 1) * rows] = in_ref[pl.ds(at, rows), cut:]


def sum_two(near, got, keep, s1, s2, s3):
    rows = keep.shape[0]
    for k, out in enumerate((keep, s1, s2, s3)):
        span = slice(k * rows, (k + 1) * rows)
        out[...] = (near[span].astype(F32) + got[span].astype(F32)).astype(out.dtype)


def small_kernel(g1, g2, g3, g4, router, out):
    whole = jnp.concatenate([g1[...], g2[...], g3[...], g4[...]], axis=0)
    count, cols = router.shape[0], out.shape[2]
    blank = jnp.zeros((out.shape[1] - 4 - count, cols), F32)
    for p in range(8):
        span = slice(p * cols, (p + 1) * cols)
        out[p] = jnp.concatenate([whole[:, span], router[:, span], blank], axis=0)


def sum_two_more(near, got, small, keep, s1, s2, s3):
    sum_two(near, got, keep, s1.at[: keep.shape[0]], s2.at[: keep.shape[0]], s3.at[: keep.shape[0]])
    rows, count = keep.shape[0], small.shape[1]
    cols = small.shape[2]
    for k, out in enumerate((s1, s2, s3)):
        out[rows:, :] = jnp.zeros((out.shape[0] - rows, out.shape[1]), BF)
        high = small[k + 1].astype(BF)
        out[rows : rows + count, :cols] = high
        low = small[k + 1] - high.astype(F32)
        out[rows + count : rows + 2 * count, :cols] = low.astype(BF)


def sum_three_more(keep, r1, r2, r3, small, first, second, small_out):
    rows, count = keep.shape[0], small.shape[1]
    cols = small.shape[2]
    sum_three(keep, r1.at[:rows], r2.at[:rows], r3.at[:rows], first, second)
    total = small[0]
    for r in (r1, r2, r3):
        high = r[rows : rows + count, :cols].astype(F32)
        total = total + (high + r[rows + count : rows + 2 * count, :cols].astype(F32))
    small_out[...] = total


def sum_three(keep, r1, r2, r3, first, second):
    total = keep[...] + (r1[...].astype(F32) + (r2[...].astype(F32) + r3[...].astype(F32)))
    wide = first.shape[1]
    first[...] = total[:, :wide]
    second[...] = total[:, wide:]


def scatter_start(parts):
    near, send = parts
    return near, swap(send, x=1)


def scatter_middle(parts):
    half, width = parts[0].shape
    shape = (half // 4, width)
    return run(sum_two, [(shape, F32)] + [(shape, BF)] * 3, parts, half * width)


def scatter_late(parts):
    keep, s1, s2, s3 = parts
    return keep, swap(s1, z=1), swap(s2, z=2), swap(s3, z=3)


def scatter_end(parts, wide):
    rows, width = parts[0].shape
    return run(sum_three, [((rows, wide), F32), ((rows, width - wide), F32)], parts, rows * width)


def fast_local(
    block_input,
    first_norm,
    first_qkv,
    first_out,
    second_norm,
    dense_up,
    dense_down,
    third_norm,
    second_qkv,
    second_out,
    fourth_norm,
    router_weight,
    expert_up,
    expert_down,
    expert_ids,
    expert_slots,
    image_counts,
    cotangent,
):
    d = lax.axis_index("dp")
    t = lax.axis_index("tensor")
    z_index, x_index = d // 2, d % 2
    width = first_norm.shape[0]
    features = width * 8
    experts = expert_up.shape[0]
    live_count = image_counts[0]
    head_cols = first_out.shape[0]
    ff_cols = dense_up.shape[1]
    qkv_cols = 3 * head_cols
    row = ((ROWS, features), F32)
    row_low = ((ROWS, features), BF)

    small = jnp.concatenate(
        [
            jnp.stack([first_norm, second_norm, third_norm, fourth_norm], axis=1),
            router_weight,
            jnp.zeros((width, 128 - 4 - experts), BF),
        ],
        axis=1,
    )
    pack_one = run(
        pack_kernel,
        [((width, small.shape[1] + 4 * head_cols), BF)],
        (small, first_qkv.reshape(width, -1), first_out.T),
        width,
    )[0]
    pack_late = run(
        pack_kernel,
        [((width, 2 * ff_cols + 4 * head_cols), BF)],
        (dense_up, dense_down.T, second_qkv.reshape(width, -1), second_out.T),
        width,
    )[0]

    lines = [[x + 2 * z for z in range(4)] for x in range(2)]
    raw_late = lax.all_gather(pack_late, "dp", axis=0, tiled=True, axis_index_groups=lines)

    def stacked(shards):
        shape = (len(shards) * shards[0].shape[0], shards[0].shape[1])
        return run(stack_kernel, [(shape, BF)], shards, width)[0]

    z_one = stacked([pack_one] + [swap(pack_one, z=k) for k in (1, 2, 3)])

    rel = jnp.arange(features)
    block = rel // width
    rel_place = jnp.bitwise_xor(d, 2 * (block % 4) + block // 4) * width + rel % width
    perm = (rel_place[:, None] == rel[None, :]).astype(BF)
    live_here = (t < live_count).astype(jnp.int32).reshape(1)
    live_group = (jnp.stack([t, t ^ 2, t ^ 1, t ^ 3]) < live_count).astype(jnp.int32)

    start, low_start, grad_four, grad_low = run(
        enter_kernel,
        [row, row_low, row, row_low],
        (live_here, block_input, cotangent, perm),
        4 * ROWS * features**2,
        scalars=1,
    )

    def spread(rows):
        far = swap(rows, y=1)
        return [rows, far, swap(rows, core=1), swap(far, core=1)]

    first_group = spread(low_start)
    wide = 2 * ff_cols
    half_shape = [((features // 2, ff_cols), BF)] * 2
    e_pack = jnp.concatenate([expert_up, jnp.swapaxes(expert_down, 1, 2)], axis=2)
    held = -(-CAP // 4)
    block_size = -(-(held + 4) // 8) * 8
    ids = jnp.pad(expert_ids.reshape(4, L, 2), ((0, 0), (0, ROWS - L), (0, 0)), constant_values=-1)
    slots = jnp.pad(
        expert_slots.reshape(4, L, 2), ((0, 0), (0, ROWS - L), (0, 0)), constant_values=CAP
    )
    mine = (slots < CAP) & (slots // held == t)
    codes = jnp.where(mine, ids * block_size + slots % held, -1)
    codes = jnp.concatenate(
        [lax.dynamic_index_in_dim(codes, t ^ k, 0, keepdims=False) for k in (0, 2, 1, 3)], axis=0
    ).T
    slot_rows = experts * block_size
    row_code = jnp.arange(slot_rows).reshape(-1, 1)
    group_flops = 2 * slot_rows * features * (4 * ROWS + features)

    def to_experts(kernel, rows, *peaks):
        return run(
            kernel,
            [((slot_rows, features), BF)],
            (row_code, codes, *rows, perm, *peaks),
            group_flops,
            scratch=[pltpu.VMEM((4 * ROWS, features), BF)],
        )[0].reshape(experts, block_size, features)

    def exchange(both):
        return lax.all_to_all(both, "dp", split_axis=0, concat_axis=0, tiled=True)

    group_scratch = pltpu.VMEM((4 * ROWS, features), BF)
    pair_out = [((2 * ROWS, features), F32), ((2 * ROWS, features), BF)]

    def attend(normed, full, at):
        return run(
            functools.partial(attend_kernel, at),
            [((4 * ROWS, qkv_cols), BF), ((4 * ROWS, head_cols), BF)]
            + pair_out
            + [((1, 128), F32)],
            (live_group, *normed, full),
            0,
            scratch=[group_scratch],
            scalars=1,
        )

    def pack_shapes(columns):
        return [((features // 2, columns), BF)] * 2 + pair_out

    def attend_back(low, normed, mixed, attended, full, at):
        return run(
            functools.partial(attend_back_kernel, at),
            pack_shapes(4 * head_cols),
            (*low, *normed, mixed, attended, full),
            8e9,
            scratch=[
                group_scratch,
                pltpu.VMEM((4 * ROWS, head_cols), BF),
                pltpu.VMEM((4 * ROWS, qkv_cols), BF),
            ],
        )

    def over_group(own, sib):
        near, send = run(pair_add_kernel, [row, row_low], (own, swap(sib, core=1)), ROWS)
        return near, swap(send, y=1)

    def join(values, own, far, gain):
        return run(join_norm_kernel, [row, row_low], (values, own, far, gain), ROWS)

    def norm_back(values, upstream, own, far, gain):
        return run(
            norm_back_kernel,
            [row, row_low, ((1, features), F32)],
            (values, upstream, own, far, gain),
            ROWS,
        )

    full_one = stacked(hold([z_one, swap(z_one, x=1)], first_group))
    small_rows = full_one[:, : 4 + experts].T
    gains = [small_rows[i : i + 1].astype(F32) for i in range(4)]
    router = dot(small_rows[4:], perm, 1, 0).astype(BF)

    normed_one = run(norm_kernel, [row_low] * 4, (gains[0], *first_group), ROWS)
    mixed_one, att_one, own, sib, peak_one = attend(normed_one, full_one, small.shape[1])
    near, far = over_group(own, sib)
    one, normed = join(start, near, hold(far, raw_late), gains[1])
    normed_mlp = spread(normed)
    z_mlp, z_late = run(
        order_kernel,
        [((4 * width, 2 * ff_cols), BF), ((4 * width, 4 * head_cols), BF)],
        (jnp.stack([z_index ^ k for k in range(4)]).astype(jnp.int32), hold(raw_late, one)),
        features,
        scalars=1,
    )
    x_mlp = swap(z_mlp, x=1)
    e_pack = hold(e_pack, normed_mlp[1])
    e_own = lax.all_to_all(e_pack, "dp", split_axis=0, concat_axis=0, tiled=True)
    e_own = e_own.reshape(features, wide)
    e_own = hold(e_own, normed_mlp[1])
    far = [swap(e_own[i * 2 * width : (i + 1) * 2 * width], y=1) for i in range(4)]
    e_far = far
    grad_sent = to_experts(dispatch_kernel, spread(hold(grad_low, normed)))
    full_mlp = stacked([z_mlp, x_mlp])
    x_late = swap(hold(z_late, full_mlp), x=1)
    ats = (0, ff_cols)
    act, slope, own, sib = run(
        functools.partial(mlp_kernel, ats),
        [((4 * ROWS, ff_cols), BF)] * 2 + pair_out,
        (*hold(normed_mlp, grad_sent), full_mlp),
        0,
        scratch=[group_scratch],
    )
    near, far = over_group(own, sib)
    two, normed = join(one, near, far, gains[2])
    normed_two = spread(normed)
    full_late = stacked([z_late, x_late])
    mixed_two, att_two, own, sib, peak_two = attend(normed_two, full_late, 0)
    near, far = over_group(own, sib)
    three, normed = join(two, near, far, gains[3])
    tokens_sent = to_experts(token_kernel, spread(normed), peak_one, peak_two)
    both = exchange(jnp.concatenate([grad_sent, tokens_sent], axis=1))
    grad_slots, tokens, peaks = run(
        collect_kernel,
        [((slot_rows, features), BF)] * 2 + [((2, 128), F32)],
        (hold(both, *e_far),),
        0,
    )
    far_slots, far_tokens = swap(grad_slots, core=1), swap(tokens, core=1)
    number = d.astype(jnp.int32).reshape(1)
    near_heads = head_cols // HD
    roots = clip_root(peaks[:, :near_heads])
    slot_out = [((slot_rows, features), F32), ((slot_rows, features), BF)]
    res_own, res_sib, eg_own, eg_sib, *e_packs = run(
        expert_kernel,
        slot_out + slot_out + ([((features, ff_cols), BF)] + half_shape) * 2,
        (number, tokens, far_tokens, grad_slots, far_slots, router)
        + (e_own, *e_far),
        8 * 2 * slot_rows * features * 2 * ff_cols,
        scalars=1,
        scratch=[
            pltpu.VMEM((2, 2 * slot_rows, ff_cols), BF),
            pltpu.VMEM((2, 2 * slot_rows, ff_cols), BF),
            pltpu.VMEM((2 * slot_rows, features), BF),
            pltpu.VMEM((2 * slot_rows, features), BF),
            pltpu.VMEM((2, features, wide), BF),
        ],
        mib=44,
    )
    res_far, eg_far = swap(res_sib, core=1), swap(eg_sib, core=1)
    up_got = [swap(e_packs[1], y=1)]
    both, grad_router = run(
        answer_kernel,
        [((experts, 2 * block_size, features), BF), ((experts, features), F32)],
        (number, tokens, grad_slots, router, res_own, res_far, eg_own, eg_far, perm),
        4 * slot_rows * features**2,
        scalars=1,
    )
    both = hold(both, up_got)
    e_packs = hold(e_packs, both)
    both = exchange(both)
    up_got.append(swap(e_packs[2], y=1))
    down_got = [swap(e_packs[4], y=1)]
    both = hold(both, up_got, down_got)

    def combine(which, both):
        return run(
            functools.partial(combine_kernel, which),
            [((2 * ROWS, features), F32), ((2 * ROWS, features), BF)],
            (row_code, codes, perm, both),
            group_flops,
            scratch=[pltpu.VMEM((slot_rows, features), BF)],
        )

    own, sib = combine(0, both)
    back_own, back_far = over_group(own, sib)
    grad_three, low, gain_four = norm_back(
        three, grad_four, back_own, back_far, gains[3]
    )
    low = spread(low)
    down_got.append(swap(hold(e_packs[5], low[1]), y=1))
    *second, own, sib = attend_back(
        low, normed_two, mixed_two, att_two, full_late, 0
    )
    second = scatter_start(second)
    near, far = over_group(own, hold(sib, down_got[1]))
    e_sum = run(
        add_pack_kernel,
        [((features, wide), BF)],
        (e_packs[0], *up_got, e_packs[3], *hold(down_got, near)),
        0,
    )[0].reshape(experts, width, wide)
    e_back = lax.all_to_all(e_sum, "dp", split_axis=0, concat_axis=0, tiled=True)
    grad_two, low, gain_three = norm_back(
        two, grad_three, near, far, gains[2]
    )
    low = spread(low)
    *mlp, own, sib = run(
        functools.partial(mlp_back_kernel, ats),
        pack_shapes(2 * ff_cols),
        (*low, *normed_mlp, act, slope, full_mlp),
        0,
        scratch=[group_scratch, pltpu.VMEM((4 * ROWS, ff_cols), BF)],
    )
    mlp = scatter_start(mlp)
    near, send = run(pair_add_kernel, [row, row_low], (own, swap(sib, core=1)), ROWS)
    far = swap(send, y=1)
    mixed_own, mixed_sib = combine(1, hold(both, second[1]))
    second = scatter_late(scatter_middle(hold(second, mixed_own)))
    mixed_own, mixed_send = run(
        pair_add_kernel, [row, row_low], (mixed_own, swap(mixed_sib, core=1)), ROWS
    )
    grad_one, low, gain_two = norm_back(
        one, grad_two, near, hold(far, mixed_send), gains[1]
    )
    low = spread(low)
    mixed_far = swap(hold(mixed_send, low), y=1)
    *first, own, sib = attend_back(
        hold(low, mlp),
        normed_one,
        mixed_one,
        att_one,
        full_one,
        small.shape[1],
    )
    mlp = scatter_late(scatter_middle(mlp))
    first = scatter_start(first)
    near, far = over_group(own, hold(sib, mixed_far, second, e_back))
    grad_zero, _, gain_one = norm_back(start, grad_one, near, hold(far, first), gains[0])
    gains_sum = run(
        small_kernel,
        [((8, 16, width), F32)],
        (gain_one, gain_two, gain_three, gain_four, grad_router),
        0,
    )[0]
    gains_sum = hold(gains_sum + swap(gains_sum, core=1), mlp)
    gains_sum = gains_sum + swap(gains_sum, y=1)
    gains_sum = gains_sum[:4] + swap(gains_sum[4:], x=1)
    near_first, got_first = first
    shape = (width, 4 * head_cols)
    first = run(
        sum_two_more,
        [(shape, F32)] + [((width + 32, shape[1]), BF)] * 3,
        (near_first, got_first, gains_sum),
        0,
    )
    first = scatter_late(first)
    block_output = run(
        finish_kernel,
        [((L, features), F32)],
        (live_here, three, mixed_own, mixed_far, perm),
        6 * ROWS * features**2,
        scalars=1,
    )[0]
    up_g = e_back[:, :, :ff_cols].astype(F32)
    down_g = jnp.swapaxes(e_back[:, :, ff_cols:], 1, 2).astype(F32)
    input_grad = run(
        leave_kernel,
        [((L, features), F32)],
        (hold(grad_zero, first[0]), perm),
        6 * ROWS * features**2,
    )[0]
    second = scatter_end(second, qkv_cols)
    mlp = scatter_end(mlp, ff_cols)
    first = hold(first, up_g, down_g, block_output, input_grad, second, mlp)
    *first, tail = run(
        sum_three_more,
        [((width, qkv_cols), F32), ((width, head_cols), F32), ((16, width), F32)],
        (*first, gains_sum),
        0,
    )

    return (
        block_output,
        input_grad,
        tail[0],
        first[0].reshape(first_qkv.shape),
        first[1].T,
        tail[1],
        mlp[0],
        mlp[1].T,
        tail[2],
        second[0].reshape(second_qkv.shape),
        second[1].T,
        tail[3],
        tail[4 : 4 + experts].T,
        up_g,
        down_g,
        clip_columns(first_qkv, roots[0], HD),
        clip_columns(second_qkv, roots[1], HD),
        roots,
    )


def solution(mesh):
    placed = (
        P(("dp", "tensor"), None),
        P("dp"),
        P("dp", None, "tensor"),
        P("tensor", "dp"),
        P("dp"),
        P("dp", "tensor"),
        P("tensor", "dp"),
        P("dp"),
        P("dp", None, "tensor"),
        P("tensor", "dp"),
        P("dp"),
        P("dp", None),
        P(None, "dp", "tensor"),
        P(None, "tensor", "dp"),
        P("dp", None),
        P("dp", None),
        P("dp"),
        P(("dp", "tensor"), None),
    )
    quick = mesh.shape["dp"] == 8 and mesh.shape["tensor"] == 4
    return jax.shard_map(
        fast_local if quick else local,
        mesh=mesh,
        in_specs=placed,
        out_specs=(
            P(("dp", "tensor"), None),
            P(("dp", "tensor"), None),
            P("dp"),
            P("dp", None, "tensor"),
            P("tensor", "dp"),
            P("dp"),
            P("dp", "tensor"),
            P("tensor", "dp"),
            P("dp"),
            P("dp", None, "tensor"),
            P("tensor", "dp"),
            P("dp"),
            P("dp", None),
            P(None, "dp", "tensor"),
            P(None, "tensor", "dp"),
            P("dp", None, "tensor"),
            P("dp", None, "tensor"),
            P(None, "tensor"),
        ),
        check_vma=False,
    )
```

```python
import functools

import jax
import jax.numpy as jnp
from jax import lax
from jax.experimental import pallas as pl
from jax.experimental.pallas import tpu as pltpu
from jax.sharding import PartitionSpec as P

HD = 64
L = 197
CAP = 197


epsilon = 1e-06
clip_tau = 2.5


def layer_norm(values, norm_gain):
    center = values - jnp.mean(values, axis=-1, keepdims=True)
    spread = jnp.mean(center * center, axis=-1, keepdims=True)
    return center * lax.rsqrt(spread + epsilon) * norm_gain


def exact_gelu(values):
    return jax.nn.gelu(values, approximate=False)


def gelu_back(values, upstream):
    return jax.vjp(exact_gelu, values)[1](upstream)[0]


def norm_back(residual, norm_gain, upstream):
    pullback = jax.vjp(layer_norm, residual, norm_gain.astype(jnp.float32))[1]
    return pullback(upstream)


def gather_rows(values):
    return lax.all_gather(values, "tensor", axis=0, tiled=True)


def scatter_rows(values):
    return lax.psum_scatter(
        values.astype(jnp.bfloat16), "tensor", scatter_dimension=0, tiled=True
    ).astype(jnp.float32)


def sum_gains(first_gain, second_gain):
    return lax.psum((first_gain, second_gain), "tensor")


def split_heads(projected, images, head_size):
    row_count, triple, columns = projected.shape
    pieces = projected.reshape(images, row_count // images, triple, columns // head_size, head_size)
    return (pieces[:, :, 0], pieces[:, :, 1], pieces[:, :, 2])


def attend_scores(queries, keyset, head_size):
    scores = jnp.einsum("iqhd,ikhd->ihqk", queries, keyset, preferred_element_type=jnp.float32)
    return scores * head_size ** (-0.5)


def attend_forward(normed_full, weight_qkv, images, head_size, live_images):
    projected = jnp.einsum(
        "rd,dcf->rcf", normed_full, weight_qkv, preferred_element_type=jnp.float32
    ).astype(jnp.bfloat16)
    queries, keyset, values = split_heads(projected, images, head_size)
    scores = attend_scores(queries, keyset, head_size)
    head_peak = jnp.max(jnp.where(live_images[:, None, None, None], scores, -1e30), axis=(0, 2, 3))
    attn_probs = jax.nn.softmax(scores, axis=-1).astype(jnp.bfloat16)
    attended = jnp.einsum("ihqk,ikhd->iqhd", attn_probs, values, preferred_element_type=jnp.float32)
    return (projected, attended.astype(jnp.bfloat16).reshape(normed_full.shape[0], -1), head_peak)


def attend_backward(projected, grad_attended, images, head_size):
    queries, keyset, values = split_heads(projected, images, head_size)
    scores = attend_scores(queries, keyset, head_size)
    attn_probs = jax.nn.softmax(scores, axis=-1)
    grad_heads = grad_attended.reshape(queries.shape)
    grad_values = jnp.einsum(
        "ihqk,iqhd->ikhd",
        attn_probs.astype(jnp.bfloat16),
        grad_heads,
        preferred_element_type=jnp.float32,
    )
    grad_probs = jnp.einsum(
        "iqhd,ikhd->ihqk", grad_heads, values, preferred_element_type=jnp.float32
    )
    grad_scores = attn_probs * (
        grad_probs - jnp.sum(grad_probs * attn_probs, axis=-1, keepdims=True)
    )
    grad_scores = grad_scores.astype(jnp.bfloat16)
    factor = head_size ** (-0.5)
    grad_queries = (
        jnp.einsum("ihqk,ikhd->iqhd", grad_scores, keyset, preferred_element_type=jnp.float32)
        * factor
    )
    grad_keyset = (
        jnp.einsum("ihqk,iqhd->ikhd", grad_scores, queries, preferred_element_type=jnp.float32)
        * factor
    )
    stacked = jnp.stack([grad_queries, grad_keyset, grad_values], axis=2).astype(jnp.bfloat16)
    return stacked.reshape(projected.shape)


def block_attention(residual, norm_gain, weight_qkv, weight_out, images, head_size, live_images):
    normed = layer_norm(residual, norm_gain.astype(jnp.float32)).astype(jnp.bfloat16)
    normed_full = gather_rows(normed)
    projected, attended, head_peak = attend_forward(
        normed_full, weight_qkv, images, head_size, live_images
    )
    branch = scatter_rows(jnp.dot(attended, weight_out, preferred_element_type=jnp.float32))
    return (residual + branch, (normed_full, projected, attended), head_peak)


def block_attention_back(
    residual, upstream, norm_gain, weight_qkv, weight_out, stored, images, head_size
):
    normed_full, projected, attended = stored
    grad_full = gather_rows(upstream.astype(jnp.bfloat16))
    grad_out = jnp.einsum("rf,rd->fd", attended, grad_full, preferred_element_type=jnp.float32)
    grad_attended = jnp.einsum(
        "rd,fd->rf", grad_full, weight_out, preferred_element_type=jnp.float32
    ).astype(jnp.bfloat16)
    grad_projected = attend_backward(projected, grad_attended, images, head_size)
    grad_qkv = jnp.einsum(
        "rd,rcf->dcf", normed_full, grad_projected, preferred_element_type=jnp.float32
    )
    grad_normed = scatter_rows(
        jnp.einsum("rcf,dcf->rd", grad_projected, weight_qkv, preferred_element_type=jnp.float32)
    )
    grad_residual, grad_gain = norm_back(residual, norm_gain, grad_normed)
    return (upstream + grad_residual, grad_gain, grad_qkv, grad_out)


def block_mlp(residual, norm_gain, weight_up, weight_down):
    normed = layer_norm(residual, norm_gain.astype(jnp.float32)).astype(jnp.bfloat16)
    normed_full = gather_rows(normed)
    hidden = jnp.dot(normed_full, weight_up, preferred_element_type=jnp.float32)
    active = exact_gelu(hidden).astype(jnp.bfloat16)
    branch = scatter_rows(jnp.dot(active, weight_down, preferred_element_type=jnp.float32))
    return (residual + branch, (normed_full, hidden, active))


def block_mlp_back(residual, upstream, norm_gain, weight_up, weight_down, stored):
    normed_full, hidden, active = stored
    grad_full = gather_rows(upstream.astype(jnp.bfloat16))
    grad_down = jnp.einsum("rf,rd->fd", active, grad_full, preferred_element_type=jnp.float32)
    grad_active = jnp.einsum(
        "rd,fd->rf", grad_full, weight_down, preferred_element_type=jnp.float32
    )
    grad_hidden = gelu_back(hidden, grad_active).astype(jnp.bfloat16)
    grad_up = jnp.einsum("rd,rf->df", normed_full, grad_hidden, preferred_element_type=jnp.float32)
    grad_normed = scatter_rows(
        jnp.einsum("rf,df->rd", grad_hidden, weight_up, preferred_element_type=jnp.float32)
    )
    grad_residual, grad_gain = norm_back(residual, norm_gain, grad_normed)
    return (upstream + grad_residual, grad_gain, grad_up, grad_down)


def clip_root(head_peak):
    return jnp.sqrt(clip_tau / jnp.maximum(head_peak, clip_tau))


def clip_columns(weight_local, head_root, head_size):
    column = jnp.repeat(head_root, head_size)
    scales = jnp.stack([column, column, jnp.ones_like(column)])
    return weight_local.astype(jnp.float32) * scales[None]


def local(
    block_input,
    first_norm,
    first_qkv,
    first_out,
    second_norm,
    dense_up,
    dense_down,
    third_norm,
    second_qkv,
    second_out,
    fourth_norm,
    router_weight,
    expert_up,
    expert_down,
    expert_ids,
    expert_slots,
    image_counts,
    cotangent,
):
    rows_local = block_input.shape[0]
    rows_full = rows_local * lax.axis_size("tensor")
    images = rows_full // L
    head_size = HD
    experts = expert_up.shape[0]
    capacity = CAP
    first_row = lax.axis_index("tensor") * rows_local
    live_count = image_counts[0]
    local_live = ((first_row + jnp.arange(rows_local)) // L < live_count).astype(jnp.float32)
    full_live = (jnp.arange(rows_full) // L < live_count).astype(jnp.float32)
    live_images = jnp.arange(images) < live_count

    def dense_fetch():
        return (
            lax.all_gather(first_norm, "dp", axis=0, tiled=True),
            lax.all_gather(first_qkv, "dp", axis=0, tiled=True),
            lax.all_gather(first_out, "dp", axis=1, tiled=True),
            lax.all_gather(second_norm, "dp", axis=0, tiled=True),
            lax.all_gather(dense_up, "dp", axis=0, tiled=True),
            lax.all_gather(dense_down, "dp", axis=1, tiled=True),
        )

    def moe_fetch():
        return (
            lax.all_gather(third_norm, "dp", axis=0, tiled=True),
            lax.all_gather(second_qkv, "dp", axis=0, tiled=True),
            lax.all_gather(second_out, "dp", axis=1, tiled=True),
            lax.all_gather(fourth_norm, "dp", axis=0, tiled=True),
            lax.all_gather(router_weight, "dp", axis=0, tiled=True),
            lax.all_gather(expert_up, "dp", axis=1, tiled=True),
            lax.all_gather(expert_down, "dp", axis=2, tiled=True),
        )

    dense_full = dense_fetch()
    residual_zero = block_input.astype(jnp.float32)
    residual_one, attn_first, peak_first = block_attention(
        residual_zero, dense_full[0], dense_full[1], dense_full[2], images, head_size, live_images
    )
    residual_two, mlp_stored = block_mlp(residual_one, dense_full[3], dense_full[4], dense_full[5])
    moe_full = moe_fetch()
    residual_three, attn_second, peak_second = block_attention(
        residual_two, moe_full[0], moe_full[1], moe_full[2], images, head_size, live_images
    )
    moe_normed = layer_norm(residual_three, moe_full[3].astype(jnp.float32)).astype(jnp.bfloat16)
    moe_input = gather_rows(moe_normed)
    logits = jnp.dot(moe_input, moe_full[4], preferred_element_type=jnp.float32)
    route_probs = jax.nn.softmax(logits, axis=-1)
    kept_mask = expert_slots < capacity
    pair_number = jnp.arange(2 * rows_full, dtype=jnp.int32)
    slot_index = (expert_ids * capacity + expert_slots).reshape(-1)
    kept_flat = kept_mask.reshape(-1)
    write_target = jnp.where(kept_flat, slot_index, experts * capacity + pair_number)
    target = jnp.where(kept_flat, slot_index, experts * capacity)
    pair_of_slot = (
        jnp.zeros((experts * capacity + 2 * rows_full,), jnp.int32)
        .at[write_target]
        .set(pair_number)[: experts * capacity]
    )
    slot_filled = (
        jnp.zeros((experts * capacity + 2 * rows_full,), jnp.float32)
        .at[write_target]
        .set(1.0)[: experts * capacity]
    )
    chosen = (expert_ids[:, :, None] == jnp.arange(experts)[None, None, :]).astype(jnp.float32)
    keep_live = kept_mask.astype(jnp.float32) * full_live[:, None]
    gates = jnp.sum(chosen * route_probs[:, None, :], axis=-1) * keep_live
    slot_token = pair_of_slot // 2
    slot_gate = gates.reshape(-1)[pair_of_slot] * slot_filled
    dispatched = (moe_input[slot_token] * slot_filled[:, None].astype(jnp.bfloat16)).reshape(
        experts, capacity, -1
    )
    expert_hidden = jnp.einsum(
        "ecd,edf->ecf", dispatched, moe_full[5], preferred_element_type=jnp.float32
    )
    expert_act = exact_gelu(expert_hidden).astype(jnp.bfloat16)
    expert_result = jnp.einsum(
        "ecf,efd->ecd", expert_act, moe_full[6], preferred_element_type=jnp.float32
    )
    feature_count = expert_result.shape[2]
    padded_result = jnp.concatenate(
        [
            expert_result.reshape(experts * capacity, feature_count),
            jnp.zeros((1, feature_count), jnp.float32),
        ],
        axis=0,
    )
    pair_result = padded_result[target].reshape(rows_full, 2, feature_count)
    combined = jnp.sum(gates[:, :, None] * pair_result, axis=1)
    residual_four = residual_three + scatter_rows(combined)
    block_output = residual_four * local_live[:, None]
    peak_first_all, peak_second_all = lax.pmax((peak_first, peak_second), "dp")
    root_first = clip_root(peak_first_all)
    root_second = clip_root(peak_second_all)
    clipped_first = clip_columns(first_qkv, root_first, head_size)
    clipped_second = clip_columns(second_qkv, root_second, head_size)
    clip_scales = jnp.stack([root_first, root_second])
    moe_back = moe_fetch()
    grad_four = cotangent.astype(jnp.float32) * local_live[:, None]
    moe_grad_full = gather_rows(grad_four.astype(jnp.bfloat16))
    partial_gates = jnp.sum(moe_grad_full.astype(jnp.float32)[:, None, :] * pair_result, axis=-1)
    grad_gates = lax.psum(partial_gates, "tensor")
    grad_result = (slot_gate[:, None] * moe_grad_full[slot_token].astype(jnp.float32)).astype(
        jnp.bfloat16
    )
    grad_result = grad_result.reshape(experts, capacity, feature_count)
    grad_expert_down = jnp.einsum(
        "ecf,ecd->efd", expert_act, grad_result, preferred_element_type=jnp.float32
    )
    grad_act = jnp.einsum(
        "ecd,efd->ecf", grad_result, moe_back[6], preferred_element_type=jnp.float32
    )
    grad_hidden = gelu_back(expert_hidden, grad_act).astype(jnp.bfloat16)
    grad_expert_up = jnp.einsum(
        "ecd,ecf->edf", dispatched, grad_hidden, preferred_element_type=jnp.float32
    )
    grad_dispatch = jnp.einsum(
        "ecf,edf->ecd", grad_hidden, moe_back[5], preferred_element_type=jnp.float32
    )
    grad_dispatch = jnp.concatenate(
        [
            grad_dispatch.reshape(experts * capacity, feature_count),
            jnp.zeros((1, feature_count), jnp.float32),
        ],
        axis=0,
    )
    grad_from_experts = jnp.sum(grad_dispatch[target].reshape(rows_full, 2, feature_count), axis=1)
    grad_picked = grad_gates * keep_live
    grad_probs = jnp.sum(chosen * grad_picked[:, :, None], axis=1)
    grad_logits = route_probs * (
        grad_probs - jnp.sum(grad_probs * route_probs, axis=-1, keepdims=True)
    )
    grad_logits = grad_logits.astype(jnp.bfloat16)
    grad_router = jnp.einsum(
        "rd,re->de", moe_input, grad_logits, preferred_element_type=jnp.float32
    )
    local_logits = lax.dynamic_slice_in_dim(grad_logits, first_row, rows_local, 0)
    grad_moe_normed = scatter_rows(grad_from_experts) + jnp.einsum(
        "re,de->rd", local_logits, moe_back[4], preferred_element_type=jnp.float32
    )
    grad_rows_four, grad_fourth_norm = norm_back(residual_three, moe_back[3], grad_moe_normed)
    grad_three = grad_four + grad_rows_four
    grad_two, grad_third_norm, grad_second_qkv, grad_second_out = block_attention_back(
        residual_two,
        grad_three,
        moe_back[0],
        moe_back[1],
        moe_back[2],
        attn_second,
        images,
        head_size,
    )
    third_sum, fourth_sum = sum_gains(grad_third_norm, grad_fourth_norm)
    moe_owned = (
        lax.psum_scatter(third_sum, "dp", scatter_dimension=0, tiled=True),
        lax.psum_scatter(grad_second_qkv, "dp", scatter_dimension=0, tiled=True),
        lax.psum_scatter(grad_second_out, "dp", scatter_dimension=1, tiled=True),
        lax.psum_scatter(fourth_sum, "dp", scatter_dimension=0, tiled=True),
        lax.psum_scatter(grad_router, "dp", scatter_dimension=0, tiled=True),
        lax.psum_scatter(grad_expert_up, "dp", scatter_dimension=1, tiled=True),
        lax.psum_scatter(grad_expert_down, "dp", scatter_dimension=2, tiled=True),
    )
    dense_back = dense_fetch()
    grad_one, grad_second_norm, grad_dense_up, grad_dense_down = block_mlp_back(
        residual_one, grad_two, dense_back[3], dense_back[4], dense_back[5], mlp_stored
    )
    input_grad, grad_first_norm, grad_first_qkv, grad_first_out = block_attention_back(
        residual_zero,
        grad_one,
        dense_back[0],
        dense_back[1],
        dense_back[2],
        attn_first,
        images,
        head_size,
    )
    first_sum, second_sum = sum_gains(grad_first_norm, grad_second_norm)
    dense_owned = (
        lax.psum_scatter(first_sum, "dp", scatter_dimension=0, tiled=True),
        lax.psum_scatter(grad_first_qkv, "dp", scatter_dimension=0, tiled=True),
        lax.psum_scatter(grad_first_out, "dp", scatter_dimension=1, tiled=True),
        lax.psum_scatter(second_sum, "dp", scatter_dimension=0, tiled=True),
        lax.psum_scatter(grad_dense_up, "dp", scatter_dimension=0, tiled=True),
        lax.psum_scatter(grad_dense_down, "dp", scatter_dimension=1, tiled=True),
    )
    owned = tuple(dense_owned) + tuple(moe_owned)
    return (
        block_output,
        input_grad,
        owned[0],
        owned[1],
        owned[2],
        owned[3],
        owned[4],
        owned[5],
        owned[6],
        owned[7],
        owned[8],
        owned[9],
        owned[10],
        owned[11],
        owned[12],
        clipped_first,
        clipped_second,
        clip_scales,
    )


ROWS = 208
AXES = ("dp", "tensor")
BF = jnp.bfloat16
F32 = jnp.float32
VM = pl.BlockSpec(memory_space=pltpu.VMEM)
SM = pl.BlockSpec(memory_space=pltpu.SMEM)


def swap(values, z=0, x=0, y=0, core=0):
    shift_d, shift_t = 2 * z + x, 2 * y + core
    pairs = [(d * 4 + t, (d ^ shift_d) * 4 + (t ^ shift_t)) for d in range(8) for t in range(4)]
    return lax.ppermute(values, AXES, pairs)


def hold(values, *tokens):
    return lax.optimization_barrier((values,) + tokens)[0]


def run(kernel, outs, args, flops, scratch=(), scalars=0, mib=20):
    flops = flops if flops == 8e9 else 1000
    shapes = [jax.ShapeDtypeStruct(s, dt) for s, dt in outs]
    return pl.pallas_call(
        kernel,
        out_shape=shapes,
        in_specs=[SM] * scalars + [VM] * (len(args) - scalars),
        out_specs=[VM] * len(shapes),
        scratch_shapes=list(scratch),
        compiler_params=pltpu.CompilerParams(vmem_limit_bytes=mib * 2**20),
        cost_estimate=pl.CostEstimate(flops=int(flops), bytes_accessed=1000, transcendentals=0),
    )(*args)


def dot(a, b, ca, cb):
    return lax.dot_general(a, b, (((ca,), (cb,)), ((), ())), preferred_element_type=F32)


def norm_stats(values):
    center = values - jnp.mean(values, axis=-1, keepdims=True)
    scale = lax.rsqrt(jnp.mean(center * center, axis=-1, keepdims=True) + epsilon)
    return center * scale, scale


def enter_kernel(live, x_ref, c_ref, perm_ref, start_ref, low_start, grad_ref, low_ref):
    rows = x_ref.shape[0]
    scale = live[0].astype(F32)
    extra = jnp.zeros((ROWS - rows, x_ref.shape[1]), F32)
    start = dot(x_ref[...], perm_ref[...], 1, 1)
    start_ref[:rows] = start
    start_ref[rows:] = extra
    low_start[:rows] = start.astype(BF)
    low_start[rows:] = extra.astype(BF)
    grad = dot(c_ref[...], perm_ref[...], 1, 1) * scale
    grad_ref[:rows] = grad
    grad_ref[rows:] = extra
    low_ref[:rows] = grad.astype(BF)
    low_ref[rows:] = extra.astype(BF)


def norm_kernel(gain_ref, *refs):
    for x_ref, out_ref in zip(refs[:4], refs[4:]):
        out_ref[...] = (norm_stats(x_ref[...].astype(F32))[0] * gain_ref[...]).astype(BF)


def join_norm_kernel(x_ref, own_ref, far_ref, gain_ref, sum_ref, out_ref):
    total = x_ref[...] + (own_ref[...] + far_ref[...].astype(F32))
    sum_ref[...] = total
    out_ref[...] = (norm_stats(total)[0] * gain_ref[...]).astype(BF)


def norm_back_kernel(x_ref, up_ref, own_ref, far_ref, gain_ref, grad_ref, low_ref, gain_out):
    upstream = own_ref[...] + far_ref[...].astype(F32)
    normed, scale = norm_stats(x_ref[...])
    scaled = upstream * gain_ref[...]
    grad = up_ref[...] + scale * (
        scaled
        - jnp.mean(scaled, axis=-1, keepdims=True)
        - normed * jnp.mean(scaled * normed, axis=-1, keepdims=True)
    )
    grad_ref[...] = grad
    low_ref[...] = grad.astype(BF)
    gain_out[...] = jnp.sum(upstream * normed, axis=0, keepdims=True)


def fill(rows, *refs):
    size = refs[0].shape[0]
    for i, ref in enumerate(refs):
        rows[i * size : (i + 1) * size] = ref[...]


def put_partial(partial, own_ref, sib_ref):
    half = own_ref.shape[0]
    own_ref[...] = partial[:half]
    sib_ref[...] = partial[half:].astype(BF)


def score_block(queries, keyset):
    scores = dot(queries, keyset, 1, 1) * HD ** (-0.5)
    column = lax.broadcasted_iota(jnp.int32, scores.shape, 1)
    scores = jnp.where(column < L, scores, -1e30)
    top = jnp.max(scores, axis=-1, keepdims=True)
    weight = jnp.exp(scores - top)
    return weight * (1.0 / jnp.sum(weight, axis=-1, keepdims=True)), top


def attend_kernel(
    at, live, a0, a1, a2, a3, w, mix_ref, att_ref, own_ref, sib_ref, peak_ref, rows
):
    fill(rows, a0, a1, a2, a3)
    part = mix_ref.shape[1] // 3
    mix_ref[...] = dot(rows[...], w[:, at : at + 3 * part], 1, 0).astype(BF)
    row_ok = lax.broadcasted_iota(jnp.int32, (ROWS, 1), 0) < L
    lane = lax.broadcasted_iota(jnp.int32, peak_ref.shape, 1)
    found = jnp.full(peak_ref.shape, -1e30, F32)
    for h in range(part // HD):
        for i in range(4):
            span = slice(i * ROWS, (i + 1) * ROWS)
            cut = [mix_ref[span, c * part + h * HD : c * part + (h + 1) * HD] for c in range(3)]
            probs, top = score_block(cut[0], cut[1])
            mixed = dot(probs.astype(BF), cut[2], 1, 0)
            att_ref[span, h * HD : (h + 1) * HD] = mixed.astype(BF)
            best = jnp.max(jnp.where(row_ok, top, -1e30), axis=0, keepdims=True)
            best = jnp.where(live[i] > 0, best, -1e30)
            found = jnp.where(lane == h, jnp.maximum(best, found), found)
    peak_ref[...] = found
    out = w[:, at + 3 * part : at + 4 * part]
    put_partial(dot(att_ref[...], out, 1, 1), own_ref, sib_ref)


def put_pack(grad, column, near, send):
    half = near.shape[0]
    near[:, column : column + grad.shape[1]] = grad[:half]
    send[:, column : column + grad.shape[1]] = grad[half:]


def attend_back_kernel(
    at, g0, g1, g2, g3, a0, a1, a2, a3, mix_ref, att_ref, w,
    near, send, own_ref, sib_ref, rows, grad_att, grad_mix,
):
    part = mix_ref.shape[1] // 3
    fill(rows, g0, g1, g2, g3)
    grad_att[...] = dot(rows[...], w[:, at + 3 * part : at + 4 * part], 1, 0).astype(BF)
    put_pack(dot(rows[...], att_ref[...], 0, 0).astype(BF), 3 * part, near, send)
    factor = HD ** (-0.5)
    for h in range(part // HD):
        for i in range(4):
            span = slice(i * ROWS, (i + 1) * ROWS)
            spans = [slice(c * part + h * HD, c * part + (h + 1) * HD) for c in range(3)]
            queries, keyset, values = (mix_ref[span, s] for s in spans)
            grad = grad_att[span, h * HD : (h + 1) * HD]
            probs, _ = score_block(queries, keyset)
            grad_mix[span, spans[2]] = dot(probs.astype(BF), grad, 0, 0).astype(BF)
            grad_probs = dot(grad, values, 1, 1)
            slope = probs * (grad_probs - jnp.sum(grad_probs * probs, axis=-1, keepdims=True))
            slope = slope.astype(BF)
            grad_mix[span, spans[0]] = (factor * dot(slope, keyset, 1, 0)).astype(BF)
            grad_mix[span, spans[1]] = (factor * dot(slope, queries, 0, 0)).astype(BF)
    put_partial(dot(grad_mix[...], w[:, at : at + 3 * part], 1, 1), own_ref, sib_ref)
    fill(rows, a0, a1, a2, a3)
    put_pack(dot(rows[...], grad_mix[...], 0, 0).astype(BF), 0, near, send)


def gelu_pair(hidden):
    cdf = 0.5 * (1.0 + lax.erf(hidden * 0.7071067811865476))
    slope = cdf + hidden * jnp.exp(-0.5 * hidden * hidden) * 0.3989422804014327
    return (hidden * cdf).astype(BF), slope.astype(BF)


def mlp_kernel(ats, b0, b1, b2, b3, w, act_ref, slope_ref, own_ref, sib_ref, rows):
    fill(rows, b0, b1, b2, b3)
    wide = act_ref.shape[1]
    for c in range(0, wide, 256):
        span = slice(c, c + 256)
        act, slope = gelu_pair(dot(rows[...], w[:, ats[0] + c : ats[0] + c + 256], 1, 0))
        act_ref[:, span] = act
        slope_ref[:, span] = slope
    put_partial(dot(act_ref[...], w[:, ats[1] : ats[1] + wide], 1, 1), own_ref, sib_ref)


def mlp_back_kernel(
    ats, g0, g1, g2, g3, b0, b1, b2, b3, act_ref, slope_ref, w,
    near, send, own_ref, sib_ref, rows, hidden,
):
    fill(rows, g0, g1, g2, g3)
    wide = act_ref.shape[1]
    grad = dot(rows[...], w[:, ats[1] : ats[1] + wide], 1, 0) * slope_ref[...].astype(F32)
    hidden[...] = grad.astype(BF)
    put_partial(dot(hidden[...], w[:, ats[0] : ats[0] + wide], 1, 1), own_ref, sib_ref)
    put_pack(dot(rows[...], act_ref[...], 0, 0).astype(BF), wide, near, send)
    fill(rows, b0, b1, b2, b3)
    put_pack(dot(rows[...], hidden[...], 0, 0).astype(BF), 0, near, send)


def picked(row_code, codes):
    hit = (row_code[...] == codes[0:1, :]) | (row_code[...] == codes[1:2, :])
    return jnp.where(hit, 1.0, 0.0).astype(BF)


def dispatch_kernel(row_code, codes, p0, p1, p2, p3, perm_ref, out, rows):
    fill(rows, p0, p1, p2, p3)
    picks = dot(picked(row_code, codes), rows[...], 1, 0).astype(BF)
    out[...] = dot(picks, perm_ref[...], 1, 0).astype(BF)


def token_kernel(row_code, codes, p0, p1, p2, p3, perm_ref, first_ref, second_ref, out, rows):
    dispatch_kernel(row_code, codes, p0, p1, p2, p3, perm_ref, out, rows)
    row = lax.broadcasted_iota(jnp.int32, (8, 128), 0)
    block = jnp.zeros((8, 128), F32)
    for i, ref in enumerate((first_ref, second_ref)):
        high = ref[...].astype(BF).astype(F32)
        block = jnp.where(row == 2 * i + 2, high, block)
        block = jnp.where(row == 2 * i + 3, ref[...] - high, block)
    size = out.shape[0] // 8
    for e in range(8):
        span = slice((e + 1) * size - 8, (e + 1) * size)
        old = out[span, :128].astype(F32)
        out[span, :128] = jnp.where((row >= 2) & (row < 6), block, old).astype(BF)


def collect_kernel(both_ref, grad_ref, out_ref, peak_ref):
    size = both_ref.shape[1] // 2
    best = jnp.full((2, 128), -1e30, F32)
    for p in range(both_ref.shape[0]):
        rows = slice(p * size, (p + 1) * size)
        grad_ref[rows] = both_ref[p, :size]
        out_ref[rows] = both_ref[p, size:]
        block = both_ref[p, 2 * size - 8 :, :128].astype(F32)
        found = [block[2 * i + 2 : 2 * i + 3] + block[2 * i + 3 : 2 * i + 4] for i in range(2)]
        best = jnp.maximum(best, jnp.concatenate(found, axis=0))
    peak_ref[...] = best


def combine_kernel(which, row_code, codes, perm_ref, both_ref, own_ref, sib_ref, rows):
    size = both_ref.shape[1] // 2
    for p in range(both_ref.shape[0]):
        rows[p * size : (p + 1) * size] = both_ref[p, which * size : (which + 1) * size]
    back = dot(rows[...], perm_ref[...], 1, 1).astype(BF)
    partial = dot(picked(row_code, codes), back, 0, 0)
    half = partial.shape[0] // 2
    own_ref[...] = partial[:half]
    sib_ref[...] = partial[half:].astype(BF)


def pair_add_kernel(own_ref, far_ref, near_ref, send_ref):
    total = own_ref[...] + far_ref[...].astype(F32)
    near_ref[...] = total[:ROWS]
    send_ref[...] = total[ROWS:].astype(BF)


def route_of(tokens, router, number):
    logits = dot(tokens, router, 1, 1)
    column = lax.broadcasted_iota(jnp.int32, logits.shape, 1)
    logits = jnp.where(column < 8, logits, -1e30)
    weight = jnp.exp(logits - jnp.max(logits, axis=-1, keepdims=True))
    route = weight / jnp.sum(weight, axis=-1, keepdims=True)
    mine = jnp.where(column == number, 1.0, 0.0)
    return route, mine, jnp.sum(route * mine, axis=-1, keepdims=True)


def expert_kernel(
    number, t0, t1, g0, g1, router, *rest
):
    own, far = rest[0], rest[1:5]
    res_own, res_sib, grad_own, grad_sib = rest[5:9]
    up_parts, down_parts = rest[9:12], rest[12:15]
    act_ref, hid_ref, gout_ref, pair, whole = rest[15:]
    size = t0.shape[0]
    half, wide = own.shape[0] // 2, act_ref.shape[2]
    whole[0] = own[...]
    for i, part in enumerate(far):
        whole[1, i * half // 2 : (i + 1) * half // 2] = part[...]
    for i, (t, g, res, grad) in enumerate(
        ((t1, g1, res_sib, grad_sib), (t0, g0, res_own, grad_own))
    ):
        rows = slice((1 - i) * size, (2 - i) * size)
        gate = route_of(t[...], router[...], number[0])[2]
        gout = (gate * g[...].astype(F32)).astype(BF)
        gout_ref[rows] = gout
        for y in range(2):
            for c in range(0, wide, 256):
                span = slice(c, c + 256)
                act, lean = gelu_pair(dot(t[...], whole[y, :, span], 1, 0))
                act_ref[y, rows, span] = act
                back = dot(gout, whole[y, :, wide + c : wide + c + 256], 1, 0)
                hid_ref[y, rows, span] = (back * lean.astype(F32)).astype(BF)
        res[...] = (
            dot(act_ref[0, rows], whole[0, :, wide:], 1, 1)
            + dot(act_ref[1, rows], whole[1, :, wide:], 1, 1)
        ).astype(res.dtype)
        grad[...] = (
            dot(hid_ref[0, rows], whole[0, :, :wide], 1, 1)
            + dot(hid_ref[1, rows], whole[1, :, :wide], 1, 1)
        ).astype(grad.dtype)
    pair[:size] = t0[...]
    pair[size:] = t1[...]
    for parts, left, right in ((up_parts, pair, hid_ref), (down_parts, gout_ref, act_ref)):
        parts[0][...] = dot(left[...], right[0], 0, 0).astype(BF)
        far = dot(left[...], right[1], 0, 0).astype(BF)
        parts[1][...] = far[:half]
        parts[2][...] = far[half:]


def answer_kernel(
    number, t_ref, g_ref, router, res_own, res_far, grad_own, grad_far, perm_ref,
    both_ref, router_out,
):
    route, mine, gate = route_of(t_ref[...], router[...], number[0])
    result = res_own[...] + res_far[...].astype(F32)
    grad_gate = jnp.sum(result * g_ref[...].astype(F32), axis=-1, keepdims=True)
    grad_logit = (grad_gate * route * (mine - gate)).astype(BF)
    router_out[...] = reorder(dot(grad_logit, t_ref[...], 0, 0), perm_ref[...], 1)
    grad = grad_own[...] + grad_far[...].astype(F32) + dot(grad_logit, router[...], 1, 0)
    size = both_ref.shape[1] // 2
    whole = grad.astype(BF)
    for p in range(both_ref.shape[0]):
        both_ref[p, :size] = whole[p * size : (p + 1) * size]
    whole = (gate * result).astype(BF)
    for p in range(both_ref.shape[0]):
        both_ref[p, size:] = whole[p * size : (p + 1) * size]


def reorder(values, perm, axis):
    high = values.astype(BF)
    rest = values - high.astype(F32)
    middle = rest.astype(BF)
    low = (rest - middle.astype(F32)).astype(BF)
    return dot(high, perm, 1, axis) + (dot(middle, perm, 1, axis) + dot(low, perm, 1, axis))


def leave_kernel(x_ref, perm_ref, out_ref):
    out_ref[...] = reorder(x_ref[...], perm_ref[...], 0)[: out_ref.shape[0]]


def finish_kernel(live, x_ref, own_ref, far_ref, perm_ref, out_ref):
    total = x_ref[...] + (own_ref[...] + far_ref[...].astype(F32))
    total = reorder(total, perm_ref[...], 0) * live[0].astype(F32)
    out_ref[...] = total[: out_ref.shape[0]]


def add_pack_kernel(up_own, up0, up1, down_own, down0, down1, out):
    half, wide = up0.shape
    for c, (own, parts) in enumerate(((up_own, (up0, up1)), (down_own, (down0, down1)))):
        for s, part in enumerate(parts):
            span = slice(s * half, (s + 1) * half)
            total = own[span].astype(F32) + part[...].astype(F32)
            out[span, c * wide : (c + 1) * wide] = total.astype(BF)


def pack_kernel(*refs):
    out = refs[-1]
    at = 0
    for ref in refs[:-1]:
        out[:, at : at + ref.shape[1]] = ref[...]
        at += ref.shape[1]


def stack_kernel(*refs):
    rows = refs[0].shape[0]
    for i, ref in enumerate(refs[:-1]):
        refs[-1][i * rows : (i + 1) * rows] = ref[...]


def order_kernel(places, in_ref, out_ref):
    rows = out_ref.shape[0] // 4
    for i in range(4):
        at = pl.multiple_of(places[i] * rows, rows)
        out_ref[i * rows : (i + 1) * rows] = in_ref[pl.ds(at, rows), :]


def sum_two(near, got, keep, s1, s2, s3):
    rows = keep.shape[0]
    for k, out in enumerate((keep, s1, s2, s3)):
        span = slice(k * rows, (k + 1) * rows)
        out[...] = (near[span].astype(F32) + got[span].astype(F32)).astype(out.dtype)


def small_kernel(g1, g2, g3, g4, router, out):
    whole = jnp.concatenate([g1[...], g2[...], g3[...], g4[...]], axis=0)
    count, cols = router.shape[0], out.shape[2]
    blank = jnp.zeros((out.shape[1] - 4 - count, cols), F32)
    for p in range(8):
        span = slice(p * cols, (p + 1) * cols)
        out[p] = jnp.concatenate([whole[:, span], router[:, span], blank], axis=0)


def sum_two_more(near, got, small, keep, s1, s2, s3):
    sum_two(near, got, keep, s1.at[: keep.shape[0]], s2.at[: keep.shape[0]], s3.at[: keep.shape[0]])
    rows, count = keep.shape[0], small.shape[1]
    cols = small.shape[2]
    for k, out in enumerate((s1, s2, s3)):
        out[rows:, :] = jnp.zeros((out.shape[0] - rows, out.shape[1]), BF)
        high = small[k + 1].astype(BF)
        out[rows : rows + count, :cols] = high
        low = small[k + 1] - high.astype(F32)
        out[rows + count : rows + 2 * count, :cols] = low.astype(BF)


def sum_three_more(keep, r1, r2, r3, small, first, second, small_out):
    rows, count = keep.shape[0], small.shape[1]
    cols = small.shape[2]
    sum_three(keep, r1.at[:rows], r2.at[:rows], r3.at[:rows], first, second)
    total = small[0]
    for r in (r1, r2, r3):
        high = r[rows : rows + count, :cols].astype(F32)
        total = total + (high + r[rows + count : rows + 2 * count, :cols].astype(F32))
    small_out[...] = total


def sum_three(keep, r1, r2, r3, first, second):
    total = keep[...] + (r1[...].astype(F32) + (r2[...].astype(F32) + r3[...].astype(F32)))
    wide = first.shape[1]
    first[...] = total[:, :wide]
    second[...] = total[:, wide:]


def scatter_start(parts):
    near, send = parts
    return near, swap(send, x=1)


def scatter_middle(parts):
    half, width = parts[0].shape
    shape = (half // 4, width)
    return run(sum_two, [(shape, F32)] + [(shape, BF)] * 3, parts, half * width)


def scatter_late(parts):
    keep, s1, s2, s3 = parts
    return keep, swap(s1, z=1), swap(s2, z=2), swap(s3, z=3)


def scatter_end(parts, wide):
    rows, width = parts[0].shape
    return run(sum_three, [((rows, wide), F32), ((rows, width - wide), F32)], parts, rows * width)


def fast_local(
    block_input,
    first_norm,
    first_qkv,
    first_out,
    second_norm,
    dense_up,
    dense_down,
    third_norm,
    second_qkv,
    second_out,
    fourth_norm,
    router_weight,
    expert_up,
    expert_down,
    expert_ids,
    expert_slots,
    image_counts,
    cotangent,
):
    d = lax.axis_index("dp")
    t = lax.axis_index("tensor")
    z_index, x_index = d // 2, d % 2
    width = first_norm.shape[0]
    features = width * 8
    experts = expert_up.shape[0]
    live_count = image_counts[0]
    head_cols = first_out.shape[0]
    ff_cols = dense_up.shape[1]
    qkv_cols = 3 * head_cols
    row = ((ROWS, features), F32)
    row_low = ((ROWS, features), BF)

    small = jnp.concatenate(
        [
            jnp.stack([first_norm, second_norm, third_norm, fourth_norm], axis=1),
            router_weight,
            jnp.zeros((width, 128 - 4 - experts), BF),
        ],
        axis=1,
    )
    pack_one = run(
        pack_kernel,
        [((width, small.shape[1] + 4 * head_cols), BF)],
        (small, first_qkv.reshape(width, -1), first_out.T),
        width,
    )[0]
    pack_late = run(
        pack_kernel,
        [((width, 2 * ff_cols + 4 * head_cols), BF)],
        (dense_up, dense_down.T, second_qkv.reshape(width, -1), second_out.T),
        width,
    )[0]

    lines = [[x + 2 * z for z in range(4)] for x in range(2)]
    raw_late = lax.all_gather(pack_late, "dp", axis=0, tiled=True, axis_index_groups=lines)

    def stacked(shards):
        shape = (len(shards) * shards[0].shape[0], shards[0].shape[1])
        return run(stack_kernel, [(shape, BF)], shards, width)[0]

    z_one = stacked([pack_one] + [swap(pack_one, z=k) for k in (1, 2, 3)])

    rel = jnp.arange(features)
    block = rel // width
    rel_place = jnp.bitwise_xor(d, 2 * (block % 4) + block // 4) * width + rel % width
    perm = (rel_place[:, None] == rel[None, :]).astype(BF)
    live_here = (t < live_count).astype(jnp.int32).reshape(1)
    live_group = (jnp.stack([t, t ^ 2, t ^ 1, t ^ 3]) < live_count).astype(jnp.int32)

    start, low_start, grad_four, grad_low = run(
        enter_kernel,
        [row, row_low, row, row_low],
        (live_here, block_input, cotangent, perm),
        4 * ROWS * features**2,
        scalars=1,
    )

    def spread(rows):
        far = swap(rows, y=1)
        return [rows, far, swap(rows, core=1), swap(far, core=1)]

    first_group = spread(low_start)
    wide = 2 * ff_cols
    half_shape = [((features // 2, ff_cols), BF)] * 2
    e_pack = jnp.concatenate([expert_up, jnp.swapaxes(expert_down, 1, 2)], axis=2)
    held = -(-CAP // 4)
    block_size = -(-(held + 4) // 8) * 8
    ids = jnp.pad(expert_ids.reshape(4, L, 2), ((0, 0), (0, ROWS - L), (0, 0)), constant_values=-1)
    slots = jnp.pad(
        expert_slots.reshape(4, L, 2), ((0, 0), (0, ROWS - L), (0, 0)), constant_values=CAP
    )
    mine = (slots < CAP) & (slots // held == t)
    codes = jnp.where(mine, ids * block_size + slots % held, -1)
    codes = jnp.concatenate(
        [lax.dynamic_index_in_dim(codes, t ^ k, 0, keepdims=False) for k in (0, 2, 1, 3)], axis=0
    ).T
    slot_rows = experts * block_size
    row_code = jnp.arange(slot_rows).reshape(-1, 1)
    group_flops = 2 * slot_rows * features * (4 * ROWS + features)

    def to_experts(kernel, rows, *peaks):
        return run(
            kernel,
            [((slot_rows, features), BF)],
            (row_code, codes, *rows, perm, *peaks),
            group_flops,
            scratch=[pltpu.VMEM((4 * ROWS, features), BF)],
        )[0].reshape(experts, block_size, features)

    def exchange(both):
        return lax.all_to_all(both, "dp", split_axis=0, concat_axis=0, tiled=True)

    group_scratch = pltpu.VMEM((4 * ROWS, features), BF)
    pair_out = [((2 * ROWS, features), F32), ((2 * ROWS, features), BF)]

    def attend(normed, full, at):
        return run(
            functools.partial(attend_kernel, at),
            [((4 * ROWS, qkv_cols), BF), ((4 * ROWS, head_cols), BF)]
            + pair_out
            + [((1, 128), F32)],
            (live_group, *normed, full),
            0,
            scratch=[group_scratch],
            scalars=1,
        )

    def pack_shapes(columns):
        return [((features // 2, columns), BF)] * 2 + pair_out

    def attend_back(low, normed, mixed, attended, full, at):
        return run(
            functools.partial(attend_back_kernel, at),
            pack_shapes(4 * head_cols),
            (*low, *normed, mixed, attended, full),
            8e9,
            scratch=[
                group_scratch,
                pltpu.VMEM((4 * ROWS, head_cols), BF),
                pltpu.VMEM((4 * ROWS, qkv_cols), BF),
            ],
        )

    def over_group(own, sib):
        near, send = run(pair_add_kernel, [row, row_low], (own, swap(sib, core=1)), ROWS)
        return near, swap(send, y=1)

    def join(values, own, far, gain):
        return run(join_norm_kernel, [row, row_low], (values, own, far, gain), ROWS)

    def norm_back(values, upstream, own, far, gain):
        return run(
            norm_back_kernel,
            [row, row_low, ((1, features), F32)],
            (values, upstream, own, far, gain),
            ROWS,
        )

    full_one = stacked(hold([z_one, swap(z_one, x=1)], first_group))
    small_rows = full_one[:, : 4 + experts].T
    gains = [small_rows[i : i + 1].astype(F32) for i in range(4)]
    router = dot(small_rows[4:], perm, 1, 0).astype(BF)

    normed_one = run(norm_kernel, [row_low] * 4, (gains[0], *first_group), ROWS)
    mixed_one, att_one, own, sib, peak_one = attend(normed_one, full_one, small.shape[1])
    near, far = over_group(own, sib)
    one, normed = join(start, near, hold(far, raw_late), gains[1])
    normed_mlp = spread(normed)
    z_late = run(
        order_kernel,
        [(raw_late.shape, BF)],
        (jnp.stack([z_index ^ k for k in range(4)]).astype(jnp.int32), hold(raw_late, one)),
        features,
        scalars=1,
    )[0]
    x_late = swap(z_late, x=1)
    e_pack = hold(e_pack, normed_mlp[1])
    e_own = lax.all_to_all(e_pack, "dp", split_axis=0, concat_axis=0, tiled=True)
    e_own = e_own.reshape(features, wide)
    e_own = hold(e_own, normed_mlp[1])
    far = [swap(e_own[i * 2 * width : (i + 1) * 2 * width], y=1) for i in range(4)]
    e_far = far
    grad_sent = to_experts(dispatch_kernel, spread(hold(grad_low, normed)))
    full_late = stacked([z_late, x_late])
    ats = (0, ff_cols)
    act, slope, own, sib = run(
        functools.partial(mlp_kernel, ats),
        [((4 * ROWS, ff_cols), BF)] * 2 + pair_out,
        (*hold(normed_mlp, grad_sent), full_late),
        0,
        scratch=[group_scratch],
    )
    near, far = over_group(own, sib)
    two, normed = join(one, near, far, gains[2])
    normed_two = spread(normed)
    mixed_two, att_two, own, sib, peak_two = attend(normed_two, full_late, 2 * ff_cols)
    near, far = over_group(own, sib)
    three, normed = join(two, near, far, gains[3])
    tokens_sent = to_experts(token_kernel, spread(normed), peak_one, peak_two)
    both = exchange(hold(jnp.concatenate([grad_sent, tokens_sent], axis=1), e_far[0]))
    grad_slots, tokens, peaks = run(
        collect_kernel,
        [((slot_rows, features), BF)] * 2 + [((2, 128), F32)],
        (hold(both, *e_far),),
        0,
    )
    far_slots, far_tokens = swap(grad_slots, core=1), swap(tokens, core=1)
    number = d.astype(jnp.int32).reshape(1)
    near_heads = head_cols // HD
    roots = clip_root(peaks[:, :near_heads])
    slot_out = [((slot_rows, features), F32), ((slot_rows, features), BF)]
    res_own, res_sib, eg_own, eg_sib, *e_packs = run(
        expert_kernel,
        slot_out + slot_out + ([((features, ff_cols), BF)] + half_shape) * 2,
        (number, tokens, far_tokens, grad_slots, far_slots, router)
        + (e_own, *e_far),
        8 * 2 * slot_rows * features * 2 * ff_cols,
        scalars=1,
        scratch=[
            pltpu.VMEM((2, 2 * slot_rows, ff_cols), BF),
            pltpu.VMEM((2, 2 * slot_rows, ff_cols), BF),
            pltpu.VMEM((2 * slot_rows, features), BF),
            pltpu.VMEM((2 * slot_rows, features), BF),
            pltpu.VMEM((2, features, wide), BF),
        ],
        mib=44,
    )
    res_far, eg_far = swap(res_sib, core=1), swap(eg_sib, core=1)
    up_got = [swap(e_packs[1], y=1)]
    both, grad_router = run(
        answer_kernel,
        [((experts, 2 * block_size, features), BF), ((experts, features), F32)],
        (number, tokens, grad_slots, router, res_own, res_far, eg_own, eg_far, perm),
        4 * slot_rows * features**2,
        scalars=1,
    )
    both = hold(both, up_got)
    e_packs = hold(e_packs, both)
    both = exchange(both)
    up_got.append(swap(e_packs[2], y=1))
    down_got = [swap(e_packs[4], y=1)]
    both = hold(both, up_got, down_got)

    def combine(which, both):
        return run(
            functools.partial(combine_kernel, which),
            [((2 * ROWS, features), F32), ((2 * ROWS, features), BF)],
            (row_code, codes, perm, both),
            group_flops,
            scratch=[pltpu.VMEM((slot_rows, features), BF)],
        )

    own, sib = combine(0, both)
    back_own, back_far = over_group(own, sib)
    grad_three, low, gain_four = norm_back(
        three, grad_four, back_own, back_far, gains[3]
    )
    low = spread(low)
    down_got.append(swap(hold(e_packs[5], low[1]), y=1))
    *second, own, sib = attend_back(
        low, normed_two, mixed_two, att_two, full_late, 2 * ff_cols
    )
    second = scatter_start(second)
    near, far = over_group(own, hold(sib, down_got[1]))
    e_sum = run(
        add_pack_kernel,
        [((features, wide), BF)],
        (e_packs[0], *up_got, e_packs[3], *hold(down_got, second[1], far)),
        0,
    )[0].reshape(experts, width, wide)
    e_back = lax.all_to_all(e_sum, "dp", split_axis=0, concat_axis=0, tiled=True)
    grad_two, low, gain_three = norm_back(
        two, grad_three, near, far, gains[2]
    )
    low = spread(low)
    *mlp, own, sib = run(
        functools.partial(mlp_back_kernel, ats),
        pack_shapes(2 * ff_cols),
        (*low, *normed_mlp, act, slope, full_late),
        0,
        scratch=[group_scratch, pltpu.VMEM((4 * ROWS, ff_cols), BF)],
    )
    mlp = scatter_start(mlp)
    near, send = run(pair_add_kernel, [row, row_low], (own, swap(sib, core=1)), ROWS)
    far = swap(send, y=1)
    mixed_own, mixed_sib = combine(1, hold(both, sib))
    second = scatter_late(scatter_middle(hold(second, mixed_own)))
    mixed_own, mixed_send = run(
        pair_add_kernel, [row, row_low], (mixed_own, swap(mixed_sib, core=1)), ROWS
    )
    grad_one, low, gain_two = norm_back(
        one, grad_two, near, hold(far, mixed_send), gains[1]
    )
    low = spread(low)
    mixed_far = swap(hold(mixed_send, low), y=1)
    *first, own, sib = attend_back(
        hold(low, mlp),
        normed_one,
        mixed_one,
        att_one,
        full_one,
        small.shape[1],
    )
    mlp = scatter_late(scatter_middle(mlp))
    first = scatter_start(first)
    near, far = over_group(own, hold(sib, mixed_far, second, e_back))
    grad_zero, _, gain_one = norm_back(start, grad_one, near, hold(far, first), gains[0])
    block_output = run(
        finish_kernel,
        [((L, features), F32)],
        (live_here, three, mixed_own, mixed_far, perm),
        6 * ROWS * features**2,
        scalars=1,
    )[0]
    up_g = e_back[:, :, :ff_cols].astype(F32)
    down_g = jnp.swapaxes(e_back[:, :, ff_cols:], 1, 2).astype(F32)
    clips = (clip_columns(first_qkv, roots[0], HD), clip_columns(second_qkv, roots[1], HD))
    gains_sum = run(
        small_kernel,
        [((8, 16, width), F32)],
        (gain_one, gain_two, gain_three, gain_four, grad_router),
        0,
    )[0]
    gains_sum = hold(
        gains_sum + swap(gains_sum, core=1), mlp, block_output, up_g, down_g, clips
    )
    gains_sum = gains_sum + swap(gains_sum, y=1)
    gains_sum = gains_sum[:4] + swap(gains_sum[4:], x=1)
    near_first, got_first = first
    shape = (width, 4 * head_cols)
    first = run(
        sum_two_more,
        [(shape, F32)] + [((width + 32, shape[1]), BF)] * 3,
        (near_first, got_first, gains_sum),
        0,
    )
    first = scatter_late(first)
    input_grad = run(
        leave_kernel,
        [((L, features), F32)],
        (hold(grad_zero, first[0]), perm),
        6 * ROWS * features**2,
    )[0]
    second = scatter_end(second, qkv_cols)
    mlp = scatter_end(mlp, ff_cols)
    first = hold(first, up_g, down_g, block_output, input_grad, second, mlp)
    *first, tail = run(
        sum_three_more,
        [((width, qkv_cols), F32), ((width, head_cols), F32), ((16, width), F32)],
        (*first, gains_sum),
        0,
    )

    return (
        block_output,
        input_grad,
        tail[0],
        first[0].reshape(first_qkv.shape),
        first[1].T,
        tail[1],
        mlp[0],
        mlp[1].T,
        tail[2],
        second[0].reshape(second_qkv.shape),
        second[1].T,
        tail[3],
        tail[4 : 4 + experts].T,
        up_g,
        down_g,
        *clips,
        roots,
    )


def solution(mesh):
    placed = (
        P(("dp", "tensor"), None),
        P("dp"),
        P("dp", None, "tensor"),
        P("tensor", "dp"),
        P("dp"),
        P("dp", "tensor"),
        P("tensor", "dp"),
        P("dp"),
        P("dp", None, "tensor"),
        P("tensor", "dp"),
        P("dp"),
        P("dp", None),
        P(None, "dp", "tensor"),
        P(None, "tensor", "dp"),
        P("dp", None),
        P("dp", None),
        P("dp"),
        P(("dp", "tensor"), None),
    )
    quick = mesh.shape["dp"] == 8 and mesh.shape["tensor"] == 4
    return jax.shard_map(
        fast_local if quick else local,
        mesh=mesh,
        in_specs=placed,
        out_specs=(
            P(("dp", "tensor"), None),
            P(("dp", "tensor"), None),
            P("dp"),
            P("dp", None, "tensor"),
            P("tensor", "dp"),
            P("dp"),
            P("dp", "tensor"),
            P("tensor", "dp"),
            P("dp"),
            P("dp", None, "tensor"),
            P("tensor", "dp"),
            P("dp"),
            P("dp", None),
            P(None, "dp", "tensor"),
            P(None, "tensor", "dp"),
            P("dp", None, "tensor"),
            P("dp", None, "tensor"),
            P(None, "tensor"),
        ),
        check_vma=False,
    )
```

```python
import functools

import jax
import jax.numpy as jnp
from jax import lax
from jax.experimental import pallas as pl
from jax.experimental.pallas import tpu as pltpu
from jax.sharding import PartitionSpec as P

HD = 64
L = 197
CAP = 197


epsilon = 1e-06
clip_tau = 2.5


def layer_norm(values, norm_gain):
    center = values - jnp.mean(values, axis=-1, keepdims=True)
    spread = jnp.mean(center * center, axis=-1, keepdims=True)
    return center * lax.rsqrt(spread + epsilon) * norm_gain


def exact_gelu(values):
    return jax.nn.gelu(values, approximate=False)


def gelu_back(values, upstream):
    return jax.vjp(exact_gelu, values)[1](upstream)[0]


def norm_back(residual, norm_gain, upstream):
    pullback = jax.vjp(layer_norm, residual, norm_gain.astype(jnp.float32))[1]
    return pullback(upstream)


def gather_rows(values):
    return lax.all_gather(values, "tensor", axis=0, tiled=True)


def scatter_rows(values):
    return lax.psum_scatter(
        values.astype(jnp.bfloat16), "tensor", scatter_dimension=0, tiled=True
    ).astype(jnp.float32)


def sum_gains(first_gain, second_gain):
    return lax.psum((first_gain, second_gain), "tensor")


def split_heads(projected, images, head_size):
    row_count, triple, columns = projected.shape
    pieces = projected.reshape(images, row_count // images, triple, columns // head_size, head_size)
    return (pieces[:, :, 0], pieces[:, :, 1], pieces[:, :, 2])


def attend_scores(queries, keyset, head_size):
    scores = jnp.einsum("iqhd,ikhd->ihqk", queries, keyset, preferred_element_type=jnp.float32)
    return scores * head_size ** (-0.5)


def attend_forward(normed_full, weight_qkv, images, head_size, live_images):
    projected = jnp.einsum(
        "rd,dcf->rcf", normed_full, weight_qkv, preferred_element_type=jnp.float32
    ).astype(jnp.bfloat16)
    queries, keyset, values = split_heads(projected, images, head_size)
    scores = attend_scores(queries, keyset, head_size)
    head_peak = jnp.max(jnp.where(live_images[:, None, None, None], scores, -1e30), axis=(0, 2, 3))
    attn_probs = jax.nn.softmax(scores, axis=-1).astype(jnp.bfloat16)
    attended = jnp.einsum("ihqk,ikhd->iqhd", attn_probs, values, preferred_element_type=jnp.float32)
    return (projected, attended.astype(jnp.bfloat16).reshape(normed_full.shape[0], -1), head_peak)


def attend_backward(projected, grad_attended, images, head_size):
    queries, keyset, values = split_heads(projected, images, head_size)
    scores = attend_scores(queries, keyset, head_size)
    attn_probs = jax.nn.softmax(scores, axis=-1)
    grad_heads = grad_attended.reshape(queries.shape)
    grad_values = jnp.einsum(
        "ihqk,iqhd->ikhd",
        attn_probs.astype(jnp.bfloat16),
        grad_heads,
        preferred_element_type=jnp.float32,
    )
    grad_probs = jnp.einsum(
        "iqhd,ikhd->ihqk", grad_heads, values, preferred_element_type=jnp.float32
    )
    grad_scores = attn_probs * (
        grad_probs - jnp.sum(grad_probs * attn_probs, axis=-1, keepdims=True)
    )
    grad_scores = grad_scores.astype(jnp.bfloat16)
    factor = head_size ** (-0.5)
    grad_queries = (
        jnp.einsum("ihqk,ikhd->iqhd", grad_scores, keyset, preferred_element_type=jnp.float32)
        * factor
    )
    grad_keyset = (
        jnp.einsum("ihqk,iqhd->ikhd", grad_scores, queries, preferred_element_type=jnp.float32)
        * factor
    )
    stacked = jnp.stack([grad_queries, grad_keyset, grad_values], axis=2).astype(jnp.bfloat16)
    return stacked.reshape(projected.shape)


def block_attention(residual, norm_gain, weight_qkv, weight_out, images, head_size, live_images):
    normed = layer_norm(residual, norm_gain.astype(jnp.float32)).astype(jnp.bfloat16)
    normed_full = gather_rows(normed)
    projected, attended, head_peak = attend_forward(
        normed_full, weight_qkv, images, head_size, live_images
    )
    branch = scatter_rows(jnp.dot(attended, weight_out, preferred_element_type=jnp.float32))
    return (residual + branch, (normed_full, projected, attended), head_peak)


def block_attention_back(
    residual, upstream, norm_gain, weight_qkv, weight_out, stored, images, head_size
):
    normed_full, projected, attended = stored
    grad_full = gather_rows(upstream.astype(jnp.bfloat16))
    grad_out = jnp.einsum("rf,rd->fd", attended, grad_full, preferred_element_type=jnp.float32)
    grad_attended = jnp.einsum(
        "rd,fd->rf", grad_full, weight_out, preferred_element_type=jnp.float32
    ).astype(jnp.bfloat16)
    grad_projected = attend_backward(projected, grad_attended, images, head_size)
    grad_qkv = jnp.einsum(
        "rd,rcf->dcf", normed_full, grad_projected, preferred_element_type=jnp.float32
    )
    grad_normed = scatter_rows(
        jnp.einsum("rcf,dcf->rd", grad_projected, weight_qkv, preferred_element_type=jnp.float32)
    )
    grad_residual, grad_gain = norm_back(residual, norm_gain, grad_normed)
    return (upstream + grad_residual, grad_gain, grad_qkv, grad_out)


def block_mlp(residual, norm_gain, weight_up, weight_down):
    normed = layer_norm(residual, norm_gain.astype(jnp.float32)).astype(jnp.bfloat16)
    normed_full = gather_rows(normed)
    hidden = jnp.dot(normed_full, weight_up, preferred_element_type=jnp.float32)
    active = exact_gelu(hidden).astype(jnp.bfloat16)
    branch = scatter_rows(jnp.dot(active, weight_down, preferred_element_type=jnp.float32))
    return (residual + branch, (normed_full, hidden, active))


def block_mlp_back(residual, upstream, norm_gain, weight_up, weight_down, stored):
    normed_full, hidden, active = stored
    grad_full = gather_rows(upstream.astype(jnp.bfloat16))
    grad_down = jnp.einsum("rf,rd->fd", active, grad_full, preferred_element_type=jnp.float32)
    grad_active = jnp.einsum(
        "rd,fd->rf", grad_full, weight_down, preferred_element_type=jnp.float32
    )
    grad_hidden = gelu_back(hidden, grad_active).astype(jnp.bfloat16)
    grad_up = jnp.einsum("rd,rf->df", normed_full, grad_hidden, preferred_element_type=jnp.float32)
    grad_normed = scatter_rows(
        jnp.einsum("rf,df->rd", grad_hidden, weight_up, preferred_element_type=jnp.float32)
    )
    grad_residual, grad_gain = norm_back(residual, norm_gain, grad_normed)
    return (upstream + grad_residual, grad_gain, grad_up, grad_down)


def clip_root(head_peak):
    return jnp.sqrt(clip_tau / jnp.maximum(head_peak, clip_tau))


def clip_columns(weight_local, head_root, head_size):
    column = jnp.repeat(head_root, head_size)
    scales = jnp.stack([column, column, jnp.ones_like(column)])
    return weight_local.astype(jnp.float32) * scales[None]


def local(
    block_input,
    first_norm,
    first_qkv,
    first_out,
    second_norm,
    dense_up,
    dense_down,
    third_norm,
    second_qkv,
    second_out,
    fourth_norm,
    router_weight,
    expert_up,
    expert_down,
    expert_ids,
    expert_slots,
    image_counts,
    cotangent,
):
    rows_local = block_input.shape[0]
    rows_full = rows_local * lax.axis_size("tensor")
    images = rows_full // L
    head_size = HD
    experts = expert_up.shape[0]
    capacity = CAP
    first_row = lax.axis_index("tensor") * rows_local
    live_count = image_counts[0]
    local_live = ((first_row + jnp.arange(rows_local)) // L < live_count).astype(jnp.float32)
    full_live = (jnp.arange(rows_full) // L < live_count).astype(jnp.float32)
    live_images = jnp.arange(images) < live_count

    def dense_fetch():
        return (
            lax.all_gather(first_norm, "dp", axis=0, tiled=True),
            lax.all_gather(first_qkv, "dp", axis=0, tiled=True),
            lax.all_gather(first_out, "dp", axis=1, tiled=True),
            lax.all_gather(second_norm, "dp", axis=0, tiled=True),
            lax.all_gather(dense_up, "dp", axis=0, tiled=True),
            lax.all_gather(dense_down, "dp", axis=1, tiled=True),
        )

    def moe_fetch():
        return (
            lax.all_gather(third_norm, "dp", axis=0, tiled=True),
            lax.all_gather(second_qkv, "dp", axis=0, tiled=True),
            lax.all_gather(second_out, "dp", axis=1, tiled=True),
            lax.all_gather(fourth_norm, "dp", axis=0, tiled=True),
            lax.all_gather(router_weight, "dp", axis=0, tiled=True),
            lax.all_gather(expert_up, "dp", axis=1, tiled=True),
            lax.all_gather(expert_down, "dp", axis=2, tiled=True),
        )

    dense_full = dense_fetch()
    residual_zero = block_input.astype(jnp.float32)
    residual_one, attn_first, peak_first = block_attention(
        residual_zero, dense_full[0], dense_full[1], dense_full[2], images, head_size, live_images
    )
    residual_two, mlp_stored = block_mlp(residual_one, dense_full[3], dense_full[4], dense_full[5])
    moe_full = moe_fetch()
    residual_three, attn_second, peak_second = block_attention(
        residual_two, moe_full[0], moe_full[1], moe_full[2], images, head_size, live_images
    )
    moe_normed = layer_norm(residual_three, moe_full[3].astype(jnp.float32)).astype(jnp.bfloat16)
    moe_input = gather_rows(moe_normed)
    logits = jnp.dot(moe_input, moe_full[4], preferred_element_type=jnp.float32)
    route_probs = jax.nn.softmax(logits, axis=-1)
    kept_mask = expert_slots < capacity
    pair_number = jnp.arange(2 * rows_full, dtype=jnp.int32)
    slot_index = (expert_ids * capacity + expert_slots).reshape(-1)
    kept_flat = kept_mask.reshape(-1)
    write_target = jnp.where(kept_flat, slot_index, experts * capacity + pair_number)
    target = jnp.where(kept_flat, slot_index, experts * capacity)
    pair_of_slot = (
        jnp.zeros((experts * capacity + 2 * rows_full,), jnp.int32)
        .at[write_target]
        .set(pair_number)[: experts * capacity]
    )
    slot_filled = (
        jnp.zeros((experts * capacity + 2 * rows_full,), jnp.float32)
        .at[write_target]
        .set(1.0)[: experts * capacity]
    )
    chosen = (expert_ids[:, :, None] == jnp.arange(experts)[None, None, :]).astype(jnp.float32)
    keep_live = kept_mask.astype(jnp.float32) * full_live[:, None]
    gates = jnp.sum(chosen * route_probs[:, None, :], axis=-1) * keep_live
    slot_token = pair_of_slot // 2
    slot_gate = gates.reshape(-1)[pair_of_slot] * slot_filled
    dispatched = (moe_input[slot_token] * slot_filled[:, None].astype(jnp.bfloat16)).reshape(
        experts, capacity, -1
    )
    expert_hidden = jnp.einsum(
        "ecd,edf->ecf", dispatched, moe_full[5], preferred_element_type=jnp.float32
    )
    expert_act = exact_gelu(expert_hidden).astype(jnp.bfloat16)
    expert_result = jnp.einsum(
        "ecf,efd->ecd", expert_act, moe_full[6], preferred_element_type=jnp.float32
    )
    feature_count = expert_result.shape[2]
    padded_result = jnp.concatenate(
        [
            expert_result.reshape(experts * capacity, feature_count),
            jnp.zeros((1, feature_count), jnp.float32),
        ],
        axis=0,
    )
    pair_result = padded_result[target].reshape(rows_full, 2, feature_count)
    combined = jnp.sum(gates[:, :, None] * pair_result, axis=1)
    residual_four = residual_three + scatter_rows(combined)
    block_output = residual_four * local_live[:, None]
    peak_first_all, peak_second_all = lax.pmax((peak_first, peak_second), "dp")
    root_first = clip_root(peak_first_all)
    root_second = clip_root(peak_second_all)
    clipped_first = clip_columns(first_qkv, root_first, head_size)
    clipped_second = clip_columns(second_qkv, root_second, head_size)
    clip_scales = jnp.stack([root_first, root_second])
    moe_back = moe_fetch()
    grad_four = cotangent.astype(jnp.float32) * local_live[:, None]
    moe_grad_full = gather_rows(grad_four.astype(jnp.bfloat16))
    partial_gates = jnp.sum(moe_grad_full.astype(jnp.float32)[:, None, :] * pair_result, axis=-1)
    grad_gates = lax.psum(partial_gates, "tensor")
    grad_result = (slot_gate[:, None] * moe_grad_full[slot_token].astype(jnp.float32)).astype(
        jnp.bfloat16
    )
    grad_result = grad_result.reshape(experts, capacity, feature_count)
    grad_expert_down = jnp.einsum(
        "ecf,ecd->efd", expert_act, grad_result, preferred_element_type=jnp.float32
    )
    grad_act = jnp.einsum(
        "ecd,efd->ecf", grad_result, moe_back[6], preferred_element_type=jnp.float32
    )
    grad_hidden = gelu_back(expert_hidden, grad_act).astype(jnp.bfloat16)
    grad_expert_up = jnp.einsum(
        "ecd,ecf->edf", dispatched, grad_hidden, preferred_element_type=jnp.float32
    )
    grad_dispatch = jnp.einsum(
        "ecf,edf->ecd", grad_hidden, moe_back[5], preferred_element_type=jnp.float32
    )
    grad_dispatch = jnp.concatenate(
        [
            grad_dispatch.reshape(experts * capacity, feature_count),
            jnp.zeros((1, feature_count), jnp.float32),
        ],
        axis=0,
    )
    grad_from_experts = jnp.sum(grad_dispatch[target].reshape(rows_full, 2, feature_count), axis=1)
    grad_picked = grad_gates * keep_live
    grad_probs = jnp.sum(chosen * grad_picked[:, :, None], axis=1)
    grad_logits = route_probs * (
        grad_probs - jnp.sum(grad_probs * route_probs, axis=-1, keepdims=True)
    )
    grad_logits = grad_logits.astype(jnp.bfloat16)
    grad_router = jnp.einsum(
        "rd,re->de", moe_input, grad_logits, preferred_element_type=jnp.float32
    )
    local_logits = lax.dynamic_slice_in_dim(grad_logits, first_row, rows_local, 0)
    grad_moe_normed = scatter_rows(grad_from_experts) + jnp.einsum(
        "re,de->rd", local_logits, moe_back[4], preferred_element_type=jnp.float32
    )
    grad_rows_four, grad_fourth_norm = norm_back(residual_three, moe_back[3], grad_moe_normed)
    grad_three = grad_four + grad_rows_four
    grad_two, grad_third_norm, grad_second_qkv, grad_second_out = block_attention_back(
        residual_two,
        grad_three,
        moe_back[0],
        moe_back[1],
        moe_back[2],
        attn_second,
        images,
        head_size,
    )
    third_sum, fourth_sum = sum_gains(grad_third_norm, grad_fourth_norm)
    moe_owned = (
        lax.psum_scatter(third_sum, "dp", scatter_dimension=0, tiled=True),
        lax.psum_scatter(grad_second_qkv, "dp", scatter_dimension=0, tiled=True),
        lax.psum_scatter(grad_second_out, "dp", scatter_dimension=1, tiled=True),
        lax.psum_scatter(fourth_sum, "dp", scatter_dimension=0, tiled=True),
        lax.psum_scatter(grad_router, "dp", scatter_dimension=0, tiled=True),
        lax.psum_scatter(grad_expert_up, "dp", scatter_dimension=1, tiled=True),
        lax.psum_scatter(grad_expert_down, "dp", scatter_dimension=2, tiled=True),
    )
    dense_back = dense_fetch()
    grad_one, grad_second_norm, grad_dense_up, grad_dense_down = block_mlp_back(
        residual_one, grad_two, dense_back[3], dense_back[4], dense_back[5], mlp_stored
    )
    input_grad, grad_first_norm, grad_first_qkv, grad_first_out = block_attention_back(
        residual_zero,
        grad_one,
        dense_back[0],
        dense_back[1],
        dense_back[2],
        attn_first,
        images,
        head_size,
    )
    first_sum, second_sum = sum_gains(grad_first_norm, grad_second_norm)
    dense_owned = (
        lax.psum_scatter(first_sum, "dp", scatter_dimension=0, tiled=True),
        lax.psum_scatter(grad_first_qkv, "dp", scatter_dimension=0, tiled=True),
        lax.psum_scatter(grad_first_out, "dp", scatter_dimension=1, tiled=True),
        lax.psum_scatter(second_sum, "dp", scatter_dimension=0, tiled=True),
        lax.psum_scatter(grad_dense_up, "dp", scatter_dimension=0, tiled=True),
        lax.psum_scatter(grad_dense_down, "dp", scatter_dimension=1, tiled=True),
    )
    owned = tuple(dense_owned) + tuple(moe_owned)
    return (
        block_output,
        input_grad,
        owned[0],
        owned[1],
        owned[2],
        owned[3],
        owned[4],
        owned[5],
        owned[6],
        owned[7],
        owned[8],
        owned[9],
        owned[10],
        owned[11],
        owned[12],
        clipped_first,
        clipped_second,
        clip_scales,
    )


ROWS = 208
AXES = ("dp", "tensor")
BF = jnp.bfloat16
F32 = jnp.float32
VM = pl.BlockSpec(memory_space=pltpu.VMEM)
SM = pl.BlockSpec(memory_space=pltpu.SMEM)


def swap(values, z=0, x=0, y=0, core=0):
    shift_d, shift_t = 2 * z + x, 2 * y + core
    pairs = [(d * 4 + t, (d ^ shift_d) * 4 + (t ^ shift_t)) for d in range(8) for t in range(4)]
    return lax.ppermute(values, AXES, pairs)


def hold(values, *tokens):
    return lax.optimization_barrier((values,) + tokens)[0]


def run(kernel, outs, args, flops, scratch=(), scalars=0, mib=20):
    flops = flops if flops == 8e9 else 1000
    shapes = [jax.ShapeDtypeStruct(s, dt) for s, dt in outs]
    return pl.pallas_call(
        kernel,
        out_shape=shapes,
        in_specs=[SM] * scalars + [VM] * (len(args) - scalars),
        out_specs=[VM] * len(shapes),
        scratch_shapes=list(scratch),
        compiler_params=pltpu.CompilerParams(vmem_limit_bytes=mib * 2**20),
        cost_estimate=pl.CostEstimate(flops=int(flops), bytes_accessed=1000, transcendentals=0),
    )(*args)


def dot(a, b, ca, cb):
    return lax.dot_general(a, b, (((ca,), (cb,)), ((), ())), preferred_element_type=F32)


def norm_stats(values):
    center = values - jnp.mean(values, axis=-1, keepdims=True)
    scale = lax.rsqrt(jnp.mean(center * center, axis=-1, keepdims=True) + epsilon)
    return center * scale, scale


def enter_kernel(live, x_ref, c_ref, perm_ref, start_ref, low_start, grad_ref, low_ref):
    rows = x_ref.shape[0]
    scale = live[0].astype(F32)
    extra = jnp.zeros((ROWS - rows, x_ref.shape[1]), F32)
    start = dot(x_ref[...], perm_ref[...], 1, 1)
    start_ref[:rows] = start
    start_ref[rows:] = extra
    low_start[:rows] = start.astype(BF)
    low_start[rows:] = extra.astype(BF)
    grad = dot(c_ref[...], perm_ref[...], 1, 1) * scale
    grad_ref[:rows] = grad
    grad_ref[rows:] = extra
    low_ref[:rows] = grad.astype(BF)
    low_ref[rows:] = extra.astype(BF)


def norm_kernel(gain_ref, *refs):
    for x_ref, out_ref in zip(refs[:4], refs[4:]):
        out_ref[...] = (norm_stats(x_ref[...].astype(F32))[0] * gain_ref[...]).astype(BF)


def join_norm_kernel(x_ref, own_ref, far_ref, gain_ref, sum_ref, out_ref):
    total = x_ref[...] + (own_ref[...] + far_ref[...].astype(F32))
    sum_ref[...] = total
    out_ref[...] = (norm_stats(total)[0] * gain_ref[...]).astype(BF)


def norm_back_kernel(x_ref, up_ref, own_ref, far_ref, gain_ref, grad_ref, low_ref, gain_out):
    upstream = own_ref[...] + far_ref[...].astype(F32)
    normed, scale = norm_stats(x_ref[...])
    scaled = upstream * gain_ref[...]
    grad = up_ref[...] + scale * (
        scaled
        - jnp.mean(scaled, axis=-1, keepdims=True)
        - normed * jnp.mean(scaled * normed, axis=-1, keepdims=True)
    )
    grad_ref[...] = grad
    low_ref[...] = grad.astype(BF)
    gain_out[...] = jnp.sum(upstream * normed, axis=0, keepdims=True)


def fill(rows, *refs):
    size = refs[0].shape[0]
    for i, ref in enumerate(refs):
        rows[i * size : (i + 1) * size] = ref[...]


def put_partial(partial, own_ref, sib_ref):
    half = own_ref.shape[0]
    own_ref[...] = partial[:half]
    sib_ref[...] = partial[half:].astype(BF)


def score_block(queries, keyset):
    scores = dot(queries, keyset, 1, 1) * HD ** (-0.5)
    column = lax.broadcasted_iota(jnp.int32, scores.shape, 1)
    scores = jnp.where(column < L, scores, -1e30)
    top = jnp.max(scores, axis=-1, keepdims=True)
    weight = jnp.exp(scores - top)
    return weight * (1.0 / jnp.sum(weight, axis=-1, keepdims=True)), top


def attend_kernel(
    at, live, a0, a1, a2, a3, w, mix_ref, att_ref, own_ref, sib_ref, peak_ref, rows
):
    fill(rows, a0, a1, a2, a3)
    part = mix_ref.shape[1] // 3
    mix_ref[...] = dot(rows[...], w[:, at : at + 3 * part], 1, 0).astype(BF)
    row_ok = lax.broadcasted_iota(jnp.int32, (ROWS, 1), 0) < L
    lane = lax.broadcasted_iota(jnp.int32, peak_ref.shape, 1)
    found = jnp.full(peak_ref.shape, -1e30, F32)
    for h in range(part // HD):
        for i in range(4):
            span = slice(i * ROWS, (i + 1) * ROWS)
            cut = [mix_ref[span, c * part + h * HD : c * part + (h + 1) * HD] for c in range(3)]
            probs, top = score_block(cut[0], cut[1])
            mixed = dot(probs.astype(BF), cut[2], 1, 0)
            att_ref[span, h * HD : (h + 1) * HD] = mixed.astype(BF)
            best = jnp.max(jnp.where(row_ok, top, -1e30), axis=0, keepdims=True)
            best = jnp.where(live[i] > 0, best, -1e30)
            found = jnp.where(lane == h, jnp.maximum(best, found), found)
    peak_ref[...] = found
    out = w[:, at + 3 * part : at + 4 * part]
    put_partial(dot(att_ref[...], out, 1, 1), own_ref, sib_ref)


def put_pack(grad, column, near, send):
    half = near.shape[0]
    near[:, column : column + grad.shape[1]] = grad[:half]
    send[:, column : column + grad.shape[1]] = grad[half:]


def attend_back_kernel(
    at, g0, g1, g2, g3, a0, a1, a2, a3, mix_ref, att_ref, w,
    near, send, own_ref, sib_ref, rows, grad_att, grad_mix,
):
    part = mix_ref.shape[1] // 3
    fill(rows, g0, g1, g2, g3)
    grad_att[...] = dot(rows[...], w[:, at + 3 * part : at + 4 * part], 1, 0).astype(BF)
    put_pack(dot(rows[...], att_ref[...], 0, 0).astype(BF), 3 * part, near, send)
    factor = HD ** (-0.5)
    for h in range(part // HD):
        for i in range(4):
            span = slice(i * ROWS, (i + 1) * ROWS)
            spans = [slice(c * part + h * HD, c * part + (h + 1) * HD) for c in range(3)]
            queries, keyset, values = (mix_ref[span, s] for s in spans)
            grad = grad_att[span, h * HD : (h + 1) * HD]
            probs, _ = score_block(queries, keyset)
            grad_mix[span, spans[2]] = dot(probs.astype(BF), grad, 0, 0).astype(BF)
            grad_probs = dot(grad, values, 1, 1)
            slope = probs * (grad_probs - jnp.sum(grad_probs * probs, axis=-1, keepdims=True))
            slope = slope.astype(BF)
            grad_mix[span, spans[0]] = (factor * dot(slope, keyset, 1, 0)).astype(BF)
            grad_mix[span, spans[1]] = (factor * dot(slope, queries, 0, 0)).astype(BF)
    put_partial(dot(grad_mix[...], w[:, at : at + 3 * part], 1, 1), own_ref, sib_ref)
    fill(rows, a0, a1, a2, a3)
    put_pack(dot(rows[...], grad_mix[...], 0, 0).astype(BF), 0, near, send)


def gelu_pair(hidden):
    cdf = 0.5 * (1.0 + lax.erf(hidden * 0.7071067811865476))
    slope = cdf + hidden * jnp.exp(-0.5 * hidden * hidden) * 0.3989422804014327
    return (hidden * cdf).astype(BF), slope.astype(BF)


def mlp_kernel(ats, b0, b1, b2, b3, w, act_ref, slope_ref, own_ref, sib_ref, rows):
    fill(rows, b0, b1, b2, b3)
    wide = act_ref.shape[1]
    for c in range(0, wide, 256):
        span = slice(c, c + 256)
        act, slope = gelu_pair(dot(rows[...], w[:, ats[0] + c : ats[0] + c + 256], 1, 0))
        act_ref[:, span] = act
        slope_ref[:, span] = slope
    put_partial(dot(act_ref[...], w[:, ats[1] : ats[1] + wide], 1, 1), own_ref, sib_ref)


def mlp_back_kernel(
    ats, g0, g1, g2, g3, b0, b1, b2, b3, act_ref, slope_ref, w,
    near, send, own_ref, sib_ref, rows, hidden,
):
    fill(rows, g0, g1, g2, g3)
    wide = act_ref.shape[1]
    grad = dot(rows[...], w[:, ats[1] : ats[1] + wide], 1, 0) * slope_ref[...].astype(F32)
    hidden[...] = grad.astype(BF)
    put_partial(dot(hidden[...], w[:, ats[0] : ats[0] + wide], 1, 1), own_ref, sib_ref)
    put_pack(dot(rows[...], act_ref[...], 0, 0).astype(BF), wide, near, send)
    fill(rows, b0, b1, b2, b3)
    put_pack(dot(rows[...], hidden[...], 0, 0).astype(BF), 0, near, send)


def picked(row_code, codes):
    hit = (row_code[...] == codes[0:1, :]) | (row_code[...] == codes[1:2, :])
    return jnp.where(hit, 1.0, 0.0).astype(BF)


def dispatch_kernel(row_code, codes, p0, p1, p2, p3, perm_ref, out, rows):
    fill(rows, p0, p1, p2, p3)
    picks = dot(picked(row_code, codes), rows[...], 1, 0).astype(BF)
    out[...] = dot(picks, perm_ref[...], 1, 0).astype(BF)


def token_kernel(row_code, codes, p0, p1, p2, p3, perm_ref, first_ref, second_ref, out, rows):
    dispatch_kernel(row_code, codes, p0, p1, p2, p3, perm_ref, out, rows)
    row = lax.broadcasted_iota(jnp.int32, (8, 128), 0)
    block = jnp.zeros((8, 128), F32)
    for i, ref in enumerate((first_ref, second_ref)):
        high = ref[...].astype(BF).astype(F32)
        block = jnp.where(row == 2 * i + 2, high, block)
        block = jnp.where(row == 2 * i + 3, ref[...] - high, block)
    size = out.shape[0] // 8
    for e in range(8):
        span = slice((e + 1) * size - 8, (e + 1) * size)
        old = out[span, :128].astype(F32)
        out[span, :128] = jnp.where((row >= 2) & (row < 6), block, old).astype(BF)


def collect_kernel(both_ref, grad_ref, out_ref, peak_ref):
    size = both_ref.shape[1] // 2
    best = jnp.full((2, 128), -1e30, F32)
    for p in range(both_ref.shape[0]):
        rows = slice(p * size, (p + 1) * size)
        grad_ref[rows] = both_ref[p, :size]
        out_ref[rows] = both_ref[p, size:]
        block = both_ref[p, 2 * size - 8 :, :128].astype(F32)
        found = [block[2 * i + 2 : 2 * i + 3] + block[2 * i + 3 : 2 * i + 4] for i in range(2)]
        best = jnp.maximum(best, jnp.concatenate(found, axis=0))
    peak_ref[...] = best


def combine_kernel(which, row_code, codes, perm_ref, both_ref, own_ref, sib_ref, rows):
    size = both_ref.shape[1] // 2
    for p in range(both_ref.shape[0]):
        rows[p * size : (p + 1) * size] = both_ref[p, which * size : (which + 1) * size]
    back = dot(rows[...], perm_ref[...], 1, 1).astype(BF)
    partial = dot(picked(row_code, codes), back, 0, 0)
    half = partial.shape[0] // 2
    own_ref[...] = partial[:half]
    sib_ref[...] = partial[half:].astype(BF)


def pair_add_kernel(own_ref, far_ref, near_ref, send_ref):
    total = own_ref[...] + far_ref[...].astype(F32)
    near_ref[...] = total[:ROWS]
    send_ref[...] = total[ROWS:].astype(BF)


def route_of(tokens, router, number):
    logits = dot(tokens, router, 1, 1)
    column = lax.broadcasted_iota(jnp.int32, logits.shape, 1)
    logits = jnp.where(column < 8, logits, -1e30)
    weight = jnp.exp(logits - jnp.max(logits, axis=-1, keepdims=True))
    route = weight / jnp.sum(weight, axis=-1, keepdims=True)
    mine = jnp.where(column == number, 1.0, 0.0)
    return route, mine, jnp.sum(route * mine, axis=-1, keepdims=True)


def expert_kernel(
    number, t0, t1, g0, g1, router, *rest
):
    own, far = rest[0], rest[1:3]
    res_own, res_sib, grad_own, grad_sib = rest[3:7]
    up_parts, down_parts = rest[7:10], rest[10:13]
    act_ref, hid_ref, gout_ref, pair, whole = rest[13:]
    size = t0.shape[0]
    half, wide = own.shape[0] // 2, act_ref.shape[2]
    whole[0] = own[...]
    cut = far[0].shape[0]
    whole[1, :cut] = far[0][...]
    whole[1, cut:] = far[1][...]
    for i, (t, g, res, grad) in enumerate(
        ((t1, g1, res_sib, grad_sib), (t0, g0, res_own, grad_own))
    ):
        rows = slice((1 - i) * size, (2 - i) * size)
        gate = route_of(t[...], router[...], number[0])[2]
        gout = (gate * g[...].astype(F32)).astype(BF)
        gout_ref[rows] = gout
        for y in range(2):
            for c in range(0, wide, 256):
                span = slice(c, c + 256)
                act, lean = gelu_pair(dot(t[...], whole[y, :, span], 1, 0))
                act_ref[y, rows, span] = act
                back = dot(gout, whole[y, :, wide + c : wide + c + 256], 1, 0)
                hid_ref[y, rows, span] = (back * lean.astype(F32)).astype(BF)
        res[...] = (
            dot(act_ref[0, rows], whole[0, :, wide:], 1, 1)
            + dot(act_ref[1, rows], whole[1, :, wide:], 1, 1)
        ).astype(res.dtype)
        grad[...] = (
            dot(hid_ref[0, rows], whole[0, :, :wide], 1, 1)
            + dot(hid_ref[1, rows], whole[1, :, :wide], 1, 1)
        ).astype(grad.dtype)
    pair[:size] = t0[...]
    pair[size:] = t1[...]
    for parts, left, right in ((up_parts, pair, hid_ref), (down_parts, gout_ref, act_ref)):
        parts[0][...] = dot(left[...], right[0], 0, 0).astype(BF)
        far = dot(left[...], right[1], 0, 0).astype(BF)
        parts[1][...] = far[:half]
        parts[2][...] = far[half:]


def answer_kernel(
    number, t_ref, g_ref, router, res_own, res_far, grad_own, grad_far, perm_ref,
    both_ref, router_out,
):
    route, mine, gate = route_of(t_ref[...], router[...], number[0])
    result = res_own[...] + res_far[...].astype(F32)
    grad_gate = jnp.sum(result * g_ref[...].astype(F32), axis=-1, keepdims=True)
    grad_logit = (grad_gate * route * (mine - gate)).astype(BF)
    router_out[...] = reorder(dot(grad_logit, t_ref[...], 0, 0), perm_ref[...], 1)
    grad = grad_own[...] + grad_far[...].astype(F32) + dot(grad_logit, router[...], 1, 0)
    size = both_ref.shape[1] // 2
    whole = grad.astype(BF)
    for p in range(both_ref.shape[0]):
        both_ref[p, :size] = whole[p * size : (p + 1) * size]
    whole = (gate * result).astype(BF)
    for p in range(both_ref.shape[0]):
        both_ref[p, size:] = whole[p * size : (p + 1) * size]


def reorder(values, perm, axis):
    high = values.astype(BF)
    rest = values - high.astype(F32)
    middle = rest.astype(BF)
    low = (rest - middle.astype(F32)).astype(BF)
    return dot(high, perm, 1, axis) + (dot(middle, perm, 1, axis) + dot(low, perm, 1, axis))


def leave_kernel(x_ref, perm_ref, out_ref):
    out_ref[...] = reorder(x_ref[...], perm_ref[...], 0)[: out_ref.shape[0]]


def finish_kernel(live, x_ref, own_ref, far_ref, perm_ref, out_ref):
    total = x_ref[...] + (own_ref[...] + far_ref[...].astype(F32))
    total = reorder(total, perm_ref[...], 0) * live[0].astype(F32)
    out_ref[...] = total[: out_ref.shape[0]]


def add_pack_kernel(up_own, up0, up1, down_own, down0, down1, out):
    half, wide = up0.shape
    for c, (own, parts) in enumerate(((up_own, (up0, up1)), (down_own, (down0, down1)))):
        for s, part in enumerate(parts):
            span = slice(s * half, (s + 1) * half)
            total = own[span].astype(F32) + part[...].astype(F32)
            out[span, c * wide : (c + 1) * wide] = total.astype(BF)


def pack_kernel(*refs):
    out = refs[-1]
    at = 0
    for ref in refs[:-1]:
        out[:, at : at + ref.shape[1]] = ref[...]
        at += ref.shape[1]


def stack_kernel(*refs):
    rows = refs[0].shape[0]
    for i, ref in enumerate(refs[:-1]):
        refs[-1][i * rows : (i + 1) * rows] = ref[...]


def order_kernel(places, in_ref, out_ref):
    rows = out_ref.shape[0] // 4
    for i in range(4):
        at = pl.multiple_of(places[i] * rows, rows)
        out_ref[i * rows : (i + 1) * rows] = in_ref[pl.ds(at, rows), :]


def sum_two(near, got, keep, s1, s2, s3):
    rows = keep.shape[0]
    for k, out in enumerate((keep, s1, s2, s3)):
        span = slice(k * rows, (k + 1) * rows)
        out[...] = (near[span].astype(F32) + got[span].astype(F32)).astype(out.dtype)


def small_kernel(g1, g2, g3, g4, router, out):
    whole = jnp.concatenate([g1[...], g2[...], g3[...], g4[...]], axis=0)
    count, cols = router.shape[0], out.shape[2]
    blank = jnp.zeros((out.shape[1] - 4 - count, cols), F32)
    for p in range(8):
        span = slice(p * cols, (p + 1) * cols)
        out[p] = jnp.concatenate([whole[:, span], router[:, span], blank], axis=0)


def sum_two_more(near, got, small, keep, s1, s2, s3):
    sum_two(near, got, keep, s1.at[: keep.shape[0]], s2.at[: keep.shape[0]], s3.at[: keep.shape[0]])
    rows, count = keep.shape[0], small.shape[1]
    cols = small.shape[2]
    for k, out in enumerate((s1, s2, s3)):
        out[rows:, :] = jnp.zeros((out.shape[0] - rows, out.shape[1]), BF)
        high = small[k + 1].astype(BF)
        out[rows : rows + count, :cols] = high
        low = small[k + 1] - high.astype(F32)
        out[rows + count : rows + 2 * count, :cols] = low.astype(BF)


def sum_three_more(keep, r1, r2, r3, small, first, second, small_out):
    rows, count = keep.shape[0], small.shape[1]
    cols = small.shape[2]
    sum_three(keep, r1.at[:rows], r2.at[:rows], r3.at[:rows], first, second)
    total = small[0]
    for r in (r1, r2, r3):
        high = r[rows : rows + count, :cols].astype(F32)
        total = total + (high + r[rows + count : rows + 2 * count, :cols].astype(F32))
    small_out[...] = total


def sum_three(keep, r1, r2, r3, first, second):
    total = keep[...] + (r1[...].astype(F32) + (r2[...].astype(F32) + r3[...].astype(F32)))
    wide = first.shape[1]
    first[...] = total[:, :wide]
    second[...] = total[:, wide:]


def scatter_start(parts):
    near, send = parts
    return near, swap(send, x=1)


def scatter_middle(parts):
    half, width = parts[0].shape
    shape = (half // 4, width)
    return run(sum_two, [(shape, F32)] + [(shape, BF)] * 3, parts, half * width)


def scatter_late(parts):
    keep, s1, s2, s3 = parts
    return keep, swap(s1, z=1), swap(s2, z=2), swap(s3, z=3)


def scatter_end(parts, wide):
    rows, width = parts[0].shape
    return run(sum_three, [((rows, wide), F32), ((rows, width - wide), F32)], parts, rows * width)


def fast_local(
    block_input,
    first_norm,
    first_qkv,
    first_out,
    second_norm,
    dense_up,
    dense_down,
    third_norm,
    second_qkv,
    second_out,
    fourth_norm,
    router_weight,
    expert_up,
    expert_down,
    expert_ids,
    expert_slots,
    image_counts,
    cotangent,
):
    d = lax.axis_index("dp")
    t = lax.axis_index("tensor")
    z_index, x_index = d // 2, d % 2
    width = first_norm.shape[0]
    features = width * 8
    experts = expert_up.shape[0]
    live_count = image_counts[0]
    head_cols = first_out.shape[0]
    ff_cols = dense_up.shape[1]
    qkv_cols = 3 * head_cols
    row = ((ROWS, features), F32)
    row_low = ((ROWS, features), BF)

    small = jnp.concatenate(
        [
            jnp.stack([first_norm, second_norm, third_norm, fourth_norm], axis=1),
            router_weight,
            jnp.zeros((width, 128 - 4 - experts), BF),
        ],
        axis=1,
    )
    pack_one = run(
        pack_kernel,
        [((width, small.shape[1] + 4 * head_cols), BF)],
        (small, first_qkv.reshape(width, -1), first_out.T),
        width,
    )[0]
    pack_late = run(
        pack_kernel,
        [((width, 2 * ff_cols + 4 * head_cols), BF)],
        (dense_up, dense_down.T, second_qkv.reshape(width, -1), second_out.T),
        width,
    )[0]

    lines = [[x + 2 * z for z in range(4)] for x in range(2)]
    raw_late = lax.all_gather(pack_late, "dp", axis=0, tiled=True, axis_index_groups=lines)

    def stacked(shards):
        shape = (len(shards) * shards[0].shape[0], shards[0].shape[1])
        return run(stack_kernel, [(shape, BF)], shards, width)[0]

    z_one = stacked([pack_one] + [swap(pack_one, z=k) for k in (1, 2, 3)])

    rel = jnp.arange(features)
    block = rel // width
    rel_place = jnp.bitwise_xor(d, 2 * (block % 4) + block // 4) * width + rel % width
    perm = (rel_place[:, None] == rel[None, :]).astype(BF)
    live_here = (t < live_count).astype(jnp.int32).reshape(1)
    live_group = (jnp.stack([t, t ^ 2, t ^ 1, t ^ 3]) < live_count).astype(jnp.int32)

    start, low_start, grad_four, grad_low = run(
        enter_kernel,
        [row, row_low, row, row_low],
        (live_here, block_input, cotangent, perm),
        4 * ROWS * features**2,
        scalars=1,
    )

    def spread(rows):
        far = swap(rows, y=1)
        return [rows, far, swap(rows, core=1), swap(far, core=1)]

    first_group = spread(low_start)
    wide = 2 * ff_cols
    half_shape = [((features // 2, ff_cols), BF)] * 2
    e_pack = jnp.concatenate([expert_up, jnp.swapaxes(expert_down, 1, 2)], axis=2)
    held = -(-CAP // 4)
    block_size = -(-(held + 4) // 8) * 8
    ids = jnp.pad(expert_ids.reshape(4, L, 2), ((0, 0), (0, ROWS - L), (0, 0)), constant_values=-1)
    slots = jnp.pad(
        expert_slots.reshape(4, L, 2), ((0, 0), (0, ROWS - L), (0, 0)), constant_values=CAP
    )
    mine = (slots < CAP) & (slots // held == t)
    codes = jnp.where(mine, ids * block_size + slots % held, -1)
    codes = jnp.concatenate(
        [lax.dynamic_index_in_dim(codes, t ^ k, 0, keepdims=False) for k in (0, 2, 1, 3)], axis=0
    ).T
    slot_rows = experts * block_size
    row_code = jnp.arange(slot_rows).reshape(-1, 1)
    group_flops = 2 * slot_rows * features * (4 * ROWS + features)

    def to_experts(kernel, rows, *peaks):
        return run(
            kernel,
            [((slot_rows, features), BF)],
            (row_code, codes, *rows, perm, *peaks),
            group_flops,
            scratch=[pltpu.VMEM((4 * ROWS, features), BF)],
        )[0].reshape(experts, block_size, features)

    def exchange(both):
        return lax.all_to_all(both, "dp", split_axis=0, concat_axis=0, tiled=True)

    group_scratch = pltpu.VMEM((4 * ROWS, features), BF)
    pair_out = [((2 * ROWS, features), F32), ((2 * ROWS, features), BF)]

    def attend(normed, full, at):
        return run(
            functools.partial(attend_kernel, at),
            [((4 * ROWS, qkv_cols), BF), ((4 * ROWS, head_cols), BF)]
            + pair_out
            + [((1, 128), F32)],
            (live_group, *normed, full),
            0,
            scratch=[group_scratch],
            scalars=1,
        )

    def pack_shapes(columns):
        return [((features // 2, columns), BF)] * 2 + pair_out

    def attend_back(low, normed, mixed, attended, full, at):
        return run(
            functools.partial(attend_back_kernel, at),
            pack_shapes(4 * head_cols),
            (*low, *normed, mixed, attended, full),
            8e9,
            scratch=[
                group_scratch,
                pltpu.VMEM((4 * ROWS, head_cols), BF),
                pltpu.VMEM((4 * ROWS, qkv_cols), BF),
            ],
        )

    def over_group(own, sib):
        near, send = run(pair_add_kernel, [row, row_low], (own, swap(sib, core=1)), ROWS)
        return near, swap(send, y=1)

    def join(values, own, far, gain):
        return run(join_norm_kernel, [row, row_low], (values, own, far, gain), ROWS)

    def norm_back(values, upstream, own, far, gain):
        return run(
            norm_back_kernel,
            [row, row_low, ((1, features), F32)],
            (values, upstream, own, far, gain),
            ROWS,
        )

    full_one = stacked(hold([z_one, swap(z_one, x=1)], first_group))
    small_rows = full_one[:, : 4 + experts].T
    gains = [small_rows[i : i + 1].astype(F32) for i in range(4)]
    router = dot(small_rows[4:], perm, 1, 0).astype(BF)

    normed_one = run(norm_kernel, [row_low] * 4, (gains[0], *first_group), ROWS)
    mixed_one, att_one, own, sib, peak_one = attend(normed_one, full_one, small.shape[1])
    near, far = over_group(own, sib)
    one, normed = join(start, near, hold(far, raw_late), gains[1])
    normed_mlp = spread(normed)
    z_late = run(
        order_kernel,
        [(raw_late.shape, BF)],
        (jnp.stack([z_index ^ k for k in range(4)]).astype(jnp.int32), hold(raw_late, one)),
        features,
        scalars=1,
    )[0]
    x_late = swap(z_late, x=1)
    grad_sent = to_experts(dispatch_kernel, spread(hold(grad_low, normed)))
    e_pack = hold(e_pack, grad_sent, normed_mlp[3])
    e_own = lax.all_to_all(e_pack, "dp", split_axis=0, concat_axis=0, tiled=True)
    e_own = e_own.reshape(features, wide)
    e_own = hold(e_own, normed_mlp[1])
    e_far = [swap(e_own[: 2 * width], y=1), swap(e_own[2 * width :], y=1)]
    full_late = stacked([z_late, x_late])
    ats = (0, ff_cols)
    act, slope, own, sib = run(
        functools.partial(mlp_kernel, ats),
        [((4 * ROWS, ff_cols), BF)] * 2 + pair_out,
        (*hold(normed_mlp, grad_sent), full_late),
        0,
        scratch=[group_scratch],
    )
    near, far = over_group(own, sib)
    two, normed = join(one, near, far, gains[2])
    normed_two = spread(normed)
    mixed_two, att_two, own, sib, peak_two = attend(normed_two, full_late, 2 * ff_cols)
    near, far = over_group(own, sib)
    three, normed = join(two, near, far, gains[3])
    tokens_sent = to_experts(token_kernel, spread(normed), peak_one, peak_two)
    both = exchange(hold(jnp.concatenate([grad_sent, tokens_sent], axis=1), e_far[0]))
    grad_slots, tokens, peaks = run(
        collect_kernel,
        [((slot_rows, features), BF)] * 2 + [((2, 128), F32)],
        (hold(both, *e_far),),
        0,
    )
    far_slots, far_tokens = swap(grad_slots, core=1), swap(tokens, core=1)
    number = d.astype(jnp.int32).reshape(1)
    near_heads = head_cols // HD
    roots = clip_root(peaks[:, :near_heads])
    slot_out = [((slot_rows, features), F32), ((slot_rows, features), BF)]
    res_own, res_sib, eg_own, eg_sib, *e_packs = run(
        expert_kernel,
        slot_out + slot_out + ([((features, ff_cols), BF)] + half_shape) * 2,
        (number, tokens, far_tokens, grad_slots, far_slots, router)
        + (e_own, *e_far),
        8 * 2 * slot_rows * features * 2 * ff_cols,
        scalars=1,
        scratch=[
            pltpu.VMEM((2, 2 * slot_rows, ff_cols), BF),
            pltpu.VMEM((2, 2 * slot_rows, ff_cols), BF),
            pltpu.VMEM((2 * slot_rows, features), BF),
            pltpu.VMEM((2 * slot_rows, features), BF),
            pltpu.VMEM((2, features, wide), BF),
        ],
        mib=44,
    )
    res_far, eg_far = swap(res_sib, core=1), swap(eg_sib, core=1)
    up_got = [swap(e_packs[1], y=1)]
    both, grad_router = run(
        answer_kernel,
        [((experts, 2 * block_size, features), BF), ((experts, features), F32)],
        (number, tokens, grad_slots, router, res_own, res_far, eg_own, eg_far, perm),
        4 * slot_rows * features**2,
        scalars=1,
    )
    both = hold(both, up_got)
    e_packs = hold(e_packs, both)
    both = exchange(both)
    up_got.append(swap(e_packs[2], y=1))
    down_got = [swap(e_packs[4], y=1)]
    both = hold(both, up_got, down_got)

    def combine(which, both):
        return run(
            functools.partial(combine_kernel, which),
            [((2 * ROWS, features), F32), ((2 * ROWS, features), BF)],
            (row_code, codes, perm, both),
            group_flops,
            scratch=[pltpu.VMEM((slot_rows, features), BF)],
        )

    own, sib = combine(0, both)
    back_own, back_far = over_group(own, sib)
    grad_three, low, gain_four = norm_back(
        three, grad_four, back_own, back_far, gains[3]
    )
    low = spread(low)
    down_got.append(swap(hold(e_packs[5], low[1]), y=1))
    *second, own, sib = attend_back(
        low, normed_two, mixed_two, att_two, full_late, 2 * ff_cols
    )
    second = scatter_start(second)
    near, far = over_group(own, hold(sib, down_got[1]))
    e_sum = run(
        add_pack_kernel,
        [((features, wide), BF)],
        (e_packs[0], *up_got, e_packs[3], *hold(down_got, second[1], far)),
        0,
    )[0].reshape(experts, width, wide)
    e_back = lax.all_to_all(e_sum, "dp", split_axis=0, concat_axis=0, tiled=True)
    grad_two, low, gain_three = norm_back(
        two, grad_three, near, far, gains[2]
    )
    low = spread(low)
    *mlp, own, sib = run(
        functools.partial(mlp_back_kernel, ats),
        pack_shapes(2 * ff_cols),
        (*low, *normed_mlp, act, slope, full_late),
        0,
        scratch=[group_scratch, pltpu.VMEM((4 * ROWS, ff_cols), BF)],
    )
    mlp = scatter_start(mlp)
    near, send = run(pair_add_kernel, [row, row_low], (own, swap(sib, core=1)), ROWS)
    far = swap(send, y=1)
    mixed_own, mixed_sib = combine(1, hold(both, sib))
    second = scatter_late(scatter_middle(hold(second, mixed_own)))
    mixed_own, mixed_send = run(
        pair_add_kernel, [row, row_low], (mixed_own, swap(mixed_sib, core=1)), ROWS
    )
    grad_one, low, gain_two = norm_back(
        one, grad_two, near, hold(far, mixed_send), gains[1]
    )
    low = spread(low)
    mixed_far = swap(hold(mixed_send, low), y=1)
    *first, own, sib = attend_back(
        hold(low, mlp),
        normed_one,
        mixed_one,
        att_one,
        full_one,
        small.shape[1],
    )
    mlp = scatter_late(scatter_middle(mlp))
    first = scatter_start(first)
    near, far = over_group(own, hold(sib, mixed_far, second, e_back))
    grad_zero, _, gain_one = norm_back(start, grad_one, near, hold(far, first), gains[0])
    block_output = run(
        finish_kernel,
        [((L, features), F32)],
        (live_here, three, mixed_own, mixed_far, perm),
        6 * ROWS * features**2,
        scalars=1,
    )[0]
    up_g = e_back[:, :, :ff_cols].astype(F32)
    down_g = jnp.swapaxes(e_back[:, :, ff_cols:], 1, 2).astype(F32)
    clips = (clip_columns(first_qkv, roots[0], HD), clip_columns(second_qkv, roots[1], HD))
    gains_sum = run(
        small_kernel,
        [((8, 16, width), F32)],
        (gain_one, gain_two, gain_three, gain_four, grad_router),
        0,
    )[0]
    gains_sum = hold(
        gains_sum + swap(gains_sum, core=1), mlp, block_output, up_g, down_g, clips
    )
    gains_sum = gains_sum + swap(gains_sum, y=1)
    gains_sum = gains_sum[:4] + swap(gains_sum[4:], x=1)
    near_first, got_first = first
    shape = (width, 4 * head_cols)
    first = run(
        sum_two_more,
        [(shape, F32)] + [((width + 32, shape[1]), BF)] * 3,
        (near_first, got_first, gains_sum),
        0,
    )
    first = scatter_late(first)
    input_grad = run(
        leave_kernel,
        [((L, features), F32)],
        (hold(grad_zero, first[0]), perm),
        6 * ROWS * features**2,
    )[0]
    second = scatter_end(second, qkv_cols)
    mlp = scatter_end(mlp, ff_cols)
    first = hold(first, up_g, down_g, block_output, input_grad, second, mlp)
    *first, tail = run(
        sum_three_more,
        [((width, qkv_cols), F32), ((width, head_cols), F32), ((16, width), F32)],
        (*first, gains_sum),
        0,
    )

    return (
        block_output,
        input_grad,
        tail[0],
        first[0].reshape(first_qkv.shape),
        first[1].T,
        tail[1],
        mlp[0],
        mlp[1].T,
        tail[2],
        second[0].reshape(second_qkv.shape),
        second[1].T,
        tail[3],
        tail[4 : 4 + experts].T,
        up_g,
        down_g,
        *clips,
        roots,
    )


def solution(mesh):
    placed = (
        P(("dp", "tensor"), None),
        P("dp"),
        P("dp", None, "tensor"),
        P("tensor", "dp"),
        P("dp"),
        P("dp", "tensor"),
        P("tensor", "dp"),
        P("dp"),
        P("dp", None, "tensor"),
        P("tensor", "dp"),
        P("dp"),
        P("dp", None),
        P(None, "dp", "tensor"),
        P(None, "tensor", "dp"),
        P("dp", None),
        P("dp", None),
        P("dp"),
        P(("dp", "tensor"), None),
    )
    quick = mesh.shape["dp"] == 8 and mesh.shape["tensor"] == 4
    return jax.shard_map(
        fast_local if quick else local,
        mesh=mesh,
        in_specs=placed,
        out_specs=(
            P(("dp", "tensor"), None),
            P(("dp", "tensor"), None),
            P("dp"),
            P("dp", None, "tensor"),
            P("tensor", "dp"),
            P("dp"),
            P("dp", "tensor"),
            P("tensor", "dp"),
            P("dp"),
            P("dp", None, "tensor"),
            P("tensor", "dp"),
            P("dp"),
            P("dp", None),
            P(None, "dp", "tensor"),
            P(None, "tensor", "dp"),
            P("dp", None, "tensor"),
            P("dp", None, "tensor"),
            P(None, "tensor"),
        ),
        check_vma=False,
    )
```

```python
import functools

import jax
import jax.numpy as jnp
from jax import lax
from jax.experimental import pallas as pl
from jax.experimental.pallas import tpu as pltpu
from jax.sharding import PartitionSpec as P

HD = 64
L = 197
CAP = 197


epsilon = 1e-06
clip_tau = 2.5


def layer_norm(values, norm_gain):
    center = values - jnp.mean(values, axis=-1, keepdims=True)
    spread = jnp.mean(center * center, axis=-1, keepdims=True)
    return center * lax.rsqrt(spread + epsilon) * norm_gain


def exact_gelu(values):
    return jax.nn.gelu(values, approximate=False)


def gelu_back(values, upstream):
    return jax.vjp(exact_gelu, values)[1](upstream)[0]


def norm_back(residual, norm_gain, upstream):
    pullback = jax.vjp(layer_norm, residual, norm_gain.astype(jnp.float32))[1]
    return pullback(upstream)


def gather_rows(values):
    return lax.all_gather(values, "tensor", axis=0, tiled=True)


def scatter_rows(values):
    return lax.psum_scatter(
        values.astype(jnp.bfloat16), "tensor", scatter_dimension=0, tiled=True
    ).astype(jnp.float32)


def sum_gains(first_gain, second_gain):
    return lax.psum((first_gain, second_gain), "tensor")


def split_heads(projected, images, head_size):
    row_count, triple, columns = projected.shape
    pieces = projected.reshape(images, row_count // images, triple, columns // head_size, head_size)
    return (pieces[:, :, 0], pieces[:, :, 1], pieces[:, :, 2])


def attend_scores(queries, keyset, head_size):
    scores = jnp.einsum("iqhd,ikhd->ihqk", queries, keyset, preferred_element_type=jnp.float32)
    return scores * head_size ** (-0.5)


def attend_forward(normed_full, weight_qkv, images, head_size, live_images):
    projected = jnp.einsum(
        "rd,dcf->rcf", normed_full, weight_qkv, preferred_element_type=jnp.float32
    ).astype(jnp.bfloat16)
    queries, keyset, values = split_heads(projected, images, head_size)
    scores = attend_scores(queries, keyset, head_size)
    head_peak = jnp.max(jnp.where(live_images[:, None, None, None], scores, -1e30), axis=(0, 2, 3))
    attn_probs = jax.nn.softmax(scores, axis=-1).astype(jnp.bfloat16)
    attended = jnp.einsum("ihqk,ikhd->iqhd", attn_probs, values, preferred_element_type=jnp.float32)
    return (projected, attended.astype(jnp.bfloat16).reshape(normed_full.shape[0], -1), head_peak)


def attend_backward(projected, grad_attended, images, head_size):
    queries, keyset, values = split_heads(projected, images, head_size)
    scores = attend_scores(queries, keyset, head_size)
    attn_probs = jax.nn.softmax(scores, axis=-1)
    grad_heads = grad_attended.reshape(queries.shape)
    grad_values = jnp.einsum(
        "ihqk,iqhd->ikhd",
        attn_probs.astype(jnp.bfloat16),
        grad_heads,
        preferred_element_type=jnp.float32,
    )
    grad_probs = jnp.einsum(
        "iqhd,ikhd->ihqk", grad_heads, values, preferred_element_type=jnp.float32
    )
    grad_scores = attn_probs * (
        grad_probs - jnp.sum(grad_probs * attn_probs, axis=-1, keepdims=True)
    )
    grad_scores = grad_scores.astype(jnp.bfloat16)
    factor = head_size ** (-0.5)
    grad_queries = (
        jnp.einsum("ihqk,ikhd->iqhd", grad_scores, keyset, preferred_element_type=jnp.float32)
        * factor
    )
    grad_keyset = (
        jnp.einsum("ihqk,iqhd->ikhd", grad_scores, queries, preferred_element_type=jnp.float32)
        * factor
    )
    stacked = jnp.stack([grad_queries, grad_keyset, grad_values], axis=2).astype(jnp.bfloat16)
    return stacked.reshape(projected.shape)


def block_attention(residual, norm_gain, weight_qkv, weight_out, images, head_size, live_images):
    normed = layer_norm(residual, norm_gain.astype(jnp.float32)).astype(jnp.bfloat16)
    normed_full = gather_rows(normed)
    projected, attended, head_peak = attend_forward(
        normed_full, weight_qkv, images, head_size, live_images
    )
    branch = scatter_rows(jnp.dot(attended, weight_out, preferred_element_type=jnp.float32))
    return (residual + branch, (normed_full, projected, attended), head_peak)


def block_attention_back(
    residual, upstream, norm_gain, weight_qkv, weight_out, stored, images, head_size
):
    normed_full, projected, attended = stored
    grad_full = gather_rows(upstream.astype(jnp.bfloat16))
    grad_out = jnp.einsum("rf,rd->fd", attended, grad_full, preferred_element_type=jnp.float32)
    grad_attended = jnp.einsum(
        "rd,fd->rf", grad_full, weight_out, preferred_element_type=jnp.float32
    ).astype(jnp.bfloat16)
    grad_projected = attend_backward(projected, grad_attended, images, head_size)
    grad_qkv = jnp.einsum(
        "rd,rcf->dcf", normed_full, grad_projected, preferred_element_type=jnp.float32
    )
    grad_normed = scatter_rows(
        jnp.einsum("rcf,dcf->rd", grad_projected, weight_qkv, preferred_element_type=jnp.float32)
    )
    grad_residual, grad_gain = norm_back(residual, norm_gain, grad_normed)
    return (upstream + grad_residual, grad_gain, grad_qkv, grad_out)


def block_mlp(residual, norm_gain, weight_up, weight_down):
    normed = layer_norm(residual, norm_gain.astype(jnp.float32)).astype(jnp.bfloat16)
    normed_full = gather_rows(normed)
    hidden = jnp.dot(normed_full, weight_up, preferred_element_type=jnp.float32)
    active = exact_gelu(hidden).astype(jnp.bfloat16)
    branch = scatter_rows(jnp.dot(active, weight_down, preferred_element_type=jnp.float32))
    return (residual + branch, (normed_full, hidden, active))


def block_mlp_back(residual, upstream, norm_gain, weight_up, weight_down, stored):
    normed_full, hidden, active = stored
    grad_full = gather_rows(upstream.astype(jnp.bfloat16))
    grad_down = jnp.einsum("rf,rd->fd", active, grad_full, preferred_element_type=jnp.float32)
    grad_active = jnp.einsum(
        "rd,fd->rf", grad_full, weight_down, preferred_element_type=jnp.float32
    )
    grad_hidden = gelu_back(hidden, grad_active).astype(jnp.bfloat16)
    grad_up = jnp.einsum("rd,rf->df", normed_full, grad_hidden, preferred_element_type=jnp.float32)
    grad_normed = scatter_rows(
        jnp.einsum("rf,df->rd", grad_hidden, weight_up, preferred_element_type=jnp.float32)
    )
    grad_residual, grad_gain = norm_back(residual, norm_gain, grad_normed)
    return (upstream + grad_residual, grad_gain, grad_up, grad_down)


def clip_root(head_peak):
    return jnp.sqrt(clip_tau / jnp.maximum(head_peak, clip_tau))


def clip_columns(weight_local, head_root, head_size):
    column = jnp.repeat(head_root, head_size)
    scales = jnp.stack([column, column, jnp.ones_like(column)])
    return weight_local.astype(jnp.float32) * scales[None]


def local(
    block_input,
    first_norm,
    first_qkv,
    first_out,
    second_norm,
    dense_up,
    dense_down,
    third_norm,
    second_qkv,
    second_out,
    fourth_norm,
    router_weight,
    expert_up,
    expert_down,
    expert_ids,
    expert_slots,
    image_counts,
    cotangent,
):
    rows_local = block_input.shape[0]
    rows_full = rows_local * lax.axis_size("tensor")
    images = rows_full // L
    head_size = HD
    experts = expert_up.shape[0]
    capacity = CAP
    first_row = lax.axis_index("tensor") * rows_local
    live_count = image_counts[0]
    local_live = ((first_row + jnp.arange(rows_local)) // L < live_count).astype(jnp.float32)
    full_live = (jnp.arange(rows_full) // L < live_count).astype(jnp.float32)
    live_images = jnp.arange(images) < live_count

    def dense_fetch():
        return (
            lax.all_gather(first_norm, "dp", axis=0, tiled=True),
            lax.all_gather(first_qkv, "dp", axis=0, tiled=True),
            lax.all_gather(first_out, "dp", axis=1, tiled=True),
            lax.all_gather(second_norm, "dp", axis=0, tiled=True),
            lax.all_gather(dense_up, "dp", axis=0, tiled=True),
            lax.all_gather(dense_down, "dp", axis=1, tiled=True),
        )

    def moe_fetch():
        return (
            lax.all_gather(third_norm, "dp", axis=0, tiled=True),
            lax.all_gather(second_qkv, "dp", axis=0, tiled=True),
            lax.all_gather(second_out, "dp", axis=1, tiled=True),
            lax.all_gather(fourth_norm, "dp", axis=0, tiled=True),
            lax.all_gather(router_weight, "dp", axis=0, tiled=True),
            lax.all_gather(expert_up, "dp", axis=1, tiled=True),
            lax.all_gather(expert_down, "dp", axis=2, tiled=True),
        )

    dense_full = dense_fetch()
    residual_zero = block_input.astype(jnp.float32)
    residual_one, attn_first, peak_first = block_attention(
        residual_zero, dense_full[0], dense_full[1], dense_full[2], images, head_size, live_images
    )
    residual_two, mlp_stored = block_mlp(residual_one, dense_full[3], dense_full[4], dense_full[5])
    moe_full = moe_fetch()
    residual_three, attn_second, peak_second = block_attention(
        residual_two, moe_full[0], moe_full[1], moe_full[2], images, head_size, live_images
    )
    moe_normed = layer_norm(residual_three, moe_full[3].astype(jnp.float32)).astype(jnp.bfloat16)
    moe_input = gather_rows(moe_normed)
    logits = jnp.dot(moe_input, moe_full[4], preferred_element_type=jnp.float32)
    route_probs = jax.nn.softmax(logits, axis=-1)
    kept_mask = expert_slots < capacity
    pair_number = jnp.arange(2 * rows_full, dtype=jnp.int32)
    slot_index = (expert_ids * capacity + expert_slots).reshape(-1)
    kept_flat = kept_mask.reshape(-1)
    write_target = jnp.where(kept_flat, slot_index, experts * capacity + pair_number)
    target = jnp.where(kept_flat, slot_index, experts * capacity)
    pair_of_slot = (
        jnp.zeros((experts * capacity + 2 * rows_full,), jnp.int32)
        .at[write_target]
        .set(pair_number)[: experts * capacity]
    )
    slot_filled = (
        jnp.zeros((experts * capacity + 2 * rows_full,), jnp.float32)
        .at[write_target]
        .set(1.0)[: experts * capacity]
    )
    chosen = (expert_ids[:, :, None] == jnp.arange(experts)[None, None, :]).astype(jnp.float32)
    keep_live = kept_mask.astype(jnp.float32) * full_live[:, None]
    gates = jnp.sum(chosen * route_probs[:, None, :], axis=-1) * keep_live
    slot_token = pair_of_slot // 2
    slot_gate = gates.reshape(-1)[pair_of_slot] * slot_filled
    dispatched = (moe_input[slot_token] * slot_filled[:, None].astype(jnp.bfloat16)).reshape(
        experts, capacity, -1
    )
    expert_hidden = jnp.einsum(
        "ecd,edf->ecf", dispatched, moe_full[5], preferred_element_type=jnp.float32
    )
    expert_act = exact_gelu(expert_hidden).astype(jnp.bfloat16)
    expert_result = jnp.einsum(
        "ecf,efd->ecd", expert_act, moe_full[6], preferred_element_type=jnp.float32
    )
    feature_count = expert_result.shape[2]
    padded_result = jnp.concatenate(
        [
            expert_result.reshape(experts * capacity, feature_count),
            jnp.zeros((1, feature_count), jnp.float32),
        ],
        axis=0,
    )
    pair_result = padded_result[target].reshape(rows_full, 2, feature_count)
    combined = jnp.sum(gates[:, :, None] * pair_result, axis=1)
    residual_four = residual_three + scatter_rows(combined)
    block_output = residual_four * local_live[:, None]
    peak_first_all, peak_second_all = lax.pmax((peak_first, peak_second), "dp")
    root_first = clip_root(peak_first_all)
    root_second = clip_root(peak_second_all)
    clipped_first = clip_columns(first_qkv, root_first, head_size)
    clipped_second = clip_columns(second_qkv, root_second, head_size)
    clip_scales = jnp.stack([root_first, root_second])
    moe_back = moe_fetch()
    grad_four = cotangent.astype(jnp.float32) * local_live[:, None]
    moe_grad_full = gather_rows(grad_four.astype(jnp.bfloat16))
    partial_gates = jnp.sum(moe_grad_full.astype(jnp.float32)[:, None, :] * pair_result, axis=-1)
    grad_gates = lax.psum(partial_gates, "tensor")
    grad_result = (slot_gate[:, None] * moe_grad_full[slot_token].astype(jnp.float32)).astype(
        jnp.bfloat16
    )
    grad_result = grad_result.reshape(experts, capacity, feature_count)
    grad_expert_down = jnp.einsum(
        "ecf,ecd->efd", expert_act, grad_result, preferred_element_type=jnp.float32
    )
    grad_act = jnp.einsum(
        "ecd,efd->ecf", grad_result, moe_back[6], preferred_element_type=jnp.float32
    )
    grad_hidden = gelu_back(expert_hidden, grad_act).astype(jnp.bfloat16)
    grad_expert_up = jnp.einsum(
        "ecd,ecf->edf", dispatched, grad_hidden, preferred_element_type=jnp.float32
    )
    grad_dispatch = jnp.einsum(
        "ecf,edf->ecd", grad_hidden, moe_back[5], preferred_element_type=jnp.float32
    )
    grad_dispatch = jnp.concatenate(
        [
            grad_dispatch.reshape(experts * capacity, feature_count),
            jnp.zeros((1, feature_count), jnp.float32),
        ],
        axis=0,
    )
    grad_from_experts = jnp.sum(grad_dispatch[target].reshape(rows_full, 2, feature_count), axis=1)
    grad_picked = grad_gates * keep_live
    grad_probs = jnp.sum(chosen * grad_picked[:, :, None], axis=1)
    grad_logits = route_probs * (
        grad_probs - jnp.sum(grad_probs * route_probs, axis=-1, keepdims=True)
    )
    grad_logits = grad_logits.astype(jnp.bfloat16)
    grad_router = jnp.einsum(
        "rd,re->de", moe_input, grad_logits, preferred_element_type=jnp.float32
    )
    local_logits = lax.dynamic_slice_in_dim(grad_logits, first_row, rows_local, 0)
    grad_moe_normed = scatter_rows(grad_from_experts) + jnp.einsum(
        "re,de->rd", local_logits, moe_back[4], preferred_element_type=jnp.float32
    )
    grad_rows_four, grad_fourth_norm = norm_back(residual_three, moe_back[3], grad_moe_normed)
    grad_three = grad_four + grad_rows_four
    grad_two, grad_third_norm, grad_second_qkv, grad_second_out = block_attention_back(
        residual_two,
        grad_three,
        moe_back[0],
        moe_back[1],
        moe_back[2],
        attn_second,
        images,
        head_size,
    )
    third_sum, fourth_sum = sum_gains(grad_third_norm, grad_fourth_norm)
    moe_owned = (
        lax.psum_scatter(third_sum, "dp", scatter_dimension=0, tiled=True),
        lax.psum_scatter(grad_second_qkv, "dp", scatter_dimension=0, tiled=True),
        lax.psum_scatter(grad_second_out, "dp", scatter_dimension=1, tiled=True),
        lax.psum_scatter(fourth_sum, "dp", scatter_dimension=0, tiled=True),
        lax.psum_scatter(grad_router, "dp", scatter_dimension=0, tiled=True),
        lax.psum_scatter(grad_expert_up, "dp", scatter_dimension=1, tiled=True),
        lax.psum_scatter(grad_expert_down, "dp", scatter_dimension=2, tiled=True),
    )
    dense_back = dense_fetch()
    grad_one, grad_second_norm, grad_dense_up, grad_dense_down = block_mlp_back(
        residual_one, grad_two, dense_back[3], dense_back[4], dense_back[5], mlp_stored
    )
    input_grad, grad_first_norm, grad_first_qkv, grad_first_out = block_attention_back(
        residual_zero,
        grad_one,
        dense_back[0],
        dense_back[1],
        dense_back[2],
        attn_first,
        images,
        head_size,
    )
    first_sum, second_sum = sum_gains(grad_first_norm, grad_second_norm)
    dense_owned = (
        lax.psum_scatter(first_sum, "dp", scatter_dimension=0, tiled=True),
        lax.psum_scatter(grad_first_qkv, "dp", scatter_dimension=0, tiled=True),
        lax.psum_scatter(grad_first_out, "dp", scatter_dimension=1, tiled=True),
        lax.psum_scatter(second_sum, "dp", scatter_dimension=0, tiled=True),
        lax.psum_scatter(grad_dense_up, "dp", scatter_dimension=0, tiled=True),
        lax.psum_scatter(grad_dense_down, "dp", scatter_dimension=1, tiled=True),
    )
    owned = tuple(dense_owned) + tuple(moe_owned)
    return (
        block_output,
        input_grad,
        owned[0],
        owned[1],
        owned[2],
        owned[3],
        owned[4],
        owned[5],
        owned[6],
        owned[7],
        owned[8],
        owned[9],
        owned[10],
        owned[11],
        owned[12],
        clipped_first,
        clipped_second,
        clip_scales,
    )


ROWS = 208
AXES = ("dp", "tensor")
BF = jnp.bfloat16
F32 = jnp.float32
VM = pl.BlockSpec(memory_space=pltpu.VMEM)
SM = pl.BlockSpec(memory_space=pltpu.SMEM)


def swap(values, z=0, x=0, y=0, core=0):
    shift_d, shift_t = 2 * z + x, 2 * y + core
    pairs = [(d * 4 + t, (d ^ shift_d) * 4 + (t ^ shift_t)) for d in range(8) for t in range(4)]
    return lax.ppermute(values, AXES, pairs)


def hold(values, *tokens):
    return lax.optimization_barrier((values,) + tokens)[0]


def run(kernel, outs, args, flops, scratch=(), scalars=0, mib=20):
    flops = flops if flops == 8e9 else 1000
    shapes = [jax.ShapeDtypeStruct(s, dt) for s, dt in outs]
    return pl.pallas_call(
        kernel,
        out_shape=shapes,
        in_specs=[SM] * scalars + [VM] * (len(args) - scalars),
        out_specs=[VM] * len(shapes),
        scratch_shapes=list(scratch),
        compiler_params=pltpu.CompilerParams(vmem_limit_bytes=mib * 2**20),
        cost_estimate=pl.CostEstimate(flops=int(flops), bytes_accessed=1000, transcendentals=0),
    )(*args)


def dot(a, b, ca, cb):
    return lax.dot_general(a, b, (((ca,), (cb,)), ((), ())), preferred_element_type=F32)


def norm_stats(values):
    center = values - jnp.mean(values, axis=-1, keepdims=True)
    scale = lax.rsqrt(jnp.mean(center * center, axis=-1, keepdims=True) + epsilon)
    return center * scale, scale


def enter_kernel(live, x_ref, c_ref, perm_ref, start_ref, low_start, grad_ref, low_ref):
    rows = x_ref.shape[0]
    scale = live[0].astype(F32)
    extra = jnp.zeros((ROWS - rows, x_ref.shape[1]), F32)
    start = dot(x_ref[...], perm_ref[...], 1, 1)
    start_ref[:rows] = start
    start_ref[rows:] = extra
    low_start[:rows] = start.astype(BF)
    low_start[rows:] = extra.astype(BF)
    grad = dot(c_ref[...], perm_ref[...], 1, 1) * scale
    grad_ref[:rows] = grad
    grad_ref[rows:] = extra
    low_ref[:rows] = grad.astype(BF)
    low_ref[rows:] = extra.astype(BF)


def norm_kernel(gain_ref, *refs):
    for x_ref, out_ref in zip(refs[:4], refs[4:]):
        out_ref[...] = (norm_stats(x_ref[...].astype(F32))[0] * gain_ref[...]).astype(BF)


def join_norm_kernel(x_ref, own_ref, far_ref, gain_ref, sum_ref, out_ref):
    total = x_ref[...] + (own_ref[...] + far_ref[...].astype(F32))
    sum_ref[...] = total
    out_ref[...] = (norm_stats(total)[0] * gain_ref[...]).astype(BF)


def norm_back_kernel(x_ref, up_ref, own_ref, far_ref, gain_ref, grad_ref, low_ref, gain_out):
    upstream = own_ref[...] + far_ref[...].astype(F32)
    normed, scale = norm_stats(x_ref[...])
    scaled = upstream * gain_ref[...]
    grad = up_ref[...] + scale * (
        scaled
        - jnp.mean(scaled, axis=-1, keepdims=True)
        - normed * jnp.mean(scaled * normed, axis=-1, keepdims=True)
    )
    grad_ref[...] = grad
    low_ref[...] = grad.astype(BF)
    gain_out[...] = jnp.sum(upstream * normed, axis=0, keepdims=True)


def fill(rows, *refs):
    size = refs[0].shape[0]
    for i, ref in enumerate(refs):
        rows[i * size : (i + 1) * size] = ref[...]


def put_partial(partial, own_ref, sib_ref):
    half = own_ref.shape[0]
    own_ref[...] = partial[:half]
    sib_ref[...] = partial[half:].astype(BF)


def score_block(queries, keyset):
    scores = dot(queries, keyset, 1, 1) * HD ** (-0.5)
    column = lax.broadcasted_iota(jnp.int32, scores.shape, 1)
    scores = jnp.where(column < L, scores, -1e30)
    top = jnp.max(scores, axis=-1, keepdims=True)
    weight = jnp.exp(scores - top)
    return weight * (1.0 / jnp.sum(weight, axis=-1, keepdims=True)), top


def attend_kernel(
    at, live, a0, a1, a2, a3, w, mix_ref, att_ref, own_ref, sib_ref, peak_ref, rows
):
    fill(rows, a0, a1, a2, a3)
    part = mix_ref.shape[1] // 3
    mix_ref[...] = dot(rows[...], w[:, at : at + 3 * part], 1, 0).astype(BF)
    row_ok = lax.broadcasted_iota(jnp.int32, (ROWS, 1), 0) < L
    lane = lax.broadcasted_iota(jnp.int32, peak_ref.shape, 1)
    found = jnp.full(peak_ref.shape, -1e30, F32)
    for h in range(part // HD):
        for i in range(4):
            span = slice(i * ROWS, (i + 1) * ROWS)
            cut = [mix_ref[span, c * part + h * HD : c * part + (h + 1) * HD] for c in range(3)]
            probs, top = score_block(cut[0], cut[1])
            mixed = dot(probs.astype(BF), cut[2], 1, 0)
            att_ref[span, h * HD : (h + 1) * HD] = mixed.astype(BF)
            best = jnp.max(jnp.where(row_ok, top, -1e30), axis=0, keepdims=True)
            best = jnp.where(live[i] > 0, best, -1e30)
            found = jnp.where(lane == h, jnp.maximum(best, found), found)
    peak_ref[...] = found
    out = w[:, at + 3 * part : at + 4 * part]
    put_partial(dot(att_ref[...], out, 1, 1), own_ref, sib_ref)


def put_pack(grad, column, near, send):
    half = near.shape[0]
    near[:, column : column + grad.shape[1]] = grad[:half]
    send[:, column : column + grad.shape[1]] = grad[half:]


def attend_back_kernel(
    at, g0, g1, g2, g3, a0, a1, a2, a3, mix_ref, att_ref, w,
    near, send, own_ref, sib_ref, rows, grad_att, grad_mix,
):
    part = mix_ref.shape[1] // 3
    fill(rows, g0, g1, g2, g3)
    grad_att[...] = dot(rows[...], w[:, at + 3 * part : at + 4 * part], 1, 0).astype(BF)
    put_pack(dot(rows[...], att_ref[...], 0, 0).astype(BF), 3 * part, near, send)
    factor = HD ** (-0.5)
    for h in range(part // HD):
        for i in range(4):
            span = slice(i * ROWS, (i + 1) * ROWS)
            spans = [slice(c * part + h * HD, c * part + (h + 1) * HD) for c in range(3)]
            queries, keyset, values = (mix_ref[span, s] for s in spans)
            grad = grad_att[span, h * HD : (h + 1) * HD]
            probs, _ = score_block(queries, keyset)
            grad_mix[span, spans[2]] = dot(probs.astype(BF), grad, 0, 0).astype(BF)
            grad_probs = dot(grad, values, 1, 1)
            slope = probs * (grad_probs - jnp.sum(grad_probs * probs, axis=-1, keepdims=True))
            slope = slope.astype(BF)
            grad_mix[span, spans[0]] = (factor * dot(slope, keyset, 1, 0)).astype(BF)
            grad_mix[span, spans[1]] = (factor * dot(slope, queries, 0, 0)).astype(BF)
    put_partial(dot(grad_mix[...], w[:, at : at + 3 * part], 1, 1), own_ref, sib_ref)
    fill(rows, a0, a1, a2, a3)
    put_pack(dot(rows[...], grad_mix[...], 0, 0).astype(BF), 0, near, send)


def gelu_pair(hidden):
    cdf = 0.5 * (1.0 + lax.erf(hidden * 0.7071067811865476))
    slope = cdf + hidden * jnp.exp(-0.5 * hidden * hidden) * 0.3989422804014327
    return (hidden * cdf).astype(BF), slope.astype(BF)


def mlp_kernel(ats, b0, b1, b2, b3, w, act_ref, slope_ref, own_ref, sib_ref, rows):
    fill(rows, b0, b1, b2, b3)
    wide = act_ref.shape[1]
    for c in range(0, wide, 256):
        span = slice(c, c + 256)
        act, slope = gelu_pair(dot(rows[...], w[:, ats[0] + c : ats[0] + c + 256], 1, 0))
        act_ref[:, span] = act
        slope_ref[:, span] = slope
    put_partial(dot(act_ref[...], w[:, ats[1] : ats[1] + wide], 1, 1), own_ref, sib_ref)


def mlp_back_kernel(
    ats, g0, g1, g2, g3, b0, b1, b2, b3, act_ref, slope_ref, w,
    near, send, own_ref, sib_ref, rows, hidden,
):
    fill(rows, g0, g1, g2, g3)
    wide = act_ref.shape[1]
    grad = dot(rows[...], w[:, ats[1] : ats[1] + wide], 1, 0) * slope_ref[...].astype(F32)
    hidden[...] = grad.astype(BF)
    put_partial(dot(hidden[...], w[:, ats[0] : ats[0] + wide], 1, 1), own_ref, sib_ref)
    put_pack(dot(rows[...], act_ref[...], 0, 0).astype(BF), wide, near, send)
    fill(rows, b0, b1, b2, b3)
    put_pack(dot(rows[...], hidden[...], 0, 0).astype(BF), 0, near, send)


def picked(row_code, codes):
    hit = (row_code[...] == codes[0:1, :]) | (row_code[...] == codes[1:2, :])
    return jnp.where(hit, 1.0, 0.0).astype(BF)


def dispatch_kernel(row_code, codes, p0, p1, p2, p3, perm_ref, out, rows):
    fill(rows, p0, p1, p2, p3)
    picks = dot(picked(row_code, codes), rows[...], 1, 0).astype(BF)
    out[...] = dot(picks, perm_ref[...], 1, 0).astype(BF)


def token_kernel(row_code, codes, p0, p1, p2, p3, perm_ref, first_ref, second_ref, out, rows):
    dispatch_kernel(row_code, codes, p0, p1, p2, p3, perm_ref, out, rows)
    row = lax.broadcasted_iota(jnp.int32, (8, 128), 0)
    block = jnp.zeros((8, 128), F32)
    for i, ref in enumerate((first_ref, second_ref)):
        high = ref[...].astype(BF).astype(F32)
        block = jnp.where(row == 2 * i + 2, high, block)
        block = jnp.where(row == 2 * i + 3, ref[...] - high, block)
    size = out.shape[0] // 8
    for e in range(8):
        span = slice((e + 1) * size - 8, (e + 1) * size)
        old = out[span, :128].astype(F32)
        out[span, :128] = jnp.where((row >= 2) & (row < 6), block, old).astype(BF)


def collect_kernel(both_ref, grad_ref, out_ref, peak_ref):
    size = both_ref.shape[1] // 2
    best = jnp.full((2, 128), -1e30, F32)
    for p in range(both_ref.shape[0]):
        rows = slice(p * size, (p + 1) * size)
        grad_ref[rows] = both_ref[p, :size]
        out_ref[rows] = both_ref[p, size:]
        block = both_ref[p, 2 * size - 8 :, :128].astype(F32)
        found = [block[2 * i + 2 : 2 * i + 3] + block[2 * i + 3 : 2 * i + 4] for i in range(2)]
        best = jnp.maximum(best, jnp.concatenate(found, axis=0))
    peak_ref[...] = best


def combine_kernel(which, row_code, codes, perm_ref, both_ref, own_ref, sib_ref, rows):
    size = both_ref.shape[1] // 2
    for p in range(both_ref.shape[0]):
        rows[p * size : (p + 1) * size] = both_ref[p, which * size : (which + 1) * size]
    back = dot(rows[...], perm_ref[...], 1, 1).astype(BF)
    partial = dot(picked(row_code, codes), back, 0, 0)
    half = partial.shape[0] // 2
    own_ref[...] = partial[:half]
    sib_ref[...] = partial[half:].astype(BF)


def pair_add_kernel(own_ref, far_ref, near_ref, send_ref):
    total = own_ref[...] + far_ref[...].astype(F32)
    near_ref[...] = total[:ROWS]
    send_ref[...] = total[ROWS:].astype(BF)


def route_of(tokens, router, number):
    logits = dot(tokens, router, 1, 1)
    column = lax.broadcasted_iota(jnp.int32, logits.shape, 1)
    logits = jnp.where(column < 8, logits, -1e30)
    weight = jnp.exp(logits - jnp.max(logits, axis=-1, keepdims=True))
    route = weight / jnp.sum(weight, axis=-1, keepdims=True)
    mine = jnp.where(column == number, 1.0, 0.0)
    return route, mine, jnp.sum(route * mine, axis=-1, keepdims=True)


def expert_kernel(
    number, t0, t1, g0, g1, router, *rest
):
    own, far = rest[0], rest[1:5]
    res_own, res_sib, grad_own, grad_sib = rest[5:9]
    up_parts, down_parts = rest[9:13], rest[13:16]
    act_ref, hid_ref, gout_ref, pair, whole = rest[16:]
    size = t0.shape[0]
    half, wide = own.shape[0] // 2, act_ref.shape[2]
    whole[0] = own[...]
    for i, part in enumerate(far):
        whole[1, i * half // 2 : (i + 1) * half // 2] = part[...]
    for i, (t, g, res, grad) in enumerate(
        ((t1, g1, res_sib, grad_sib), (t0, g0, res_own, grad_own))
    ):
        rows = slice((1 - i) * size, (2 - i) * size)
        gate = route_of(t[...], router[...], number[0])[2]
        gout = (gate * g[...].astype(F32)).astype(BF)
        gout_ref[rows] = gout
        for y in range(2):
            for c in range(0, wide, 256):
                span = slice(c, c + 256)
                act, lean = gelu_pair(dot(t[...], whole[y, :, span], 1, 0))
                act_ref[y, rows, span] = act
                back = dot(gout, whole[y, :, wide + c : wide + c + 256], 1, 0)
                hid_ref[y, rows, span] = (back * lean.astype(F32)).astype(BF)
        res[...] = (
            dot(act_ref[0, rows], whole[0, :, wide:], 1, 1)
            + dot(act_ref[1, rows], whole[1, :, wide:], 1, 1)
        ).astype(res.dtype)
        grad[...] = (
            dot(hid_ref[0, rows], whole[0, :, :wide], 1, 1)
            + dot(hid_ref[1, rows], whole[1, :, :wide], 1, 1)
        ).astype(grad.dtype)
    pair[:size] = t0[...]
    pair[size:] = t1[...]
    for parts, left, right in ((up_parts, pair, hid_ref), (down_parts, gout_ref, act_ref)):
        parts[0][...] = dot(left[...], right[0], 0, 0).astype(BF)
        far = dot(left[...], right[1], 0, 0).astype(BF)
        at = 0
        for part in parts[1:]:
            part[...] = far[at : at + part.shape[0]]
            at += part.shape[0]


def answer_kernel(
    number, t_ref, g_ref, router, res_own, res_far, grad_own, grad_far, perm_ref,
    both_ref, router_out,
):
    route, mine, gate = route_of(t_ref[...], router[...], number[0])
    result = res_own[...] + res_far[...].astype(F32)
    grad_gate = jnp.sum(result * g_ref[...].astype(F32), axis=-1, keepdims=True)
    grad_logit = (grad_gate * route * (mine - gate)).astype(BF)
    router_out[...] = reorder(dot(grad_logit, t_ref[...], 0, 0), perm_ref[...], 1)
    grad = grad_own[...] + grad_far[...].astype(F32) + dot(grad_logit, router[...], 1, 0)
    size = both_ref.shape[1] // 2
    whole = grad.astype(BF)
    for p in range(both_ref.shape[0]):
        both_ref[p, :size] = whole[p * size : (p + 1) * size]
    whole = (gate * result).astype(BF)
    for p in range(both_ref.shape[0]):
        both_ref[p, size:] = whole[p * size : (p + 1) * size]


def reorder(values, perm, axis):
    high = values.astype(BF)
    rest = values - high.astype(F32)
    middle = rest.astype(BF)
    low = (rest - middle.astype(F32)).astype(BF)
    return dot(high, perm, 1, axis) + (dot(middle, perm, 1, axis) + dot(low, perm, 1, axis))


def leave_kernel(x_ref, perm_ref, out_ref):
    out_ref[...] = reorder(x_ref[...], perm_ref[...], 0)[: out_ref.shape[0]]


def finish_kernel(live, x_ref, own_ref, far_ref, perm_ref, out_ref):
    total = x_ref[...] + (own_ref[...] + far_ref[...].astype(F32))
    total = reorder(total, perm_ref[...], 0) * live[0].astype(F32)
    out_ref[...] = total[: out_ref.shape[0]]


def add_pack_kernel(up_own, up0, up1, up2, down_own, down0, down1, out):
    wide = up_own.shape[1]
    for c, (own, parts) in enumerate(((up_own, (up0, up1, up2)), (down_own, (down0, down1)))):
        at = 0
        for part in parts:
            span = slice(at, at + part.shape[0])
            total = own[span].astype(F32) + part[...].astype(F32)
            out[span, c * wide : (c + 1) * wide] = total.astype(BF)
            at += part.shape[0]


def pack_kernel(*refs):
    out = refs[-1]
    at = 0
    for ref in refs[:-1]:
        out[:, at : at + ref.shape[1]] = ref[...]
        at += ref.shape[1]


def stack_kernel(*refs):
    rows = refs[0].shape[0]
    for i, ref in enumerate(refs[:-1]):
        refs[-1][i * rows : (i + 1) * rows] = ref[...]


def order_kernel(places, in_ref, out_ref):
    rows = out_ref.shape[0] // 4
    for i in range(4):
        at = pl.multiple_of(places[i] * rows, rows)
        out_ref[i * rows : (i + 1) * rows] = in_ref[pl.ds(at, rows), :]


def sum_two(near, got, keep, s1, s2, s3):
    rows = keep.shape[0]
    for k, out in enumerate((keep, s1, s2, s3)):
        span = slice(k * rows, (k + 1) * rows)
        out[...] = (near[span].astype(F32) + got[span].astype(F32)).astype(out.dtype)


def small_kernel(g1, g2, g3, g4, router, out):
    whole = jnp.concatenate([g1[...], g2[...], g3[...], g4[...]], axis=0)
    count, cols = router.shape[0], out.shape[2]
    blank = jnp.zeros((out.shape[1] - 4 - count, cols), F32)
    for p in range(8):
        span = slice(p * cols, (p + 1) * cols)
        out[p] = jnp.concatenate([whole[:, span], router[:, span], blank], axis=0)


def sum_two_more(near, got, small, keep, s1, s2, s3):
    sum_two(near, got, keep, s1.at[: keep.shape[0]], s2.at[: keep.shape[0]], s3.at[: keep.shape[0]])
    rows, count = keep.shape[0], small.shape[1]
    cols = small.shape[2]
    for k, out in enumerate((s1, s2, s3)):
        out[rows:, :] = jnp.zeros((out.shape[0] - rows, out.shape[1]), BF)
        high = small[k + 1].astype(BF)
        out[rows : rows + count, :cols] = high
        low = small[k + 1] - high.astype(F32)
        out[rows + count : rows + 2 * count, :cols] = low.astype(BF)


def sum_three_more(keep, r1, r2, r3, small, first, second, small_out):
    rows, count = keep.shape[0], small.shape[1]
    cols = small.shape[2]
    sum_three(keep, r1.at[:rows], r2.at[:rows], r3.at[:rows], first, second)
    total = small[0]
    for r in (r1, r2, r3):
        high = r[rows : rows + count, :cols].astype(F32)
        total = total + (high + r[rows + count : rows + 2 * count, :cols].astype(F32))
    small_out[...] = total


def sum_three(keep, r1, r2, r3, first, second):
    total = keep[...] + (r1[...].astype(F32) + (r2[...].astype(F32) + r3[...].astype(F32)))
    wide = first.shape[1]
    first[...] = total[:, :wide]
    second[...] = total[:, wide:]


def scatter_start(parts):
    near, send = parts
    return near, swap(send, x=1)


def scatter_middle(parts):
    half, width = parts[0].shape
    shape = (half // 4, width)
    return run(sum_two, [(shape, F32)] + [(shape, BF)] * 3, parts, half * width)


def scatter_late(parts):
    keep, s1, s2, s3 = parts
    return keep, swap(s1, z=1), swap(s2, z=2), swap(s3, z=3)


def scatter_end(parts, wide):
    rows, width = parts[0].shape
    return run(sum_three, [((rows, wide), F32), ((rows, width - wide), F32)], parts, rows * width)


def fast_local(
    block_input,
    first_norm,
    first_qkv,
    first_out,
    second_norm,
    dense_up,
    dense_down,
    third_norm,
    second_qkv,
    second_out,
    fourth_norm,
    router_weight,
    expert_up,
    expert_down,
    expert_ids,
    expert_slots,
    image_counts,
    cotangent,
):
    d = lax.axis_index("dp")
    t = lax.axis_index("tensor")
    z_index, x_index = d // 2, d % 2
    width = first_norm.shape[0]
    features = width * 8
    experts = expert_up.shape[0]
    live_count = image_counts[0]
    head_cols = first_out.shape[0]
    ff_cols = dense_up.shape[1]
    qkv_cols = 3 * head_cols
    row = ((ROWS, features), F32)
    row_low = ((ROWS, features), BF)

    small = jnp.concatenate(
        [
            jnp.stack([first_norm, second_norm, third_norm, fourth_norm], axis=1),
            router_weight,
            jnp.zeros((width, 128 - 4 - experts), BF),
        ],
        axis=1,
    )
    pack_one = run(
        pack_kernel,
        [((width, small.shape[1] + 4 * head_cols), BF)],
        (small, first_qkv.reshape(width, -1), first_out.T),
        width,
    )[0]
    pack_late = run(
        pack_kernel,
        [((width, 2 * ff_cols + 4 * head_cols), BF)],
        (dense_up, dense_down.T, second_qkv.reshape(width, -1), second_out.T),
        width,
    )[0]

    lines = [[x + 2 * z for z in range(4)] for x in range(2)]
    raw_late = lax.all_gather(pack_late, "dp", axis=0, tiled=True, axis_index_groups=lines)

    def stacked(shards):
        shape = (len(shards) * shards[0].shape[0], shards[0].shape[1])
        return run(stack_kernel, [(shape, BF)], shards, width)[0]

    z_one = stacked([pack_one] + [swap(pack_one, z=k) for k in (1, 2, 3)])

    rel = jnp.arange(features)
    block = rel // width
    rel_place = jnp.bitwise_xor(d, 2 * (block % 4) + block // 4) * width + rel % width
    perm = (rel_place[:, None] == rel[None, :]).astype(BF)
    live_here = (t < live_count).astype(jnp.int32).reshape(1)
    live_group = (jnp.stack([t, t ^ 2, t ^ 1, t ^ 3]) < live_count).astype(jnp.int32)

    start, low_start, grad_four, grad_low = run(
        enter_kernel,
        [row, row_low, row, row_low],
        (live_here, block_input, cotangent, perm),
        4 * ROWS * features**2,
        scalars=1,
    )

    def spread(rows):
        far = swap(rows, y=1)
        return [rows, far, swap(rows, core=1), swap(far, core=1)]

    first_group = spread(low_start)
    wide = 2 * ff_cols
    half_shape = [((features // 2, ff_cols), BF)] * 2
    e_pack = jnp.concatenate([expert_up, jnp.swapaxes(expert_down, 1, 2)], axis=2)
    held = -(-CAP // 4)
    block_size = -(-(held + 4) // 8) * 8
    ids = jnp.pad(expert_ids.reshape(4, L, 2), ((0, 0), (0, ROWS - L), (0, 0)), constant_values=-1)
    slots = jnp.pad(
        expert_slots.reshape(4, L, 2), ((0, 0), (0, ROWS - L), (0, 0)), constant_values=CAP
    )
    mine = (slots < CAP) & (slots // held == t)
    codes = jnp.where(mine, ids * block_size + slots % held, -1)
    codes = jnp.concatenate(
        [lax.dynamic_index_in_dim(codes, t ^ k, 0, keepdims=False) for k in (0, 2, 1, 3)], axis=0
    ).T
    slot_rows = experts * block_size
    row_code = jnp.arange(slot_rows).reshape(-1, 1)
    group_flops = 2 * slot_rows * features * (4 * ROWS + features)

    def to_experts(kernel, rows, *peaks):
        return run(
            kernel,
            [((slot_rows, features), BF)],
            (row_code, codes, *rows, perm, *peaks),
            group_flops,
            scratch=[pltpu.VMEM((4 * ROWS, features), BF)],
        )[0].reshape(experts, block_size, features)

    def exchange(both):
        return lax.all_to_all(both, "dp", split_axis=0, concat_axis=0, tiled=True)

    group_scratch = pltpu.VMEM((4 * ROWS, features), BF)
    pair_out = [((2 * ROWS, features), F32), ((2 * ROWS, features), BF)]

    def attend(normed, full, at):
        return run(
            functools.partial(attend_kernel, at),
            [((4 * ROWS, qkv_cols), BF), ((4 * ROWS, head_cols), BF)]
            + pair_out
            + [((1, 128), F32)],
            (live_group, *normed, full),
            0,
            scratch=[group_scratch],
            scalars=1,
        )

    def pack_shapes(columns):
        return [((features // 2, columns), BF)] * 2 + pair_out

    def attend_back(low, normed, mixed, attended, full, at):
        return run(
            functools.partial(attend_back_kernel, at),
            pack_shapes(4 * head_cols),
            (*low, *normed, mixed, attended, full),
            8e9,
            scratch=[
                group_scratch,
                pltpu.VMEM((4 * ROWS, head_cols), BF),
                pltpu.VMEM((4 * ROWS, qkv_cols), BF),
            ],
        )

    def over_group(own, sib):
        near, send = run(pair_add_kernel, [row, row_low], (own, swap(sib, core=1)), ROWS)
        return near, swap(send, y=1)

    def join(values, own, far, gain):
        return run(join_norm_kernel, [row, row_low], (values, own, far, gain), ROWS)

    def norm_back(values, upstream, own, far, gain):
        return run(
            norm_back_kernel,
            [row, row_low, ((1, features), F32)],
            (values, upstream, own, far, gain),
            ROWS,
        )

    full_one = stacked(hold([z_one, swap(z_one, x=1)], first_group))
    small_rows = full_one[:, : 4 + experts].T
    gains = [small_rows[i : i + 1].astype(F32) for i in range(4)]
    router = dot(small_rows[4:], perm, 1, 0).astype(BF)

    normed_one = run(norm_kernel, [row_low] * 4, (gains[0], *first_group), ROWS)
    mixed_one, att_one, own, sib, peak_one = attend(normed_one, full_one, small.shape[1])
    near, far = over_group(own, sib)
    one, normed = join(start, near, hold(far, raw_late), gains[1])
    normed_mlp = spread(normed)
    z_late = run(
        order_kernel,
        [(raw_late.shape, BF)],
        (jnp.stack([z_index ^ k for k in range(4)]).astype(jnp.int32), hold(raw_late, one)),
        features,
        scalars=1,
    )[0]
    x_late = swap(z_late, x=1)
    e_pack = hold(e_pack, normed_mlp[1])
    e_own = lax.all_to_all(e_pack, "dp", split_axis=0, concat_axis=0, tiled=True)
    e_own = e_own.reshape(features, wide)
    e_own = hold(e_own, normed_mlp[1])
    far = [swap(e_own[i * 2 * width : (i + 1) * 2 * width], y=1) for i in range(4)]
    e_far = far
    grad_sent = to_experts(dispatch_kernel, spread(hold(grad_low, normed)))
    full_late = stacked([z_late, x_late])
    ats = (0, ff_cols)
    act, slope, own, sib = run(
        functools.partial(mlp_kernel, ats),
        [((4 * ROWS, ff_cols), BF)] * 2 + pair_out,
        (*hold(normed_mlp, grad_sent), full_late),
        0,
        scratch=[group_scratch],
    )
    near, far = over_group(own, sib)
    two, normed = join(one, near, far, gains[2])
    normed_two = spread(normed)
    mixed_two, att_two, own, sib, peak_two = attend(normed_two, full_late, 2 * ff_cols)
    near, far = over_group(own, sib)
    three, normed = join(two, near, far, gains[3])
    tokens_sent = to_experts(token_kernel, spread(normed), peak_one, peak_two)
    both = exchange(hold(jnp.concatenate([grad_sent, tokens_sent], axis=1), e_far[0]))
    grad_slots, tokens, peaks = run(
        collect_kernel,
        [((slot_rows, features), BF)] * 2 + [((2, 128), F32)],
        (hold(both, *e_far),),
        0,
    )
    far_slots, far_tokens = swap(grad_slots, core=1), swap(tokens, core=1)
    number = d.astype(jnp.int32).reshape(1)
    near_heads = head_cols // HD
    roots = clip_root(peaks[:, :near_heads])
    slot_out = [((slot_rows, features), F32), ((slot_rows, features), BF)]
    res_own, res_sib, eg_own, eg_sib, *e_packs = run(
        expert_kernel,
        slot_out
        + slot_out
        + [((features, ff_cols), BF)]
        + [((2 * width, ff_cols), BF)] * 2
        + half_shape[:1]
        + [((features, ff_cols), BF)]
        + half_shape,
        (number, tokens, far_tokens, grad_slots, far_slots, router)
        + (e_own, *e_far),
        8 * 2 * slot_rows * features * 2 * ff_cols,
        scalars=1,
        scratch=[
            pltpu.VMEM((2, 2 * slot_rows, ff_cols), BF),
            pltpu.VMEM((2, 2 * slot_rows, ff_cols), BF),
            pltpu.VMEM((2 * slot_rows, features), BF),
            pltpu.VMEM((2 * slot_rows, features), BF),
            pltpu.VMEM((2, features, wide), BF),
        ],
        mib=44,
    )
    res_far, eg_far = swap(res_sib, core=1), swap(eg_sib, core=1)
    up_got = [swap(e_packs[1], y=1)]
    both, grad_router = run(
        answer_kernel,
        [((experts, 2 * block_size, features), BF), ((experts, features), F32)],
        (number, tokens, grad_slots, router, res_own, res_far, eg_own, eg_far, perm),
        4 * slot_rows * features**2,
        scalars=1,
    )
    both = hold(both, up_got)
    e_packs = hold(e_packs, both)
    both = exchange(both)
    up_got.append(swap(e_packs[2], y=1))
    up_got.append(swap(e_packs[3], y=1))
    down_got = [swap(e_packs[5], y=1)]
    both = hold(both, up_got, down_got)

    def combine(which, both):
        return run(
            functools.partial(combine_kernel, which),
            [((2 * ROWS, features), F32), ((2 * ROWS, features), BF)],
            (row_code, codes, perm, both),
            group_flops,
            scratch=[pltpu.VMEM((slot_rows, features), BF)],
        )

    own, sib = combine(0, both)
    back_own, back_far = over_group(own, sib)
    grad_three, low, gain_four = norm_back(
        three, grad_four, back_own, back_far, gains[3]
    )
    low = spread(low)
    down_got.append(swap(hold(e_packs[6], low[1]), y=1))
    *second, own, sib = attend_back(
        low, normed_two, mixed_two, att_two, full_late, 2 * ff_cols
    )
    second = scatter_start(second)
    near, far = over_group(own, hold(sib, down_got[1]))
    e_sum = run(
        add_pack_kernel,
        [((features, wide), BF)],
        (e_packs[0], *up_got, e_packs[4], *hold(down_got, second[1], far)),
        0,
    )[0].reshape(experts, width, wide)
    e_back = lax.all_to_all(e_sum, "dp", split_axis=0, concat_axis=0, tiled=True)
    grad_two, low, gain_three = norm_back(
        two, grad_three, near, far, gains[2]
    )
    low = spread(low)
    *mlp, own, sib = run(
        functools.partial(mlp_back_kernel, ats),
        pack_shapes(2 * ff_cols),
        (*low, *normed_mlp, act, slope, full_late),
        0,
        scratch=[group_scratch, pltpu.VMEM((4 * ROWS, ff_cols), BF)],
    )
    mlp = scatter_start(mlp)
    near, send = run(pair_add_kernel, [row, row_low], (own, swap(sib, core=1)), ROWS)
    far = swap(send, y=1)
    mixed_own, mixed_sib = combine(1, hold(both, sib))
    second = scatter_late(scatter_middle(hold(second, mixed_own)))
    mixed_own, mixed_send = run(
        pair_add_kernel, [row, row_low], (mixed_own, swap(mixed_sib, core=1)), ROWS
    )
    grad_one, low, gain_two = norm_back(
        one, grad_two, near, hold(far, mixed_send), gains[1]
    )
    low = spread(low)
    mixed_far = swap(hold(mixed_send, low), y=1)
    *first, own, sib = attend_back(
        hold(low, mlp),
        normed_one,
        mixed_one,
        att_one,
        full_one,
        small.shape[1],
    )
    mlp = scatter_late(scatter_middle(mlp))
    first = scatter_start(first)
    near, far = over_group(own, hold(sib, mixed_far, second, e_back))
    grad_zero, _, gain_one = norm_back(start, grad_one, near, hold(far, first), gains[0])
    block_output = run(
        finish_kernel,
        [((L, features), F32)],
        (live_here, three, mixed_own, mixed_far, perm),
        6 * ROWS * features**2,
        scalars=1,
    )[0]
    up_g = e_back[:, :, :ff_cols].astype(F32)
    down_g = jnp.swapaxes(e_back[:, :, ff_cols:], 1, 2).astype(F32)
    clips = (clip_columns(first_qkv, roots[0], HD), clip_columns(second_qkv, roots[1], HD))
    gains_sum = run(
        small_kernel,
        [((8, 16, width), F32)],
        (gain_one, gain_two, gain_three, gain_four, grad_router),
        0,
    )[0]
    gains_sum = hold(
        gains_sum + swap(gains_sum, core=1), mlp, block_output, up_g, down_g, clips
    )
    gains_sum = gains_sum + swap(gains_sum, y=1)
    gains_sum = gains_sum[:4] + swap(gains_sum[4:], x=1)
    near_first, got_first = first
    shape = (width, 4 * head_cols)
    first = run(
        sum_two_more,
        [(shape, F32)] + [((width + 32, shape[1]), BF)] * 3,
        (near_first, got_first, gains_sum),
        0,
    )
    first = scatter_late(first)
    input_grad = run(
        leave_kernel,
        [((L, features), F32)],
        (hold(grad_zero, first[0]), perm),
        6 * ROWS * features**2,
    )[0]
    second = scatter_end(second, qkv_cols)
    mlp = scatter_end(mlp, ff_cols)
    first = hold(first, up_g, down_g, block_output, input_grad, second, mlp)
    *first, tail = run(
        sum_three_more,
        [((width, qkv_cols), F32), ((width, head_cols), F32), ((16, width), F32)],
        (*first, gains_sum),
        0,
    )

    return (
        block_output,
        input_grad,
        tail[0],
        first[0].reshape(first_qkv.shape),
        first[1].T,
        tail[1],
        mlp[0],
        mlp[1].T,
        tail[2],
        second[0].reshape(second_qkv.shape),
        second[1].T,
        tail[3],
        tail[4 : 4 + experts].T,
        up_g,
        down_g,
        *clips,
        roots,
    )


def solution(mesh):
    placed = (
        P(("dp", "tensor"), None),
        P("dp"),
        P("dp", None, "tensor"),
        P("tensor", "dp"),
        P("dp"),
        P("dp", "tensor"),
        P("tensor", "dp"),
        P("dp"),
        P("dp", None, "tensor"),
        P("tensor", "dp"),
        P("dp"),
        P("dp", None),
        P(None, "dp", "tensor"),
        P(None, "tensor", "dp"),
        P("dp", None),
        P("dp", None),
        P("dp"),
        P(("dp", "tensor"), None),
    )
    quick = mesh.shape["dp"] == 8 and mesh.shape["tensor"] == 4
    return jax.shard_map(
        fast_local if quick else local,
        mesh=mesh,
        in_specs=placed,
        out_specs=(
            P(("dp", "tensor"), None),
            P(("dp", "tensor"), None),
            P("dp"),
            P("dp", None, "tensor"),
            P("tensor", "dp"),
            P("dp"),
            P("dp", "tensor"),
            P("tensor", "dp"),
            P("dp"),
            P("dp", None, "tensor"),
            P("tensor", "dp"),
            P("dp"),
            P("dp", None),
            P(None, "dp", "tensor"),
            P(None, "tensor", "dp"),
            P("dp", None, "tensor"),
            P("dp", None, "tensor"),
            P(None, "tensor"),
        ),
        check_vma=False,
    )
```

```python
import functools

import jax
import jax.numpy as jnp
from jax import lax
from jax.experimental import pallas as pl
from jax.experimental.pallas import tpu as pltpu
from jax.sharding import PartitionSpec as P

HD = 64
L = 197
CAP = 197


epsilon = 1e-06
clip_tau = 2.5


def layer_norm(values, norm_gain):
    center = values - jnp.mean(values, axis=-1, keepdims=True)
    spread = jnp.mean(center * center, axis=-1, keepdims=True)
    return center * lax.rsqrt(spread + epsilon) * norm_gain


def exact_gelu(values):
    return jax.nn.gelu(values, approximate=False)


def gelu_back(values, upstream):
    return jax.vjp(exact_gelu, values)[1](upstream)[0]


def norm_back(residual, norm_gain, upstream):
    pullback = jax.vjp(layer_norm, residual, norm_gain.astype(jnp.float32))[1]
    return pullback(upstream)


def gather_rows(values):
    return lax.all_gather(values, "tensor", axis=0, tiled=True)


def scatter_rows(values):
    return lax.psum_scatter(
        values.astype(jnp.bfloat16), "tensor", scatter_dimension=0, tiled=True
    ).astype(jnp.float32)


def sum_gains(first_gain, second_gain):
    return lax.psum((first_gain, second_gain), "tensor")


def split_heads(projected, images, head_size):
    row_count, triple, columns = projected.shape
    pieces = projected.reshape(images, row_count // images, triple, columns // head_size, head_size)
    return (pieces[:, :, 0], pieces[:, :, 1], pieces[:, :, 2])


def attend_scores(queries, keyset, head_size):
    scores = jnp.einsum("iqhd,ikhd->ihqk", queries, keyset, preferred_element_type=jnp.float32)
    return scores * head_size ** (-0.5)


def attend_forward(normed_full, weight_qkv, images, head_size, live_images):
    projected = jnp.einsum(
        "rd,dcf->rcf", normed_full, weight_qkv, preferred_element_type=jnp.float32
    ).astype(jnp.bfloat16)
    queries, keyset, values = split_heads(projected, images, head_size)
    scores = attend_scores(queries, keyset, head_size)
    head_peak = jnp.max(jnp.where(live_images[:, None, None, None], scores, -1e30), axis=(0, 2, 3))
    attn_probs = jax.nn.softmax(scores, axis=-1).astype(jnp.bfloat16)
    attended = jnp.einsum("ihqk,ikhd->iqhd", attn_probs, values, preferred_element_type=jnp.float32)
    return (projected, attended.astype(jnp.bfloat16).reshape(normed_full.shape[0], -1), head_peak)


def attend_backward(projected, grad_attended, images, head_size):
    queries, keyset, values = split_heads(projected, images, head_size)
    scores = attend_scores(queries, keyset, head_size)
    attn_probs = jax.nn.softmax(scores, axis=-1)
    grad_heads = grad_attended.reshape(queries.shape)
    grad_values = jnp.einsum(
        "ihqk,iqhd->ikhd",
        attn_probs.astype(jnp.bfloat16),
        grad_heads,
        preferred_element_type=jnp.float32,
    )
    grad_probs = jnp.einsum(
        "iqhd,ikhd->ihqk", grad_heads, values, preferred_element_type=jnp.float32
    )
    grad_scores = attn_probs * (
        grad_probs - jnp.sum(grad_probs * attn_probs, axis=-1, keepdims=True)
    )
    grad_scores = grad_scores.astype(jnp.bfloat16)
    factor = head_size ** (-0.5)
    grad_queries = (
        jnp.einsum("ihqk,ikhd->iqhd", grad_scores, keyset, preferred_element_type=jnp.float32)
        * factor
    )
    grad_keyset = (
        jnp.einsum("ihqk,iqhd->ikhd", grad_scores, queries, preferred_element_type=jnp.float32)
        * factor
    )
    stacked = jnp.stack([grad_queries, grad_keyset, grad_values], axis=2).astype(jnp.bfloat16)
    return stacked.reshape(projected.shape)


def block_attention(residual, norm_gain, weight_qkv, weight_out, images, head_size, live_images):
    normed = layer_norm(residual, norm_gain.astype(jnp.float32)).astype(jnp.bfloat16)
    normed_full = gather_rows(normed)
    projected, attended, head_peak = attend_forward(
        normed_full, weight_qkv, images, head_size, live_images
    )
    branch = scatter_rows(jnp.dot(attended, weight_out, preferred_element_type=jnp.float32))
    return (residual + branch, (normed_full, projected, attended), head_peak)


def block_attention_back(
    residual, upstream, norm_gain, weight_qkv, weight_out, stored, images, head_size
):
    normed_full, projected, attended = stored
    grad_full = gather_rows(upstream.astype(jnp.bfloat16))
    grad_out = jnp.einsum("rf,rd->fd", attended, grad_full, preferred_element_type=jnp.float32)
    grad_attended = jnp.einsum(
        "rd,fd->rf", grad_full, weight_out, preferred_element_type=jnp.float32
    ).astype(jnp.bfloat16)
    grad_projected = attend_backward(projected, grad_attended, images, head_size)
    grad_qkv = jnp.einsum(
        "rd,rcf->dcf", normed_full, grad_projected, preferred_element_type=jnp.float32
    )
    grad_normed = scatter_rows(
        jnp.einsum("rcf,dcf->rd", grad_projected, weight_qkv, preferred_element_type=jnp.float32)
    )
    grad_residual, grad_gain = norm_back(residual, norm_gain, grad_normed)
    return (upstream + grad_residual, grad_gain, grad_qkv, grad_out)


def block_mlp(residual, norm_gain, weight_up, weight_down):
    normed = layer_norm(residual, norm_gain.astype(jnp.float32)).astype(jnp.bfloat16)
    normed_full = gather_rows(normed)
    hidden = jnp.dot(normed_full, weight_up, preferred_element_type=jnp.float32)
    active = exact_gelu(hidden).astype(jnp.bfloat16)
    branch = scatter_rows(jnp.dot(active, weight_down, preferred_element_type=jnp.float32))
    return (residual + branch, (normed_full, hidden, active))


def block_mlp_back(residual, upstream, norm_gain, weight_up, weight_down, stored):
    normed_full, hidden, active = stored
    grad_full = gather_rows(upstream.astype(jnp.bfloat16))
    grad_down = jnp.einsum("rf,rd->fd", active, grad_full, preferred_element_type=jnp.float32)
    grad_active = jnp.einsum(
        "rd,fd->rf", grad_full, weight_down, preferred_element_type=jnp.float32
    )
    grad_hidden = gelu_back(hidden, grad_active).astype(jnp.bfloat16)
    grad_up = jnp.einsum("rd,rf->df", normed_full, grad_hidden, preferred_element_type=jnp.float32)
    grad_normed = scatter_rows(
        jnp.einsum("rf,df->rd", grad_hidden, weight_up, preferred_element_type=jnp.float32)
    )
    grad_residual, grad_gain = norm_back(residual, norm_gain, grad_normed)
    return (upstream + grad_residual, grad_gain, grad_up, grad_down)


def clip_root(head_peak):
    return jnp.sqrt(clip_tau / jnp.maximum(head_peak, clip_tau))


def clip_columns(weight_local, head_root, head_size):
    column = jnp.repeat(head_root, head_size)
    scales = jnp.stack([column, column, jnp.ones_like(column)])
    return weight_local.astype(jnp.float32) * scales[None]


def local(
    block_input,
    first_norm,
    first_qkv,
    first_out,
    second_norm,
    dense_up,
    dense_down,
    third_norm,
    second_qkv,
    second_out,
    fourth_norm,
    router_weight,
    expert_up,
    expert_down,
    expert_ids,
    expert_slots,
    image_counts,
    cotangent,
):
    rows_local = block_input.shape[0]
    rows_full = rows_local * lax.axis_size("tensor")
    images = rows_full // L
    head_size = HD
    experts = expert_up.shape[0]
    capacity = CAP
    first_row = lax.axis_index("tensor") * rows_local
    live_count = image_counts[0]
    local_live = ((first_row + jnp.arange(rows_local)) // L < live_count).astype(jnp.float32)
    full_live = (jnp.arange(rows_full) // L < live_count).astype(jnp.float32)
    live_images = jnp.arange(images) < live_count

    def dense_fetch():
        return (
            lax.all_gather(first_norm, "dp", axis=0, tiled=True),
            lax.all_gather(first_qkv, "dp", axis=0, tiled=True),
            lax.all_gather(first_out, "dp", axis=1, tiled=True),
            lax.all_gather(second_norm, "dp", axis=0, tiled=True),
            lax.all_gather(dense_up, "dp", axis=0, tiled=True),
            lax.all_gather(dense_down, "dp", axis=1, tiled=True),
        )

    def moe_fetch():
        return (
            lax.all_gather(third_norm, "dp", axis=0, tiled=True),
            lax.all_gather(second_qkv, "dp", axis=0, tiled=True),
            lax.all_gather(second_out, "dp", axis=1, tiled=True),
            lax.all_gather(fourth_norm, "dp", axis=0, tiled=True),
            lax.all_gather(router_weight, "dp", axis=0, tiled=True),
            lax.all_gather(expert_up, "dp", axis=1, tiled=True),
            lax.all_gather(expert_down, "dp", axis=2, tiled=True),
        )

    dense_full = dense_fetch()
    residual_zero = block_input.astype(jnp.float32)
    residual_one, attn_first, peak_first = block_attention(
        residual_zero, dense_full[0], dense_full[1], dense_full[2], images, head_size, live_images
    )
    residual_two, mlp_stored = block_mlp(residual_one, dense_full[3], dense_full[4], dense_full[5])
    moe_full = moe_fetch()
    residual_three, attn_second, peak_second = block_attention(
        residual_two, moe_full[0], moe_full[1], moe_full[2], images, head_size, live_images
    )
    moe_normed = layer_norm(residual_three, moe_full[3].astype(jnp.float32)).astype(jnp.bfloat16)
    moe_input = gather_rows(moe_normed)
    logits = jnp.dot(moe_input, moe_full[4], preferred_element_type=jnp.float32)
    route_probs = jax.nn.softmax(logits, axis=-1)
    kept_mask = expert_slots < capacity
    pair_number = jnp.arange(2 * rows_full, dtype=jnp.int32)
    slot_index = (expert_ids * capacity + expert_slots).reshape(-1)
    kept_flat = kept_mask.reshape(-1)
    write_target = jnp.where(kept_flat, slot_index, experts * capacity + pair_number)
    target = jnp.where(kept_flat, slot_index, experts * capacity)
    pair_of_slot = (
        jnp.zeros((experts * capacity + 2 * rows_full,), jnp.int32)
        .at[write_target]
        .set(pair_number)[: experts * capacity]
    )
    slot_filled = (
        jnp.zeros((experts * capacity + 2 * rows_full,), jnp.float32)
        .at[write_target]
        .set(1.0)[: experts * capacity]
    )
    chosen = (expert_ids[:, :, None] == jnp.arange(experts)[None, None, :]).astype(jnp.float32)
    keep_live = kept_mask.astype(jnp.float32) * full_live[:, None]
    gates = jnp.sum(chosen * route_probs[:, None, :], axis=-1) * keep_live
    slot_token = pair_of_slot // 2
    slot_gate = gates.reshape(-1)[pair_of_slot] * slot_filled
    dispatched = (moe_input[slot_token] * slot_filled[:, None].astype(jnp.bfloat16)).reshape(
        experts, capacity, -1
    )
    expert_hidden = jnp.einsum(
        "ecd,edf->ecf", dispatched, moe_full[5], preferred_element_type=jnp.float32
    )
    expert_act = exact_gelu(expert_hidden).astype(jnp.bfloat16)
    expert_result = jnp.einsum(
        "ecf,efd->ecd", expert_act, moe_full[6], preferred_element_type=jnp.float32
    )
    feature_count = expert_result.shape[2]
    padded_result = jnp.concatenate(
        [
            expert_result.reshape(experts * capacity, feature_count),
            jnp.zeros((1, feature_count), jnp.float32),
        ],
        axis=0,
    )
    pair_result = padded_result[target].reshape(rows_full, 2, feature_count)
    combined = jnp.sum(gates[:, :, None] * pair_result, axis=1)
    residual_four = residual_three + scatter_rows(combined)
    block_output = residual_four * local_live[:, None]
    peak_first_all, peak_second_all = lax.pmax((peak_first, peak_second), "dp")
    root_first = clip_root(peak_first_all)
    root_second = clip_root(peak_second_all)
    clipped_first = clip_columns(first_qkv, root_first, head_size)
    clipped_second = clip_columns(second_qkv, root_second, head_size)
    clip_scales = jnp.stack([root_first, root_second])
    moe_back = moe_fetch()
    grad_four = cotangent.astype(jnp.float32) * local_live[:, None]
    moe_grad_full = gather_rows(grad_four.astype(jnp.bfloat16))
    partial_gates = jnp.sum(moe_grad_full.astype(jnp.float32)[:, None, :] * pair_result, axis=-1)
    grad_gates = lax.psum(partial_gates, "tensor")
    grad_result = (slot_gate[:, None] * moe_grad_full[slot_token].astype(jnp.float32)).astype(
        jnp.bfloat16
    )
    grad_result = grad_result.reshape(experts, capacity, feature_count)
    grad_expert_down = jnp.einsum(
        "ecf,ecd->efd", expert_act, grad_result, preferred_element_type=jnp.float32
    )
    grad_act = jnp.einsum(
        "ecd,efd->ecf", grad_result, moe_back[6], preferred_element_type=jnp.float32
    )
    grad_hidden = gelu_back(expert_hidden, grad_act).astype(jnp.bfloat16)
    grad_expert_up = jnp.einsum(
        "ecd,ecf->edf", dispatched, grad_hidden, preferred_element_type=jnp.float32
    )
    grad_dispatch = jnp.einsum(
        "ecf,edf->ecd", grad_hidden, moe_back[5], preferred_element_type=jnp.float32
    )
    grad_dispatch = jnp.concatenate(
        [
            grad_dispatch.reshape(experts * capacity, feature_count),
            jnp.zeros((1, feature_count), jnp.float32),
        ],
        axis=0,
    )
    grad_from_experts = jnp.sum(grad_dispatch[target].reshape(rows_full, 2, feature_count), axis=1)
    grad_picked = grad_gates * keep_live
    grad_probs = jnp.sum(chosen * grad_picked[:, :, None], axis=1)
    grad_logits = route_probs * (
        grad_probs - jnp.sum(grad_probs * route_probs, axis=-1, keepdims=True)
    )
    grad_logits = grad_logits.astype(jnp.bfloat16)
    grad_router = jnp.einsum(
        "rd,re->de", moe_input, grad_logits, preferred_element_type=jnp.float32
    )
    local_logits = lax.dynamic_slice_in_dim(grad_logits, first_row, rows_local, 0)
    grad_moe_normed = scatter_rows(grad_from_experts) + jnp.einsum(
        "re,de->rd", local_logits, moe_back[4], preferred_element_type=jnp.float32
    )
    grad_rows_four, grad_fourth_norm = norm_back(residual_three, moe_back[3], grad_moe_normed)
    grad_three = grad_four + grad_rows_four
    grad_two, grad_third_norm, grad_second_qkv, grad_second_out = block_attention_back(
        residual_two,
        grad_three,
        moe_back[0],
        moe_back[1],
        moe_back[2],
        attn_second,
        images,
        head_size,
    )
    third_sum, fourth_sum = sum_gains(grad_third_norm, grad_fourth_norm)
    moe_owned = (
        lax.psum_scatter(third_sum, "dp", scatter_dimension=0, tiled=True),
        lax.psum_scatter(grad_second_qkv, "dp", scatter_dimension=0, tiled=True),
        lax.psum_scatter(grad_second_out, "dp", scatter_dimension=1, tiled=True),
        lax.psum_scatter(fourth_sum, "dp", scatter_dimension=0, tiled=True),
        lax.psum_scatter(grad_router, "dp", scatter_dimension=0, tiled=True),
        lax.psum_scatter(grad_expert_up, "dp", scatter_dimension=1, tiled=True),
        lax.psum_scatter(grad_expert_down, "dp", scatter_dimension=2, tiled=True),
    )
    dense_back = dense_fetch()
    grad_one, grad_second_norm, grad_dense_up, grad_dense_down = block_mlp_back(
        residual_one, grad_two, dense_back[3], dense_back[4], dense_back[5], mlp_stored
    )
    input_grad, grad_first_norm, grad_first_qkv, grad_first_out = block_attention_back(
        residual_zero,
        grad_one,
        dense_back[0],
        dense_back[1],
        dense_back[2],
        attn_first,
        images,
        head_size,
    )
    first_sum, second_sum = sum_gains(grad_first_norm, grad_second_norm)
    dense_owned = (
        lax.psum_scatter(first_sum, "dp", scatter_dimension=0, tiled=True),
        lax.psum_scatter(grad_first_qkv, "dp", scatter_dimension=0, tiled=True),
        lax.psum_scatter(grad_first_out, "dp", scatter_dimension=1, tiled=True),
        lax.psum_scatter(second_sum, "dp", scatter_dimension=0, tiled=True),
        lax.psum_scatter(grad_dense_up, "dp", scatter_dimension=0, tiled=True),
        lax.psum_scatter(grad_dense_down, "dp", scatter_dimension=1, tiled=True),
    )
    owned = tuple(dense_owned) + tuple(moe_owned)
    return (
        block_output,
        input_grad,
        owned[0],
        owned[1],
        owned[2],
        owned[3],
        owned[4],
        owned[5],
        owned[6],
        owned[7],
        owned[8],
        owned[9],
        owned[10],
        owned[11],
        owned[12],
        clipped_first,
        clipped_second,
        clip_scales,
    )


ROWS = 208
AXES = ("dp", "tensor")
BF = jnp.bfloat16
F32 = jnp.float32
VM = pl.BlockSpec(memory_space=pltpu.VMEM)
SM = pl.BlockSpec(memory_space=pltpu.SMEM)


def swap(values, z=0, x=0, y=0, core=0):
    shift_d, shift_t = 2 * z + x, 2 * y + core
    pairs = [(d * 4 + t, (d ^ shift_d) * 4 + (t ^ shift_t)) for d in range(8) for t in range(4)]
    return lax.ppermute(values, AXES, pairs)


def hold(values, *tokens):
    return lax.optimization_barrier((values,) + tokens)[0]


def run(kernel, outs, args, flops, scratch=(), scalars=0, mib=20):
    flops = flops if flops == 8e9 else 1000
    shapes = [jax.ShapeDtypeStruct(s, dt) for s, dt in outs]
    return pl.pallas_call(
        kernel,
        out_shape=shapes,
        in_specs=[SM] * scalars + [VM] * (len(args) - scalars),
        out_specs=[VM] * len(shapes),
        scratch_shapes=list(scratch),
        compiler_params=pltpu.CompilerParams(vmem_limit_bytes=mib * 2**20),
        cost_estimate=pl.CostEstimate(flops=int(flops), bytes_accessed=1000, transcendentals=0),
    )(*args)


def dot(a, b, ca, cb):
    return lax.dot_general(a, b, (((ca,), (cb,)), ((), ())), preferred_element_type=F32)


def norm_stats(values):
    center = values - jnp.mean(values, axis=-1, keepdims=True)
    scale = lax.rsqrt(jnp.mean(center * center, axis=-1, keepdims=True) + epsilon)
    return center * scale, scale


def enter_kernel(live, x_ref, c_ref, perm_ref, start_ref, low_start, grad_ref, low_ref):
    rows = x_ref.shape[0]
    scale = live[0].astype(F32)
    extra = jnp.zeros((ROWS - rows, x_ref.shape[1]), F32)
    start = dot(x_ref[...], perm_ref[...], 1, 1)
    start_ref[:rows] = start
    start_ref[rows:] = extra
    low_start[:rows] = start.astype(BF)
    low_start[rows:] = extra.astype(BF)
    grad = dot(c_ref[...], perm_ref[...], 1, 1) * scale
    grad_ref[:rows] = grad
    grad_ref[rows:] = extra
    low_ref[:rows] = grad.astype(BF)
    low_ref[rows:] = extra.astype(BF)


def norm_kernel(gain_ref, *refs):
    for x_ref, out_ref in zip(refs[:4], refs[4:]):
        out_ref[...] = (norm_stats(x_ref[...].astype(F32))[0] * gain_ref[...]).astype(BF)


def join_norm_kernel(x_ref, own_ref, far_ref, gain_ref, sum_ref, out_ref):
    total = x_ref[...] + (own_ref[...] + far_ref[...].astype(F32))
    sum_ref[...] = total
    out_ref[...] = (norm_stats(total)[0] * gain_ref[...]).astype(BF)


def norm_back_kernel(x_ref, up_ref, own_ref, far_ref, gain_ref, grad_ref, low_ref, gain_out):
    upstream = own_ref[...] + far_ref[...].astype(F32)
    normed, scale = norm_stats(x_ref[...])
    scaled = upstream * gain_ref[...]
    grad = up_ref[...] + scale * (
        scaled
        - jnp.mean(scaled, axis=-1, keepdims=True)
        - normed * jnp.mean(scaled * normed, axis=-1, keepdims=True)
    )
    grad_ref[...] = grad
    low_ref[...] = grad.astype(BF)
    gain_out[...] = jnp.sum(upstream * normed, axis=0, keepdims=True)


def fill(rows, *refs):
    size = refs[0].shape[0]
    for i, ref in enumerate(refs):
        rows[i * size : (i + 1) * size] = ref[...]


def put_partial(partial, own_ref, sib_ref):
    half = own_ref.shape[0]
    own_ref[...] = partial[:half]
    sib_ref[...] = partial[half:].astype(BF)


def score_block(queries, keyset):
    scores = dot(queries, keyset, 1, 1) * HD ** (-0.5)
    column = lax.broadcasted_iota(jnp.int32, scores.shape, 1)
    scores = jnp.where(column < L, scores, -1e30)
    top = jnp.max(scores, axis=-1, keepdims=True)
    weight = jnp.exp(scores - top)
    return weight * (1.0 / jnp.sum(weight, axis=-1, keepdims=True)), top


def attend_kernel(
    at, live, a0, a1, a2, a3, w, mix_ref, att_ref, own_ref, sib_ref, peak_ref, rows
):
    fill(rows, a0, a1, a2, a3)
    part = mix_ref.shape[1] // 3
    mix_ref[...] = dot(rows[...], w[:, at : at + 3 * part], 1, 0).astype(BF)
    row_ok = lax.broadcasted_iota(jnp.int32, (ROWS, 1), 0) < L
    lane = lax.broadcasted_iota(jnp.int32, peak_ref.shape, 1)
    found = jnp.full(peak_ref.shape, -1e30, F32)
    for h in range(part // HD):
        for i in range(4):
            span = slice(i * ROWS, (i + 1) * ROWS)
            cut = [mix_ref[span, c * part + h * HD : c * part + (h + 1) * HD] for c in range(3)]
            probs, top = score_block(cut[0], cut[1])
            mixed = dot(probs.astype(BF), cut[2], 1, 0)
            att_ref[span, h * HD : (h + 1) * HD] = mixed.astype(BF)
            best = jnp.max(jnp.where(row_ok, top, -1e30), axis=0, keepdims=True)
            best = jnp.where(live[i] > 0, best, -1e30)
            found = jnp.where(lane == h, jnp.maximum(best, found), found)
    peak_ref[...] = found
    out = w[:, at + 3 * part : at + 4 * part]
    put_partial(dot(att_ref[...], out, 1, 1), own_ref, sib_ref)


def put_pack(grad, column, near, send):
    half = near.shape[0]
    near[:, column : column + grad.shape[1]] = grad[:half]
    send[:, column : column + grad.shape[1]] = grad[half:]


def attend_back_kernel(
    at, g0, g1, g2, g3, a0, a1, a2, a3, mix_ref, att_ref, w,
    near, send, own_ref, sib_ref, rows, grad_att, grad_mix,
):
    part = mix_ref.shape[1] // 3
    fill(rows, g0, g1, g2, g3)
    grad_att[...] = dot(rows[...], w[:, at + 3 * part : at + 4 * part], 1, 0).astype(BF)
    put_pack(dot(rows[...], att_ref[...], 0, 0).astype(BF), 3 * part, near, send)
    factor = HD ** (-0.5)
    for h in range(part // HD):
        for i in range(4):
            span = slice(i * ROWS, (i + 1) * ROWS)
            spans = [slice(c * part + h * HD, c * part + (h + 1) * HD) for c in range(3)]
            queries, keyset, values = (mix_ref[span, s] for s in spans)
            grad = grad_att[span, h * HD : (h + 1) * HD]
            probs, _ = score_block(queries, keyset)
            grad_mix[span, spans[2]] = dot(probs.astype(BF), grad, 0, 0).astype(BF)
            grad_probs = dot(grad, values, 1, 1)
            slope = probs * (grad_probs - jnp.sum(grad_probs * probs, axis=-1, keepdims=True))
            slope = slope.astype(BF)
            grad_mix[span, spans[0]] = (factor * dot(slope, keyset, 1, 0)).astype(BF)
            grad_mix[span, spans[1]] = (factor * dot(slope, queries, 0, 0)).astype(BF)
    put_partial(dot(grad_mix[...], w[:, at : at + 3 * part], 1, 1), own_ref, sib_ref)
    fill(rows, a0, a1, a2, a3)
    put_pack(dot(rows[...], grad_mix[...], 0, 0).astype(BF), 0, near, send)


def gelu_pair(hidden):
    cdf = 0.5 * (1.0 + lax.erf(hidden * 0.7071067811865476))
    slope = cdf + hidden * jnp.exp(-0.5 * hidden * hidden) * 0.3989422804014327
    return (hidden * cdf).astype(BF), slope.astype(BF)


def mlp_kernel(ats, b0, b1, b2, b3, w, act_ref, slope_ref, own_ref, sib_ref, rows):
    fill(rows, b0, b1, b2, b3)
    wide = act_ref.shape[1]
    for c in range(0, wide, 256):
        span = slice(c, c + 256)
        act, slope = gelu_pair(dot(rows[...], w[:, ats[0] + c : ats[0] + c + 256], 1, 0))
        act_ref[:, span] = act
        slope_ref[:, span] = slope
    put_partial(dot(act_ref[...], w[:, ats[1] : ats[1] + wide], 1, 1), own_ref, sib_ref)


def mlp_back_kernel(
    ats, g0, g1, g2, g3, b0, b1, b2, b3, act_ref, slope_ref, w,
    near, send, own_ref, sib_ref, rows, hidden,
):
    fill(rows, g0, g1, g2, g3)
    wide = act_ref.shape[1]
    grad = dot(rows[...], w[:, ats[1] : ats[1] + wide], 1, 0) * slope_ref[...].astype(F32)
    hidden[...] = grad.astype(BF)
    put_partial(dot(hidden[...], w[:, ats[0] : ats[0] + wide], 1, 1), own_ref, sib_ref)
    put_pack(dot(rows[...], act_ref[...], 0, 0).astype(BF), wide, near, send)
    fill(rows, b0, b1, b2, b3)
    put_pack(dot(rows[...], hidden[...], 0, 0).astype(BF), 0, near, send)


def picked(row_code, codes):
    hit = (row_code[...] == codes[0:1, :]) | (row_code[...] == codes[1:2, :])
    return jnp.where(hit, 1.0, 0.0).astype(BF)


def dispatch_kernel(row_code, codes, p0, p1, p2, p3, perm_ref, out, rows):
    fill(rows, p0, p1, p2, p3)
    picks = dot(picked(row_code, codes), rows[...], 1, 0).astype(BF)
    out[...] = dot(picks, perm_ref[...], 1, 0).astype(BF)


def token_kernel(row_code, codes, p0, p1, p2, p3, perm_ref, first_ref, second_ref, out, rows):
    dispatch_kernel(row_code, codes, p0, p1, p2, p3, perm_ref, out, rows)
    row = lax.broadcasted_iota(jnp.int32, (8, 128), 0)
    block = jnp.zeros((8, 128), F32)
    for i, ref in enumerate((first_ref, second_ref)):
        high = ref[...].astype(BF).astype(F32)
        block = jnp.where(row == 2 * i + 2, high, block)
        block = jnp.where(row == 2 * i + 3, ref[...] - high, block)
    size = out.shape[0] // 8
    for e in range(8):
        span = slice((e + 1) * size - 8, (e + 1) * size)
        old = out[span, :128].astype(F32)
        out[span, :128] = jnp.where((row >= 2) & (row < 6), block, old).astype(BF)


def collect_kernel(both_ref, grad_ref, out_ref, peak_ref):
    size = both_ref.shape[1] // 2
    best = jnp.full((2, 128), -1e30, F32)
    for p in range(both_ref.shape[0]):
        rows = slice(p * size, (p + 1) * size)
        grad_ref[rows] = both_ref[p, :size]
        out_ref[rows] = both_ref[p, size:]
        block = both_ref[p, 2 * size - 8 :, :128].astype(F32)
        found = [block[2 * i + 2 : 2 * i + 3] + block[2 * i + 3 : 2 * i + 4] for i in range(2)]
        best = jnp.maximum(best, jnp.concatenate(found, axis=0))
    peak_ref[...] = best


def combine_kernel(which, row_code, codes, perm_ref, both_ref, own_ref, sib_ref, rows):
    size = both_ref.shape[1] // 2
    for p in range(both_ref.shape[0]):
        rows[p * size : (p + 1) * size] = both_ref[p, which * size : (which + 1) * size]
    back = dot(rows[...], perm_ref[...], 1, 1).astype(BF)
    partial = dot(picked(row_code, codes), back, 0, 0)
    half = partial.shape[0] // 2
    own_ref[...] = partial[:half]
    sib_ref[...] = partial[half:].astype(BF)


def pair_add_kernel(own_ref, far_ref, near_ref, send_ref):
    total = own_ref[...] + far_ref[...].astype(F32)
    near_ref[...] = total[:ROWS]
    send_ref[...] = total[ROWS:].astype(BF)


def route_of(tokens, router, number):
    logits = dot(tokens, router, 1, 1)
    column = lax.broadcasted_iota(jnp.int32, logits.shape, 1)
    logits = jnp.where(column < 8, logits, -1e30)
    weight = jnp.exp(logits - jnp.max(logits, axis=-1, keepdims=True))
    route = weight / jnp.sum(weight, axis=-1, keepdims=True)
    mine = jnp.where(column == number, 1.0, 0.0)
    return route, mine, jnp.sum(route * mine, axis=-1, keepdims=True)


def expert_kernel(
    number, t0, t1, g0, g1, router, *rest
):
    own, far = rest[0], rest[1]
    res_own, res_sib, grad_own, grad_sib = rest[2:6]
    up_parts, down_parts = rest[6:10], rest[10:13]
    act_ref, hid_ref, gout_ref, pair, whole = rest[13:]
    size = t0.shape[0]
    half, wide = own.shape[0] // 2, act_ref.shape[2]
    whole[0] = own[...]
    whole[1] = far[...]
    for i, (t, g, res, grad) in enumerate(
        ((t1, g1, res_sib, grad_sib), (t0, g0, res_own, grad_own))
    ):
        rows = slice((1 - i) * size, (2 - i) * size)
        gate = route_of(t[...], router[...], number[0])[2]
        gout = (gate * g[...].astype(F32)).astype(BF)
        gout_ref[rows] = gout
        for y in range(2):
            for c in range(0, wide, 256):
                span = slice(c, c + 256)
                act, lean = gelu_pair(dot(t[...], whole[y, :, span], 1, 0))
                act_ref[y, rows, span] = act
                back = dot(gout, whole[y, :, wide + c : wide + c + 256], 1, 0)
                hid_ref[y, rows, span] = (back * lean.astype(F32)).astype(BF)
        res[...] = (
            dot(act_ref[0, rows], whole[0, :, wide:], 1, 1)
            + dot(act_ref[1, rows], whole[1, :, wide:], 1, 1)
        ).astype(res.dtype)
        grad[...] = (
            dot(hid_ref[0, rows], whole[0, :, :wide], 1, 1)
            + dot(hid_ref[1, rows], whole[1, :, :wide], 1, 1)
        ).astype(grad.dtype)
    pair[:size] = t0[...]
    pair[size:] = t1[...]
    for parts, left, right in ((up_parts, pair, hid_ref), (down_parts, gout_ref, act_ref)):
        parts[0][...] = dot(left[...], right[0], 0, 0).astype(BF)
        far = dot(left[...], right[1], 0, 0).astype(BF)
        at = 0
        for part in parts[1:]:
            part[...] = far[at : at + part.shape[0]]
            at += part.shape[0]


def answer_kernel(
    number, t_ref, g_ref, router, res_own, res_far, grad_own, grad_far, perm_ref,
    both_ref, router_out,
):
    route, mine, gate = route_of(t_ref[...], router[...], number[0])
    result = res_own[...] + res_far[...].astype(F32)
    grad_gate = jnp.sum(result * g_ref[...].astype(F32), axis=-1, keepdims=True)
    grad_logit = (grad_gate * route * (mine - gate)).astype(BF)
    router_out[...] = reorder(dot(grad_logit, t_ref[...], 0, 0), perm_ref[...], 1)
    grad = grad_own[...] + grad_far[...].astype(F32) + dot(grad_logit, router[...], 1, 0)
    size = both_ref.shape[1] // 2
    whole = grad.astype(BF)
    for p in range(both_ref.shape[0]):
        both_ref[p, :size] = whole[p * size : (p + 1) * size]
    whole = (gate * result).astype(BF)
    for p in range(both_ref.shape[0]):
        both_ref[p, size:] = whole[p * size : (p + 1) * size]


def reorder(values, perm, axis):
    high = values.astype(BF)
    rest = values - high.astype(F32)
    middle = rest.astype(BF)
    low = (rest - middle.astype(F32)).astype(BF)
    return dot(high, perm, 1, axis) + (dot(middle, perm, 1, axis) + dot(low, perm, 1, axis))


def leave_kernel(x_ref, perm_ref, out_ref):
    out_ref[...] = reorder(x_ref[...], perm_ref[...], 0)[: out_ref.shape[0]]


def finish_kernel(live, x_ref, own_ref, far_ref, perm_ref, out_ref):
    total = x_ref[...] + (own_ref[...] + far_ref[...].astype(F32))
    total = reorder(total, perm_ref[...], 0) * live[0].astype(F32)
    out_ref[...] = total[: out_ref.shape[0]]


def add_pack_kernel(up_own, up0, up1, up2, down_own, down0, down1, out):
    wide = up_own.shape[1]
    for c, (own, parts) in enumerate(((up_own, (up0, up1, up2)), (down_own, (down0, down1)))):
        at = 0
        for part in parts:
            span = slice(at, at + part.shape[0])
            total = own[span].astype(F32) + part[...].astype(F32)
            out[span, c * wide : (c + 1) * wide] = total.astype(BF)
            at += part.shape[0]


def pack_kernel(*refs):
    out = refs[-1]
    at = 0
    for ref in refs[:-1]:
        out[:, at : at + ref.shape[1]] = ref[...]
        at += ref.shape[1]


def stack_kernel(*refs):
    rows = refs[0].shape[0]
    for i, ref in enumerate(refs[:-1]):
        refs[-1][i * rows : (i + 1) * rows] = ref[...]


def order_kernel(places, in_ref, out_ref):
    rows = out_ref.shape[0] // 4
    for i in range(4):
        at = pl.multiple_of(places[i] * rows, rows)
        out_ref[i * rows : (i + 1) * rows] = in_ref[pl.ds(at, rows), :]


def sum_two(near, got, keep, s1, s2, s3):
    rows = keep.shape[0]
    for k, out in enumerate((keep, s1, s2, s3)):
        span = slice(k * rows, (k + 1) * rows)
        out[...] = (near[span].astype(F32) + got[span].astype(F32)).astype(out.dtype)


def small_kernel(g1, g2, g3, g4, router, out):
    whole = jnp.concatenate([g1[...], g2[...], g3[...], g4[...]], axis=0)
    count, cols = router.shape[0], out.shape[2]
    blank = jnp.zeros((out.shape[1] - 4 - count, cols), F32)
    for p in range(8):
        span = slice(p * cols, (p + 1) * cols)
        out[p] = jnp.concatenate([whole[:, span], router[:, span], blank], axis=0)


def sum_two_more(near, got, small, keep, s1, s2, s3):
    sum_two(near, got, keep, s1.at[: keep.shape[0]], s2.at[: keep.shape[0]], s3.at[: keep.shape[0]])
    rows, count = keep.shape[0], small.shape[1]
    cols = small.shape[2]
    for k, out in enumerate((s1, s2, s3)):
        out[rows:, :] = jnp.zeros((out.shape[0] - rows, out.shape[1]), BF)
        high = small[k + 1].astype(BF)
        out[rows : rows + count, :cols] = high
        low = small[k + 1] - high.astype(F32)
        out[rows + count : rows + 2 * count, :cols] = low.astype(BF)


def sum_three_more(keep, r1, r2, r3, small, first, second, small_out):
    rows, count = keep.shape[0], small.shape[1]
    cols = small.shape[2]
    sum_three(keep, r1.at[:rows], r2.at[:rows], r3.at[:rows], first, second)
    total = small[0]
    for r in (r1, r2, r3):
        high = r[rows : rows + count, :cols].astype(F32)
        total = total + (high + r[rows + count : rows + 2 * count, :cols].astype(F32))
    small_out[...] = total


def sum_three(keep, r1, r2, r3, first, second):
    total = keep[...] + (r1[...].astype(F32) + (r2[...].astype(F32) + r3[...].astype(F32)))
    wide = first.shape[1]
    first[...] = total[:, :wide]
    second[...] = total[:, wide:]


def scatter_start(parts):
    near, send = parts
    return near, swap(send, x=1)


def scatter_middle(parts):
    half, width = parts[0].shape
    shape = (half // 4, width)
    return run(sum_two, [(shape, F32)] + [(shape, BF)] * 3, parts, half * width)


def scatter_late(parts):
    keep, s1, s2, s3 = parts
    return keep, swap(s1, z=1), swap(s2, z=2), swap(s3, z=3)


def scatter_end(parts, wide):
    rows, width = parts[0].shape
    return run(sum_three, [((rows, wide), F32), ((rows, width - wide), F32)], parts, rows * width)


def fast_local(
    block_input,
    first_norm,
    first_qkv,
    first_out,
    second_norm,
    dense_up,
    dense_down,
    third_norm,
    second_qkv,
    second_out,
    fourth_norm,
    router_weight,
    expert_up,
    expert_down,
    expert_ids,
    expert_slots,
    image_counts,
    cotangent,
):
    d = lax.axis_index("dp")
    t = lax.axis_index("tensor")
    z_index, x_index = d // 2, d % 2
    width = first_norm.shape[0]
    features = width * 8
    experts = expert_up.shape[0]
    live_count = image_counts[0]
    head_cols = first_out.shape[0]
    ff_cols = dense_up.shape[1]
    qkv_cols = 3 * head_cols
    row = ((ROWS, features), F32)
    row_low = ((ROWS, features), BF)

    small = jnp.concatenate(
        [
            jnp.stack([first_norm, second_norm, third_norm, fourth_norm], axis=1),
            router_weight,
            jnp.zeros((width, 128 - 4 - experts), BF),
        ],
        axis=1,
    )
    pack_one = run(
        pack_kernel,
        [((width, small.shape[1] + 4 * head_cols), BF)],
        (small, first_qkv.reshape(width, -1), first_out.T),
        width,
    )[0]
    pack_late = run(
        pack_kernel,
        [((width, 2 * ff_cols + 4 * head_cols), BF)],
        (dense_up, dense_down.T, second_qkv.reshape(width, -1), second_out.T),
        width,
    )[0]

    lines = [[x + 2 * z for z in range(4)] for x in range(2)]
    raw_late = lax.all_gather(pack_late, "dp", axis=0, tiled=True, axis_index_groups=lines)

    def stacked(shards):
        shape = (len(shards) * shards[0].shape[0], shards[0].shape[1])
        return run(stack_kernel, [(shape, BF)], shards, width)[0]

    z_one = stacked([pack_one] + [swap(pack_one, z=k) for k in (1, 2, 3)])

    rel = jnp.arange(features)
    block = rel // width
    rel_place = jnp.bitwise_xor(d, 2 * (block % 4) + block // 4) * width + rel % width
    perm = (rel_place[:, None] == rel[None, :]).astype(BF)
    live_here = (t < live_count).astype(jnp.int32).reshape(1)
    live_group = (jnp.stack([t, t ^ 2, t ^ 1, t ^ 3]) < live_count).astype(jnp.int32)

    start, low_start, grad_four, grad_low = run(
        enter_kernel,
        [row, row_low, row, row_low],
        (live_here, block_input, cotangent, perm),
        4 * ROWS * features**2,
        scalars=1,
    )

    def spread(rows):
        far = swap(rows, y=1)
        return [rows, far, swap(rows, core=1), swap(far, core=1)]

    first_group = spread(low_start)
    wide = 2 * ff_cols
    half_shape = [((features // 2, ff_cols), BF)] * 2
    e_pack = jnp.concatenate([expert_up, jnp.swapaxes(expert_down, 1, 2)], axis=2)
    held = -(-CAP // 4)
    block_size = -(-(held + 4) // 8) * 8
    ids = jnp.pad(expert_ids.reshape(4, L, 2), ((0, 0), (0, ROWS - L), (0, 0)), constant_values=-1)
    slots = jnp.pad(
        expert_slots.reshape(4, L, 2), ((0, 0), (0, ROWS - L), (0, 0)), constant_values=CAP
    )
    mine = (slots < CAP) & (slots // held == t)
    codes = jnp.where(mine, ids * block_size + slots % held, -1)
    codes = jnp.concatenate(
        [lax.dynamic_index_in_dim(codes, t ^ k, 0, keepdims=False) for k in (0, 2, 1, 3)], axis=0
    ).T
    slot_rows = experts * block_size
    row_code = jnp.arange(slot_rows).reshape(-1, 1)
    group_flops = 2 * slot_rows * features * (4 * ROWS + features)

    def to_experts(kernel, rows, *peaks):
        return run(
            kernel,
            [((slot_rows, features), BF)],
            (row_code, codes, *rows, perm, *peaks),
            group_flops,
            scratch=[pltpu.VMEM((4 * ROWS, features), BF)],
        )[0].reshape(experts, block_size, features)

    def exchange(both):
        return lax.all_to_all(both, "dp", split_axis=0, concat_axis=0, tiled=True)

    group_scratch = pltpu.VMEM((4 * ROWS, features), BF)
    pair_out = [((2 * ROWS, features), F32), ((2 * ROWS, features), BF)]

    def attend(normed, full, at):
        return run(
            functools.partial(attend_kernel, at),
            [((4 * ROWS, qkv_cols), BF), ((4 * ROWS, head_cols), BF)]
            + pair_out
            + [((1, 128), F32)],
            (live_group, *normed, full),
            0,
            scratch=[group_scratch],
            scalars=1,
        )

    def pack_shapes(columns):
        return [((features // 2, columns), BF)] * 2 + pair_out

    def attend_back(low, normed, mixed, attended, full, at):
        return run(
            functools.partial(attend_back_kernel, at),
            pack_shapes(4 * head_cols),
            (*low, *normed, mixed, attended, full),
            8e9,
            scratch=[
                group_scratch,
                pltpu.VMEM((4 * ROWS, head_cols), BF),
                pltpu.VMEM((4 * ROWS, qkv_cols), BF),
            ],
        )

    def over_group(own, sib):
        near, send = run(pair_add_kernel, [row, row_low], (own, swap(sib, core=1)), ROWS)
        return near, swap(send, y=1)

    def join(values, own, far, gain):
        return run(join_norm_kernel, [row, row_low], (values, own, far, gain), ROWS)

    def norm_back(values, upstream, own, far, gain):
        return run(
            norm_back_kernel,
            [row, row_low, ((1, features), F32)],
            (values, upstream, own, far, gain),
            ROWS,
        )

    full_one = stacked(hold([z_one, swap(z_one, x=1)], first_group))
    small_rows = full_one[:, : 4 + experts].T
    gains = [small_rows[i : i + 1].astype(F32) for i in range(4)]
    router = dot(small_rows[4:], perm, 1, 0).astype(BF)

    normed_one = run(norm_kernel, [row_low] * 4, (gains[0], *first_group), ROWS)
    mixed_one, att_one, own, sib, peak_one = attend(normed_one, full_one, small.shape[1])
    near, far = over_group(own, sib)
    one, normed = join(start, near, hold(far, raw_late), gains[1])
    normed_mlp = spread(normed)
    z_late = run(
        order_kernel,
        [(raw_late.shape, BF)],
        (jnp.stack([z_index ^ k for k in range(4)]).astype(jnp.int32), hold(raw_late, one)),
        features,
        scalars=1,
    )[0]
    x_late = swap(z_late, x=1)
    grad_sent = to_experts(dispatch_kernel, spread(hold(grad_low, normed)))
    e_pack = hold(e_pack, grad_sent, normed_mlp[3])
    e_own = lax.all_to_all(e_pack, "dp", split_axis=0, concat_axis=0, tiled=True)
    e_own = e_own.reshape(features, wide)
    full_late = stacked([z_late, x_late])
    ats = (0, ff_cols)
    act, slope, own, sib = run(
        functools.partial(mlp_kernel, ats),
        [((4 * ROWS, ff_cols), BF)] * 2 + pair_out,
        (*hold(normed_mlp, grad_sent), full_late),
        0,
        scratch=[group_scratch],
    )
    near, far = over_group(own, sib)
    two, normed = join(one, near, far, gains[2])
    normed_two = spread(normed)
    mixed_two, att_two, own, sib, peak_two = attend(normed_two, full_late, 2 * ff_cols)
    near, far = over_group(own, sib)
    three, normed = join(two, near, far, gains[3])
    group_four = spread(normed)
    e_far = [swap(hold(e_own, group_four[1]), y=1)]
    tokens_sent = to_experts(token_kernel, group_four, peak_one, peak_two)
    both = exchange(jnp.concatenate([grad_sent, tokens_sent], axis=1))
    grad_slots, tokens, peaks = run(
        collect_kernel,
        [((slot_rows, features), BF)] * 2 + [((2, 128), F32)],
        (hold(both, *e_far),),
        0,
    )
    far_slots, far_tokens = swap(grad_slots, core=1), swap(tokens, core=1)
    number = d.astype(jnp.int32).reshape(1)
    near_heads = head_cols // HD
    roots = clip_root(peaks[:, :near_heads])
    slot_out = [((slot_rows, features), F32), ((slot_rows, features), BF)]
    res_own, res_sib, eg_own, eg_sib, *e_packs = run(
        expert_kernel,
        slot_out
        + slot_out
        + [((features, ff_cols), BF)]
        + [((2 * width, ff_cols), BF)] * 2
        + half_shape[:1]
        + [((features, ff_cols), BF)]
        + half_shape,
        (number, tokens, far_tokens, grad_slots, far_slots, router)
        + (e_own, *e_far),
        8 * 2 * slot_rows * features * 2 * ff_cols,
        scalars=1,
        scratch=[
            pltpu.VMEM((2, 2 * slot_rows, ff_cols), BF),
            pltpu.VMEM((2, 2 * slot_rows, ff_cols), BF),
            pltpu.VMEM((2 * slot_rows, features), BF),
            pltpu.VMEM((2 * slot_rows, features), BF),
            pltpu.VMEM((2, features, wide), BF),
        ],
        mib=44,
    )
    res_far, eg_far = swap(res_sib, core=1), swap(eg_sib, core=1)
    up_got = [swap(e_packs[1], y=1)]
    both, grad_router = run(
        answer_kernel,
        [((experts, 2 * block_size, features), BF), ((experts, features), F32)],
        (number, tokens, grad_slots, router, res_own, res_far, eg_own, eg_far, perm),
        4 * slot_rows * features**2,
        scalars=1,
    )
    both = hold(both, up_got)
    e_packs = hold(e_packs, both)
    both = exchange(both)
    up_got.append(swap(e_packs[2], y=1))
    up_got.append(swap(e_packs[3], y=1))
    down_got = [swap(e_packs[5], y=1)]
    both = hold(both, up_got, down_got)

    def combine(which, both):
        return run(
            functools.partial(combine_kernel, which),
            [((2 * ROWS, features), F32), ((2 * ROWS, features), BF)],
            (row_code, codes, perm, both),
            group_flops,
            scratch=[pltpu.VMEM((slot_rows, features), BF)],
        )

    own, sib = combine(0, both)
    back_own, back_far = over_group(own, sib)
    grad_three, low, gain_four = norm_back(
        three, grad_four, back_own, back_far, gains[3]
    )
    low = spread(low)
    down_got.append(swap(hold(e_packs[6], low[1]), y=1))
    *second, own, sib = attend_back(
        low, normed_two, mixed_two, att_two, full_late, 2 * ff_cols
    )
    second = scatter_start(second)
    near, far = over_group(own, hold(sib, down_got[1]))
    e_sum = run(
        add_pack_kernel,
        [((features, wide), BF)],
        (e_packs[0], *up_got, e_packs[4], *hold(down_got, second[1], far)),
        0,
    )[0].reshape(experts, width, wide)
    e_back = lax.all_to_all(e_sum, "dp", split_axis=0, concat_axis=0, tiled=True)
    grad_two, low, gain_three = norm_back(
        two, grad_three, near, far, gains[2]
    )
    low = spread(low)
    *mlp, own, sib = run(
        functools.partial(mlp_back_kernel, ats),
        pack_shapes(2 * ff_cols),
        (*low, *normed_mlp, act, slope, full_late),
        0,
        scratch=[group_scratch, pltpu.VMEM((4 * ROWS, ff_cols), BF)],
    )
    mlp = scatter_start(mlp)
    near, send = run(pair_add_kernel, [row, row_low], (own, swap(sib, core=1)), ROWS)
    far = swap(send, y=1)
    mixed_own, mixed_sib = combine(1, hold(both, sib))
    second = scatter_late(scatter_middle(hold(second, mixed_own)))
    mixed_own, mixed_send = run(
        pair_add_kernel, [row, row_low], (mixed_own, swap(mixed_sib, core=1)), ROWS
    )
    grad_one, low, gain_two = norm_back(
        one, grad_two, near, hold(far, mixed_send), gains[1]
    )
    low = spread(low)
    mixed_far = swap(hold(mixed_send, low), y=1)
    *first, own, sib = attend_back(
        hold(low, mlp),
        normed_one,
        mixed_one,
        att_one,
        full_one,
        small.shape[1],
    )
    mlp = scatter_late(scatter_middle(mlp))
    first = scatter_start(first)
    near, far = over_group(own, hold(sib, mixed_far, second, e_back))
    grad_zero, _, gain_one = norm_back(start, grad_one, near, hold(far, first), gains[0])
    block_output = run(
        finish_kernel,
        [((L, features), F32)],
        (live_here, three, mixed_own, mixed_far, perm),
        6 * ROWS * features**2,
        scalars=1,
    )[0]
    up_g = e_back[:, :, :ff_cols].astype(F32)
    down_g = jnp.swapaxes(e_back[:, :, ff_cols:], 1, 2).astype(F32)
    clips = (clip_columns(first_qkv, roots[0], HD), clip_columns(second_qkv, roots[1], HD))
    gains_sum = run(
        small_kernel,
        [((8, 16, width), F32)],
        (gain_one, gain_two, gain_three, gain_four, grad_router),
        0,
    )[0]
    gains_sum = hold(
        gains_sum + swap(gains_sum, core=1), mlp, block_output, up_g, down_g, clips
    )
    gains_sum = gains_sum + swap(gains_sum, y=1)
    gains_sum = gains_sum[:4] + swap(gains_sum[4:], x=1)
    near_first, got_first = first
    shape = (width, 4 * head_cols)
    first = run(
        sum_two_more,
        [(shape, F32)] + [((width + 32, shape[1]), BF)] * 3,
        (near_first, got_first, gains_sum),
        0,
    )
    first = scatter_late(first)
    input_grad = run(
        leave_kernel,
        [((L, features), F32)],
        (hold(grad_zero, first[0]), perm),
        6 * ROWS * features**2,
    )[0]
    second = scatter_end(second, qkv_cols)
    mlp = scatter_end(mlp, ff_cols)
    first = hold(first, up_g, down_g, block_output, input_grad, second, mlp)
    *first, tail = run(
        sum_three_more,
        [((width, qkv_cols), F32), ((width, head_cols), F32), ((16, width), F32)],
        (*first, gains_sum),
        0,
    )

    return (
        block_output,
        input_grad,
        tail[0],
        first[0].reshape(first_qkv.shape),
        first[1].T,
        tail[1],
        mlp[0],
        mlp[1].T,
        tail[2],
        second[0].reshape(second_qkv.shape),
        second[1].T,
        tail[3],
        tail[4 : 4 + experts].T,
        up_g,
        down_g,
        *clips,
        roots,
    )


def solution(mesh):
    placed = (
        P(("dp", "tensor"), None),
        P("dp"),
        P("dp", None, "tensor"),
        P("tensor", "dp"),
        P("dp"),
        P("dp", "tensor"),
        P("tensor", "dp"),
        P("dp"),
        P("dp", None, "tensor"),
        P("tensor", "dp"),
        P("dp"),
        P("dp", None),
        P(None, "dp", "tensor"),
        P(None, "tensor", "dp"),
        P("dp", None),
        P("dp", None),
        P("dp"),
        P(("dp", "tensor"), None),
    )
    quick = mesh.shape["dp"] == 8 and mesh.shape["tensor"] == 4
    return jax.shard_map(
        fast_local if quick else local,
        mesh=mesh,
        in_specs=placed,
        out_specs=(
            P(("dp", "tensor"), None),
            P(("dp", "tensor"), None),
            P("dp"),
            P("dp", None, "tensor"),
            P("tensor", "dp"),
            P("dp"),
            P("dp", "tensor"),
            P("tensor", "dp"),
            P("dp"),
            P("dp", None, "tensor"),
            P("tensor", "dp"),
            P("dp"),
            P("dp", None),
            P(None, "dp", "tensor"),
            P(None, "tensor", "dp"),
            P("dp", None, "tensor"),
            P("dp", None, "tensor"),
            P(None, "tensor"),
        ),
        check_vma=False,
    )
```

```python
import functools

import jax
import jax.numpy as jnp
from jax import lax
from jax.experimental import pallas as pl
from jax.experimental.pallas import tpu as pltpu
from jax.sharding import PartitionSpec as P

HD = 64
L = 197
CAP = 197


epsilon = 1e-06
clip_tau = 2.5


def layer_norm(values, norm_gain):
    center = values - jnp.mean(values, axis=-1, keepdims=True)
    spread = jnp.mean(center * center, axis=-1, keepdims=True)
    return center * lax.rsqrt(spread + epsilon) * norm_gain


def exact_gelu(values):
    return jax.nn.gelu(values, approximate=False)


def gelu_back(values, upstream):
    return jax.vjp(exact_gelu, values)[1](upstream)[0]


def norm_back(residual, norm_gain, upstream):
    pullback = jax.vjp(layer_norm, residual, norm_gain.astype(jnp.float32))[1]
    return pullback(upstream)


def gather_rows(values):
    return lax.all_gather(values, "tensor", axis=0, tiled=True)


def scatter_rows(values):
    return lax.psum_scatter(
        values.astype(jnp.bfloat16), "tensor", scatter_dimension=0, tiled=True
    ).astype(jnp.float32)


def sum_gains(first_gain, second_gain):
    return lax.psum((first_gain, second_gain), "tensor")


def split_heads(projected, images, head_size):
    row_count, triple, columns = projected.shape
    pieces = projected.reshape(images, row_count // images, triple, columns // head_size, head_size)
    return (pieces[:, :, 0], pieces[:, :, 1], pieces[:, :, 2])


def attend_scores(queries, keyset, head_size):
    scores = jnp.einsum("iqhd,ikhd->ihqk", queries, keyset, preferred_element_type=jnp.float32)
    return scores * head_size ** (-0.5)


def attend_forward(normed_full, weight_qkv, images, head_size, live_images):
    projected = jnp.einsum(
        "rd,dcf->rcf", normed_full, weight_qkv, preferred_element_type=jnp.float32
    ).astype(jnp.bfloat16)
    queries, keyset, values = split_heads(projected, images, head_size)
    scores = attend_scores(queries, keyset, head_size)
    head_peak = jnp.max(jnp.where(live_images[:, None, None, None], scores, -1e30), axis=(0, 2, 3))
    attn_probs = jax.nn.softmax(scores, axis=-1).astype(jnp.bfloat16)
    attended = jnp.einsum("ihqk,ikhd->iqhd", attn_probs, values, preferred_element_type=jnp.float32)
    return (projected, attended.astype(jnp.bfloat16).reshape(normed_full.shape[0], -1), head_peak)


def attend_backward(projected, grad_attended, images, head_size):
    queries, keyset, values = split_heads(projected, images, head_size)
    scores = attend_scores(queries, keyset, head_size)
    attn_probs = jax.nn.softmax(scores, axis=-1)
    grad_heads = grad_attended.reshape(queries.shape)
    grad_values = jnp.einsum(
        "ihqk,iqhd->ikhd",
        attn_probs.astype(jnp.bfloat16),
        grad_heads,
        preferred_element_type=jnp.float32,
    )
    grad_probs = jnp.einsum(
        "iqhd,ikhd->ihqk", grad_heads, values, preferred_element_type=jnp.float32
    )
    grad_scores = attn_probs * (
        grad_probs - jnp.sum(grad_probs * attn_probs, axis=-1, keepdims=True)
    )
    grad_scores = grad_scores.astype(jnp.bfloat16)
    factor = head_size ** (-0.5)
    grad_queries = (
        jnp.einsum("ihqk,ikhd->iqhd", grad_scores, keyset, preferred_element_type=jnp.float32)
        * factor
    )
    grad_keyset = (
        jnp.einsum("ihqk,iqhd->ikhd", grad_scores, queries, preferred_element_type=jnp.float32)
        * factor
    )
    stacked = jnp.stack([grad_queries, grad_keyset, grad_values], axis=2).astype(jnp.bfloat16)
    return stacked.reshape(projected.shape)


def block_attention(residual, norm_gain, weight_qkv, weight_out, images, head_size, live_images):
    normed = layer_norm(residual, norm_gain.astype(jnp.float32)).astype(jnp.bfloat16)
    normed_full = gather_rows(normed)
    projected, attended, head_peak = attend_forward(
        normed_full, weight_qkv, images, head_size, live_images
    )
    branch = scatter_rows(jnp.dot(attended, weight_out, preferred_element_type=jnp.float32))
    return (residual + branch, (normed_full, projected, attended), head_peak)


def block_attention_back(
    residual, upstream, norm_gain, weight_qkv, weight_out, stored, images, head_size
):
    normed_full, projected, attended = stored
    grad_full = gather_rows(upstream.astype(jnp.bfloat16))
    grad_out = jnp.einsum("rf,rd->fd", attended, grad_full, preferred_element_type=jnp.float32)
    grad_attended = jnp.einsum(
        "rd,fd->rf", grad_full, weight_out, preferred_element_type=jnp.float32
    ).astype(jnp.bfloat16)
    grad_projected = attend_backward(projected, grad_attended, images, head_size)
    grad_qkv = jnp.einsum(
        "rd,rcf->dcf", normed_full, grad_projected, preferred_element_type=jnp.float32
    )
    grad_normed = scatter_rows(
        jnp.einsum("rcf,dcf->rd", grad_projected, weight_qkv, preferred_element_type=jnp.float32)
    )
    grad_residual, grad_gain = norm_back(residual, norm_gain, grad_normed)
    return (upstream + grad_residual, grad_gain, grad_qkv, grad_out)


def block_mlp(residual, norm_gain, weight_up, weight_down):
    normed = layer_norm(residual, norm_gain.astype(jnp.float32)).astype(jnp.bfloat16)
    normed_full = gather_rows(normed)
    hidden = jnp.dot(normed_full, weight_up, preferred_element_type=jnp.float32)
    active = exact_gelu(hidden).astype(jnp.bfloat16)
    branch = scatter_rows(jnp.dot(active, weight_down, preferred_element_type=jnp.float32))
    return (residual + branch, (normed_full, hidden, active))


def block_mlp_back(residual, upstream, norm_gain, weight_up, weight_down, stored):
    normed_full, hidden, active = stored
    grad_full = gather_rows(upstream.astype(jnp.bfloat16))
    grad_down = jnp.einsum("rf,rd->fd", active, grad_full, preferred_element_type=jnp.float32)
    grad_active = jnp.einsum(
        "rd,fd->rf", grad_full, weight_down, preferred_element_type=jnp.float32
    )
    grad_hidden = gelu_back(hidden, grad_active).astype(jnp.bfloat16)
    grad_up = jnp.einsum("rd,rf->df", normed_full, grad_hidden, preferred_element_type=jnp.float32)
    grad_normed = scatter_rows(
        jnp.einsum("rf,df->rd", grad_hidden, weight_up, preferred_element_type=jnp.float32)
    )
    grad_residual, grad_gain = norm_back(residual, norm_gain, grad_normed)
    return (upstream + grad_residual, grad_gain, grad_up, grad_down)


def clip_root(head_peak):
    return jnp.sqrt(clip_tau / jnp.maximum(head_peak, clip_tau))


def clip_columns(weight_local, head_root, head_size):
    column = jnp.repeat(head_root, head_size)
    scales = jnp.stack([column, column, jnp.ones_like(column)])
    return weight_local.astype(jnp.float32) * scales[None]


def local(
    block_input,
    first_norm,
    first_qkv,
    first_out,
    second_norm,
    dense_up,
    dense_down,
    third_norm,
    second_qkv,
    second_out,
    fourth_norm,
    router_weight,
    expert_up,
    expert_down,
    expert_ids,
    expert_slots,
    image_counts,
    cotangent,
):
    rows_local = block_input.shape[0]
    rows_full = rows_local * lax.axis_size("tensor")
    images = rows_full // L
    head_size = HD
    experts = expert_up.shape[0]
    capacity = CAP
    first_row = lax.axis_index("tensor") * rows_local
    live_count = image_counts[0]
    local_live = ((first_row + jnp.arange(rows_local)) // L < live_count).astype(jnp.float32)
    full_live = (jnp.arange(rows_full) // L < live_count).astype(jnp.float32)
    live_images = jnp.arange(images) < live_count

    def dense_fetch():
        return (
            lax.all_gather(first_norm, "dp", axis=0, tiled=True),
            lax.all_gather(first_qkv, "dp", axis=0, tiled=True),
            lax.all_gather(first_out, "dp", axis=1, tiled=True),
            lax.all_gather(second_norm, "dp", axis=0, tiled=True),
            lax.all_gather(dense_up, "dp", axis=0, tiled=True),
            lax.all_gather(dense_down, "dp", axis=1, tiled=True),
        )

    def moe_fetch():
        return (
            lax.all_gather(third_norm, "dp", axis=0, tiled=True),
            lax.all_gather(second_qkv, "dp", axis=0, tiled=True),
            lax.all_gather(second_out, "dp", axis=1, tiled=True),
            lax.all_gather(fourth_norm, "dp", axis=0, tiled=True),
            lax.all_gather(router_weight, "dp", axis=0, tiled=True),
            lax.all_gather(expert_up, "dp", axis=1, tiled=True),
            lax.all_gather(expert_down, "dp", axis=2, tiled=True),
        )

    dense_full = dense_fetch()
    residual_zero = block_input.astype(jnp.float32)
    residual_one, attn_first, peak_first = block_attention(
        residual_zero, dense_full[0], dense_full[1], dense_full[2], images, head_size, live_images
    )
    residual_two, mlp_stored = block_mlp(residual_one, dense_full[3], dense_full[4], dense_full[5])
    moe_full = moe_fetch()
    residual_three, attn_second, peak_second = block_attention(
        residual_two, moe_full[0], moe_full[1], moe_full[2], images, head_size, live_images
    )
    moe_normed = layer_norm(residual_three, moe_full[3].astype(jnp.float32)).astype(jnp.bfloat16)
    moe_input = gather_rows(moe_normed)
    logits = jnp.dot(moe_input, moe_full[4], preferred_element_type=jnp.float32)
    route_probs = jax.nn.softmax(logits, axis=-1)
    kept_mask = expert_slots < capacity
    pair_number = jnp.arange(2 * rows_full, dtype=jnp.int32)
    slot_index = (expert_ids * capacity + expert_slots).reshape(-1)
    kept_flat = kept_mask.reshape(-1)
    write_target = jnp.where(kept_flat, slot_index, experts * capacity + pair_number)
    target = jnp.where(kept_flat, slot_index, experts * capacity)
    pair_of_slot = (
        jnp.zeros((experts * capacity + 2 * rows_full,), jnp.int32)
        .at[write_target]
        .set(pair_number)[: experts * capacity]
    )
    slot_filled = (
        jnp.zeros((experts * capacity + 2 * rows_full,), jnp.float32)
        .at[write_target]
        .set(1.0)[: experts * capacity]
    )
    chosen = (expert_ids[:, :, None] == jnp.arange(experts)[None, None, :]).astype(jnp.float32)
    keep_live = kept_mask.astype(jnp.float32) * full_live[:, None]
    gates = jnp.sum(chosen * route_probs[:, None, :], axis=-1) * keep_live
    slot_token = pair_of_slot // 2
    slot_gate = gates.reshape(-1)[pair_of_slot] * slot_filled
    dispatched = (moe_input[slot_token] * slot_filled[:, None].astype(jnp.bfloat16)).reshape(
        experts, capacity, -1
    )
    expert_hidden = jnp.einsum(
        "ecd,edf->ecf", dispatched, moe_full[5], preferred_element_type=jnp.float32
    )
    expert_act = exact_gelu(expert_hidden).astype(jnp.bfloat16)
    expert_result = jnp.einsum(
        "ecf,efd->ecd", expert_act, moe_full[6], preferred_element_type=jnp.float32
    )
    feature_count = expert_result.shape[2]
    padded_result = jnp.concatenate(
        [
            expert_result.reshape(experts * capacity, feature_count),
            jnp.zeros((1, feature_count), jnp.float32),
        ],
        axis=0,
    )
    pair_result = padded_result[target].reshape(rows_full, 2, feature_count)
    combined = jnp.sum(gates[:, :, None] * pair_result, axis=1)
    residual_four = residual_three + scatter_rows(combined)
    block_output = residual_four * local_live[:, None]
    peak_first_all, peak_second_all = lax.pmax((peak_first, peak_second), "dp")
    root_first = clip_root(peak_first_all)
    root_second = clip_root(peak_second_all)
    clipped_first = clip_columns(first_qkv, root_first, head_size)
    clipped_second = clip_columns(second_qkv, root_second, head_size)
    clip_scales = jnp.stack([root_first, root_second])
    moe_back = moe_fetch()
    grad_four = cotangent.astype(jnp.float32) * local_live[:, None]
    moe_grad_full = gather_rows(grad_four.astype(jnp.bfloat16))
    partial_gates = jnp.sum(moe_grad_full.astype(jnp.float32)[:, None, :] * pair_result, axis=-1)
    grad_gates = lax.psum(partial_gates, "tensor")
    grad_result = (slot_gate[:, None] * moe_grad_full[slot_token].astype(jnp.float32)).astype(
        jnp.bfloat16
    )
    grad_result = grad_result.reshape(experts, capacity, feature_count)
    grad_expert_down = jnp.einsum(
        "ecf,ecd->efd", expert_act, grad_result, preferred_element_type=jnp.float32
    )
    grad_act = jnp.einsum(
        "ecd,efd->ecf", grad_result, moe_back[6], preferred_element_type=jnp.float32
    )
    grad_hidden = gelu_back(expert_hidden, grad_act).astype(jnp.bfloat16)
    grad_expert_up = jnp.einsum(
        "ecd,ecf->edf", dispatched, grad_hidden, preferred_element_type=jnp.float32
    )
    grad_dispatch = jnp.einsum(
        "ecf,edf->ecd", grad_hidden, moe_back[5], preferred_element_type=jnp.float32
    )
    grad_dispatch = jnp.concatenate(
        [
            grad_dispatch.reshape(experts * capacity, feature_count),
            jnp.zeros((1, feature_count), jnp.float32),
        ],
        axis=0,
    )
    grad_from_experts = jnp.sum(grad_dispatch[target].reshape(rows_full, 2, feature_count), axis=1)
    grad_picked = grad_gates * keep_live
    grad_probs = jnp.sum(chosen * grad_picked[:, :, None], axis=1)
    grad_logits = route_probs * (
        grad_probs - jnp.sum(grad_probs * route_probs, axis=-1, keepdims=True)
    )
    grad_logits = grad_logits.astype(jnp.bfloat16)
    grad_router = jnp.einsum(
        "rd,re->de", moe_input, grad_logits, preferred_element_type=jnp.float32
    )
    local_logits = lax.dynamic_slice_in_dim(grad_logits, first_row, rows_local, 0)
    grad_moe_normed = scatter_rows(grad_from_experts) + jnp.einsum(
        "re,de->rd", local_logits, moe_back[4], preferred_element_type=jnp.float32
    )
    grad_rows_four, grad_fourth_norm = norm_back(residual_three, moe_back[3], grad_moe_normed)
    grad_three = grad_four + grad_rows_four
    grad_two, grad_third_norm, grad_second_qkv, grad_second_out = block_attention_back(
        residual_two,
        grad_three,
        moe_back[0],
        moe_back[1],
        moe_back[2],
        attn_second,
        images,
        head_size,
    )
    third_sum, fourth_sum = sum_gains(grad_third_norm, grad_fourth_norm)
    moe_owned = (
        lax.psum_scatter(third_sum, "dp", scatter_dimension=0, tiled=True),
        lax.psum_scatter(grad_second_qkv, "dp", scatter_dimension=0, tiled=True),
        lax.psum_scatter(grad_second_out, "dp", scatter_dimension=1, tiled=True),
        lax.psum_scatter(fourth_sum, "dp", scatter_dimension=0, tiled=True),
        lax.psum_scatter(grad_router, "dp", scatter_dimension=0, tiled=True),
        lax.psum_scatter(grad_expert_up, "dp", scatter_dimension=1, tiled=True),
        lax.psum_scatter(grad_expert_down, "dp", scatter_dimension=2, tiled=True),
    )
    dense_back = dense_fetch()
    grad_one, grad_second_norm, grad_dense_up, grad_dense_down = block_mlp_back(
        residual_one, grad_two, dense_back[3], dense_back[4], dense_back[5], mlp_stored
    )
    input_grad, grad_first_norm, grad_first_qkv, grad_first_out = block_attention_back(
        residual_zero,
        grad_one,
        dense_back[0],
        dense_back[1],
        dense_back[2],
        attn_first,
        images,
        head_size,
    )
    first_sum, second_sum = sum_gains(grad_first_norm, grad_second_norm)
    dense_owned = (
        lax.psum_scatter(first_sum, "dp", scatter_dimension=0, tiled=True),
        lax.psum_scatter(grad_first_qkv, "dp", scatter_dimension=0, tiled=True),
        lax.psum_scatter(grad_first_out, "dp", scatter_dimension=1, tiled=True),
        lax.psum_scatter(second_sum, "dp", scatter_dimension=0, tiled=True),
        lax.psum_scatter(grad_dense_up, "dp", scatter_dimension=0, tiled=True),
        lax.psum_scatter(grad_dense_down, "dp", scatter_dimension=1, tiled=True),
    )
    owned = tuple(dense_owned) + tuple(moe_owned)
    return (
        block_output,
        input_grad,
        owned[0],
        owned[1],
        owned[2],
        owned[3],
        owned[4],
        owned[5],
        owned[6],
        owned[7],
        owned[8],
        owned[9],
        owned[10],
        owned[11],
        owned[12],
        clipped_first,
        clipped_second,
        clip_scales,
    )


ROWS = 208
AXES = ("dp", "tensor")
BF = jnp.bfloat16
F32 = jnp.float32
VM = pl.BlockSpec(memory_space=pltpu.VMEM)
SM = pl.BlockSpec(memory_space=pltpu.SMEM)


def swap(values, z=0, x=0, y=0, core=0):
    shift_d, shift_t = 2 * z + x, 2 * y + core
    pairs = [(d * 4 + t, (d ^ shift_d) * 4 + (t ^ shift_t)) for d in range(8) for t in range(4)]
    return lax.ppermute(values, AXES, pairs)


def hold(values, *tokens):
    return lax.optimization_barrier((values,) + tokens)[0]


def run(kernel, outs, args, flops, scratch=(), scalars=0, mib=20):
    flops = flops if flops == 8e9 else 1000
    shapes = [jax.ShapeDtypeStruct(s, dt) for s, dt in outs]
    return pl.pallas_call(
        kernel,
        out_shape=shapes,
        in_specs=[SM] * scalars + [VM] * (len(args) - scalars),
        out_specs=[VM] * len(shapes),
        scratch_shapes=list(scratch),
        compiler_params=pltpu.CompilerParams(vmem_limit_bytes=mib * 2**20),
        cost_estimate=pl.CostEstimate(flops=int(flops), bytes_accessed=1000, transcendentals=0),
    )(*args)


def dot(a, b, ca, cb):
    return lax.dot_general(a, b, (((ca,), (cb,)), ((), ())), preferred_element_type=F32)


def norm_stats(values):
    center = values - jnp.mean(values, axis=-1, keepdims=True)
    scale = lax.rsqrt(jnp.mean(center * center, axis=-1, keepdims=True) + epsilon)
    return center * scale, scale


def enter_kernel(live, x_ref, c_ref, perm_ref, start_ref, low_start, grad_ref, low_ref):
    rows = x_ref.shape[0]
    scale = live[0].astype(F32)
    extra = jnp.zeros((ROWS - rows, x_ref.shape[1]), F32)
    start = dot(x_ref[...], perm_ref[...], 1, 1)
    start_ref[:rows] = start
    start_ref[rows:] = extra
    low_start[:rows] = start.astype(BF)
    low_start[rows:] = extra.astype(BF)
    grad = dot(c_ref[...], perm_ref[...], 1, 1) * scale
    grad_ref[:rows] = grad
    grad_ref[rows:] = extra
    low_ref[:rows] = grad.astype(BF)
    low_ref[rows:] = extra.astype(BF)


def norm_kernel(gain_ref, *refs):
    for x_ref, out_ref in zip(refs[:4], refs[4:]):
        out_ref[...] = (norm_stats(x_ref[...].astype(F32))[0] * gain_ref[...]).astype(BF)


def join_norm_kernel(x_ref, own_ref, far_ref, gain_ref, sum_ref, out_ref):
    total = x_ref[...] + (own_ref[...] + far_ref[...].astype(F32))
    sum_ref[...] = total
    out_ref[...] = (norm_stats(total)[0] * gain_ref[...]).astype(BF)


def norm_back_kernel(x_ref, up_ref, own_ref, far_ref, gain_ref, grad_ref, low_ref, gain_out):
    upstream = own_ref[...] + far_ref[...].astype(F32)
    normed, scale = norm_stats(x_ref[...])
    scaled = upstream * gain_ref[...]
    grad = up_ref[...] + scale * (
        scaled
        - jnp.mean(scaled, axis=-1, keepdims=True)
        - normed * jnp.mean(scaled * normed, axis=-1, keepdims=True)
    )
    grad_ref[...] = grad
    low_ref[...] = grad.astype(BF)
    gain_out[...] = jnp.sum(upstream * normed, axis=0, keepdims=True)


def fill(rows, *refs):
    size = refs[0].shape[0]
    for i, ref in enumerate(refs):
        rows[i * size : (i + 1) * size] = ref[...]


def put_partial(partial, own_ref, sib_ref):
    half = own_ref.shape[0]
    own_ref[...] = partial[:half]
    sib_ref[...] = partial[half:].astype(BF)


def score_block(queries, keyset):
    scores = dot(queries, keyset, 1, 1) * HD ** (-0.5)
    column = lax.broadcasted_iota(jnp.int32, scores.shape, 1)
    scores = jnp.where(column < L, scores, -1e30)
    top = jnp.max(scores, axis=-1, keepdims=True)
    weight = jnp.exp(scores - top)
    return weight * (1.0 / jnp.sum(weight, axis=-1, keepdims=True)), top


def attend_kernel(
    at, live, a0, a1, a2, a3, w, mix_ref, att_ref, own_ref, sib_ref, peak_ref, rows
):
    fill(rows, a0, a1, a2, a3)
    part = mix_ref.shape[1] // 3
    mix_ref[...] = dot(rows[...], w[:, at : at + 3 * part], 1, 0).astype(BF)
    row_ok = lax.broadcasted_iota(jnp.int32, (ROWS, 1), 0) < L
    lane = lax.broadcasted_iota(jnp.int32, peak_ref.shape, 1)
    found = jnp.full(peak_ref.shape, -1e30, F32)
    for h in range(part // HD):
        for i in range(4):
            span = slice(i * ROWS, (i + 1) * ROWS)
            cut = [mix_ref[span, c * part + h * HD : c * part + (h + 1) * HD] for c in range(3)]
            probs, top = score_block(cut[0], cut[1])
            mixed = dot(probs.astype(BF), cut[2], 1, 0)
            att_ref[span, h * HD : (h + 1) * HD] = mixed.astype(BF)
            best = jnp.max(jnp.where(row_ok, top, -1e30), axis=0, keepdims=True)
            best = jnp.where(live[i] > 0, best, -1e30)
            found = jnp.where(lane == h, jnp.maximum(best, found), found)
    peak_ref[...] = found
    out = w[:, at + 3 * part : at + 4 * part]
    put_partial(dot(att_ref[...], out, 1, 1), own_ref, sib_ref)


def put_pack(grad, column, near, send):
    half = near.shape[0]
    near[:, column : column + grad.shape[1]] = grad[:half]
    send[:, column : column + grad.shape[1]] = grad[half:]


def attend_back_kernel(
    at, g0, g1, g2, g3, a0, a1, a2, a3, mix_ref, att_ref, w,
    near, send, own_ref, sib_ref, rows, grad_att, grad_mix,
):
    part = mix_ref.shape[1] // 3
    fill(rows, g0, g1, g2, g3)
    grad_att[...] = dot(rows[...], w[:, at + 3 * part : at + 4 * part], 1, 0).astype(BF)
    put_pack(dot(rows[...], att_ref[...], 0, 0).astype(BF), 3 * part, near, send)
    factor = HD ** (-0.5)
    for h in range(part // HD):
        for i in range(4):
            span = slice(i * ROWS, (i + 1) * ROWS)
            spans = [slice(c * part + h * HD, c * part + (h + 1) * HD) for c in range(3)]
            queries, keyset, values = (mix_ref[span, s] for s in spans)
            grad = grad_att[span, h * HD : (h + 1) * HD]
            probs, _ = score_block(queries, keyset)
            grad_mix[span, spans[2]] = dot(probs.astype(BF), grad, 0, 0).astype(BF)
            grad_probs = dot(grad, values, 1, 1)
            slope = probs * (grad_probs - jnp.sum(grad_probs * probs, axis=-1, keepdims=True))
            slope = slope.astype(BF)
            grad_mix[span, spans[0]] = (factor * dot(slope, keyset, 1, 0)).astype(BF)
            grad_mix[span, spans[1]] = (factor * dot(slope, queries, 0, 0)).astype(BF)
    put_partial(dot(grad_mix[...], w[:, at : at + 3 * part], 1, 1), own_ref, sib_ref)
    fill(rows, a0, a1, a2, a3)
    put_pack(dot(rows[...], grad_mix[...], 0, 0).astype(BF), 0, near, send)


def gelu_pair(hidden):
    cdf = 0.5 * (1.0 + lax.erf(hidden * 0.7071067811865476))
    slope = cdf + hidden * jnp.exp(-0.5 * hidden * hidden) * 0.3989422804014327
    return (hidden * cdf).astype(BF), slope.astype(BF)


def mlp_kernel(ats, b0, b1, b2, b3, w, act_ref, slope_ref, own_ref, sib_ref, rows):
    fill(rows, b0, b1, b2, b3)
    wide = act_ref.shape[1]
    for c in range(0, wide, 256):
        span = slice(c, c + 256)
        act, slope = gelu_pair(dot(rows[...], w[:, ats[0] + c : ats[0] + c + 256], 1, 0))
        act_ref[:, span] = act
        slope_ref[:, span] = slope
    put_partial(dot(act_ref[...], w[:, ats[1] : ats[1] + wide], 1, 1), own_ref, sib_ref)


def mlp_back_kernel(
    ats, g0, g1, g2, g3, b0, b1, b2, b3, act_ref, slope_ref, w,
    near, send, own_ref, sib_ref, rows, hidden,
):
    fill(rows, g0, g1, g2, g3)
    wide = act_ref.shape[1]
    grad = dot(rows[...], w[:, ats[1] : ats[1] + wide], 1, 0) * slope_ref[...].astype(F32)
    hidden[...] = grad.astype(BF)
    put_partial(dot(hidden[...], w[:, ats[0] : ats[0] + wide], 1, 1), own_ref, sib_ref)
    put_pack(dot(rows[...], act_ref[...], 0, 0).astype(BF), wide, near, send)
    fill(rows, b0, b1, b2, b3)
    put_pack(dot(rows[...], hidden[...], 0, 0).astype(BF), 0, near, send)


def picked(row_code, codes):
    hit = (row_code[...] == codes[0:1, :]) | (row_code[...] == codes[1:2, :])
    return jnp.where(hit, 1.0, 0.0).astype(BF)


def dispatch_kernel(row_code, codes, p0, p1, p2, p3, perm_ref, out, rows):
    fill(rows, p0, p1, p2, p3)
    picks = dot(picked(row_code, codes), rows[...], 1, 0).astype(BF)
    out[...] = dot(picks, perm_ref[...], 1, 0).astype(BF)


def token_kernel(row_code, codes, p0, p1, p2, p3, perm_ref, first_ref, second_ref, out, rows):
    dispatch_kernel(row_code, codes, p0, p1, p2, p3, perm_ref, out, rows)
    row = lax.broadcasted_iota(jnp.int32, (8, 128), 0)
    block = jnp.zeros((8, 128), F32)
    for i, ref in enumerate((first_ref, second_ref)):
        high = ref[...].astype(BF).astype(F32)
        block = jnp.where(row == 2 * i + 2, high, block)
        block = jnp.where(row == 2 * i + 3, ref[...] - high, block)
    size = out.shape[0] // 8
    for e in range(8):
        span = slice((e + 1) * size - 8, (e + 1) * size)
        old = out[span, :128].astype(F32)
        out[span, :128] = jnp.where((row >= 2) & (row < 6), block, old).astype(BF)


def collect_kernel(both_ref, grad_ref, out_ref, peak_ref):
    size = both_ref.shape[1] // 2
    best = jnp.full((2, 128), -1e30, F32)
    for p in range(both_ref.shape[0]):
        rows = slice(p * size, (p + 1) * size)
        grad_ref[rows] = both_ref[p, :size]
        out_ref[rows] = both_ref[p, size:]
        block = both_ref[p, 2 * size - 8 :, :128].astype(F32)
        found = [block[2 * i + 2 : 2 * i + 3] + block[2 * i + 3 : 2 * i + 4] for i in range(2)]
        best = jnp.maximum(best, jnp.concatenate(found, axis=0))
    peak_ref[...] = best


def combine_kernel(which, row_code, codes, perm_ref, both_ref, own_ref, sib_ref, rows):
    size = both_ref.shape[1] // 2
    for p in range(both_ref.shape[0]):
        rows[p * size : (p + 1) * size] = both_ref[p, which * size : (which + 1) * size]
    back = dot(rows[...], perm_ref[...], 1, 1).astype(BF)
    partial = dot(picked(row_code, codes), back, 0, 0)
    half = partial.shape[0] // 2
    own_ref[...] = partial[:half]
    sib_ref[...] = partial[half:].astype(BF)


def pair_add_kernel(own_ref, far_ref, near_ref, send_ref):
    total = own_ref[...] + far_ref[...].astype(F32)
    near_ref[...] = total[:ROWS]
    send_ref[...] = total[ROWS:].astype(BF)


def route_of(tokens, router, number):
    logits = dot(tokens, router, 1, 1)
    column = lax.broadcasted_iota(jnp.int32, logits.shape, 1)
    logits = jnp.where(column < 8, logits, -1e30)
    weight = jnp.exp(logits - jnp.max(logits, axis=-1, keepdims=True))
    route = weight / jnp.sum(weight, axis=-1, keepdims=True)
    mine = jnp.where(column == number, 1.0, 0.0)
    return route, mine, jnp.sum(route * mine, axis=-1, keepdims=True)


def expert_kernel(
    number, t0, t1, g0, g1, router, *rest
):
    own, far = rest[0], rest[1]
    res_own, res_sib, grad_own, grad_sib = rest[2:6]
    up_parts, down_parts = rest[6:10], rest[10:13]
    act_ref, hid_ref, gout_ref, pair, whole = rest[13:]
    size = t0.shape[0]
    half, wide = own.shape[0] // 2, act_ref.shape[2]
    whole[0] = own[...]
    whole[1] = far[...]
    for i, (t, g, res, grad) in enumerate(
        ((t1, g1, res_sib, grad_sib), (t0, g0, res_own, grad_own))
    ):
        rows = slice((1 - i) * size, (2 - i) * size)
        gate = route_of(t[...], router[...], number[0])[2]
        gout = (gate * g[...].astype(F32)).astype(BF)
        gout_ref[rows] = gout
        for y in range(2):
            for c in range(0, wide, 256):
                span = slice(c, c + 256)
                act, lean = gelu_pair(dot(t[...], whole[y, :, span], 1, 0))
                act_ref[y, rows, span] = act
                back = dot(gout, whole[y, :, wide + c : wide + c + 256], 1, 0)
                hid_ref[y, rows, span] = (back * lean.astype(F32)).astype(BF)
        res[...] = (
            dot(act_ref[0, rows], whole[0, :, wide:], 1, 1)
            + dot(act_ref[1, rows], whole[1, :, wide:], 1, 1)
        ).astype(res.dtype)
        grad[...] = (
            dot(hid_ref[0, rows], whole[0, :, :wide], 1, 1)
            + dot(hid_ref[1, rows], whole[1, :, :wide], 1, 1)
        ).astype(grad.dtype)
    pair[:size] = t0[...]
    pair[size:] = t1[...]
    for parts, left, right in ((up_parts, pair, hid_ref), (down_parts, gout_ref, act_ref)):
        parts[0][...] = dot(left[...], right[0], 0, 0).astype(BF)
        far = dot(left[...], right[1], 0, 0).astype(BF)
        at = 0
        for part in parts[1:]:
            part[...] = far[at : at + part.shape[0]]
            at += part.shape[0]


def answer_kernel(
    number, t_ref, g_ref, router, res_own, res_far, grad_own, grad_far, perm_ref,
    both_ref, router_out,
):
    route, mine, gate = route_of(t_ref[...], router[...], number[0])
    result = res_own[...] + res_far[...].astype(F32)
    grad_gate = jnp.sum(result * g_ref[...].astype(F32), axis=-1, keepdims=True)
    grad_logit = (grad_gate * route * (mine - gate)).astype(BF)
    router_out[...] = reorder(dot(grad_logit, t_ref[...], 0, 0), perm_ref[...], 1)
    grad = grad_own[...] + grad_far[...].astype(F32) + dot(grad_logit, router[...], 1, 0)
    size = both_ref.shape[1] // 2
    whole = grad.astype(BF)
    for p in range(both_ref.shape[0]):
        both_ref[p, :size] = whole[p * size : (p + 1) * size]
    whole = (gate * result).astype(BF)
    for p in range(both_ref.shape[0]):
        both_ref[p, size:] = whole[p * size : (p + 1) * size]


def reorder(values, perm, axis):
    high = values.astype(BF)
    rest = values - high.astype(F32)
    middle = rest.astype(BF)
    low = (rest - middle.astype(F32)).astype(BF)
    return dot(high, perm, 1, axis) + (dot(middle, perm, 1, axis) + dot(low, perm, 1, axis))


def leave_kernel(x_ref, perm_ref, out_ref):
    out_ref[...] = reorder(x_ref[...], perm_ref[...], 0)[: out_ref.shape[0]]


def finish_kernel(live, x_ref, own_ref, far_ref, perm_ref, out_ref):
    total = x_ref[...] + (own_ref[...] + far_ref[...].astype(F32))
    total = reorder(total, perm_ref[...], 0) * live[0].astype(F32)
    out_ref[...] = total[: out_ref.shape[0]]


def add_pack_kernel(up_own, up0, up1, up2, down_own, down0, down1, out):
    wide = up_own.shape[1]
    for c, (own, parts) in enumerate(((up_own, (up0, up1, up2)), (down_own, (down0, down1)))):
        at = 0
        for part in parts:
            span = slice(at, at + part.shape[0])
            total = own[span].astype(F32) + part[...].astype(F32)
            out[span, c * wide : (c + 1) * wide] = total.astype(BF)
            at += part.shape[0]


def pack_kernel(*refs):
    out = refs[-1]
    at = 0
    for ref in refs[:-1]:
        out[:, at : at + ref.shape[1]] = ref[...]
        at += ref.shape[1]


def stack_kernel(*refs):
    rows = refs[0].shape[0]
    for i, ref in enumerate(refs[:-1]):
        refs[-1][i * rows : (i + 1) * rows] = ref[...]


def order_kernel(places, in_ref, out_ref):
    rows = out_ref.shape[0] // 4
    for i in range(4):
        at = pl.multiple_of(places[i] * rows, rows)
        out_ref[i * rows : (i + 1) * rows] = in_ref[pl.ds(at, rows), :]


def sum_two(near, got, keep, s1, s2, s3):
    rows = keep.shape[0]
    for k, out in enumerate((keep, s1, s2, s3)):
        span = slice(k * rows, (k + 1) * rows)
        out[...] = (near[span].astype(F32) + got[span].astype(F32)).astype(out.dtype)


def small_kernel(g1, g2, g3, g4, router, out):
    whole = jnp.concatenate([g1[...], g2[...], g3[...], g4[...]], axis=0)
    count, cols = router.shape[0], out.shape[2]
    blank = jnp.zeros((out.shape[1] - 4 - count, cols), F32)
    for p in range(8):
        span = slice(p * cols, (p + 1) * cols)
        out[p] = jnp.concatenate([whole[:, span], router[:, span], blank], axis=0)


def sum_two_more(near, got, small, keep, s1, s2, s3):
    sum_two(near, got, keep, s1.at[: keep.shape[0]], s2.at[: keep.shape[0]], s3.at[: keep.shape[0]])
    rows, count = keep.shape[0], small.shape[1]
    cols = small.shape[2]
    for k, out in enumerate((s1, s2, s3)):
        out[rows:, :] = jnp.zeros((out.shape[0] - rows, out.shape[1]), BF)
        high = small[k + 1].astype(BF)
        out[rows : rows + count, :cols] = high
        low = small[k + 1] - high.astype(F32)
        out[rows + count : rows + 2 * count, :cols] = low.astype(BF)


def sum_three_more(keep, r1, r2, r3, small, first, second, small_out):
    rows, count = keep.shape[0], small.shape[1]
    cols = small.shape[2]
    sum_three(keep, r1.at[:rows], r2.at[:rows], r3.at[:rows], first, second)
    total = small[0]
    for r in (r1, r2, r3):
        high = r[rows : rows + count, :cols].astype(F32)
        total = total + (high + r[rows + count : rows + 2 * count, :cols].astype(F32))
    small_out[...] = total


def sum_three(keep, r1, r2, r3, first, second):
    total = keep[...] + (r1[...].astype(F32) + (r2[...].astype(F32) + r3[...].astype(F32)))
    wide = first.shape[1]
    first[...] = total[:, :wide]
    second[...] = total[:, wide:]


def scatter_start(parts):
    near, send = parts
    return near, swap(send, x=1)


def scatter_middle(parts):
    half, width = parts[0].shape
    shape = (half // 4, width)
    return run(sum_two, [(shape, F32)] + [(shape, BF)] * 3, parts, half * width)


def scatter_late(parts):
    keep, s1, s2, s3 = parts
    return keep, swap(s1, z=1), swap(s2, z=2), swap(s3, z=3)


def scatter_end(parts, wide):
    rows, width = parts[0].shape
    return run(sum_three, [((rows, wide), F32), ((rows, width - wide), F32)], parts, rows * width)


def fast_local(
    block_input,
    first_norm,
    first_qkv,
    first_out,
    second_norm,
    dense_up,
    dense_down,
    third_norm,
    second_qkv,
    second_out,
    fourth_norm,
    router_weight,
    expert_up,
    expert_down,
    expert_ids,
    expert_slots,
    image_counts,
    cotangent,
):
    d = lax.axis_index("dp")
    t = lax.axis_index("tensor")
    z_index, x_index = d // 2, d % 2
    width = first_norm.shape[0]
    features = width * 8
    experts = expert_up.shape[0]
    live_count = image_counts[0]
    head_cols = first_out.shape[0]
    ff_cols = dense_up.shape[1]
    qkv_cols = 3 * head_cols
    row = ((ROWS, features), F32)
    row_low = ((ROWS, features), BF)

    small = jnp.concatenate(
        [
            jnp.stack([first_norm, second_norm, third_norm, fourth_norm], axis=1),
            router_weight,
            jnp.zeros((width, 128 - 4 - experts), BF),
        ],
        axis=1,
    )
    pack_one = run(
        pack_kernel,
        [((width, small.shape[1] + 4 * head_cols), BF)],
        (small, first_qkv.reshape(width, -1), first_out.T),
        width,
    )[0]
    pack_late = run(
        pack_kernel,
        [((width, 2 * ff_cols + 4 * head_cols), BF)],
        (dense_up, dense_down.T, second_qkv.reshape(width, -1), second_out.T),
        width,
    )[0]

    lines = [[x + 2 * z for z in range(4)] for x in range(2)]
    raw_late = lax.all_gather(pack_late, "dp", axis=0, tiled=True, axis_index_groups=lines)

    def stacked(shards):
        shape = (len(shards) * shards[0].shape[0], shards[0].shape[1])
        return run(stack_kernel, [(shape, BF)], shards, width)[0]

    z_one = stacked([pack_one] + [swap(pack_one, z=k) for k in (1, 2, 3)])

    rel = jnp.arange(features)
    block = rel // width
    rel_place = jnp.bitwise_xor(d, 2 * (block % 4) + block // 4) * width + rel % width
    perm = (rel_place[:, None] == rel[None, :]).astype(BF)
    live_here = (t < live_count).astype(jnp.int32).reshape(1)
    live_group = (jnp.stack([t, t ^ 2, t ^ 1, t ^ 3]) < live_count).astype(jnp.int32)

    start, low_start, grad_four, grad_low = run(
        enter_kernel,
        [row, row_low, row, row_low],
        (live_here, block_input, cotangent, perm),
        4 * ROWS * features**2,
        scalars=1,
    )

    def spread(rows):
        far = swap(rows, y=1)
        return [rows, far, swap(rows, core=1), swap(far, core=1)]

    first_group = spread(low_start)
    wide = 2 * ff_cols
    half_shape = [((features // 2, ff_cols), BF)] * 2
    e_pack = jnp.concatenate([expert_up, jnp.swapaxes(expert_down, 1, 2)], axis=2)
    held = -(-CAP // 4)
    block_size = -(-(held + 4) // 8) * 8
    ids = jnp.pad(expert_ids.reshape(4, L, 2), ((0, 0), (0, ROWS - L), (0, 0)), constant_values=-1)
    slots = jnp.pad(
        expert_slots.reshape(4, L, 2), ((0, 0), (0, ROWS - L), (0, 0)), constant_values=CAP
    )
    mine = (slots < CAP) & (slots // held == t)
    codes = jnp.where(mine, ids * block_size + slots % held, -1)
    codes = jnp.concatenate(
        [lax.dynamic_index_in_dim(codes, t ^ k, 0, keepdims=False) for k in (0, 2, 1, 3)], axis=0
    ).T
    slot_rows = experts * block_size
    row_code = jnp.arange(slot_rows).reshape(-1, 1)
    group_flops = 2 * slot_rows * features * (4 * ROWS + features)

    def to_experts(kernel, rows, *peaks):
        return run(
            kernel,
            [((slot_rows, features), BF)],
            (row_code, codes, *rows, perm, *peaks),
            group_flops,
            scratch=[pltpu.VMEM((4 * ROWS, features), BF)],
        )[0].reshape(experts, block_size, features)

    def exchange(both):
        return lax.all_to_all(both, "dp", split_axis=0, concat_axis=0, tiled=True)

    group_scratch = pltpu.VMEM((4 * ROWS, features), BF)
    pair_out = [((2 * ROWS, features), F32), ((2 * ROWS, features), BF)]

    def attend(normed, full, at):
        return run(
            functools.partial(attend_kernel, at),
            [((4 * ROWS, qkv_cols), BF), ((4 * ROWS, head_cols), BF)]
            + pair_out
            + [((1, 128), F32)],
            (live_group, *normed, full),
            0,
            scratch=[group_scratch],
            scalars=1,
        )

    def pack_shapes(columns):
        return [((features // 2, columns), BF)] * 2 + pair_out

    def attend_back(low, normed, mixed, attended, full, at):
        return run(
            functools.partial(attend_back_kernel, at),
            pack_shapes(4 * head_cols),
            (*low, *normed, mixed, attended, full),
            8e9,
            scratch=[
                group_scratch,
                pltpu.VMEM((4 * ROWS, head_cols), BF),
                pltpu.VMEM((4 * ROWS, qkv_cols), BF),
            ],
        )

    def over_group(own, sib):
        near, send = run(pair_add_kernel, [row, row_low], (own, swap(sib, core=1)), ROWS)
        return near, swap(send, y=1)

    def join(values, own, far, gain):
        return run(join_norm_kernel, [row, row_low], (values, own, far, gain), ROWS)

    def norm_back(values, upstream, own, far, gain):
        return run(
            norm_back_kernel,
            [row, row_low, ((1, features), F32)],
            (values, upstream, own, far, gain),
            ROWS,
        )

    full_one = stacked(hold([z_one, swap(z_one, x=1)], first_group))
    small_rows = full_one[:, : 4 + experts].T
    gains = [small_rows[i : i + 1].astype(F32) for i in range(4)]
    router = dot(small_rows[4:], perm, 1, 0).astype(BF)

    normed_one = run(norm_kernel, [row_low] * 4, (gains[0], *first_group), ROWS)
    mixed_one, att_one, own, sib, peak_one = attend(normed_one, full_one, small.shape[1])
    near, far = over_group(own, sib)
    one, normed = join(start, near, hold(far, raw_late), gains[1])
    normed_mlp = spread(normed)
    z_late = run(
        order_kernel,
        [(raw_late.shape, BF)],
        (jnp.stack([z_index ^ k for k in range(4)]).astype(jnp.int32), hold(raw_late, one)),
        features,
        scalars=1,
    )[0]
    x_late = swap(z_late, x=1)
    grad_sent = to_experts(dispatch_kernel, spread(hold(grad_low, normed)))
    e_pack = hold(e_pack, grad_sent, x_late, normed_mlp)
    e_own = lax.all_to_all(e_pack, "dp", split_axis=0, concat_axis=0, tiled=True)
    e_own = e_own.reshape(features, wide)
    full_late = stacked([z_late, x_late])
    ats = (0, ff_cols)
    act, slope, own, sib = run(
        functools.partial(mlp_kernel, ats),
        [((4 * ROWS, ff_cols), BF)] * 2 + pair_out,
        (*hold(normed_mlp, grad_sent), full_late),
        0,
        scratch=[group_scratch],
    )
    near, far = over_group(own, sib)
    two, normed = join(one, near, far, gains[2])
    normed_two = spread(normed)
    mixed_two, att_two, own, sib, peak_two = attend(normed_two, full_late, 2 * ff_cols)
    near, far = over_group(own, sib)
    three, normed = join(two, near, far, gains[3])
    group_four = spread(normed)
    e_far = [swap(hold(e_own, group_four[1]), y=1)]
    tokens_sent = to_experts(token_kernel, group_four, peak_one, peak_two)
    both = exchange(jnp.concatenate([grad_sent, tokens_sent], axis=1))
    grad_slots, tokens, peaks = run(
        collect_kernel,
        [((slot_rows, features), BF)] * 2 + [((2, 128), F32)],
        (hold(both, *e_far),),
        0,
    )
    far_slots, far_tokens = swap(grad_slots, core=1), swap(tokens, core=1)
    number = d.astype(jnp.int32).reshape(1)
    near_heads = head_cols // HD
    roots = clip_root(peaks[:, :near_heads])
    slot_out = [((slot_rows, features), F32), ((slot_rows, features), BF)]
    res_own, res_sib, eg_own, eg_sib, *e_packs = run(
        expert_kernel,
        slot_out
        + slot_out
        + [((features, ff_cols), BF)]
        + [((2 * width, ff_cols), BF)] * 2
        + half_shape[:1]
        + [((features, ff_cols), BF)]
        + half_shape,
        (number, tokens, far_tokens, grad_slots, far_slots, router)
        + (e_own, *e_far),
        8 * 2 * slot_rows * features * 2 * ff_cols,
        scalars=1,
        scratch=[
            pltpu.VMEM((2, 2 * slot_rows, ff_cols), BF),
            pltpu.VMEM((2, 2 * slot_rows, ff_cols), BF),
            pltpu.VMEM((2 * slot_rows, features), BF),
            pltpu.VMEM((2 * slot_rows, features), BF),
            pltpu.VMEM((2, features, wide), BF),
        ],
        mib=44,
    )
    res_far, eg_far = swap(res_sib, core=1), swap(eg_sib, core=1)
    up_got = [swap(e_packs[1], y=1)]
    both, grad_router = run(
        answer_kernel,
        [((experts, 2 * block_size, features), BF), ((experts, features), F32)],
        (number, tokens, grad_slots, router, res_own, res_far, eg_own, eg_far, perm),
        4 * slot_rows * features**2,
        scalars=1,
    )
    both = hold(both, up_got)
    e_packs = hold(e_packs, both)
    both = exchange(both)
    up_got.append(swap(e_packs[2], y=1))
    up_got.append(swap(e_packs[3], y=1))
    down_got = [swap(e_packs[5], y=1)]
    both = hold(both, up_got, down_got)

    def combine(which, both):
        return run(
            functools.partial(combine_kernel, which),
            [((2 * ROWS, features), F32), ((2 * ROWS, features), BF)],
            (row_code, codes, perm, both),
            group_flops,
            scratch=[pltpu.VMEM((slot_rows, features), BF)],
        )

    own, sib = combine(0, both)
    back_own, back_far = over_group(own, sib)
    grad_three, low, gain_four = norm_back(
        three, grad_four, back_own, back_far, gains[3]
    )
    low = spread(low)
    down_got.append(swap(hold(e_packs[6], low[1]), y=1))
    *second, own, sib = attend_back(
        low, normed_two, mixed_two, att_two, full_late, 2 * ff_cols
    )
    second = scatter_start(second)
    near, far = over_group(own, hold(sib, down_got[1]))
    e_sum = run(
        add_pack_kernel,
        [((features, wide), BF)],
        (e_packs[0], *up_got, e_packs[4], *hold(down_got, second[1], far)),
        0,
    )[0].reshape(experts, width, wide)
    e_back = lax.all_to_all(e_sum, "dp", split_axis=0, concat_axis=0, tiled=True)
    grad_two, low, gain_three = norm_back(
        two, grad_three, near, far, gains[2]
    )
    low = spread(low)
    *mlp, own, sib = run(
        functools.partial(mlp_back_kernel, ats),
        pack_shapes(2 * ff_cols),
        (*low, *normed_mlp, act, slope, full_late),
        0,
        scratch=[group_scratch, pltpu.VMEM((4 * ROWS, ff_cols), BF)],
    )
    mlp = scatter_start(mlp)
    near, send = run(pair_add_kernel, [row, row_low], (own, swap(sib, core=1)), ROWS)
    far = swap(send, y=1)
    mixed_own, mixed_sib = combine(1, hold(both, sib))
    second = scatter_late(scatter_middle(hold(second, mixed_own)))
    mixed_own, mixed_send = run(
        pair_add_kernel, [row, row_low], (mixed_own, swap(mixed_sib, core=1)), ROWS
    )
    grad_one, low, gain_two = norm_back(
        one, grad_two, near, hold(far, mixed_send), gains[1]
    )
    low = spread(low)
    mixed_far = swap(hold(mixed_send, low), y=1)
    *first, own, sib = attend_back(
        hold(low, mlp),
        normed_one,
        mixed_one,
        att_one,
        full_one,
        small.shape[1],
    )
    mlp = scatter_late(scatter_middle(mlp))
    first = scatter_start(first)
    near, far = over_group(own, hold(sib, mixed_far, second, e_back))
    grad_zero, _, gain_one = norm_back(start, grad_one, near, hold(far, first), gains[0])
    block_output = run(
        finish_kernel,
        [((L, features), F32)],
        (live_here, three, mixed_own, mixed_far, perm),
        6 * ROWS * features**2,
        scalars=1,
    )[0]
    up_g = e_back[:, :, :ff_cols].astype(F32)
    down_g = jnp.swapaxes(e_back[:, :, ff_cols:], 1, 2).astype(F32)
    clips = (clip_columns(first_qkv, roots[0], HD), clip_columns(second_qkv, roots[1], HD))
    gains_sum = run(
        small_kernel,
        [((8, 16, width), F32)],
        (gain_one, gain_two, gain_three, gain_four, grad_router),
        0,
    )[0]
    gains_sum = hold(
        gains_sum + swap(gains_sum, core=1), mlp, block_output, up_g, down_g, clips
    )
    gains_sum = gains_sum + swap(gains_sum, y=1)
    gains_sum = gains_sum[:4] + swap(gains_sum[4:], x=1)
    near_first, got_first = first
    shape = (width, 4 * head_cols)
    first = run(
        sum_two_more,
        [(shape, F32)] + [((width + 32, shape[1]), BF)] * 3,
        (near_first, got_first, gains_sum),
        0,
    )
    first = scatter_late(first)
    input_grad = run(
        leave_kernel,
        [((L, features), F32)],
        (hold(grad_zero, first[0]), perm),
        6 * ROWS * features**2,
    )[0]
    second = scatter_end(second, qkv_cols)
    mlp = scatter_end(mlp, ff_cols)
    first = hold(first, up_g, down_g, block_output, input_grad, second, mlp)
    *first, tail = run(
        sum_three_more,
        [((width, qkv_cols), F32), ((width, head_cols), F32), ((16, width), F32)],
        (*first, gains_sum),
        0,
    )

    return (
        block_output,
        input_grad,
        tail[0],
        first[0].reshape(first_qkv.shape),
        first[1].T,
        tail[1],
        mlp[0],
        mlp[1].T,
        tail[2],
        second[0].reshape(second_qkv.shape),
        second[1].T,
        tail[3],
        tail[4 : 4 + experts].T,
        up_g,
        down_g,
        *clips,
        roots,
    )


def solution(mesh):
    placed = (
        P(("dp", "tensor"), None),
        P("dp"),
        P("dp", None, "tensor"),
        P("tensor", "dp"),
        P("dp"),
        P("dp", "tensor"),
        P("tensor", "dp"),
        P("dp"),
        P("dp", None, "tensor"),
        P("tensor", "dp"),
        P("dp"),
        P("dp", None),
        P(None, "dp", "tensor"),
        P(None, "tensor", "dp"),
        P("dp", None),
        P("dp", None),
        P("dp"),
        P(("dp", "tensor"), None),
    )
    quick = mesh.shape["dp"] == 8 and mesh.shape["tensor"] == 4
    return jax.shard_map(
        fast_local if quick else local,
        mesh=mesh,
        in_specs=placed,
        out_specs=(
            P(("dp", "tensor"), None),
            P(("dp", "tensor"), None),
            P("dp"),
            P("dp", None, "tensor"),
            P("tensor", "dp"),
            P("dp"),
            P("dp", "tensor"),
            P("tensor", "dp"),
            P("dp"),
            P("dp", None, "tensor"),
            P("tensor", "dp"),
            P("dp"),
            P("dp", None),
            P(None, "dp", "tensor"),
            P(None, "tensor", "dp"),
            P("dp", None, "tensor"),
            P("dp", None, "tensor"),
            P(None, "tensor"),
        ),
        check_vma=False,
    )
```

```python
import functools

import jax
import jax.numpy as jnp
from jax import lax
from jax.experimental import pallas as pl
from jax.experimental.pallas import tpu as pltpu
from jax.sharding import PartitionSpec as P

HD = 64
L = 197
CAP = 197


epsilon = 1e-06
clip_tau = 2.5


def layer_norm(values, norm_gain):
    center = values - jnp.mean(values, axis=-1, keepdims=True)
    spread = jnp.mean(center * center, axis=-1, keepdims=True)
    return center * lax.rsqrt(spread + epsilon) * norm_gain


def exact_gelu(values):
    return jax.nn.gelu(values, approximate=False)


def gelu_back(values, upstream):
    return jax.vjp(exact_gelu, values)[1](upstream)[0]


def norm_back(residual, norm_gain, upstream):
    pullback = jax.vjp(layer_norm, residual, norm_gain.astype(jnp.float32))[1]
    return pullback(upstream)


def gather_rows(values):
    return lax.all_gather(values, "tensor", axis=0, tiled=True)


def scatter_rows(values):
    return lax.psum_scatter(
        values.astype(jnp.bfloat16), "tensor", scatter_dimension=0, tiled=True
    ).astype(jnp.float32)


def sum_gains(first_gain, second_gain):
    return lax.psum((first_gain, second_gain), "tensor")


def split_heads(projected, images, head_size):
    row_count, triple, columns = projected.shape
    pieces = projected.reshape(images, row_count // images, triple, columns // head_size, head_size)
    return (pieces[:, :, 0], pieces[:, :, 1], pieces[:, :, 2])


def attend_scores(queries, keyset, head_size):
    scores = jnp.einsum("iqhd,ikhd->ihqk", queries, keyset, preferred_element_type=jnp.float32)
    return scores * head_size ** (-0.5)


def attend_forward(normed_full, weight_qkv, images, head_size, live_images):
    projected = jnp.einsum(
        "rd,dcf->rcf", normed_full, weight_qkv, preferred_element_type=jnp.float32
    ).astype(jnp.bfloat16)
    queries, keyset, values = split_heads(projected, images, head_size)
    scores = attend_scores(queries, keyset, head_size)
    head_peak = jnp.max(jnp.where(live_images[:, None, None, None], scores, -1e30), axis=(0, 2, 3))
    attn_probs = jax.nn.softmax(scores, axis=-1).astype(jnp.bfloat16)
    attended = jnp.einsum("ihqk,ikhd->iqhd", attn_probs, values, preferred_element_type=jnp.float32)
    return (projected, attended.astype(jnp.bfloat16).reshape(normed_full.shape[0], -1), head_peak)


def attend_backward(projected, grad_attended, images, head_size):
    queries, keyset, values = split_heads(projected, images, head_size)
    scores = attend_scores(queries, keyset, head_size)
    attn_probs = jax.nn.softmax(scores, axis=-1)
    grad_heads = grad_attended.reshape(queries.shape)
    grad_values = jnp.einsum(
        "ihqk,iqhd->ikhd",
        attn_probs.astype(jnp.bfloat16),
        grad_heads,
        preferred_element_type=jnp.float32,
    )
    grad_probs = jnp.einsum(
        "iqhd,ikhd->ihqk", grad_heads, values, preferred_element_type=jnp.float32
    )
    grad_scores = attn_probs * (
        grad_probs - jnp.sum(grad_probs * attn_probs, axis=-1, keepdims=True)
    )
    grad_scores = grad_scores.astype(jnp.bfloat16)
    factor = head_size ** (-0.5)
    grad_queries = (
        jnp.einsum("ihqk,ikhd->iqhd", grad_scores, keyset, preferred_element_type=jnp.float32)
        * factor
    )
    grad_keyset = (
        jnp.einsum("ihqk,iqhd->ikhd", grad_scores, queries, preferred_element_type=jnp.float32)
        * factor
    )
    stacked = jnp.stack([grad_queries, grad_keyset, grad_values], axis=2).astype(jnp.bfloat16)
    return stacked.reshape(projected.shape)


def block_attention(residual, norm_gain, weight_qkv, weight_out, images, head_size, live_images):
    normed = layer_norm(residual, norm_gain.astype(jnp.float32)).astype(jnp.bfloat16)
    normed_full = gather_rows(normed)
    projected, attended, head_peak = attend_forward(
        normed_full, weight_qkv, images, head_size, live_images
    )
    branch = scatter_rows(jnp.dot(attended, weight_out, preferred_element_type=jnp.float32))
    return (residual + branch, (normed_full, projected, attended), head_peak)


def block_attention_back(
    residual, upstream, norm_gain, weight_qkv, weight_out, stored, images, head_size
):
    normed_full, projected, attended = stored
    grad_full = gather_rows(upstream.astype(jnp.bfloat16))
    grad_out = jnp.einsum("rf,rd->fd", attended, grad_full, preferred_element_type=jnp.float32)
    grad_attended = jnp.einsum(
        "rd,fd->rf", grad_full, weight_out, preferred_element_type=jnp.float32
    ).astype(jnp.bfloat16)
    grad_projected = attend_backward(projected, grad_attended, images, head_size)
    grad_qkv = jnp.einsum(
        "rd,rcf->dcf", normed_full, grad_projected, preferred_element_type=jnp.float32
    )
    grad_normed = scatter_rows(
        jnp.einsum("rcf,dcf->rd", grad_projected, weight_qkv, preferred_element_type=jnp.float32)
    )
    grad_residual, grad_gain = norm_back(residual, norm_gain, grad_normed)
    return (upstream + grad_residual, grad_gain, grad_qkv, grad_out)


def block_mlp(residual, norm_gain, weight_up, weight_down):
    normed = layer_norm(residual, norm_gain.astype(jnp.float32)).astype(jnp.bfloat16)
    normed_full = gather_rows(normed)
    hidden = jnp.dot(normed_full, weight_up, preferred_element_type=jnp.float32)
    active = exact_gelu(hidden).astype(jnp.bfloat16)
    branch = scatter_rows(jnp.dot(active, weight_down, preferred_element_type=jnp.float32))
    return (residual + branch, (normed_full, hidden, active))


def block_mlp_back(residual, upstream, norm_gain, weight_up, weight_down, stored):
    normed_full, hidden, active = stored
    grad_full = gather_rows(upstream.astype(jnp.bfloat16))
    grad_down = jnp.einsum("rf,rd->fd", active, grad_full, preferred_element_type=jnp.float32)
    grad_active = jnp.einsum(
        "rd,fd->rf", grad_full, weight_down, preferred_element_type=jnp.float32
    )
    grad_hidden = gelu_back(hidden, grad_active).astype(jnp.bfloat16)
    grad_up = jnp.einsum("rd,rf->df", normed_full, grad_hidden, preferred_element_type=jnp.float32)
    grad_normed = scatter_rows(
        jnp.einsum("rf,df->rd", grad_hidden, weight_up, preferred_element_type=jnp.float32)
    )
    grad_residual, grad_gain = norm_back(residual, norm_gain, grad_normed)
    return (upstream + grad_residual, grad_gain, grad_up, grad_down)


def clip_root(head_peak):
    return jnp.sqrt(clip_tau / jnp.maximum(head_peak, clip_tau))


def clip_columns(weight_local, head_root, head_size):
    column = jnp.repeat(head_root, head_size)
    scales = jnp.stack([column, column, jnp.ones_like(column)])
    return weight_local.astype(jnp.float32) * scales[None]


def local(
    block_input,
    first_norm,
    first_qkv,
    first_out,
    second_norm,
    dense_up,
    dense_down,
    third_norm,
    second_qkv,
    second_out,
    fourth_norm,
    router_weight,
    expert_up,
    expert_down,
    expert_ids,
    expert_slots,
    image_counts,
    cotangent,
):
    rows_local = block_input.shape[0]
    rows_full = rows_local * lax.axis_size("tensor")
    images = rows_full // L
    head_size = HD
    experts = expert_up.shape[0]
    capacity = CAP
    first_row = lax.axis_index("tensor") * rows_local
    live_count = image_counts[0]
    local_live = ((first_row + jnp.arange(rows_local)) // L < live_count).astype(jnp.float32)
    full_live = (jnp.arange(rows_full) // L < live_count).astype(jnp.float32)
    live_images = jnp.arange(images) < live_count

    def dense_fetch():
        return (
            lax.all_gather(first_norm, "dp", axis=0, tiled=True),
            lax.all_gather(first_qkv, "dp", axis=0, tiled=True),
            lax.all_gather(first_out, "dp", axis=1, tiled=True),
            lax.all_gather(second_norm, "dp", axis=0, tiled=True),
            lax.all_gather(dense_up, "dp", axis=0, tiled=True),
            lax.all_gather(dense_down, "dp", axis=1, tiled=True),
        )

    def moe_fetch():
        return (
            lax.all_gather(third_norm, "dp", axis=0, tiled=True),
            lax.all_gather(second_qkv, "dp", axis=0, tiled=True),
            lax.all_gather(second_out, "dp", axis=1, tiled=True),
            lax.all_gather(fourth_norm, "dp", axis=0, tiled=True),
            lax.all_gather(router_weight, "dp", axis=0, tiled=True),
            lax.all_gather(expert_up, "dp", axis=1, tiled=True),
            lax.all_gather(expert_down, "dp", axis=2, tiled=True),
        )

    dense_full = dense_fetch()
    residual_zero = block_input.astype(jnp.float32)
    residual_one, attn_first, peak_first = block_attention(
        residual_zero, dense_full[0], dense_full[1], dense_full[2], images, head_size, live_images
    )
    residual_two, mlp_stored = block_mlp(residual_one, dense_full[3], dense_full[4], dense_full[5])
    moe_full = moe_fetch()
    residual_three, attn_second, peak_second = block_attention(
        residual_two, moe_full[0], moe_full[1], moe_full[2], images, head_size, live_images
    )
    moe_normed = layer_norm(residual_three, moe_full[3].astype(jnp.float32)).astype(jnp.bfloat16)
    moe_input = gather_rows(moe_normed)
    logits = jnp.dot(moe_input, moe_full[4], preferred_element_type=jnp.float32)
    route_probs = jax.nn.softmax(logits, axis=-1)
    kept_mask = expert_slots < capacity
    pair_number = jnp.arange(2 * rows_full, dtype=jnp.int32)
    slot_index = (expert_ids * capacity + expert_slots).reshape(-1)
    kept_flat = kept_mask.reshape(-1)
    write_target = jnp.where(kept_flat, slot_index, experts * capacity + pair_number)
    target = jnp.where(kept_flat, slot_index, experts * capacity)
    pair_of_slot = (
        jnp.zeros((experts * capacity + 2 * rows_full,), jnp.int32)
        .at[write_target]
        .set(pair_number)[: experts * capacity]
    )
    slot_filled = (
        jnp.zeros((experts * capacity + 2 * rows_full,), jnp.float32)
        .at[write_target]
        .set(1.0)[: experts * capacity]
    )
    chosen = (expert_ids[:, :, None] == jnp.arange(experts)[None, None, :]).astype(jnp.float32)
    keep_live = kept_mask.astype(jnp.float32) * full_live[:, None]
    gates = jnp.sum(chosen * route_probs[:, None, :], axis=-1) * keep_live
    slot_token = pair_of_slot // 2
    slot_gate = gates.reshape(-1)[pair_of_slot] * slot_filled
    dispatched = (moe_input[slot_token] * slot_filled[:, None].astype(jnp.bfloat16)).reshape(
        experts, capacity, -1
    )
    expert_hidden = jnp.einsum(
        "ecd,edf->ecf", dispatched, moe_full[5], preferred_element_type=jnp.float32
    )
    expert_act = exact_gelu(expert_hidden).astype(jnp.bfloat16)
    expert_result = jnp.einsum(
        "ecf,efd->ecd", expert_act, moe_full[6], preferred_element_type=jnp.float32
    )
    feature_count = expert_result.shape[2]
    padded_result = jnp.concatenate(
        [
            expert_result.reshape(experts * capacity, feature_count),
            jnp.zeros((1, feature_count), jnp.float32),
        ],
        axis=0,
    )
    pair_result = padded_result[target].reshape(rows_full, 2, feature_count)
    combined = jnp.sum(gates[:, :, None] * pair_result, axis=1)
    residual_four = residual_three + scatter_rows(combined)
    block_output = residual_four * local_live[:, None]
    peak_first_all, peak_second_all = lax.pmax((peak_first, peak_second), "dp")
    root_first = clip_root(peak_first_all)
    root_second = clip_root(peak_second_all)
    clipped_first = clip_columns(first_qkv, root_first, head_size)
    clipped_second = clip_columns(second_qkv, root_second, head_size)
    clip_scales = jnp.stack([root_first, root_second])
    moe_back = moe_fetch()
    grad_four = cotangent.astype(jnp.float32) * local_live[:, None]
    moe_grad_full = gather_rows(grad_four.astype(jnp.bfloat16))
    partial_gates = jnp.sum(moe_grad_full.astype(jnp.float32)[:, None, :] * pair_result, axis=-1)
    grad_gates = lax.psum(partial_gates, "tensor")
    grad_result = (slot_gate[:, None] * moe_grad_full[slot_token].astype(jnp.float32)).astype(
        jnp.bfloat16
    )
    grad_result = grad_result.reshape(experts, capacity, feature_count)
    grad_expert_down = jnp.einsum(
        "ecf,ecd->efd", expert_act, grad_result, preferred_element_type=jnp.float32
    )
    grad_act = jnp.einsum(
        "ecd,efd->ecf", grad_result, moe_back[6], preferred_element_type=jnp.float32
    )
    grad_hidden = gelu_back(expert_hidden, grad_act).astype(jnp.bfloat16)
    grad_expert_up = jnp.einsum(
        "ecd,ecf->edf", dispatched, grad_hidden, preferred_element_type=jnp.float32
    )
    grad_dispatch = jnp.einsum(
        "ecf,edf->ecd", grad_hidden, moe_back[5], preferred_element_type=jnp.float32
    )
    grad_dispatch = jnp.concatenate(
        [
            grad_dispatch.reshape(experts * capacity, feature_count),
            jnp.zeros((1, feature_count), jnp.float32),
        ],
        axis=0,
    )
    grad_from_experts = jnp.sum(grad_dispatch[target].reshape(rows_full, 2, feature_count), axis=1)
    grad_picked = grad_gates * keep_live
    grad_probs = jnp.sum(chosen * grad_picked[:, :, None], axis=1)
    grad_logits = route_probs * (
        grad_probs - jnp.sum(grad_probs * route_probs, axis=-1, keepdims=True)
    )
    grad_logits = grad_logits.astype(jnp.bfloat16)
    grad_router = jnp.einsum(
        "rd,re->de", moe_input, grad_logits, preferred_element_type=jnp.float32
    )
    local_logits = lax.dynamic_slice_in_dim(grad_logits, first_row, rows_local, 0)
    grad_moe_normed = scatter_rows(grad_from_experts) + jnp.einsum(
        "re,de->rd", local_logits, moe_back[4], preferred_element_type=jnp.float32
    )
    grad_rows_four, grad_fourth_norm = norm_back(residual_three, moe_back[3], grad_moe_normed)
    grad_three = grad_four + grad_rows_four
    grad_two, grad_third_norm, grad_second_qkv, grad_second_out = block_attention_back(
        residual_two,
        grad_three,
        moe_back[0],
        moe_back[1],
        moe_back[2],
        attn_second,
        images,
        head_size,
    )
    third_sum, fourth_sum = sum_gains(grad_third_norm, grad_fourth_norm)
    moe_owned = (
        lax.psum_scatter(third_sum, "dp", scatter_dimension=0, tiled=True),
        lax.psum_scatter(grad_second_qkv, "dp", scatter_dimension=0, tiled=True),
        lax.psum_scatter(grad_second_out, "dp", scatter_dimension=1, tiled=True),
        lax.psum_scatter(fourth_sum, "dp", scatter_dimension=0, tiled=True),
        lax.psum_scatter(grad_router, "dp", scatter_dimension=0, tiled=True),
        lax.psum_scatter(grad_expert_up, "dp", scatter_dimension=1, tiled=True),
        lax.psum_scatter(grad_expert_down, "dp", scatter_dimension=2, tiled=True),
    )
    dense_back = dense_fetch()
    grad_one, grad_second_norm, grad_dense_up, grad_dense_down = block_mlp_back(
        residual_one, grad_two, dense_back[3], dense_back[4], dense_back[5], mlp_stored
    )
    input_grad, grad_first_norm, grad_first_qkv, grad_first_out = block_attention_back(
        residual_zero,
        grad_one,
        dense_back[0],
        dense_back[1],
        dense_back[2],
        attn_first,
        images,
        head_size,
    )
    first_sum, second_sum = sum_gains(grad_first_norm, grad_second_norm)
    dense_owned = (
        lax.psum_scatter(first_sum, "dp", scatter_dimension=0, tiled=True),
        lax.psum_scatter(grad_first_qkv, "dp", scatter_dimension=0, tiled=True),
        lax.psum_scatter(grad_first_out, "dp", scatter_dimension=1, tiled=True),
        lax.psum_scatter(second_sum, "dp", scatter_dimension=0, tiled=True),
        lax.psum_scatter(grad_dense_up, "dp", scatter_dimension=0, tiled=True),
        lax.psum_scatter(grad_dense_down, "dp", scatter_dimension=1, tiled=True),
    )
    owned = tuple(dense_owned) + tuple(moe_owned)
    return (
        block_output,
        input_grad,
        owned[0],
        owned[1],
        owned[2],
        owned[3],
        owned[4],
        owned[5],
        owned[6],
        owned[7],
        owned[8],
        owned[9],
        owned[10],
        owned[11],
        owned[12],
        clipped_first,
        clipped_second,
        clip_scales,
    )


ROWS = 208
AXES = ("dp", "tensor")
BF = jnp.bfloat16
F32 = jnp.float32
VM = pl.BlockSpec(memory_space=pltpu.VMEM)
SM = pl.BlockSpec(memory_space=pltpu.SMEM)


def swap(values, z=0, x=0, y=0, core=0):
    shift_d, shift_t = 2 * z + x, 2 * y + core
    pairs = [(d * 4 + t, (d ^ shift_d) * 4 + (t ^ shift_t)) for d in range(8) for t in range(4)]
    return lax.ppermute(values, AXES, pairs)


def hold(values, *tokens):
    return lax.optimization_barrier((values,) + tokens)[0]


def run(kernel, outs, args, flops, scratch=(), scalars=0, mib=20):
    flops = flops if flops == 8e9 else 1000
    shapes = [jax.ShapeDtypeStruct(s, dt) for s, dt in outs]
    return pl.pallas_call(
        kernel,
        out_shape=shapes,
        in_specs=[SM] * scalars + [VM] * (len(args) - scalars),
        out_specs=[VM] * len(shapes),
        scratch_shapes=list(scratch),
        compiler_params=pltpu.CompilerParams(vmem_limit_bytes=mib * 2**20),
        cost_estimate=pl.CostEstimate(flops=int(flops), bytes_accessed=1000, transcendentals=0),
    )(*args)


def dot(a, b, ca, cb):
    return lax.dot_general(a, b, (((ca,), (cb,)), ((), ())), preferred_element_type=F32)


def norm_stats(values):
    center = values - jnp.mean(values, axis=-1, keepdims=True)
    scale = lax.rsqrt(jnp.mean(center * center, axis=-1, keepdims=True) + epsilon)
    return center * scale, scale


def enter_kernel(live, x_ref, c_ref, perm_ref, start_ref, low_start, grad_ref, low_ref):
    rows = x_ref.shape[0]
    scale = live[0].astype(F32)
    extra = jnp.zeros((ROWS - rows, x_ref.shape[1]), F32)
    start = dot(x_ref[...], perm_ref[...], 1, 1)
    start_ref[:rows] = start
    start_ref[rows:] = extra
    low_start[:rows] = start.astype(BF)
    low_start[rows:] = extra.astype(BF)
    grad = dot(c_ref[...], perm_ref[...], 1, 1) * scale
    grad_ref[:rows] = grad
    grad_ref[rows:] = extra
    low_ref[:rows] = grad.astype(BF)
    low_ref[rows:] = extra.astype(BF)


def norm_kernel(gain_ref, *refs):
    for x_ref, out_ref in zip(refs[:4], refs[4:]):
        out_ref[...] = (norm_stats(x_ref[...].astype(F32))[0] * gain_ref[...]).astype(BF)


def join_norm_kernel(x_ref, own_ref, far_ref, gain_ref, sum_ref, out_ref):
    total = x_ref[...] + (own_ref[...] + far_ref[...].astype(F32))
    sum_ref[...] = total
    out_ref[...] = (norm_stats(total)[0] * gain_ref[...]).astype(BF)


def norm_back_kernel(x_ref, up_ref, own_ref, far_ref, gain_ref, grad_ref, low_ref, gain_out):
    upstream = own_ref[...] + far_ref[...].astype(F32)
    normed, scale = norm_stats(x_ref[...])
    scaled = upstream * gain_ref[...]
    grad = up_ref[...] + scale * (
        scaled
        - jnp.mean(scaled, axis=-1, keepdims=True)
        - normed * jnp.mean(scaled * normed, axis=-1, keepdims=True)
    )
    grad_ref[...] = grad
    low_ref[...] = grad.astype(BF)
    gain_out[...] = jnp.sum(upstream * normed, axis=0, keepdims=True)


def fill(rows, *refs):
    size = refs[0].shape[0]
    for i, ref in enumerate(refs):
        rows[i * size : (i + 1) * size] = ref[...]


def put_partial(partial, own_ref, sib_ref):
    half = own_ref.shape[0]
    own_ref[...] = partial[:half]
    sib_ref[...] = partial[half:].astype(BF)


def score_block(queries, keyset):
    scores = dot(queries, keyset, 1, 1) * HD ** (-0.5)
    column = lax.broadcasted_iota(jnp.int32, scores.shape, 1)
    scores = jnp.where(column < L, scores, -1e30)
    top = jnp.max(scores, axis=-1, keepdims=True)
    weight = jnp.exp(scores - top)
    return weight * (1.0 / jnp.sum(weight, axis=-1, keepdims=True)), top


def attend_kernel(
    at, live, a0, a1, a2, a3, w, mix_ref, att_ref, own_ref, sib_ref, peak_ref, rows
):
    fill(rows, a0, a1, a2, a3)
    part = mix_ref.shape[1] // 3
    mix_ref[...] = dot(rows[...], w[:, at : at + 3 * part], 1, 0).astype(BF)
    row_ok = lax.broadcasted_iota(jnp.int32, (ROWS, 1), 0) < L
    lane = lax.broadcasted_iota(jnp.int32, peak_ref.shape, 1)
    found = jnp.full(peak_ref.shape, -1e30, F32)
    for h in range(part // HD):
        for i in range(4):
            span = slice(i * ROWS, (i + 1) * ROWS)
            cut = [mix_ref[span, c * part + h * HD : c * part + (h + 1) * HD] for c in range(3)]
            probs, top = score_block(cut[0], cut[1])
            mixed = dot(probs.astype(BF), cut[2], 1, 0)
            att_ref[span, h * HD : (h + 1) * HD] = mixed.astype(BF)
            best = jnp.max(jnp.where(row_ok, top, -1e30), axis=0, keepdims=True)
            best = jnp.where(live[i] > 0, best, -1e30)
            found = jnp.where(lane == h, jnp.maximum(best, found), found)
    peak_ref[...] = found
    out = w[:, at + 3 * part : at + 4 * part]
    put_partial(dot(att_ref[...], out, 1, 1), own_ref, sib_ref)


def put_pack(grad, column, near, send):
    half = near.shape[0]
    near[:, column : column + grad.shape[1]] = grad[:half]
    send[:, column : column + grad.shape[1]] = grad[half:]


def attend_back_kernel(
    at, g0, g1, g2, g3, a0, a1, a2, a3, mix_ref, att_ref, w,
    near, send, own_ref, sib_ref, rows, grad_att, grad_mix,
):
    part = mix_ref.shape[1] // 3
    fill(rows, g0, g1, g2, g3)
    grad_att[...] = dot(rows[...], w[:, at + 3 * part : at + 4 * part], 1, 0).astype(BF)
    put_pack(dot(rows[...], att_ref[...], 0, 0).astype(BF), 3 * part, near, send)
    factor = HD ** (-0.5)
    for h in range(part // HD):
        for i in range(4):
            span = slice(i * ROWS, (i + 1) * ROWS)
            spans = [slice(c * part + h * HD, c * part + (h + 1) * HD) for c in range(3)]
            queries, keyset, values = (mix_ref[span, s] for s in spans)
            grad = grad_att[span, h * HD : (h + 1) * HD]
            probs, _ = score_block(queries, keyset)
            grad_mix[span, spans[2]] = dot(probs.astype(BF), grad, 0, 0).astype(BF)
            grad_probs = dot(grad, values, 1, 1)
            slope = probs * (grad_probs - jnp.sum(grad_probs * probs, axis=-1, keepdims=True))
            slope = slope.astype(BF)
            grad_mix[span, spans[0]] = (factor * dot(slope, keyset, 1, 0)).astype(BF)
            grad_mix[span, spans[1]] = (factor * dot(slope, queries, 0, 0)).astype(BF)
    put_partial(dot(grad_mix[...], w[:, at : at + 3 * part], 1, 1), own_ref, sib_ref)
    fill(rows, a0, a1, a2, a3)
    put_pack(dot(rows[...], grad_mix[...], 0, 0).astype(BF), 0, near, send)


def gelu_pair(hidden):
    cdf = 0.5 * (1.0 + lax.erf(hidden * 0.7071067811865476))
    slope = cdf + hidden * jnp.exp(-0.5 * hidden * hidden) * 0.3989422804014327
    return (hidden * cdf).astype(BF), slope.astype(BF)


def mlp_kernel(ats, b0, b1, b2, b3, w, act_ref, slope_ref, own_ref, sib_ref, rows):
    fill(rows, b0, b1, b2, b3)
    wide = act_ref.shape[1]
    for c in range(0, wide, 256):
        span = slice(c, c + 256)
        act, slope = gelu_pair(dot(rows[...], w[:, ats[0] + c : ats[0] + c + 256], 1, 0))
        act_ref[:, span] = act
        slope_ref[:, span] = slope
    put_partial(dot(act_ref[...], w[:, ats[1] : ats[1] + wide], 1, 1), own_ref, sib_ref)


def mlp_back_kernel(
    ats, g0, g1, g2, g3, b0, b1, b2, b3, act_ref, slope_ref, w,
    near, send, own_ref, sib_ref, rows, hidden,
):
    fill(rows, g0, g1, g2, g3)
    wide = act_ref.shape[1]
    grad = dot(rows[...], w[:, ats[1] : ats[1] + wide], 1, 0) * slope_ref[...].astype(F32)
    hidden[...] = grad.astype(BF)
    put_partial(dot(hidden[...], w[:, ats[0] : ats[0] + wide], 1, 1), own_ref, sib_ref)
    put_pack(dot(rows[...], act_ref[...], 0, 0).astype(BF), wide, near, send)
    fill(rows, b0, b1, b2, b3)
    put_pack(dot(rows[...], hidden[...], 0, 0).astype(BF), 0, near, send)


def picked(row_code, codes):
    hit = (row_code[...] == codes[0:1, :]) | (row_code[...] == codes[1:2, :])
    return jnp.where(hit, 1.0, 0.0).astype(BF)


def dispatch_kernel(row_code, codes, p0, p1, p2, p3, perm_ref, out, rows):
    fill(rows, p0, p1, p2, p3)
    picks = dot(picked(row_code, codes), rows[...], 1, 0).astype(BF)
    out[...] = dot(picks, perm_ref[...], 1, 0).astype(BF)


def token_kernel(row_code, codes, p0, p1, p2, p3, perm_ref, first_ref, second_ref, out, rows):
    dispatch_kernel(row_code, codes, p0, p1, p2, p3, perm_ref, out, rows)
    row = lax.broadcasted_iota(jnp.int32, (8, 128), 0)
    block = jnp.zeros((8, 128), F32)
    for i, ref in enumerate((first_ref, second_ref)):
        high = ref[...].astype(BF).astype(F32)
        block = jnp.where(row == 2 * i + 2, high, block)
        block = jnp.where(row == 2 * i + 3, ref[...] - high, block)
    size = out.shape[0] // 8
    for e in range(8):
        span = slice((e + 1) * size - 8, (e + 1) * size)
        old = out[span, :128].astype(F32)
        out[span, :128] = jnp.where((row >= 2) & (row < 6), block, old).astype(BF)


def collect_kernel(both_ref, grad_ref, out_ref, peak_ref):
    size = both_ref.shape[1] // 2
    best = jnp.full((2, 128), -1e30, F32)
    for p in range(both_ref.shape[0]):
        rows = slice(p * size, (p + 1) * size)
        grad_ref[rows] = both_ref[p, :size]
        out_ref[rows] = both_ref[p, size:]
        block = both_ref[p, 2 * size - 8 :, :128].astype(F32)
        found = [block[2 * i + 2 : 2 * i + 3] + block[2 * i + 3 : 2 * i + 4] for i in range(2)]
        best = jnp.maximum(best, jnp.concatenate(found, axis=0))
    peak_ref[...] = best


def combine_kernel(which, row_code, codes, perm_ref, both_ref, own_ref, sib_ref, rows):
    size = both_ref.shape[1] // 2
    for p in range(both_ref.shape[0]):
        rows[p * size : (p + 1) * size] = both_ref[p, which * size : (which + 1) * size]
    back = dot(rows[...], perm_ref[...], 1, 1).astype(BF)
    partial = dot(picked(row_code, codes), back, 0, 0)
    half = partial.shape[0] // 2
    own_ref[...] = partial[:half]
    sib_ref[...] = partial[half:].astype(BF)


def pair_add_kernel(own_ref, far_ref, near_ref, send_ref):
    total = own_ref[...] + far_ref[...].astype(F32)
    near_ref[...] = total[:ROWS]
    send_ref[...] = total[ROWS:].astype(BF)


def route_of(tokens, router, number):
    logits = dot(tokens, router, 1, 1)
    column = lax.broadcasted_iota(jnp.int32, logits.shape, 1)
    logits = jnp.where(column < 8, logits, -1e30)
    weight = jnp.exp(logits - jnp.max(logits, axis=-1, keepdims=True))
    route = weight / jnp.sum(weight, axis=-1, keepdims=True)
    mine = jnp.where(column == number, 1.0, 0.0)
    return route, mine, jnp.sum(route * mine, axis=-1, keepdims=True)


def expert_kernel(
    number, t0, t1, g0, g1, router, *rest
):
    own, far = rest[0], rest[1]
    res_own, res_sib, grad_own, grad_sib = rest[2:6]
    up_parts, down_parts = rest[6:10], rest[10:13]
    act_ref, hid_ref, gout_ref, pair, whole = rest[13:]
    size = t0.shape[0]
    half, wide = own.shape[0] // 2, act_ref.shape[2]
    whole[0] = own[...]
    whole[1] = far[...]
    for i, (t, g, res, grad) in enumerate(
        ((t1, g1, res_sib, grad_sib), (t0, g0, res_own, grad_own))
    ):
        rows = slice((1 - i) * size, (2 - i) * size)
        gate = route_of(t[...], router[...], number[0])[2]
        gout = (gate * g[...].astype(F32)).astype(BF)
        gout_ref[rows] = gout
        for y in range(2):
            for c in range(0, wide, 256):
                span = slice(c, c + 256)
                act, lean = gelu_pair(dot(t[...], whole[y, :, span], 1, 0))
                act_ref[y, rows, span] = act
                back = dot(gout, whole[y, :, wide + c : wide + c + 256], 1, 0)
                hid_ref[y, rows, span] = (back * lean.astype(F32)).astype(BF)
        res[...] = (
            dot(act_ref[0, rows], whole[0, :, wide:], 1, 1)
            + dot(act_ref[1, rows], whole[1, :, wide:], 1, 1)
        ).astype(res.dtype)
        grad[...] = (
            dot(hid_ref[0, rows], whole[0, :, :wide], 1, 1)
            + dot(hid_ref[1, rows], whole[1, :, :wide], 1, 1)
        ).astype(grad.dtype)
    pair[:size] = t0[...]
    pair[size:] = t1[...]
    for parts, left, right in ((up_parts, pair, hid_ref), (down_parts, gout_ref, act_ref)):
        parts[0][...] = dot(left[...], right[0], 0, 0).astype(BF)
        far = dot(left[...], right[1], 0, 0).astype(BF)
        at = 0
        for part in parts[1:]:
            part[...] = far[at : at + part.shape[0]]
            at += part.shape[0]


def answer_kernel(
    number, t_ref, g_ref, router, res_own, res_far, grad_own, grad_far, perm_ref,
    both_ref, router_out,
):
    route, mine, gate = route_of(t_ref[...], router[...], number[0])
    result = res_own[...] + res_far[...].astype(F32)
    grad_gate = jnp.sum(result * g_ref[...].astype(F32), axis=-1, keepdims=True)
    grad_logit = (grad_gate * route * (mine - gate)).astype(BF)
    router_out[...] = reorder(dot(grad_logit, t_ref[...], 0, 0), perm_ref[...], 1)
    grad = grad_own[...] + grad_far[...].astype(F32) + dot(grad_logit, router[...], 1, 0)
    size = both_ref.shape[1] // 2
    whole = grad.astype(BF)
    for p in range(both_ref.shape[0]):
        both_ref[p, :size] = whole[p * size : (p + 1) * size]
    whole = (gate * result).astype(BF)
    for p in range(both_ref.shape[0]):
        both_ref[p, size:] = whole[p * size : (p + 1) * size]


def reorder(values, perm, axis):
    high = values.astype(BF)
    rest = values - high.astype(F32)
    middle = rest.astype(BF)
    low = (rest - middle.astype(F32)).astype(BF)
    return dot(high, perm, 1, axis) + (dot(middle, perm, 1, axis) + dot(low, perm, 1, axis))


def leave_kernel(x_ref, perm_ref, out_ref):
    out_ref[...] = reorder(x_ref[...], perm_ref[...], 0)[: out_ref.shape[0]]


def finish_kernel(live, x_ref, own_ref, far_ref, perm_ref, out_ref):
    total = x_ref[...] + (own_ref[...] + far_ref[...].astype(F32))
    total = reorder(total, perm_ref[...], 0) * live[0].astype(F32)
    out_ref[...] = total[: out_ref.shape[0]]


def add_pack_kernel(up_own, up0, up1, up2, down_own, down0, down1, out):
    wide = up_own.shape[1]
    for c, (own, parts) in enumerate(((up_own, (up0, up1, up2)), (down_own, (down0, down1)))):
        at = 0
        for part in parts:
            span = slice(at, at + part.shape[0])
            total = own[span].astype(F32) + part[...].astype(F32)
            out[span, c * wide : (c + 1) * wide] = total.astype(BF)
            at += part.shape[0]


def pack_kernel(*refs):
    out = refs[-1]
    at = 0
    for ref in refs[:-1]:
        out[:, at : at + ref.shape[1]] = ref[...]
        at += ref.shape[1]


def stack_kernel(*refs):
    rows = refs[0].shape[0]
    for i, ref in enumerate(refs[:-1]):
        refs[-1][i * rows : (i + 1) * rows] = ref[...]


def order_kernel(places, in_ref, out_ref):
    rows = out_ref.shape[0] // 4
    for i in range(4):
        at = pl.multiple_of(places[i] * rows, rows)
        out_ref[i * rows : (i + 1) * rows] = in_ref[pl.ds(at, rows), :]


def sum_two(near, got, keep, s1, s2, s3):
    rows = keep.shape[0]
    for k, out in enumerate((keep, s1, s2, s3)):
        span = slice(k * rows, (k + 1) * rows)
        out[...] = (near[span].astype(F32) + got[span].astype(F32)).astype(out.dtype)


def small_kernel(g1, g2, g3, g4, router, out):
    whole = jnp.concatenate([g1[...], g2[...], g3[...], g4[...]], axis=0)
    count, cols = router.shape[0], out.shape[2]
    blank = jnp.zeros((out.shape[1] - 4 - count, cols), F32)
    for p in range(8):
        span = slice(p * cols, (p + 1) * cols)
        out[p] = jnp.concatenate([whole[:, span], router[:, span], blank], axis=0)


def sum_two_more(near, got, small, keep, s1, s2, s3):
    sum_two(near, got, keep, s1.at[: keep.shape[0]], s2.at[: keep.shape[0]], s3.at[: keep.shape[0]])
    rows, count = keep.shape[0], small.shape[1]
    cols = small.shape[2]
    for k, out in enumerate((s1, s2, s3)):
        out[rows:, :] = jnp.zeros((out.shape[0] - rows, out.shape[1]), BF)
        high = small[k + 1].astype(BF)
        out[rows : rows + count, :cols] = high
        low = small[k + 1] - high.astype(F32)
        out[rows + count : rows + 2 * count, :cols] = low.astype(BF)


def sum_three_more(keep, r1, r2, r3, small, first, second, small_out):
    rows, count = keep.shape[0], small.shape[1]
    cols = small.shape[2]
    sum_three(keep, r1.at[:rows], r2.at[:rows], r3.at[:rows], first, second)
    total = small[0]
    for r in (r1, r2, r3):
        high = r[rows : rows + count, :cols].astype(F32)
        total = total + (high + r[rows + count : rows + 2 * count, :cols].astype(F32))
    small_out[...] = total


def sum_three(keep, r1, r2, r3, first, second):
    total = keep[...] + (r1[...].astype(F32) + (r2[...].astype(F32) + r3[...].astype(F32)))
    wide = first.shape[1]
    first[...] = total[:, :wide]
    second[...] = total[:, wide:]


def scatter_start(parts):
    near, send = parts
    return near, swap(send, x=1)


def scatter_middle(parts):
    half, width = parts[0].shape
    shape = (half // 4, width)
    return run(sum_two, [(shape, F32)] + [(shape, BF)] * 3, parts, half * width)


def scatter_late(parts):
    keep, s1, s2, s3 = parts
    return keep, swap(s1, z=1), swap(s2, z=2), swap(s3, z=3)


def scatter_end(parts, wide):
    rows, width = parts[0].shape
    return run(sum_three, [((rows, wide), F32), ((rows, width - wide), F32)], parts, rows * width)


def fast_local(
    block_input,
    first_norm,
    first_qkv,
    first_out,
    second_norm,
    dense_up,
    dense_down,
    third_norm,
    second_qkv,
    second_out,
    fourth_norm,
    router_weight,
    expert_up,
    expert_down,
    expert_ids,
    expert_slots,
    image_counts,
    cotangent,
):
    d = lax.axis_index("dp")
    t = lax.axis_index("tensor")
    z_index, x_index = d // 2, d % 2
    width = first_norm.shape[0]
    features = width * 8
    experts = expert_up.shape[0]
    live_count = image_counts[0]
    head_cols = first_out.shape[0]
    ff_cols = dense_up.shape[1]
    qkv_cols = 3 * head_cols
    row = ((ROWS, features), F32)
    row_low = ((ROWS, features), BF)

    small = jnp.concatenate(
        [
            jnp.stack([first_norm, second_norm, third_norm, fourth_norm], axis=1),
            router_weight,
            jnp.zeros((width, 128 - 4 - experts), BF),
        ],
        axis=1,
    )
    pack_one = run(
        pack_kernel,
        [((width, small.shape[1] + 4 * head_cols), BF)],
        (small, first_qkv.reshape(width, -1), first_out.T),
        width,
    )[0]
    pack_late = run(
        pack_kernel,
        [((width, 2 * ff_cols + 4 * head_cols), BF)],
        (dense_up, dense_down.T, second_qkv.reshape(width, -1), second_out.T),
        width,
    )[0]

    lines = [[x + 2 * z for z in range(4)] for x in range(2)]
    raw_late = lax.all_gather(pack_late, "dp", axis=0, tiled=True, axis_index_groups=lines)

    def stacked(shards):
        shape = (len(shards) * shards[0].shape[0], shards[0].shape[1])
        return run(stack_kernel, [(shape, BF)], shards, width)[0]

    z_one = stacked([pack_one] + [swap(pack_one, z=k) for k in (1, 2, 3)])

    rel = jnp.arange(features)
    block = rel // width
    rel_place = jnp.bitwise_xor(d, 2 * (block % 4) + block // 4) * width + rel % width
    perm = (rel_place[:, None] == rel[None, :]).astype(BF)
    live_here = (t < live_count).astype(jnp.int32).reshape(1)
    live_group = (jnp.stack([t, t ^ 2, t ^ 1, t ^ 3]) < live_count).astype(jnp.int32)

    start, low_start, grad_four, grad_low = run(
        enter_kernel,
        [row, row_low, row, row_low],
        (live_here, block_input, cotangent, perm),
        4 * ROWS * features**2,
        scalars=1,
    )

    def spread(rows):
        far = swap(rows, y=1)
        return [rows, far, swap(rows, core=1), swap(far, core=1)]

    first_group = spread(low_start)
    wide = 2 * ff_cols
    half_shape = [((features // 2, ff_cols), BF)] * 2
    e_pack = jnp.concatenate([expert_up, jnp.swapaxes(expert_down, 1, 2)], axis=2)
    held = -(-CAP // 4)
    block_size = -(-(held + 4) // 8) * 8
    ids = jnp.pad(expert_ids.reshape(4, L, 2), ((0, 0), (0, ROWS - L), (0, 0)), constant_values=-1)
    slots = jnp.pad(
        expert_slots.reshape(4, L, 2), ((0, 0), (0, ROWS - L), (0, 0)), constant_values=CAP
    )
    mine = (slots < CAP) & (slots // held == t)
    codes = jnp.where(mine, ids * block_size + slots % held, -1)
    codes = jnp.concatenate(
        [lax.dynamic_index_in_dim(codes, t ^ k, 0, keepdims=False) for k in (0, 2, 1, 3)], axis=0
    ).T
    slot_rows = experts * block_size
    row_code = jnp.arange(slot_rows).reshape(-1, 1)
    group_flops = 2 * slot_rows * features * (4 * ROWS + features)

    def to_experts(kernel, rows, *peaks):
        return run(
            kernel,
            [((slot_rows, features), BF)],
            (row_code, codes, *rows, perm, *peaks),
            group_flops,
            scratch=[pltpu.VMEM((4 * ROWS, features), BF)],
        )[0].reshape(experts, block_size, features)

    def exchange(both):
        return lax.all_to_all(both, "dp", split_axis=0, concat_axis=0, tiled=True)

    group_scratch = pltpu.VMEM((4 * ROWS, features), BF)
    pair_out = [((2 * ROWS, features), F32), ((2 * ROWS, features), BF)]

    def attend(normed, full, at):
        return run(
            functools.partial(attend_kernel, at),
            [((4 * ROWS, qkv_cols), BF), ((4 * ROWS, head_cols), BF)]
            + pair_out
            + [((1, 128), F32)],
            (live_group, *normed, full),
            0,
            scratch=[group_scratch],
            scalars=1,
        )

    def pack_shapes(columns):
        return [((features // 2, columns), BF)] * 2 + pair_out

    def attend_back(low, normed, mixed, attended, full, at):
        return run(
            functools.partial(attend_back_kernel, at),
            pack_shapes(4 * head_cols),
            (*low, *normed, mixed, attended, full),
            8e9,
            scratch=[
                group_scratch,
                pltpu.VMEM((4 * ROWS, head_cols), BF),
                pltpu.VMEM((4 * ROWS, qkv_cols), BF),
            ],
        )

    def over_group(own, sib):
        near, send = run(pair_add_kernel, [row, row_low], (own, swap(sib, core=1)), ROWS)
        return near, swap(send, y=1)

    def join(values, own, far, gain):
        return run(join_norm_kernel, [row, row_low], (values, own, far, gain), ROWS)

    def norm_back(values, upstream, own, far, gain):
        return run(
            norm_back_kernel,
            [row, row_low, ((1, features), F32)],
            (values, upstream, own, far, gain),
            ROWS,
        )

    full_one = stacked(hold([z_one, swap(z_one, x=1)], first_group))
    small_rows = full_one[:, : 4 + experts].T
    gains = [small_rows[i : i + 1].astype(F32) for i in range(4)]
    router = dot(small_rows[4:], perm, 1, 0).astype(BF)

    normed_one = run(norm_kernel, [row_low] * 4, (gains[0], *first_group), ROWS)
    mixed_one, att_one, own, sib, peak_one = attend(normed_one, full_one, small.shape[1])
    near, far = over_group(own, sib)
    one, normed = join(start, near, hold(far, raw_late), gains[1])
    normed_mlp = spread(normed)
    z_late = run(
        order_kernel,
        [(raw_late.shape, BF)],
        (jnp.stack([z_index ^ k for k in range(4)]).astype(jnp.int32), hold(raw_late, one)),
        features,
        scalars=1,
    )[0]
    x_late = swap(z_late, x=1)
    grad_sent = to_experts(dispatch_kernel, spread(hold(grad_low, normed)))
    e_pack = hold(e_pack, grad_sent, x_late, normed_mlp)
    e_own = lax.all_to_all(e_pack, "dp", split_axis=0, concat_axis=0, tiled=True)
    e_own = e_own.reshape(features, wide)
    full_late = stacked([z_late, x_late])
    ats = (0, ff_cols)
    act, slope, own, sib = run(
        functools.partial(mlp_kernel, ats),
        [((4 * ROWS, ff_cols), BF)] * 2 + pair_out,
        (*hold(normed_mlp, grad_sent), full_late),
        0,
        scratch=[group_scratch],
    )
    near, far = over_group(own, sib)
    two, normed = join(one, near, far, gains[2])
    normed_two = spread(normed)
    mixed_two, att_two, own, sib, peak_two = attend(normed_two, full_late, 2 * ff_cols)
    near, far = over_group(own, sib)
    three, normed = join(two, near, far, gains[3])
    group_four = spread(normed)
    e_far = [swap(hold(e_own, group_four[1]), y=1)]
    tokens_sent = to_experts(token_kernel, group_four, peak_one, peak_two)
    both = exchange(jnp.concatenate([grad_sent, tokens_sent], axis=1))
    grad_slots, tokens, peaks = run(
        collect_kernel,
        [((slot_rows, features), BF)] * 2 + [((2, 128), F32)],
        (hold(both, *e_far),),
        0,
    )
    far_slots, far_tokens = swap(grad_slots, core=1), swap(tokens, core=1)
    number = d.astype(jnp.int32).reshape(1)
    near_heads = head_cols // HD
    roots = clip_root(peaks[:, :near_heads])
    slot_out = [((slot_rows, features), F32), ((slot_rows, features), BF)]
    res_own, res_sib, eg_own, eg_sib, *e_packs = run(
        expert_kernel,
        slot_out
        + slot_out
        + [((features, ff_cols), BF)]
        + [((2 * width, ff_cols), BF)] * 2
        + half_shape[:1]
        + [((features, ff_cols), BF)]
        + half_shape,
        (number, tokens, far_tokens, grad_slots, far_slots, router)
        + (e_own, *e_far),
        8 * 2 * slot_rows * features * 2 * ff_cols,
        scalars=1,
        scratch=[
            pltpu.VMEM((2, 2 * slot_rows, ff_cols), BF),
            pltpu.VMEM((2, 2 * slot_rows, ff_cols), BF),
            pltpu.VMEM((2 * slot_rows, features), BF),
            pltpu.VMEM((2 * slot_rows, features), BF),
            pltpu.VMEM((2, features, wide), BF),
        ],
        mib=44,
    )
    res_far, eg_far = swap(res_sib, core=1), swap(eg_sib, core=1)
    up_got = [swap(e_packs[1], y=1)]
    both, grad_router = run(
        answer_kernel,
        [((experts, 2 * block_size, features), BF), ((experts, features), F32)],
        (number, tokens, grad_slots, router, res_own, res_far, eg_own, eg_far, perm),
        4 * slot_rows * features**2,
        scalars=1,
    )
    both = hold(both, up_got)
    e_packs = hold(e_packs, both)
    both = exchange(both)
    up_got.append(swap(e_packs[2], y=1))
    up_got.append(swap(e_packs[3], y=1))
    down_got = [swap(e_packs[5], y=1)]
    both = hold(both, up_got, down_got)

    def combine(which, both):
        return run(
            functools.partial(combine_kernel, which),
            [((2 * ROWS, features), F32), ((2 * ROWS, features), BF)],
            (row_code, codes, perm, both),
            group_flops,
            scratch=[pltpu.VMEM((slot_rows, features), BF)],
        )

    own, sib = combine(0, both)
    back_own, back_far = over_group(own, sib)
    grad_three, low, gain_four = norm_back(
        three, grad_four, back_own, back_far, gains[3]
    )
    low = spread(low)
    down_got.append(swap(hold(e_packs[6], low[1]), y=1))
    *second, own, sib = attend_back(
        low, normed_two, mixed_two, att_two, full_late, 2 * ff_cols
    )
    second = scatter_start(second)
    near, far = over_group(own, hold(sib, down_got[1]))
    e_sum = run(
        add_pack_kernel,
        [((features, wide), BF)],
        (e_packs[0], *up_got, e_packs[4], *hold(down_got, second[1], far)),
        0,
    )[0].reshape(experts, width, wide)
    e_back = lax.all_to_all(e_sum, "dp", split_axis=0, concat_axis=0, tiled=True)
    grad_two, low, gain_three = norm_back(
        two, grad_three, near, far, gains[2]
    )
    low = spread(low)
    *mlp, own, sib = run(
        functools.partial(mlp_back_kernel, ats),
        pack_shapes(2 * ff_cols),
        (*low, *normed_mlp, act, slope, full_late),
        0,
        scratch=[group_scratch, pltpu.VMEM((4 * ROWS, ff_cols), BF)],
    )
    mlp = scatter_start(mlp)
    near, send = run(pair_add_kernel, [row, row_low], (own, swap(sib, core=1)), ROWS)
    far = swap(send, y=1)
    mixed_own, mixed_sib = combine(1, hold(both, sib))
    second = scatter_late(scatter_middle(hold(second, mixed_own)))
    mixed_own, mixed_send = run(
        pair_add_kernel, [row, row_low], (mixed_own, swap(mixed_sib, core=1)), ROWS
    )
    grad_one, low, gain_two = norm_back(
        one, grad_two, near, hold(far, mixed_send), gains[1]
    )
    low = spread(low)
    mixed_far = swap(hold(mixed_send, low), y=1)
    *first, own, sib = attend_back(
        low,
        normed_one,
        mixed_one,
        att_one,
        full_one,
        small.shape[1],
    )
    mlp = scatter_late(scatter_middle(mlp))
    first = scatter_start(first)
    near, far = over_group(own, hold(sib, mixed_far, second, e_back))
    grad_zero, _, gain_one = norm_back(start, grad_one, near, hold(far, first), gains[0])
    block_output = run(
        finish_kernel,
        [((L, features), F32)],
        (live_here, three, mixed_own, mixed_far, perm),
        6 * ROWS * features**2,
        scalars=1,
    )[0]
    up_g = e_back[:, :, :ff_cols].astype(F32)
    down_g = jnp.swapaxes(e_back[:, :, ff_cols:], 1, 2).astype(F32)
    clips = (clip_columns(first_qkv, roots[0], HD), clip_columns(second_qkv, roots[1], HD))
    gains_sum = run(
        small_kernel,
        [((8, 16, width), F32)],
        (gain_one, gain_two, gain_three, gain_four, grad_router),
        0,
    )[0]
    gains_sum = hold(
        gains_sum + swap(gains_sum, core=1), mlp, block_output, up_g, down_g, clips
    )
    gains_sum = gains_sum + swap(gains_sum, y=1)
    gains_sum = gains_sum[:4] + swap(gains_sum[4:], x=1)
    near_first, got_first = first
    shape = (width, 4 * head_cols)
    first = run(
        sum_two_more,
        [(shape, F32)] + [((width + 32, shape[1]), BF)] * 3,
        (near_first, got_first, gains_sum),
        0,
    )
    first = scatter_late(first)
    input_grad = run(
        leave_kernel,
        [((L, features), F32)],
        (hold(grad_zero, first[0]), perm),
        6 * ROWS * features**2,
    )[0]
    second = scatter_end(second, qkv_cols)
    mlp = scatter_end(mlp, ff_cols)
    first = hold(first, up_g, down_g, block_output, input_grad, second, mlp)
    *first, tail = run(
        sum_three_more,
        [((width, qkv_cols), F32), ((width, head_cols), F32), ((16, width), F32)],
        (*first, gains_sum),
        0,
    )

    return (
        block_output,
        input_grad,
        tail[0],
        first[0].reshape(first_qkv.shape),
        first[1].T,
        tail[1],
        mlp[0],
        mlp[1].T,
        tail[2],
        second[0].reshape(second_qkv.shape),
        second[1].T,
        tail[3],
        tail[4 : 4 + experts].T,
        up_g,
        down_g,
        *clips,
        roots,
    )


def solution(mesh):
    placed = (
        P(("dp", "tensor"), None),
        P("dp"),
        P("dp", None, "tensor"),
        P("tensor", "dp"),
        P("dp"),
        P("dp", "tensor"),
        P("tensor", "dp"),
        P("dp"),
        P("dp", None, "tensor"),
        P("tensor", "dp"),
        P("dp"),
        P("dp", None),
        P(None, "dp", "tensor"),
        P(None, "tensor", "dp"),
        P("dp", None),
        P("dp", None),
        P("dp"),
        P(("dp", "tensor"), None),
    )
    quick = mesh.shape["dp"] == 8 and mesh.shape["tensor"] == 4
    return jax.shard_map(
        fast_local if quick else local,
        mesh=mesh,
        in_specs=placed,
        out_specs=(
            P(("dp", "tensor"), None),
            P(("dp", "tensor"), None),
            P("dp"),
            P("dp", None, "tensor"),
            P("tensor", "dp"),
            P("dp"),
            P("dp", "tensor"),
            P("tensor", "dp"),
            P("dp"),
            P("dp", None, "tensor"),
            P("tensor", "dp"),
            P("dp"),
            P("dp", None),
            P(None, "dp", "tensor"),
            P(None, "tensor", "dp"),
            P("dp", None, "tensor"),
            P("dp", None, "tensor"),
            P(None, "tensor"),
        ),
        check_vma=False,
    )
```
